32 devices in a mesh: pole: 2 (over y), space: 16 (over z, x, core).
Axes of the slice: x: 2, y: 2, z: 4, core: 2. Of those that a mesh axis runs over, the one named last changes fastest.
Arguments:
- conductivity: float32 [32, 64, 128], P('space'), may hold values from 0.1 to 10
- misfit: float32 [32, 64, 128], P('space'), may hold values from -6 to 6
- forward_states: float32 [4, 32, 64, 128], P('pole', 'space'), may hold values from -6 to 6
- pole_shifts: float32 [4], replicated, may hold values from 0.01 to 10
- pole_weights: float32 [4], replicated, may hold values from 0.05 to 1
- pole_order: int32 [4], P('pole'), may hold values from 0 to 3, each once
Outputs:
- adjoint_states: float32 [4, 32, 64, 128], P('pole', 'space')
- gradient: float32 [32, 64, 128], P('space', 'pole')
The draws below stay inside these ranges and needn't reach their ends.
Inputs may be any that keep to these rules, and one draw needn't show every extreme that they name: `pole_order`: every pole stands in exactly one slot.
All inputs are finite; a program needn't handle non-finite values.
Results may differ from the reference program's by a relative error of at most 0.0001.
Values sent between devices are 32-bit elements; how exact they have to be, the bound alone decides.
No kernel may reach another device: no remote copies, remote signals or barrier semaphores. Data moves between devices by JAX's collectives and lax.ppermute only.
A program may use at most 128 MiB of HBM per device.

```python
import math
import jax
import jax.numpy as jnp
from jax import lax

NY = 64
NZ = 128
ITERS = 2
POLES = 4
NX = 32


def block_levels(key, shape, cuts, low, largest):
    factor_of = 1.0
    for dim, blocks in cuts:
        steps = jax.random.uniform(jax.random.fold_in(jax.random.fold_in(key, 6), dim), (blocks,), jnp.float32, low / len(cuts), largest / len(cuts))
        factor_of = factor_of * jnp.repeat(jnp.exp(steps), shape[dim] // blocks).reshape((-1,) + (1,) * (len(shape) - 1 - dim))
    return factor_of


def centred(own_key, dims, deviation, bound, shards=(), dtype=jnp.bfloat16):
    array = deviation * jax.random.normal(own_key, dims, jnp.float32)
    if shards:
        array = array * block_levels(own_key, dims, shards, -0.22, 0.18)
    return jnp.clip(array, -bound, bound).astype(dtype)


def setup_inputs(seed: int = 0) -> dict:
    key_of = jax.random.split(jax.random.key(seed), 7)
    conductivity = jnp.clip(jnp.exp(math.log(10.0) - 4.6051702 * jax.random.uniform(key_of[0], (NX, NY, NZ), jnp.float32) ** block_levels(key_of[0], (NX, NY, NZ), ((0, 16),), -0.2, 0.2)), 0.1, 10.0)
    misfit = centred(key_of[1], (NX, NY, NZ), 1.0, 6.0, ((0, 16),), jnp.float32)
    forward_states = centred(key_of[2], (POLES, NX, NY, NZ), 1.0, 6.0, ((0, 2), (1, 16)), jnp.float32)
    pole_shifts = jnp.clip(jnp.exp(jax.random.uniform(key_of[3], (POLES,), jnp.float32, math.log(0.01), math.log(10.0))), 0.01, 10.0)
    pole_weights = jnp.clip(jnp.exp(jax.random.uniform(key_of[4], (POLES,), jnp.float32, math.log(0.05), math.log(1.0))), 0.05, 1.0)
    pole_order = jax.random.permutation(key_of[5], POLES).astype(jnp.int32)
    return dict(conductivity=conductivity, misfit=misfit, forward_states=forward_states, pole_shifts=pole_shifts, pole_weights=pole_weights, pole_order=pole_order)


DAMPING = 0.8


def plus_side(field, which_dim):
    extent = field.shape[which_dim]
    inner_part = lax.slice_in_dim(field, 1, extent, axis=which_dim)
    zero_plane = jnp.zeros_like(lax.slice_in_dim(field, 0, 1, axis=which_dim))
    return jnp.concatenate([inner_part, zero_plane], axis=which_dim)


def minus_side(field, which_dim):
    extent = field.shape[which_dim]
    inner_part = lax.slice_in_dim(field, 0, extent - 1, axis=which_dim)
    zero_plane = jnp.zeros_like(lax.slice_in_dim(field, 0, 1, axis=which_dim))
    return jnp.concatenate([zero_plane, inner_part], axis=which_dim)


def coarse_pick(faces, which_dim, offset):
    extent_x, extent_y, extent_z = faces.shape
    blocks = faces.reshape(extent_x // 2, 2, extent_y // 2, 2, extent_z // 2, 2)
    chosen = lax.index_in_dim(blocks, offset, axis=2 * which_dim + 1, keepdims=True)
    return jnp.sum(chosen, axis=(1, 3, 5))


def operate(field, plus_faces, minus_faces, shift_value):
    result = shift_value * field
    for which_dim in range(3):
        result = result + plus_faces[which_dim] * (field - plus_side(field, which_dim))
        result = result + minus_faces[which_dim] * (field - minus_side(field, which_dim))
    return result


def restrict(field):
    extent_x, extent_y, extent_z = field.shape
    return jnp.sum(field.reshape(extent_x // 2, 2, extent_y // 2, 2, extent_z // 2, 2), axis=(1, 3, 5))


def prolong(field):
    return jnp.repeat(jnp.repeat(jnp.repeat(field, 2, axis=0), 2, axis=1), 2, axis=2)


def precondition(residual, fine, coarse):
    plus_faces, minus_faces, shift_value, diagonal = fine
    coarse_plus, coarse_minus, coarse_shift, coarse_diagonal = coarse
    smooth_one = DAMPING * residual / diagonal
    coarse_rhs = restrict(residual - operate(smooth_one, plus_faces, minus_faces, shift_value))
    coarse_one = DAMPING * coarse_rhs / coarse_diagonal
    coarse_two = coarse_one + DAMPING * (coarse_rhs - operate(coarse_one, coarse_plus, coarse_minus, coarse_shift)) / coarse_diagonal
    corrected = smooth_one + prolong(coarse_two)
    return corrected + DAMPING * (residual - operate(corrected, plus_faces, minus_faces, shift_value)) / diagonal


def solve(rhs, fine, coarse):
    plus_faces, minus_faces, shift_value, diagonal = fine
    iterate = jnp.zeros_like(rhs)
    residual = rhs
    precond = precondition(residual, fine, coarse)
    gamma_now = jnp.sum(residual * precond)
    search = precond
    for turn_index in range(ITERS):
        image_field = operate(search, plus_faces, minus_faces, shift_value)
        step_length = gamma_now / jnp.sum(search * image_field)
        iterate = iterate + step_length * search
        if turn_index + 1 < ITERS:
            residual = residual - step_length * image_field
            precond = precondition(residual, fine, coarse)
            gamma_next = jnp.sum(residual * precond)
            search = precond + (gamma_next / gamma_now) * search
            gamma_now = gamma_next
    return iterate


def reference(conductivity, misfit, forward_states, pole_shifts, pole_weights, pole_order):
    plus_faces = [0.5 * (conductivity + plus_side(conductivity, which_dim)) for which_dim in range(3)]
    minus_faces = [0.5 * (conductivity + minus_side(conductivity, which_dim)) for which_dim in range(3)]
    base_diagonal = plus_faces[0] + plus_faces[1] + plus_faces[2] + minus_faces[0] + minus_faces[1] + minus_faces[2]
    coarse_plus = [coarse_pick(plus_faces[which_dim], which_dim, 1) for which_dim in range(3)]
    coarse_minus = [coarse_pick(minus_faces[which_dim], which_dim, 0) for which_dim in range(3)]
    coarse_base = coarse_plus[0] + coarse_plus[1] + coarse_plus[2] + coarse_minus[0] + coarse_minus[1] + coarse_minus[2]

    def one_slot(total, slot_items):
        state, pole = slot_items
        shift_value = pole_shifts[pole]
        weight = pole_weights[pole]
        fine = (plus_faces, minus_faces, shift_value, base_diagonal + shift_value)
        coarse = (coarse_plus, coarse_minus, 8.0 * shift_value, coarse_base + 8.0 * shift_value)
        adjoint = solve(weight * misfit, fine, coarse)
        term = jnp.zeros_like(conductivity)
        for which_dim in range(3):
            term = term + (adjoint - plus_side(adjoint, which_dim)) * (state - plus_side(state, which_dim))
            term = term + (adjoint - minus_side(adjoint, which_dim)) * (state - minus_side(state, which_dim))
        return total - 0.5 * term, adjoint

    gradient, adjoint_states = lax.scan(one_slot, jnp.zeros_like(conductivity), (forward_states, pole_order))
    return adjoint_states, gradient
```

```python
import functools

import jax
import jax.numpy as jnp
from jax import lax
from jax.experimental import pallas as pl
from jax.experimental.pallas import tpu as pltpu
from jax.sharding import PartitionSpec as P

ITERS = 2
DAMPING = 0.8
REPLICATED_CELLS = 32 * 64 * 128
HALF = 64


def extended(array, sides, width):
    for axis, dim in sides:
        peers, length = (lax.axis_size(axis), array.shape[dim])
        up = [(i, (i + 1) % peers) for i in range(peers - 1)]
        down = [(j, i) for i, j in up]
        last = lax.slice_in_dim(array, length - width, length, axis=dim)
        leading = lax.slice_in_dim(array, 0, width, axis=dim)
        before = lax.ppermute(last, axis, up)
        after = lax.ppermute(leading, axis, down)
        array = jnp.concatenate([before, array, after], axis=dim)
    return array


def lane_index(shape):
    return lax.broadcasted_iota(jnp.int32, shape, len(shape) - 1)


def row_index(shape):
    return lax.broadcasted_iota(jnp.int32, shape, len(shape) - 2)


def roll(block, shift, axis):
    return pltpu.roll(block, shift % block.shape[axis], axis)


def eights(block):
    rows = block.shape[0]
    total = block[0:8]
    for start in range(8, rows, 8):
        total = total + block[start : start + 8]
    return total


def slot_totals(acc):
    line = jnp.sum(acc, axis=0, keepdims=True)
    lane = lane_index(line.shape)
    first = jnp.sum(jnp.where(lane < HALF, line, 0.0), axis=1, keepdims=True)
    second = jnp.sum(jnp.where(lane < HALF, 0.0, line), axis=1, keepdims=True)
    return jnp.where(lane < HALF, first, second)


def solve_kernel(
    place_ref,
    shifts_ref,
    weights_ref,
    order_ref,
    kappa_ref,
    misfit_ref,
    before_ref,
    state_ref,
    after_ref,
    adjoint_ref,
    share_ref,
    half_kappa,
    inner,
    outer_x,
    outer_y,
    outer_z,
    inner_sum,
    diagonal,
    damped,
    coarse_off,
    coarse_damped,
    residual,
    scaled,
    partial,
    first_dir,
    second_dir,
    image,
    coarse_one,
    coarse_two,
    planes,
):
    coarse_x = kappa_ref.shape[0] // 2
    rows = kappa_ref.shape[1] // 2
    shape = (rows, 2 * HALF)
    lane = lane_index(shape)
    row = row_index(shape)
    slot0 = lane_index((1, 2 * HALF)) < HALF

    def pick(ref):
        return jnp.where(slot0, ref[order_ref[0]], ref[order_ref[1]])

    shift = pick(shifts_ref)
    weight = pick(weights_ref)

    def cls(a, b, c):
        return 4 * a + 2 * b + c

    classes = [(a, b, c) for a in (0, 1) for b in (0, 1) for c in (0, 1)]

    zero = jnp.zeros(shape, jnp.float32)
    for ref in (half_kappa, scaled, first_dir, second_dir):
        for k in range(8):
            ref[k, 0] = zero
            ref[k, coarse_x + 1] = zero
    for ref in (coarse_one, coarse_two):
        ref[0] = zero
        ref[coarse_x + 1] = zero

    even_lane = 2 * (lane % HALF)

    def split(ref, x, b):
        block = ref[x, pl.ds(b, rows, stride=2), :]
        even = jnp.take_along_axis(block, even_lane, axis=1)
        odd = jnp.take_along_axis(block, even_lane + 1, axis=1)
        return even, odd

    def arrange(i, carry):
        for a in (0, 1):
            for b in (0, 1):
                for c, value in enumerate(split(kappa_ref, 2 * i + a, b)):
                    half_kappa[cls(a, b, c), i + 1] = 0.5 * value
                for c, value in enumerate(split(misfit_ref, 2 * i + a, b)):
                    residual[cls(a, b, c), i] = weight * value
        return carry

    lax.fori_loop(0, coarse_x, arrange, 0)

    y_low = jnp.where(row > 0, 1.0, 0.0)
    y_high = jnp.where(row < rows - 1, 1.0, 0.0)
    z_low = jnp.where(lane % HALF > 0, 1.0, 0.0)
    z_high = jnp.where(lane % HALF < HALF - 1, 1.0, 0.0)

    def coefficients(i, carry):
        x_low = jnp.where(i > 0, 1.0, 0.0)
        kap = [half_kappa[k, i + 1] for k in range(8)]
        total = [shift + zero for _ in range(8)]
        inside = [zero for _ in range(8)]
        coarse_total = 8.0 * shift + zero
        cx = zero
        cy = [zero, zero]
        cz = [zero, zero]
        for p in (0, 1):
            for q in (0, 1):
                for kind, low, high in (
                    (0, cls(0, p, q), cls(1, p, q)),
                    (1, cls(p, 0, q), cls(p, 1, q)),
                    (2, cls(p, q, 0), cls(p, q, 1)),
                ):
                    face = kap[low] + kap[high]
                    inner[4 * kind + 2 * p + q, i] = face
                    inside[low] = inside[low] + face
                    inside[high] = inside[high] + face
                low, high = cls(0, p, q), cls(1, p, q)
                minus = kap[low] + half_kappa[high, i]
                plus = kap[high] + half_kappa[low, i + 2]
                total[low] = total[low] + minus
                total[high] = total[high] + plus
                coarse_total = coarse_total + minus + plus
                outer_x[2 * p + q, i] = x_low * minus
                cx = cx + x_low * minus
                low, high = cls(p, 0, q), cls(p, 1, q)
                minus = kap[low] + y_low * roll(kap[high], 1, 0)
                plus = kap[high] + y_high * roll(kap[low], -1, 0)
                total[low] = total[low] + minus
                total[high] = total[high] + plus
                coarse_total = coarse_total + minus + plus
                minus, plus = y_low * minus, y_high * plus
                outer_y[2 * p + q, i] = minus
                outer_y[4 + 2 * p + q, i] = plus
                cy = [cy[0] + minus, cy[1] + plus]
                low, high = cls(p, q, 0), cls(p, q, 1)
                minus = kap[low] + z_low * roll(kap[high], 1, 1)
                plus = kap[high] + z_high * roll(kap[low], -1, 1)
                total[low] = total[low] + minus
                total[high] = total[high] + plus
                coarse_total = coarse_total + minus + plus
                minus, plus = z_low * minus, z_high * plus
                outer_z[2 * p + q, i] = minus
                outer_z[4 + 2 * p + q, i] = plus
                cz = [cz[0] + minus, cz[1] + plus]
        for k in range(8):
            inner_sum[k, i] = inside[k]
            diag = total[k] + inside[k]
            diagonal[k, i] = diag
            inverse = DAMPING / diag
            damped[k, i] = inverse
            scaled[k, i + 1] = inverse * residual[k, i]
        coarse_off[0, i] = cx
        coarse_off[1, i] = cy[0]
        coarse_off[2, i] = cy[1]
        coarse_off[3, i] = cz[0]
        coarse_off[4, i] = cz[1]
        coarse_damped[i] = DAMPING / coarse_total
        return carry

    lax.fori_loop(0, coarse_x, coefficients, 0)
    for k in range(4):
        outer_x[k, coarse_x] = zero
    coarse_off[0, coarse_x] = zero

    def neighbours(field, a, b, c, i):
        k = cls(a, b, c)
        out = inner[2 * b + c, i] * field[cls(1 - a, b, c), i + 1]
        out = out + inner[4 + 2 * a + c, i] * field[cls(a, 1 - b, c), i + 1]
        out = out + inner[8 + 2 * a + b, i] * field[cls(a, b, 1 - c), i + 1]
        out = out + outer_x[2 * b + c, i + a] * field[cls(1 - a, b, c), i + 2 * a]
        out = out + outer_y[4 * b + 2 * a + c, i] * roll(
            field[cls(a, 1 - b, c), i + 1], 1 - 2 * b, 0
        )
        out = out + outer_z[4 * c + 2 * a + b, i] * roll(
            field[cls(a, b, 1 - c), i + 1], 1 - 2 * c, 1
        )
        return out

    def coarse_neighbours(field, i):
        here = field[i + 1]
        out = coarse_off[0, i] * field[i]
        out = out + coarse_off[0, i + 1] * field[i + 2]
        out = out + coarse_off[1, i] * roll(here, 1, 0)
        out = out + coarse_off[2, i] * roll(here, -1, 0)
        out = out + coarse_off[3, i] * roll(here, 1, 1)
        out = out + coarse_off[4, i] * roll(here, -1, 1)
        return out

    def precondition(result):
        def down(i, carry):
            rhs = zero
            for a, b, c in classes:
                k = cls(a, b, c)
                res = residual[k, i]
                part = res + neighbours(scaled, a, b, c, i)
                partial[k, i] = part
                rhs = rhs + (part - DAMPING * res)
            coarse_one[i + 1] = coarse_damped[i] * rhs
            return carry

        lax.fori_loop(0, coarse_x, down, 0)

        def smooth(i, carry):
            coarse_two[i + 1] = (2.0 - DAMPING) * coarse_one[
                i + 1
            ] + coarse_damped[i] * coarse_neighbours(coarse_one, i)
            return carry

        lax.fori_loop(0, coarse_x, smooth, 0)

        def up(i, acc):
            here = coarse_two[i + 1]
            sides = (
                (coarse_two[i], coarse_two[i + 2]),
                (roll(here, 1, 0), roll(here, -1, 0)),
                (roll(here, 1, 1), roll(here, -1, 1)),
            )
            for a, b, c in classes:
                k = cls(a, b, c)
                value = partial[k, i] + inner_sum[k, i] * here
                value = value + outer_x[2 * b + c, i + a] * sides[0][a]
                value = value + outer_y[4 * b + 2 * a + c, i] * sides[1][b]
                value = value + outer_z[4 * c + 2 * a + b, i] * sides[2][c]
                new = (1.0 - DAMPING) * (scaled[k, i + 1] + here) + damped[k, i] * value
                result[k, i + 1] = new
                acc = acc + eights(residual[k, i] * new)
            return acc

        return lax.fori_loop(0, coarse_x, up, jnp.zeros((8, 2 * HALF), jnp.float32))

    def curvature(field, keep):
        def step(i, acc):
            for a, b, c in classes:
                k = cls(a, b, c)
                here = field[k, i + 1]
                value = diagonal[k, i] * here - neighbours(field, a, b, c, i)
                if keep:
                    image[k, i] = value
                acc = acc + eights(here * value)
            return acc

        return lax.fori_loop(0, coarse_x, step, jnp.zeros((8, 2 * HALF), jnp.float32))

    gamma = slot_totals(precondition(first_dir))
    step_one = gamma / slot_totals(curvature(first_dir, True))

    def update(i, carry):
        for k in range(8):
            new = residual[k, i] - step_one * image[k, i]
            residual[k, i] = new
            scaled[k, i + 1] = damped[k, i] * new
        return carry

    lax.fori_loop(0, coarse_x, update, 0)

    gamma_next = slot_totals(precondition(second_dir))
    ratio = gamma_next / gamma

    def turn(i, carry):
        for k in range(8):
            second_dir[k, i + 1] = second_dir[k, i + 1] + ratio * first_dir[k, i + 1]
        return carry

    lax.fori_loop(0, coarse_x, turn, 0)
    step_two = gamma_next / slot_totals(curvature(second_dir, False))

    own = adjoint_ref.shape[1]
    start = place_ref[0] * (own // 2)
    even = lane % 2 == 0
    for j in range(own + 2):
        a = (j + 1) % 2
        spot = start + (j + 1) // 2
        for b in (0, 1):
            pair = []
            for c in (0, 1):
                k = cls(a, b, c)
                pair.append(
                    step_one * first_dir[k, spot] + step_two * second_dir[k, spot]
                )
            for slot in (0, 1):
                source = lane // 2 + HALF * slot
                value = jnp.where(
                    even,
                    jnp.take_along_axis(pair[0], source, axis=1),
                    jnp.take_along_axis(pair[1], source, axis=1),
                )
                planes[slot, j, pl.ds(b, rows, stride=2), :] = value

    full = (2 * rows, 2 * HALF)
    y_at = row_index(full)
    z_at = lane_index(full)

    def drop(value, axis, up):
        moved = roll(value, -1 if up else 1, axis)
        at = (y_at, z_at)[axis]
        edge = full[axis] - 1 if up else 0
        return value - jnp.where(at == edge, 0.0, moved)

    groups = share_ref.shape[0]
    chunk = share_ref.shape[2]
    for j in range(own):
        term = jnp.zeros(full, jnp.float32)
        for slot in (0, 1):
            here = planes[slot, j + 1]
            adjoint_ref[slot, j] = here
            f = state_ref[slot, j]
            f_low = state_ref[slot, j - 1] if j else before_ref[slot, 0]
            f_high = state_ref[slot, j + 1] if j + 1 < own else after_ref[slot, 0]
            term = term + (here - planes[slot, j + 2]) * (f - f_high)
            term = term + (here - planes[slot, j]) * (f - f_low)
            for axis in (0, 1):
                for up in (True, False):
                    term = term + drop(here, axis, up) * drop(f, axis, up)
        planes[0, j] = -0.5 * term
        for k in range(groups):
            at = lax.rem(place_ref[1] + k, groups) * chunk
            share_ref[k, j] = planes[0, j, pl.ds(pl.multiple_of(at, chunk), chunk), :]


def whole_grid(conductivity, misfit, forward_states, pole_shifts, pole_weights, pole_order):
    members, own, ny, nz = forward_states.shape
    groups = lax.axis_size("pole")
    place = jnp.stack([lax.axis_index("space"), lax.axis_index("pole")]).astype(jnp.int32)
    peers = lax.axis_size("space")
    up = [(i, i + 1) for i in range(peers - 1)]
    down = [(i + 1, i) for i in range(peers - 1)]
    before = lax.ppermute(forward_states[:, own - 1 :], "space", up)
    after = lax.ppermute(forward_states[:, :1], "space", down)
    kappa = lax.all_gather(conductivity, "space", axis=0, tiled=True)
    source = lax.all_gather(misfit, "space", axis=0, tiled=True)
    coarse_x, rows = kappa.shape[0] // 2, ny // 2
    lanes = 2 * HALF

    def scratch(count, extent):
        return pltpu.VMEM((count, extent, rows, lanes), jnp.float32)

    smem = pl.BlockSpec(memory_space=pltpu.SMEM)
    vmem = pl.BlockSpec(memory_space=pltpu.VMEM)
    adjoint, share = pl.pallas_call(
        solve_kernel,
        out_shape=(
            jax.ShapeDtypeStruct(forward_states.shape, jnp.float32),
            jax.ShapeDtypeStruct((groups, own, ny // groups, nz), jnp.float32),
        ),
        in_specs=[smem] * 4 + [vmem] * 5,
        out_specs=(vmem, vmem),
        scratch_shapes=[
            scratch(8, coarse_x + 2),
            scratch(12, coarse_x),
            scratch(4, coarse_x + 1),
            scratch(8, coarse_x),
            scratch(8, coarse_x),
            scratch(8, coarse_x),
            scratch(8, coarse_x),
            scratch(8, coarse_x),
            scratch(5, coarse_x + 1),
            pltpu.VMEM((coarse_x, rows, lanes), jnp.float32),
            scratch(8, coarse_x),
            scratch(8, coarse_x + 2),
            scratch(8, coarse_x),
            scratch(8, coarse_x + 2),
            scratch(8, coarse_x + 2),
            scratch(8, coarse_x),
            pltpu.VMEM((coarse_x + 2, rows, lanes), jnp.float32),
            pltpu.VMEM((coarse_x + 2, rows, lanes), jnp.float32),
            pltpu.VMEM((members, own + 2, ny, nz), jnp.float32),
        ],
        compiler_params=pltpu.CompilerParams(vmem_limit_bytes=48 * 1024 * 1024),
        name="solve",
    )(
        place,
        pole_shifts,
        pole_weights,
        pole_order,
        kappa,
        source,
        before,
        forward_states,
        after,
    )
    gradient = share[0]
    for k in range(1, groups):
        ring = [(i, (i + k) % groups) for i in range(groups)]
        gradient = gradient + lax.ppermute(share[k], "pole", ring)
    return adjoint, gradient


def plus_side(field, which_dim):
    extent = field.shape[which_dim]
    inner_part = lax.slice_in_dim(field, 1, extent, axis=which_dim)
    zero_plane = jnp.zeros_like(lax.slice_in_dim(field, 0, 1, axis=which_dim))
    return jnp.concatenate([inner_part, zero_plane], axis=which_dim)


def minus_side(field, which_dim):
    extent = field.shape[which_dim]
    inner_part = lax.slice_in_dim(field, 0, extent - 1, axis=which_dim)
    zero_plane = jnp.zeros_like(lax.slice_in_dim(field, 0, 1, axis=which_dim))
    return jnp.concatenate([zero_plane, inner_part], axis=which_dim)


def coarse_pick(faces, which_dim, offset):
    extent_x, extent_y, extent_z = faces.shape
    blocks = faces.reshape(extent_x // 2, 2, extent_y // 2, 2, extent_z // 2, 2)
    chosen = lax.index_in_dim(blocks, offset, axis=2 * which_dim + 1, keepdims=True)
    return jnp.sum(chosen, axis=(1, 3, 5))


def side_terms(field, plus_faces, minus_faces, widened):
    result = plus_faces[0] * (field - widened[:, 2:]) + minus_faces[0] * (field - widened[:, :-2])
    for which_dim in (1, 2):
        result = result + plus_faces[which_dim] * (field - plus_side(field, which_dim + 1))
        result = result + minus_faces[which_dim] * (field - minus_side(field, which_dim + 1))
    return result


def fine_image(field, plus_faces, minus_faces, shift_value):
    widened = extended(field, (("space", 1),), 1)
    return shift_value * field + side_terms(field, plus_faces, minus_faces, widened)


def coarse_image(field, plus_faces, minus_faces, shift_value):
    widened = extended(field, (("space", 1),), 1)
    return shift_value * field + side_terms(field, plus_faces, minus_faces, widened)


def restrict(field):
    members, extent_x, extent_y, extent_z = field.shape
    shaped = field.reshape(members, extent_x // 2, 2, extent_y // 2, 2, extent_z // 2, 2)
    return jnp.sum(shaped, axis=(2, 4, 6))


def prolong(field):
    return jnp.repeat(jnp.repeat(jnp.repeat(field, 2, axis=1), 2, axis=2), 2, axis=3)


def precondition(residual, fine, coarse):
    plus_faces, minus_faces, shift_value, diagonal = fine
    coarse_plus, coarse_minus, coarse_shift, coarse_diagonal = coarse
    smooth_one = DAMPING * residual / diagonal
    coarse_rhs = restrict(residual - fine_image(smooth_one, plus_faces, minus_faces, shift_value))
    coarse_one = DAMPING * coarse_rhs / coarse_diagonal
    coarse_two = (
        coarse_one
        + DAMPING
        * (coarse_rhs - coarse_image(coarse_one, coarse_plus, coarse_minus, coarse_shift))
        / coarse_diagonal
    )
    corrected = smooth_one + prolong(coarse_two)
    return (
        corrected
        + DAMPING
        * (residual - fine_image(corrected, plus_faces, minus_faces, shift_value))
        / diagonal
    )


def expand(values):
    return values.reshape(-1, 1, 1, 1)


def cell_sums(values):
    return jnp.sum(values, axis=(1, 2, 3))


def norm_sum(residual, precond):
    return lax.psum(cell_sums(residual * precond), "space")


def solve(rhs, fine, coarse):
    plus_faces, minus_faces, shift_value, diagonal = fine
    iterate = jnp.zeros_like(rhs)
    residual = rhs
    precond = precondition(residual, fine, coarse)
    gamma_now = norm_sum(residual, precond)
    search = precond
    for turn_index in range(ITERS):
        image_field = fine_image(search, plus_faces, minus_faces, shift_value)
        curve = lax.psum(cell_sums(search * image_field), "space")
        step_length = gamma_now / curve
        iterate = iterate + expand(step_length) * search
        if turn_index + 1 < ITERS:
            residual = residual - expand(step_length) * image_field
            precond = precondition(residual, fine, coarse)
            gamma_next = norm_sum(residual, precond)
            search = precond + expand(gamma_next / gamma_now) * search
            gamma_now = gamma_next
    return iterate


def divided(conductivity, misfit, forward_states, pole_shifts, pole_weights, pole_order):
    widened_kappa = extended(conductivity, (("space", 0),), 1)
    plus_faces = [
        0.5 * (conductivity + widened_kappa[2:]),
        0.5 * (conductivity + plus_side(conductivity, 1)),
        0.5 * (conductivity + plus_side(conductivity, 2)),
    ]
    minus_faces = [
        0.5 * (conductivity + widened_kappa[:-2]),
        0.5 * (conductivity + minus_side(conductivity, 1)),
        0.5 * (conductivity + minus_side(conductivity, 2)),
    ]
    base_diagonal = (
        plus_faces[0]
        + plus_faces[1]
        + plus_faces[2]
        + minus_faces[0]
        + minus_faces[1]
        + minus_faces[2]
    )
    coarse_plus = [coarse_pick(plus_faces[which_dim], which_dim, 1) for which_dim in range(3)]
    coarse_minus = [coarse_pick(minus_faces[which_dim], which_dim, 0) for which_dim in range(3)]
    coarse_base = (
        coarse_plus[0]
        + coarse_plus[1]
        + coarse_plus[2]
        + coarse_minus[0]
        + coarse_minus[1]
        + coarse_minus[2]
    )
    pole_index = jnp.arange(pole_shifts.shape[0], dtype=jnp.int32)
    matches = pole_order[:, None] == pole_index[None, :]
    shift_local = jnp.sum(jnp.where(matches, pole_shifts[None, :], 0.0), axis=1)
    weight_local = jnp.sum(jnp.where(matches, pole_weights[None, :], 0.0), axis=1)
    members = forward_states.shape[0]

    def solve_group(shift_part, weight_part):
        shift_value = expand(shift_part)
        fine = (plus_faces, minus_faces, shift_value, base_diagonal[None] + shift_value)
        coarse = (
            coarse_plus,
            coarse_minus,
            8.0 * shift_value,
            coarse_base[None] + 8.0 * shift_value,
        )
        return solve(expand(weight_part) * misfit[None], fine, coarse)

    adjoint_states = jnp.concatenate(
        [
            solve_group(shift_local[member : member + 1], weight_local[member : member + 1])
            for member in range(members)
        ],
        axis=0,
    )
    widened = extended(jnp.stack([adjoint_states, forward_states]), (("space", 2),), 1)
    term = (adjoint_states - widened[0, :, 2:]) * (forward_states - widened[1, :, 2:])
    term = term + (adjoint_states - widened[0, :, :-2]) * (forward_states - widened[1, :, :-2])
    for which_dim in (2, 3):
        term = term + (adjoint_states - plus_side(adjoint_states, which_dim)) * (
            forward_states - plus_side(forward_states, which_dim)
        )
        term = term + (adjoint_states - minus_side(adjoint_states, which_dim)) * (
            forward_states - minus_side(forward_states, which_dim)
        )
    local_term = -0.5 * jnp.sum(term, axis=0)
    gradient = lax.psum_scatter(local_term, "pole", scatter_dimension=1, tiled=True)
    return (adjoint_states, gradient)


def solution(mesh):
    in_specs = (
        P("space", None, None),
        P("space", None, None),
        P("pole", "space", None, None),
        P(),
        P(),
        P("pole"),
    )
    out_specs = (P("pole", "space", None, None), P("space", "pole", None))

    def body(conductivity, misfit, forward_states, *poles):
        nx = conductivity.shape[0] * lax.axis_size("space")
        _, ny, nz = conductivity.shape
        small = nx * ny * nz <= REPLICATED_CELLS
        if small and forward_states.shape[0] == 2 and nz == 2 * HALF:
            return whole_grid(conductivity, misfit, forward_states, *poles)
        return divided(conductivity, misfit, forward_states, *poles)

    return jax.shard_map(
        body, mesh=mesh, in_specs=in_specs, out_specs=out_specs, check_vma=False
    )
```

```python
import functools

import jax
import jax.numpy as jnp
from jax import lax
from jax.experimental import pallas as pl
from jax.experimental.pallas import tpu as pltpu
from jax.sharding import PartitionSpec as P

ITERS = 2
DAMPING = 0.8
REPLICATED_CELLS = 32 * 64 * 128
HALF = 64


def extended(array, sides, width):
    for axis, dim in sides:
        peers, length = (lax.axis_size(axis), array.shape[dim])
        up = [(i, (i + 1) % peers) for i in range(peers - 1)]
        down = [(j, i) for i, j in up]
        last = lax.slice_in_dim(array, length - width, length, axis=dim)
        leading = lax.slice_in_dim(array, 0, width, axis=dim)
        before = lax.ppermute(last, axis, up)
        after = lax.ppermute(leading, axis, down)
        array = jnp.concatenate([before, array, after], axis=dim)
    return array


def lane_index(shape):
    return lax.broadcasted_iota(jnp.int32, shape, len(shape) - 1)


def row_index(shape):
    return lax.broadcasted_iota(jnp.int32, shape, len(shape) - 2)


def roll(block, shift, axis):
    return pltpu.roll(block, shift % block.shape[axis], axis)


def eights(block):
    rows = block.shape[0]
    total = block[0:8]
    for start in range(8, rows, 8):
        total = total + block[start : start + 8]
    return total


def slot_totals(acc):
    line = jnp.sum(acc, axis=0, keepdims=True)
    lane = lane_index(line.shape)
    first = jnp.sum(jnp.where(lane < HALF, line, 0.0), axis=1, keepdims=True)
    second = jnp.sum(jnp.where(lane < HALF, 0.0, line), axis=1, keepdims=True)
    return jnp.where(lane < HALF, first, second)


def swap_masks(peers):
    even = []
    mask = peers // 2
    while mask > 1:
        even.append(mask)
        mask //= 2
    odd = even[-1:] + even[:-1]
    return even, odd


def offset_of(t, parity, peers):
    even, odd = swap_masks(peers)
    offset = jnp.int32(0)
    for step, (mask_even, mask_odd) in enumerate(zip(even, odd)):
        mask = jnp.where(parity == 0, mask_even, mask_odd)
        offset = offset ^ (((t >> step) & 1) * mask)
    return offset


def gather_blocks(block, axis):
    peers = lax.axis_size(axis)
    held = block[None]
    for masks in zip(*swap_masks(peers)):
        pairs = [(i, i ^ masks[i % 2]) for i in range(peers)]
        held = jnp.concatenate([held, lax.ppermute(held, axis, pairs)], axis=0)
    return held, lax.ppermute(held, axis, [(i, i ^ 1) for i in range(peers)])


def solve_kernel(
    place_ref,
    shifts_ref,
    weights_ref,
    order_ref,
    mine_ref,
    theirs_ref,
    before_ref,
    state_ref,
    after_ref,
    adjoint_ref,
    share_ref,
    half_kappa,
    inner,
    outer_x,
    outer_y,
    outer_z,
    inner_sum,
    diagonal,
    damped,
    coarse_off,
    coarse_damped,
    residual,
    scaled,
    partial,
    first_dir,
    second_dir,
    image,
    coarse_one,
    coarse_two,
    planes,
):
    blocks, _, own, rows, _ = mine_ref.shape
    coarse_x = blocks * own
    rows = rows // 2
    shape = (rows, 2 * HALF)
    lane = lane_index(shape)
    row = row_index(shape)
    slot0 = lane_index((1, 2 * HALF)) < HALF

    def pick(ref):
        return jnp.where(slot0, ref[order_ref[0]], ref[order_ref[1]])

    shift = pick(shifts_ref)
    weight = pick(weights_ref)

    def cls(a, b, c):
        return 4 * a + 2 * b + c

    classes = [(a, b, c) for a in (0, 1) for b in (0, 1) for c in (0, 1)]

    zero = jnp.zeros(shape, jnp.float32)
    for ref in (half_kappa, scaled, first_dir, second_dir):
        for k in range(8):
            ref[k, 0] = zero
            ref[k, coarse_x + 1] = zero
    for ref in (coarse_one, coarse_two):
        ref[0] = zero
        ref[coarse_x + 1] = zero

    even_lane = 2 * (lane % HALF)

    def split(ref, t, field, x, b):
        block = ref[t, field, x, pl.ds(b, rows, stride=2), :]
        even = jnp.take_along_axis(block, even_lane, axis=1)
        odd = jnp.take_along_axis(block, even_lane + 1, axis=1)
        return even, odd

    def arrange(t, carry):
        for ref, holder in ((mine_ref, place_ref[0]), (theirs_ref, place_ref[0] ^ 1)):
            home = holder ^ offset_of(t, holder % 2, 2 * blocks)
            for x in range(own):
                a = x % 2
                spot = home * (own // 2) + x // 2
                for b in (0, 1):
                    for c, value in enumerate(split(ref, t, 0, x, b)):
                        half_kappa[cls(a, b, c), spot + 1] = 0.5 * value
                    for c, value in enumerate(split(ref, t, 1, x, b)):
                        residual[cls(a, b, c), spot] = weight * value
        return carry

    lax.fori_loop(0, blocks, arrange, 0)

    y_low = jnp.where(row > 0, 1.0, 0.0)
    y_high = jnp.where(row < rows - 1, 1.0, 0.0)
    z_low = jnp.where(lane % HALF > 0, 1.0, 0.0)
    z_high = jnp.where(lane % HALF < HALF - 1, 1.0, 0.0)

    def coefficients(i, carry):
        x_low = jnp.where(i > 0, 1.0, 0.0)
        kap = [half_kappa[k, i + 1] for k in range(8)]
        total = [shift + zero for _ in range(8)]
        inside = [zero for _ in range(8)]
        coarse_total = 8.0 * shift + zero
        cx = zero
        cy = [zero, zero]
        cz = [zero, zero]
        for p in (0, 1):
            for q in (0, 1):
                for kind, low, high in (
                    (0, cls(0, p, q), cls(1, p, q)),
                    (1, cls(p, 0, q), cls(p, 1, q)),
                    (2, cls(p, q, 0), cls(p, q, 1)),
                ):
                    face = kap[low] + kap[high]
                    inner[4 * kind + 2 * p + q, i] = face
                    inside[low] = inside[low] + face
                    inside[high] = inside[high] + face
                low, high = cls(0, p, q), cls(1, p, q)
                minus = kap[low] + half_kappa[high, i]
                plus = kap[high] + half_kappa[low, i + 2]
                total[low] = total[low] + minus
                total[high] = total[high] + plus
                coarse_total = coarse_total + minus + plus
                outer_x[2 * p + q, i] = x_low * minus
                cx = cx + x_low * minus
                low, high = cls(p, 0, q), cls(p, 1, q)
                minus = kap[low] + y_low * roll(kap[high], 1, 0)
                plus = kap[high] + y_high * roll(kap[low], -1, 0)
                total[low] = total[low] + minus
                total[high] = total[high] + plus
                coarse_total = coarse_total + minus + plus
                minus, plus = y_low * minus, y_high * plus
                outer_y[2 * p + q, i] = minus
                outer_y[4 + 2 * p + q, i] = plus
                cy = [cy[0] + minus, cy[1] + plus]
                low, high = cls(p, q, 0), cls(p, q, 1)
                minus = kap[low] + z_low * roll(kap[high], 1, 1)
                plus = kap[high] + z_high * roll(kap[low], -1, 1)
                total[low] = total[low] + minus
                total[high] = total[high] + plus
                coarse_total = coarse_total + minus + plus
                minus, plus = z_low * minus, z_high * plus
                outer_z[2 * p + q, i] = minus
                outer_z[4 + 2 * p + q, i] = plus
                cz = [cz[0] + minus, cz[1] + plus]
        for k in range(8):
            inner_sum[k, i] = inside[k]
            diag = total[k] + inside[k]
            diagonal[k, i] = diag
            inverse = DAMPING / diag
            damped[k, i] = inverse
            scaled[k, i + 1] = inverse * residual[k, i]
        coarse_off[0, i] = cx
        coarse_off[1, i] = cy[0]
        coarse_off[2, i] = cy[1]
        coarse_off[3, i] = cz[0]
        coarse_off[4, i] = cz[1]
        coarse_damped[i] = DAMPING / coarse_total
        return carry

    lax.fori_loop(0, coarse_x, coefficients, 0)
    for k in range(4):
        outer_x[k, coarse_x] = zero
    coarse_off[0, coarse_x] = zero

    def neighbours(field, a, b, c, i):
        k = cls(a, b, c)
        out = inner[2 * b + c, i] * field[cls(1 - a, b, c), i + 1]
        out = out + inner[4 + 2 * a + c, i] * field[cls(a, 1 - b, c), i + 1]
        out = out + inner[8 + 2 * a + b, i] * field[cls(a, b, 1 - c), i + 1]
        out = out + outer_x[2 * b + c, i + a] * field[cls(1 - a, b, c), i + 2 * a]
        out = out + outer_y[4 * b + 2 * a + c, i] * roll(
            field[cls(a, 1 - b, c), i + 1], 1 - 2 * b, 0
        )
        out = out + outer_z[4 * c + 2 * a + b, i] * roll(
            field[cls(a, b, 1 - c), i + 1], 1 - 2 * c, 1
        )
        return out

    def coarse_neighbours(field, i):
        here = field[i + 1]
        out = coarse_off[0, i] * field[i]
        out = out + coarse_off[0, i + 1] * field[i + 2]
        out = out + coarse_off[1, i] * roll(here, 1, 0)
        out = out + coarse_off[2, i] * roll(here, -1, 0)
        out = out + coarse_off[3, i] * roll(here, 1, 1)
        out = out + coarse_off[4, i] * roll(here, -1, 1)
        return out

    def precondition(result):
        def down(i, carry):
            rhs = zero
            for a, b, c in classes:
                k = cls(a, b, c)
                res = residual[k, i]
                part = res + neighbours(scaled, a, b, c, i)
                partial[k, i] = part
                rhs = rhs + (part - DAMPING * res)
            coarse_one[i + 1] = coarse_damped[i] * rhs
            return carry

        lax.fori_loop(0, coarse_x, down, 0)

        def smooth(i, carry):
            coarse_two[i + 1] = (2.0 - DAMPING) * coarse_one[
                i + 1
            ] + coarse_damped[i] * coarse_neighbours(coarse_one, i)
            return carry

        lax.fori_loop(0, coarse_x, smooth, 0)

        def up(i, acc):
            here = coarse_two[i + 1]
            sides = (
                (coarse_two[i], coarse_two[i + 2]),
                (roll(here, 1, 0), roll(here, -1, 0)),
                (roll(here, 1, 1), roll(here, -1, 1)),
            )
            for a, b, c in classes:
                k = cls(a, b, c)
                value = partial[k, i] + inner_sum[k, i] * here
                value = value + outer_x[2 * b + c, i + a] * sides[0][a]
                value = value + outer_y[4 * b + 2 * a + c, i] * sides[1][b]
                value = value + outer_z[4 * c + 2 * a + b, i] * sides[2][c]
                new = (1.0 - DAMPING) * (scaled[k, i + 1] + here) + damped[k, i] * value
                result[k, i + 1] = new
                acc = acc + eights(residual[k, i] * new)
            return acc

        return lax.fori_loop(0, coarse_x, up, jnp.zeros((8, 2 * HALF), jnp.float32))

    def curvature(field, keep):
        def step(i, acc):
            for a, b, c in classes:
                k = cls(a, b, c)
                here = field[k, i + 1]
                value = diagonal[k, i] * here - neighbours(field, a, b, c, i)
                if keep:
                    image[k, i] = value
                acc = acc + eights(here * value)
            return acc

        return lax.fori_loop(0, coarse_x, step, jnp.zeros((8, 2 * HALF), jnp.float32))

    gamma = slot_totals(precondition(first_dir))
    step_one = gamma / slot_totals(curvature(first_dir, True))

    def update(i, carry):
        for k in range(8):
            new = residual[k, i] - step_one * image[k, i]
            residual[k, i] = new
            scaled[k, i + 1] = damped[k, i] * new
        return carry

    lax.fori_loop(0, coarse_x, update, 0)

    gamma_next = slot_totals(precondition(second_dir))
    ratio = gamma_next / gamma

    def turn(i, carry):
        for k in range(8):
            second_dir[k, i + 1] = second_dir[k, i + 1] + ratio * first_dir[k, i + 1]
        return carry

    lax.fori_loop(0, coarse_x, turn, 0)
    step_two = gamma_next / slot_totals(curvature(second_dir, False))

    own = adjoint_ref.shape[1]
    start = place_ref[0] * (own // 2)
    even = lane % 2 == 0
    for j in range(own + 2):
        a = (j + 1) % 2
        spot = start + (j + 1) // 2
        for b in (0, 1):
            pair = []
            for c in (0, 1):
                k = cls(a, b, c)
                pair.append(
                    step_one * first_dir[k, spot] + step_two * second_dir[k, spot]
                )
            for slot in (0, 1):
                source = lane // 2 + HALF * slot
                value = jnp.where(
                    even,
                    jnp.take_along_axis(pair[0], source, axis=1),
                    jnp.take_along_axis(pair[1], source, axis=1),
                )
                planes[slot, j, pl.ds(b, rows, stride=2), :] = value

    full = (2 * rows, 2 * HALF)
    y_at = row_index(full)
    z_at = lane_index(full)

    def drop(value, axis, up):
        moved = roll(value, -1 if up else 1, axis)
        at = (y_at, z_at)[axis]
        edge = full[axis] - 1 if up else 0
        return value - jnp.where(at == edge, 0.0, moved)

    groups = share_ref.shape[0]
    chunk = share_ref.shape[2]
    for j in range(own):
        term = jnp.zeros(full, jnp.float32)
        for slot in (0, 1):
            here = planes[slot, j + 1]
            adjoint_ref[slot, j] = here
            f = state_ref[slot, j]
            f_low = state_ref[slot, j - 1] if j else before_ref[slot, 0]
            f_high = state_ref[slot, j + 1] if j + 1 < own else after_ref[slot, 0]
            term = term + (here - planes[slot, j + 2]) * (f - f_high)
            term = term + (here - planes[slot, j]) * (f - f_low)
            for axis in (0, 1):
                for up in (True, False):
                    term = term + drop(here, axis, up) * drop(f, axis, up)
        planes[0, j] = -0.5 * term
        for k in range(groups):
            at = lax.rem(place_ref[1] + k, groups) * chunk
            share_ref[k, j] = planes[0, j, pl.ds(pl.multiple_of(at, chunk), chunk), :]


def whole_grid(conductivity, misfit, forward_states, pole_shifts, pole_weights, pole_order):
    members, own, ny, nz = forward_states.shape
    groups = lax.axis_size("pole")
    place = jnp.stack([lax.axis_index("space"), lax.axis_index("pole")]).astype(jnp.int32)
    peers = lax.axis_size("space")
    up = [(i, i + 1) for i in range(peers - 1)]
    down = [(i + 1, i) for i in range(peers - 1)]
    before = lax.ppermute(forward_states[:, own - 1 :], "space", up)
    after = lax.ppermute(forward_states[:, :1], "space", down)
    mine, theirs = gather_blocks(jnp.stack([conductivity, misfit]), "space")
    coarse_x, rows = peers * own // 2, ny // 2
    lanes = 2 * HALF

    def scratch(count, extent):
        return pltpu.VMEM((count, extent, rows, lanes), jnp.float32)

    smem = pl.BlockSpec(memory_space=pltpu.SMEM)
    vmem = pl.BlockSpec(memory_space=pltpu.VMEM)
    adjoint, share = pl.pallas_call(
        solve_kernel,
        out_shape=(
            jax.ShapeDtypeStruct(forward_states.shape, jnp.float32),
            jax.ShapeDtypeStruct((groups, own, ny // groups, nz), jnp.float32),
        ),
        in_specs=[smem] * 4 + [vmem] * 5,
        out_specs=(vmem, vmem),
        scratch_shapes=[
            scratch(8, coarse_x + 2),
            scratch(12, coarse_x),
            scratch(4, coarse_x + 1),
            scratch(8, coarse_x),
            scratch(8, coarse_x),
            scratch(8, coarse_x),
            scratch(8, coarse_x),
            scratch(8, coarse_x),
            scratch(5, coarse_x + 1),
            pltpu.VMEM((coarse_x, rows, lanes), jnp.float32),
            scratch(8, coarse_x),
            scratch(8, coarse_x + 2),
            scratch(8, coarse_x),
            scratch(8, coarse_x + 2),
            scratch(8, coarse_x + 2),
            scratch(8, coarse_x),
            pltpu.VMEM((coarse_x + 2, rows, lanes), jnp.float32),
            pltpu.VMEM((coarse_x + 2, rows, lanes), jnp.float32),
            pltpu.VMEM((members, own + 2, ny, nz), jnp.float32),
        ],
        compiler_params=pltpu.CompilerParams(vmem_limit_bytes=48 * 1024 * 1024),
        name="solve",
    )(
        place,
        pole_shifts,
        pole_weights,
        pole_order,
        mine,
        theirs,
        before,
        forward_states,
        after,
    )
    gradient = share[0]
    for k in range(1, groups):
        ring = [(i, (i + k) % groups) for i in range(groups)]
        gradient = gradient + lax.ppermute(share[k], "pole", ring)
    return adjoint, gradient


def plus_side(field, which_dim):
    extent = field.shape[which_dim]
    inner_part = lax.slice_in_dim(field, 1, extent, axis=which_dim)
    zero_plane = jnp.zeros_like(lax.slice_in_dim(field, 0, 1, axis=which_dim))
    return jnp.concatenate([inner_part, zero_plane], axis=which_dim)


def minus_side(field, which_dim):
    extent = field.shape[which_dim]
    inner_part = lax.slice_in_dim(field, 0, extent - 1, axis=which_dim)
    zero_plane = jnp.zeros_like(lax.slice_in_dim(field, 0, 1, axis=which_dim))
    return jnp.concatenate([zero_plane, inner_part], axis=which_dim)


def coarse_pick(faces, which_dim, offset):
    extent_x, extent_y, extent_z = faces.shape
    blocks = faces.reshape(extent_x // 2, 2, extent_y // 2, 2, extent_z // 2, 2)
    chosen = lax.index_in_dim(blocks, offset, axis=2 * which_dim + 1, keepdims=True)
    return jnp.sum(chosen, axis=(1, 3, 5))


def side_terms(field, plus_faces, minus_faces, widened):
    result = plus_faces[0] * (field - widened[:, 2:]) + minus_faces[0] * (field - widened[:, :-2])
    for which_dim in (1, 2):
        result = result + plus_faces[which_dim] * (field - plus_side(field, which_dim + 1))
        result = result + minus_faces[which_dim] * (field - minus_side(field, which_dim + 1))
    return result


def fine_image(field, plus_faces, minus_faces, shift_value):
    widened = extended(field, (("space", 1),), 1)
    return shift_value * field + side_terms(field, plus_faces, minus_faces, widened)


def coarse_image(field, plus_faces, minus_faces, shift_value):
    widened = extended(field, (("space", 1),), 1)
    return shift_value * field + side_terms(field, plus_faces, minus_faces, widened)


def restrict(field):
    members, extent_x, extent_y, extent_z = field.shape
    shaped = field.reshape(members, extent_x // 2, 2, extent_y // 2, 2, extent_z // 2, 2)
    return jnp.sum(shaped, axis=(2, 4, 6))


def prolong(field):
    return jnp.repeat(jnp.repeat(jnp.repeat(field, 2, axis=1), 2, axis=2), 2, axis=3)


def precondition(residual, fine, coarse):
    plus_faces, minus_faces, shift_value, diagonal = fine
    coarse_plus, coarse_minus, coarse_shift, coarse_diagonal = coarse
    smooth_one = DAMPING * residual / diagonal
    coarse_rhs = restrict(residual - fine_image(smooth_one, plus_faces, minus_faces, shift_value))
    coarse_one = DAMPING * coarse_rhs / coarse_diagonal
    coarse_two = (
        coarse_one
        + DAMPING
        * (coarse_rhs - coarse_image(coarse_one, coarse_plus, coarse_minus, coarse_shift))
        / coarse_diagonal
    )
    corrected = smooth_one + prolong(coarse_two)
    return (
        corrected
        + DAMPING
        * (residual - fine_image(corrected, plus_faces, minus_faces, shift_value))
        / diagonal
    )


def expand(values):
    return values.reshape(-1, 1, 1, 1)


def cell_sums(values):
    return jnp.sum(values, axis=(1, 2, 3))


def norm_sum(residual, precond):
    return lax.psum(cell_sums(residual * precond), "space")


def solve(rhs, fine, coarse):
    plus_faces, minus_faces, shift_value, diagonal = fine
    iterate = jnp.zeros_like(rhs)
    residual = rhs
    precond = precondition(residual, fine, coarse)
    gamma_now = norm_sum(residual, precond)
    search = precond
    for turn_index in range(ITERS):
        image_field = fine_image(search, plus_faces, minus_faces, shift_value)
        curve = lax.psum(cell_sums(search * image_field), "space")
        step_length = gamma_now / curve
        iterate = iterate + expand(step_length) * search
        if turn_index + 1 < ITERS:
            residual = residual - expand(step_length) * image_field
            precond = precondition(residual, fine, coarse)
            gamma_next = norm_sum(residual, precond)
            search = precond + expand(gamma_next / gamma_now) * search
            gamma_now = gamma_next
    return iterate


def divided(conductivity, misfit, forward_states, pole_shifts, pole_weights, pole_order):
    widened_kappa = extended(conductivity, (("space", 0),), 1)
    plus_faces = [
        0.5 * (conductivity + widened_kappa[2:]),
        0.5 * (conductivity + plus_side(conductivity, 1)),
        0.5 * (conductivity + plus_side(conductivity, 2)),
    ]
    minus_faces = [
        0.5 * (conductivity + widened_kappa[:-2]),
        0.5 * (conductivity + minus_side(conductivity, 1)),
        0.5 * (conductivity + minus_side(conductivity, 2)),
    ]
    base_diagonal = (
        plus_faces[0]
        + plus_faces[1]
        + plus_faces[2]
        + minus_faces[0]
        + minus_faces[1]
        + minus_faces[2]
    )
    coarse_plus = [coarse_pick(plus_faces[which_dim], which_dim, 1) for which_dim in range(3)]
    coarse_minus = [coarse_pick(minus_faces[which_dim], which_dim, 0) for which_dim in range(3)]
    coarse_base = (
        coarse_plus[0]
        + coarse_plus[1]
        + coarse_plus[2]
        + coarse_minus[0]
        + coarse_minus[1]
        + coarse_minus[2]
    )
    pole_index = jnp.arange(pole_shifts.shape[0], dtype=jnp.int32)
    matches = pole_order[:, None] == pole_index[None, :]
    shift_local = jnp.sum(jnp.where(matches, pole_shifts[None, :], 0.0), axis=1)
    weight_local = jnp.sum(jnp.where(matches, pole_weights[None, :], 0.0), axis=1)
    members = forward_states.shape[0]

    def solve_group(shift_part, weight_part):
        shift_value = expand(shift_part)
        fine = (plus_faces, minus_faces, shift_value, base_diagonal[None] + shift_value)
        coarse = (
            coarse_plus,
            coarse_minus,
            8.0 * shift_value,
            coarse_base[None] + 8.0 * shift_value,
        )
        return solve(expand(weight_part) * misfit[None], fine, coarse)

    adjoint_states = jnp.concatenate(
        [
            solve_group(shift_local[member : member + 1], weight_local[member : member + 1])
            for member in range(members)
        ],
        axis=0,
    )
    widened = extended(jnp.stack([adjoint_states, forward_states]), (("space", 2),), 1)
    term = (adjoint_states - widened[0, :, 2:]) * (forward_states - widened[1, :, 2:])
    term = term + (adjoint_states - widened[0, :, :-2]) * (forward_states - widened[1, :, :-2])
    for which_dim in (2, 3):
        term = term + (adjoint_states - plus_side(adjoint_states, which_dim)) * (
            forward_states - plus_side(forward_states, which_dim)
        )
        term = term + (adjoint_states - minus_side(adjoint_states, which_dim)) * (
            forward_states - minus_side(forward_states, which_dim)
        )
    local_term = -0.5 * jnp.sum(term, axis=0)
    gradient = lax.psum_scatter(local_term, "pole", scatter_dimension=1, tiled=True)
    return (adjoint_states, gradient)


def solution(mesh):
    in_specs = (
        P("space", None, None),
        P("space", None, None),
        P("pole", "space", None, None),
        P(),
        P(),
        P("pole"),
    )
    out_specs = (P("pole", "space", None, None), P("space", "pole", None))

    def body(conductivity, misfit, forward_states, *poles):
        nx = conductivity.shape[0] * lax.axis_size("space")
        _, ny, nz = conductivity.shape
        peers = lax.axis_size("space")
        small = nx * ny * nz <= REPLICATED_CELLS and forward_states.shape[0] == 2
        if small and nz == 2 * HALF and peers > 2 and peers & (peers - 1) == 0:
            return whole_grid(conductivity, misfit, forward_states, *poles)
        return divided(conductivity, misfit, forward_states, *poles)

    return jax.shard_map(
        body, mesh=mesh, in_specs=in_specs, out_specs=out_specs, check_vma=False
    )
```

```python
import functools

import jax
import jax.numpy as jnp
from jax import lax
from jax.experimental import pallas as pl
from jax.experimental.pallas import tpu as pltpu
from jax.sharding import PartitionSpec as P

ITERS = 2
DAMPING = 0.8
REPLICATED_CELLS = 32 * 64 * 128
HALF = 64
TILE = 8


def extended(array, sides, width):
    for axis, dim in sides:
        peers, length = (lax.axis_size(axis), array.shape[dim])
        up = [(i, (i + 1) % peers) for i in range(peers - 1)]
        down = [(j, i) for i, j in up]
        last = lax.slice_in_dim(array, length - width, length, axis=dim)
        leading = lax.slice_in_dim(array, 0, width, axis=dim)
        before = lax.ppermute(last, axis, up)
        after = lax.ppermute(leading, axis, down)
        array = jnp.concatenate([before, array, after], axis=dim)
    return array


def lane_index(shape):
    return lax.broadcasted_iota(jnp.int32, shape, len(shape) - 1)


def row_index(shape):
    return lax.broadcasted_iota(jnp.int32, shape, len(shape) - 2)


def roll(block, shift, axis):
    return pltpu.roll(block, shift % block.shape[axis], axis)


def tree_sum(values):
    while len(values) > 1:
        values = [sum(values[at : at + 2]) for at in range(0, len(values), 2)]
    return values[0]


def slot_totals(acc):
    line = jnp.sum(acc, axis=0, keepdims=True)
    lane = lane_index(line.shape)
    first = jnp.sum(jnp.where(lane < HALF, line, 0.0), axis=1, keepdims=True)
    second = jnp.sum(jnp.where(lane < HALF, 0.0, line), axis=1, keepdims=True)
    return jnp.where(lane < HALF, first, second)


def swap_masks(peers):
    even = []
    mask = peers // 2
    while mask > 1:
        even.append(mask)
        mask //= 2
    odd = even[-1:] + even[:-1]
    return even, odd


def offset_of(t, parity, peers):
    even, odd = swap_masks(peers)
    offset = jnp.int32(0)
    for step, (mask_even, mask_odd) in enumerate(zip(even, odd)):
        mask = jnp.where(parity == 0, mask_even, mask_odd)
        offset = offset ^ (((t >> step) & 1) * mask)
    return offset


def gather_blocks(block, axis):
    peers = lax.axis_size(axis)
    held = block[None]
    for masks in zip(*swap_masks(peers)):
        pairs = [(i, i ^ masks[i % 2]) for i in range(peers)]
        held = jnp.concatenate([held, lax.ppermute(held, axis, pairs)], axis=0)
    return held, lax.ppermute(held, axis, [(i, i ^ 1) for i in range(peers)])


def solve_kernel(
    place_ref,
    shifts_ref,
    weights_ref,
    order_ref,
    mine_ref,
    theirs_ref,
    before_ref,
    state_ref,
    after_ref,
    adjoint_ref,
    share_ref,
    half_kappa,
    inner,
    outer_x,
    outer_y,
    outer_z,
    inner_sum,
    diagonal,
    damped,
    coarse_off,
    coarse_damped,
    residual,
    scaled,
    partial,
    first_dir,
    second_dir,
    image,
    coarse_one,
    coarse_two,
    planes,
):
    blocks, _, own, rows, _ = mine_ref.shape
    coarse_x = blocks * own
    rows = rows // 2
    tiles = rows // TILE
    shape = (TILE, 2 * HALF)
    lane = lane_index(shape)
    row = row_index(shape)
    slot0 = lane_index((1, 2 * HALF)) < HALF
    zero = jnp.zeros(shape, jnp.float32)

    def tile(j):
        return pl.ds(TILE * j, TILE)

    def every(b, j):
        return pl.ds(b + 2 * j, TILE, stride=2 * tiles)

    def pick(ref):
        return jnp.where(slot0, ref[order_ref[0]], ref[order_ref[1]])

    shift = pick(shifts_ref) + zero
    weight = pick(weights_ref) + zero

    def cls(a, b, c):
        return 4 * a + 2 * b + c

    pairs = [(p, q) for p in (0, 1) for q in (0, 1)]

    def before_row(load, j):
        return load(j - 1) if j else roll(load(tiles - 1), 1, 0)

    def after_row(load, j):
        return load(j + 1) if j + 1 < tiles else roll(load(0), -1, 0)

    for j in range(tiles):
        for ref in (half_kappa, scaled, first_dir, second_dir):
            for k in range(8):
                ref[k, 0, tile(j)] = zero
                ref[k, coarse_x + 1, tile(j)] = zero
        for ref in (coarse_one, coarse_two):
            ref[0, tile(j)] = zero
            ref[coarse_x + 1, tile(j)] = zero
        for k in range(4):
            outer_x[k, coarse_x, tile(j)] = zero
        coarse_off[0, coarse_x, tile(j)] = zero

    even_lane = 2 * (lane % HALF)

    def split(block):
        even = jnp.take_along_axis(block, even_lane, axis=1)
        odd = jnp.take_along_axis(block, even_lane + 1, axis=1)
        return even, odd

    def arrange(t, carry):
        for ref, holder in ((mine_ref, place_ref[0]), (theirs_ref, place_ref[0] ^ 1)):
            home = holder ^ offset_of(t, holder % 2, 2 * blocks)
            for x in range(own):
                a = x % 2
                spot = home * (own // 2) + x // 2
                for b in (0, 1):
                    for j in range(tiles):
                        block = ref[t, 0, x, every(b, j), :]
                        for c, value in enumerate(split(block)):
                            half_kappa[cls(a, b, c), spot + 1, tile(j)] = 0.5 * value
                        block = ref[t, 1, x, every(b, j), :]
                        for c, value in enumerate(split(block)):
                            residual[cls(a, b, c), spot, tile(j)] = weight * value
        return carry

    lax.fori_loop(0, blocks, arrange, 0)

    z_low = jnp.where(lane % HALF > 0, 1.0, 0.0)
    z_high = jnp.where(lane % HALF < HALF - 1, 1.0, 0.0)
    y_low = [jnp.where(row > 0, 1.0, 0.0)] + [None] * (tiles - 1)
    y_high = [None] * (tiles - 1) + [jnp.where(row < TILE - 1, 1.0, 0.0)]

    def masked(mask, value):
        return value if mask is None else mask * value

    def coefficients(i, carry):
        x_low = jnp.where(i > 0, 1.0, 0.0)
        for j in range(tiles):
            kap = [half_kappa[k, i + 1, tile(j)] for k in range(8)]
            total = [shift for _ in range(8)]
            inside = [[] for _ in range(8)]
            outside = []
            cx, cy, cz = [], ([], []), ([], [])
            for p, q in pairs:
                for kind, low, high in (
                    (0, cls(0, p, q), cls(1, p, q)),
                    (1, cls(p, 0, q), cls(p, 1, q)),
                    (2, cls(p, q, 0), cls(p, q, 1)),
                ):
                    face = kap[low] + kap[high]
                    inner[4 * kind + 2 * p + q, i, tile(j)] = face
                    inside[low].append(face)
                    inside[high].append(face)

                low, high = cls(0, p, q), cls(1, p, q)
                minus = kap[low] + half_kappa[high, i, tile(j)]
                plus = kap[high] + half_kappa[low, i + 2, tile(j)]
                total[low] = total[low] + minus
                total[high] = total[high] + plus
                outside.append(minus + plus)
                minus = x_low * minus
                outer_x[2 * p + q, i, tile(j)] = minus
                cx.append(minus)

                low, high = cls(p, 0, q), cls(p, 1, q)
                minus = kap[low] + masked(
                    y_low[j],
                    before_row(lambda r: half_kappa[high, i + 1, tile(r)], j),
                )
                plus = kap[high] + masked(
                    y_high[j],
                    after_row(lambda r: half_kappa[low, i + 1, tile(r)], j),
                )
                total[low] = total[low] + minus
                total[high] = total[high] + plus
                outside.append(minus + plus)
                minus, plus = masked(y_low[j], minus), masked(y_high[j], plus)
                outer_y[2 * p + q, i, tile(j)] = minus
                outer_y[4 + 2 * p + q, i, tile(j)] = plus
                cy[0].append(minus)
                cy[1].append(plus)

                low, high = cls(p, q, 0), cls(p, q, 1)
                minus = kap[low] + z_low * roll(kap[high], 1, 1)
                plus = kap[high] + z_high * roll(kap[low], -1, 1)
                total[low] = total[low] + minus
                total[high] = total[high] + plus
                outside.append(minus + plus)
                minus, plus = z_low * minus, z_high * plus
                outer_z[2 * p + q, i, tile(j)] = minus
                outer_z[4 + 2 * p + q, i, tile(j)] = plus
                cz[0].append(minus)
                cz[1].append(plus)
            for k in range(8):
                within = sum(inside[k])
                inner_sum[k, i, tile(j)] = within
                diag = total[k] + within
                diagonal[k, i, tile(j)] = diag
                inverse = DAMPING / diag
                damped[k, i, tile(j)] = inverse
                scaled[k, i + 1, tile(j)] = inverse * residual[k, i, tile(j)]
            for at, part in enumerate((cx, cy[0], cy[1], cz[0], cz[1])):
                coarse_off[at, i, tile(j)] = tree_sum(part)
            coarse_damped[i, tile(j)] = DAMPING / (8.0 * shift + tree_sum(outside))
        return carry

    lax.fori_loop(0, coarse_x, coefficients, 0)

    def stencil(field, i, j):
        here = [field[k, i + 1, tile(j)] for k in range(8)]
        terms = [[] for _ in range(8)]
        for p, q in pairs:
            for kind, low, high in (
                (0, cls(0, p, q), cls(1, p, q)),
                (1, cls(p, 0, q), cls(p, 1, q)),
                (2, cls(p, q, 0), cls(p, q, 1)),
            ):
                face = inner[4 * kind + 2 * p + q, i, tile(j)]
                terms[low].append(face * here[high])
                terms[high].append(face * here[low])
            at = 2 * p + q
            low, high = cls(0, p, q), cls(1, p, q)
            terms[low].append(outer_x[at, i, tile(j)] * field[high, i, tile(j)])
            terms[high].append(outer_x[at, i + 1, tile(j)] * field[low, i + 2, tile(j)])
            low, high = cls(p, 0, q), cls(p, 1, q)
            side = before_row(lambda r: field[high, i + 1, tile(r)], j)
            terms[low].append(outer_y[at, i, tile(j)] * side)
            side = after_row(lambda r: field[low, i + 1, tile(r)], j)
            terms[high].append(outer_y[4 + at, i, tile(j)] * side)
            low, high = cls(p, q, 0), cls(p, q, 1)
            terms[low].append(outer_z[at, i, tile(j)] * roll(here[high], 1, 1))
            terms[high].append(outer_z[4 + at, i, tile(j)] * roll(here[low], -1, 1))
        return here, [tree_sum(part) for part in terms]

    def coarse_sides(field, i, j):
        here = field[i + 1, tile(j)]
        return here, (
            (field[i, tile(j)], field[i + 2, tile(j)]),
            (
                before_row(lambda r: field[i + 1, tile(r)], j),
                after_row(lambda r: field[i + 1, tile(r)], j),
            ),
            (roll(here, 1, 1), roll(here, -1, 1)),
        )

    def precondition(result, other):
        def down(i, carry):
            for j in range(tiles):
                res = [residual[k, i, tile(j)] for k in range(8)]
                _, sums = stencil(scaled, i, j)
                parts = [(2.0 - DAMPING) * res[k] + sums[k] for k in range(8)]
                for k in range(8):
                    partial[k, i, tile(j)] = parts[k]
                rhs = tree_sum(parts) - tree_sum(res)
                coarse_one[i + 1, tile(j)] = coarse_damped[i, tile(j)] * rhs
            return carry

        lax.fori_loop(0, coarse_x, down, 0, unroll=2)

        def smooth(i, carry):
            for j in range(tiles):
                here, sides = coarse_sides(coarse_one, i, j)
                total = coarse_off[0, i, tile(j)] * sides[0][0]
                total = total + coarse_off[0, i + 1, tile(j)] * sides[0][1]
                total = total + coarse_off[1, i, tile(j)] * sides[1][0]
                total = total + coarse_off[2, i, tile(j)] * sides[1][1]
                total = total + coarse_off[3, i, tile(j)] * sides[2][0]
                total = total + coarse_off[4, i, tile(j)] * sides[2][1]
                coarse_two[i + 1, tile(j)] = (2.0 - DAMPING) * here + coarse_damped[
                    i, tile(j)
                ] * total
            return carry

        lax.fori_loop(0, coarse_x, smooth, 0, unroll=8)

        def up(i, carry):
            gamma, cross = carry
            for j in range(tiles):
                here, sides = coarse_sides(coarse_two, i, j)
                kept = (1.0 - DAMPING) * here
                dots, crosses = [], []
                for a in (0, 1):
                    for b in (0, 1):
                        for c in (0, 1):
                            k = cls(a, b, c)
                            value = tree_sum(
                                [
                                    partial[k, i, tile(j)],
                                    inner_sum[k, i, tile(j)] * here,
                                    outer_x[2 * b + c, i + a, tile(j)] * sides[0][a],
                                    outer_y[4 * b + 2 * a + c, i, tile(j)] * sides[1][b],
                                    outer_z[4 * c + 2 * a + b, i, tile(j)] * sides[2][c],
                                ]
                            )
                            new = kept + damped[k, i, tile(j)] * value
                            result[k, i + 1, tile(j)] = new
                            dots.append(residual[k, i, tile(j)] * new)
                            if other is not None:
                                crosses.append(other[k, i, tile(j)] * new)
                gamma = gamma + tree_sum(dots)
                if other is not None:
                    cross = cross + tree_sum(crosses)
            return gamma, cross

        sums = lax.fori_loop(0, coarse_x, up, (zero, zero), unroll=2)
        return [slot_totals(part) for part in sums]

    def curvature(field, keep):
        def step(i, acc):
            for j in range(tiles):
                here, sums = stencil(field, i, j)
                dots = []
                for k in range(8):
                    value = diagonal[k, i, tile(j)] * here[k] - sums[k]
                    if keep:
                        image[k, i, tile(j)] = value
                    dots.append(here[k] * value)
                acc = acc + tree_sum(dots)
            return acc

        return slot_totals(lax.fori_loop(0, coarse_x, step, zero, unroll=2))

    gamma, _ = precondition(first_dir, None)
    curve = curvature(first_dir, True)
    step_one = gamma / curve

    def update(i, carry):
        for j in range(tiles):
            for k in range(8):
                new = residual[k, i, tile(j)] - step_one * image[k, i, tile(j)]
                residual[k, i, tile(j)] = new
                scaled[k, i + 1, tile(j)] = damped[k, i, tile(j)] * new
        return carry

    lax.fori_loop(0, coarse_x, update, 0, unroll=2)

    gamma_next, cross = precondition(second_dir, image)
    ratio = gamma_next / gamma
    step_two = gamma_next / (
        curvature(second_dir, False) + ratio * (2.0 * cross + ratio * curve)
    )
    step_first = step_one + step_two * ratio

    start = place_ref[0] * (own // 2)
    even = lane % 2 == 0
    for at in range(own + 2):
        a = (at + 1) % 2
        spot = start + (at + 1) // 2
        for b in (0, 1):
            for j in range(tiles):
                both = [
                    step_first * first_dir[cls(a, b, c), spot, tile(j)]
                    + step_two * second_dir[cls(a, b, c), spot, tile(j)]
                    for c in (0, 1)
                ]
                for slot in (0, 1):
                    source = lane // 2 + HALF * slot
                    planes[slot, at, every(b, j), :] = jnp.where(
                        even,
                        jnp.take_along_axis(both[0], source, axis=1),
                        jnp.take_along_axis(both[1], source, axis=1),
                    )

    full = (2 * rows, 2 * HALF)
    y_at = row_index(full)
    z_at = lane_index(full)

    def drop(value, axis, up):
        moved = roll(value, -1 if up else 1, axis)
        at = (y_at, z_at)[axis]
        edge = full[axis] - 1 if up else 0
        return value - jnp.where(at == edge, 0.0, moved)

    groups = share_ref.shape[0]
    chunk = share_ref.shape[2]
    for j in range(own):
        term = jnp.zeros(full, jnp.float32)
        for slot in (0, 1):
            here = planes[slot, j + 1]
            adjoint_ref[slot, j] = here
            f = state_ref[slot, j]
            f_low = state_ref[slot, j - 1] if j else before_ref[slot, 0]
            f_high = state_ref[slot, j + 1] if j + 1 < own else after_ref[slot, 0]
            term = term + (here - planes[slot, j + 2]) * (f - f_high)
            term = term + (here - planes[slot, j]) * (f - f_low)
            for axis in (0, 1):
                for up in (True, False):
                    term = term + drop(here, axis, up) * drop(f, axis, up)
        planes[0, j] = -0.5 * term
        for k in range(groups):
            at = lax.rem(place_ref[1] + k, groups) * chunk
            share_ref[k, j] = planes[0, j, pl.ds(pl.multiple_of(at, chunk), chunk), :]


def whole_grid(conductivity, misfit, forward_states, pole_shifts, pole_weights, pole_order):
    members, own, ny, nz = forward_states.shape
    groups = lax.axis_size("pole")
    place = jnp.stack([lax.axis_index("space"), lax.axis_index("pole")]).astype(jnp.int32)
    peers = lax.axis_size("space")
    up = [(i, i + 1) for i in range(peers - 1)]
    down = [(i + 1, i) for i in range(peers - 1)]
    before = lax.ppermute(forward_states[:, own - 1 :], "space", up)
    after = lax.ppermute(forward_states[:, :1], "space", down)
    mine, theirs = gather_blocks(jnp.stack([conductivity, misfit]), "space")
    coarse_x, rows = peers * own // 2, ny // 2
    lanes = 2 * HALF

    def scratch(count, extent):
        return pltpu.VMEM((count, extent, rows, lanes), jnp.float32)

    smem = pl.BlockSpec(memory_space=pltpu.SMEM)
    vmem = pl.BlockSpec(memory_space=pltpu.VMEM)
    adjoint, share = pl.pallas_call(
        solve_kernel,
        out_shape=(
            jax.ShapeDtypeStruct(forward_states.shape, jnp.float32),
            jax.ShapeDtypeStruct((groups, own, ny // groups, nz), jnp.float32),
        ),
        in_specs=[smem] * 4 + [vmem] * 5,
        out_specs=(vmem, vmem),
        scratch_shapes=[
            scratch(8, coarse_x + 2),
            scratch(12, coarse_x),
            scratch(4, coarse_x + 1),
            scratch(8, coarse_x),
            scratch(8, coarse_x),
            scratch(8, coarse_x),
            scratch(8, coarse_x),
            scratch(8, coarse_x),
            scratch(5, coarse_x + 1),
            pltpu.VMEM((coarse_x, rows, lanes), jnp.float32),
            scratch(8, coarse_x),
            scratch(8, coarse_x + 2),
            scratch(8, coarse_x),
            scratch(8, coarse_x + 2),
            scratch(8, coarse_x + 2),
            scratch(8, coarse_x),
            pltpu.VMEM((coarse_x + 2, rows, lanes), jnp.float32),
            pltpu.VMEM((coarse_x + 2, rows, lanes), jnp.float32),
            pltpu.VMEM((members, own + 2, ny, nz), jnp.float32),
        ],
        compiler_params=pltpu.CompilerParams(vmem_limit_bytes=48 * 1024 * 1024),
        name="solve",
    )(
        place,
        pole_shifts,
        pole_weights,
        pole_order,
        mine,
        theirs,
        before,
        forward_states,
        after,
    )
    gradient = share[0]
    for k in range(1, groups):
        ring = [(i, (i + k) % groups) for i in range(groups)]
        gradient = gradient + lax.ppermute(share[k], "pole", ring)
    return adjoint, gradient


def plus_side(field, which_dim):
    extent = field.shape[which_dim]
    inner_part = lax.slice_in_dim(field, 1, extent, axis=which_dim)
    zero_plane = jnp.zeros_like(lax.slice_in_dim(field, 0, 1, axis=which_dim))
    return jnp.concatenate([inner_part, zero_plane], axis=which_dim)


def minus_side(field, which_dim):
    extent = field.shape[which_dim]
    inner_part = lax.slice_in_dim(field, 0, extent - 1, axis=which_dim)
    zero_plane = jnp.zeros_like(lax.slice_in_dim(field, 0, 1, axis=which_dim))
    return jnp.concatenate([zero_plane, inner_part], axis=which_dim)


def coarse_pick(faces, which_dim, offset):
    extent_x, extent_y, extent_z = faces.shape
    blocks = faces.reshape(extent_x // 2, 2, extent_y // 2, 2, extent_z // 2, 2)
    chosen = lax.index_in_dim(blocks, offset, axis=2 * which_dim + 1, keepdims=True)
    return jnp.sum(chosen, axis=(1, 3, 5))


def side_terms(field, plus_faces, minus_faces, widened):
    result = plus_faces[0] * (field - widened[:, 2:]) + minus_faces[0] * (field - widened[:, :-2])
    for which_dim in (1, 2):
        result = result + plus_faces[which_dim] * (field - plus_side(field, which_dim + 1))
        result = result + minus_faces[which_dim] * (field - minus_side(field, which_dim + 1))
    return result


def fine_image(field, plus_faces, minus_faces, shift_value):
    widened = extended(field, (("space", 1),), 1)
    return shift_value * field + side_terms(field, plus_faces, minus_faces, widened)


def coarse_image(field, plus_faces, minus_faces, shift_value):
    widened = extended(field, (("space", 1),), 1)
    return shift_value * field + side_terms(field, plus_faces, minus_faces, widened)


def restrict(field):
    members, extent_x, extent_y, extent_z = field.shape
    shaped = field.reshape(members, extent_x // 2, 2, extent_y // 2, 2, extent_z // 2, 2)
    return jnp.sum(shaped, axis=(2, 4, 6))


def prolong(field):
    return jnp.repeat(jnp.repeat(jnp.repeat(field, 2, axis=1), 2, axis=2), 2, axis=3)


def precondition(residual, fine, coarse):
    plus_faces, minus_faces, shift_value, diagonal = fine
    coarse_plus, coarse_minus, coarse_shift, coarse_diagonal = coarse
    smooth_one = DAMPING * residual / diagonal
    coarse_rhs = restrict(residual - fine_image(smooth_one, plus_faces, minus_faces, shift_value))
    coarse_one = DAMPING * coarse_rhs / coarse_diagonal
    coarse_two = (
        coarse_one
        + DAMPING
        * (coarse_rhs - coarse_image(coarse_one, coarse_plus, coarse_minus, coarse_shift))
        / coarse_diagonal
    )
    corrected = smooth_one + prolong(coarse_two)
    return (
        corrected
        + DAMPING
        * (residual - fine_image(corrected, plus_faces, minus_faces, shift_value))
        / diagonal
    )


def expand(values):
    return values.reshape(-1, 1, 1, 1)


def cell_sums(values):
    return jnp.sum(values, axis=(1, 2, 3))


def norm_sum(residual, precond):
    return lax.psum(cell_sums(residual * precond), "space")


def solve(rhs, fine, coarse):
    plus_faces, minus_faces, shift_value, diagonal = fine
    iterate = jnp.zeros_like(rhs)
    residual = rhs
    precond = precondition(residual, fine, coarse)
    gamma_now = norm_sum(residual, precond)
    search = precond
    for turn_index in range(ITERS):
        image_field = fine_image(search, plus_faces, minus_faces, shift_value)
        curve = lax.psum(cell_sums(search * image_field), "space")
        step_length = gamma_now / curve
        iterate = iterate + expand(step_length) * search
        if turn_index + 1 < ITERS:
            residual = residual - expand(step_length) * image_field
            precond = precondition(residual, fine, coarse)
            gamma_next = norm_sum(residual, precond)
            search = precond + expand(gamma_next / gamma_now) * search
            gamma_now = gamma_next
    return iterate


def divided(conductivity, misfit, forward_states, pole_shifts, pole_weights, pole_order):
    widened_kappa = extended(conductivity, (("space", 0),), 1)
    plus_faces = [
        0.5 * (conductivity + widened_kappa[2:]),
        0.5 * (conductivity + plus_side(conductivity, 1)),
        0.5 * (conductivity + plus_side(conductivity, 2)),
    ]
    minus_faces = [
        0.5 * (conductivity + widened_kappa[:-2]),
        0.5 * (conductivity + minus_side(conductivity, 1)),
        0.5 * (conductivity + minus_side(conductivity, 2)),
    ]
    base_diagonal = (
        plus_faces[0]
        + plus_faces[1]
        + plus_faces[2]
        + minus_faces[0]
        + minus_faces[1]
        + minus_faces[2]
    )
    coarse_plus = [coarse_pick(plus_faces[which_dim], which_dim, 1) for which_dim in range(3)]
    coarse_minus = [coarse_pick(minus_faces[which_dim], which_dim, 0) for which_dim in range(3)]
    coarse_base = (
        coarse_plus[0]
        + coarse_plus[1]
        + coarse_plus[2]
        + coarse_minus[0]
        + coarse_minus[1]
        + coarse_minus[2]
    )
    pole_index = jnp.arange(pole_shifts.shape[0], dtype=jnp.int32)
    matches = pole_order[:, None] == pole_index[None, :]
    shift_local = jnp.sum(jnp.where(matches, pole_shifts[None, :], 0.0), axis=1)
    weight_local = jnp.sum(jnp.where(matches, pole_weights[None, :], 0.0), axis=1)
    members = forward_states.shape[0]

    def solve_group(shift_part, weight_part):
        shift_value = expand(shift_part)
        fine = (plus_faces, minus_faces, shift_value, base_diagonal[None] + shift_value)
        coarse = (
            coarse_plus,
            coarse_minus,
            8.0 * shift_value,
            coarse_base[None] + 8.0 * shift_value,
        )
        return solve(expand(weight_part) * misfit[None], fine, coarse)

    adjoint_states = jnp.concatenate(
        [
            solve_group(shift_local[member : member + 1], weight_local[member : member + 1])
            for member in range(members)
        ],
        axis=0,
    )
    widened = extended(jnp.stack([adjoint_states, forward_states]), (("space", 2),), 1)
    term = (adjoint_states - widened[0, :, 2:]) * (forward_states - widened[1, :, 2:])
    term = term + (adjoint_states - widened[0, :, :-2]) * (forward_states - widened[1, :, :-2])
    for which_dim in (2, 3):
        term = term + (adjoint_states - plus_side(adjoint_states, which_dim)) * (
            forward_states - plus_side(forward_states, which_dim)
        )
        term = term + (adjoint_states - minus_side(adjoint_states, which_dim)) * (
            forward_states - minus_side(forward_states, which_dim)
        )
    local_term = -0.5 * jnp.sum(term, axis=0)
    gradient = lax.psum_scatter(local_term, "pole", scatter_dimension=1, tiled=True)
    return (adjoint_states, gradient)


def solution(mesh):
    in_specs = (
        P("space", None, None),
        P("space", None, None),
        P("pole", "space", None, None),
        P(),
        P(),
        P("pole"),
    )
    out_specs = (P("pole", "space", None, None), P("space", "pole", None))

    def body(conductivity, misfit, forward_states, *poles):
        nx = conductivity.shape[0] * lax.axis_size("space")
        _, ny, nz = conductivity.shape
        peers = lax.axis_size("space")
        small = nx * ny * nz <= REPLICATED_CELLS and forward_states.shape[0] == 2
        if small and nz == 2 * HALF and peers > 2 and peers & (peers - 1) == 0:
            return whole_grid(conductivity, misfit, forward_states, *poles)
        return divided(conductivity, misfit, forward_states, *poles)

    return jax.shard_map(
        body, mesh=mesh, in_specs=in_specs, out_specs=out_specs, check_vma=False
    )
```

```python
import functools

import jax
import jax.numpy as jnp
from jax import lax
from jax.experimental import pallas as pl
from jax.experimental.pallas import tpu as pltpu
from jax.sharding import PartitionSpec as P

ITERS = 2
DAMPING = 0.8
REPLICATED_CELLS = 32 * 64 * 128
HALF = 64
TILE = 8


def extended(array, sides, width):
    for axis, dim in sides:
        peers, length = (lax.axis_size(axis), array.shape[dim])
        up = [(i, (i + 1) % peers) for i in range(peers - 1)]
        down = [(j, i) for i, j in up]
        last = lax.slice_in_dim(array, length - width, length, axis=dim)
        leading = lax.slice_in_dim(array, 0, width, axis=dim)
        before = lax.ppermute(last, axis, up)
        after = lax.ppermute(leading, axis, down)
        array = jnp.concatenate([before, array, after], axis=dim)
    return array


def lane_index(shape):
    return lax.broadcasted_iota(jnp.int32, shape, len(shape) - 1)


def row_index(shape):
    return lax.broadcasted_iota(jnp.int32, shape, len(shape) - 2)


def roll(block, shift, axis):
    return pltpu.roll(block, shift % block.shape[axis], axis)


def tree_sum(values):
    while len(values) > 1:
        values = [sum(values[at : at + 2]) for at in range(0, len(values), 2)]
    return values[0]


def slot_totals(acc):
    line = jnp.sum(acc, axis=0, keepdims=True)
    lane = lane_index(line.shape)
    first = jnp.sum(jnp.where(lane < HALF, line, 0.0), axis=1, keepdims=True)
    second = jnp.sum(jnp.where(lane < HALF, 0.0, line), axis=1, keepdims=True)
    return jnp.where(lane < HALF, first, second)


def swap_masks(peers, flip):
    even = []
    mask = peers // 2
    while mask > 1:
        even.append(mask)
        mask //= 2
    odd = even[-1:] + even[:-1]
    return (odd, even) if flip else (even, odd)


def offset_of(t, parity, peers, flip):
    even, odd = swap_masks(peers, flip)
    offset = jnp.int32(0)
    for step, (mask_even, mask_odd) in enumerate(zip(even, odd)):
        mask = jnp.where(parity == 0, mask_even, mask_odd)
        offset = offset ^ (((t >> step) & 1) * mask)
    return offset


def gather_blocks(blocks, halos, axis):
    peers = lax.axis_size(axis)
    held = [block[None] for block in blocks]
    swaps = [list(zip(*swap_masks(peers, flip))) for flip in (False, True)]
    steps = len(swaps[0])
    for step in range(steps):
        if step == steps - 1:
            held[0], arrays = lax.optimization_barrier((held[0], [array for array, _ in halos]))
            halos = [lax.ppermute(array, axis, pairs) for array, (_, pairs) in zip(arrays, halos)]
        for at in (0, 1):
            masks = swaps[at][step]
            pairs = [(i, i ^ masks[i % 2]) for i in range(peers)]
            held[at] = jnp.concatenate([held[at], lax.ppermute(held[at], axis, pairs)], axis=0)
    held[0], halos = lax.optimization_barrier((held[0], halos))
    other = [lax.ppermute(part, axis, [(i, i ^ 1) for i in range(peers)]) for part in held]
    return held, other, halos


def solve_kernel(
    place_ref,
    shifts_ref,
    weights_ref,
    order_ref,
    kappa_mine_ref,
    misfit_mine_ref,
    kappa_theirs_ref,
    misfit_theirs_ref,
    before_ref,
    state_ref,
    after_ref,
    adjoint_ref,
    share_ref,
    half_kappa,
    inner,
    outer_x,
    outer_y,
    outer_z,
    inner_sum,
    diagonal,
    damped,
    coarse_off,
    coarse_damped,
    residual,
    scaled,
    partial,
    first_dir,
    second_dir,
    image,
    coarse_one,
    coarse_two,
    planes,
):
    blocks, own, rows, _ = kappa_mine_ref.shape
    coarse_x = blocks * own
    rows = rows // 2
    tiles = rows // TILE
    shape = (TILE, 2 * HALF)
    lane = lane_index(shape)
    row = row_index(shape)
    slot0 = lane_index((1, 2 * HALF)) < HALF
    zero = jnp.zeros(shape, jnp.float32)

    def tile(j):
        return pl.ds(TILE * j, TILE)

    def every(b, j):
        return pl.ds(b + 2 * j, TILE, stride=2 * tiles)

    def pick(ref):
        return jnp.where(slot0, ref[order_ref[0]], ref[order_ref[1]])

    shift = pick(shifts_ref) + zero
    weight = pick(weights_ref) + zero

    def cls(a, b, c):
        return 4 * a + 2 * b + c

    pairs = [(p, q) for p in (0, 1) for q in (0, 1)]

    def before_row(load, j):
        return load(j - 1) if j else roll(load(tiles - 1), 1, 0)

    def after_row(load, j):
        return load(j + 1) if j + 1 < tiles else roll(load(0), -1, 0)

    for j in range(tiles):
        for ref in (half_kappa, scaled, first_dir, second_dir):
            for k in range(8):
                ref[k, 0, tile(j)] = zero
                ref[k, coarse_x + 1, tile(j)] = zero
        for ref in (coarse_one, coarse_two):
            ref[0, tile(j)] = zero
            ref[coarse_x + 1, tile(j)] = zero
        for k in range(4):
            outer_x[k, coarse_x, tile(j)] = zero
        coarse_off[0, coarse_x, tile(j)] = zero

    even_lane = 2 * (lane % HALF)

    def split(block):
        even = jnp.take_along_axis(block, even_lane, axis=1)
        odd = jnp.take_along_axis(block, even_lane + 1, axis=1)
        return even, odd

    def arrange(t, carry):
        for flip, ref, holder in (
            (False, kappa_mine_ref, place_ref[0]),
            (False, kappa_theirs_ref, place_ref[0] ^ 1),
            (True, misfit_mine_ref, place_ref[0]),
            (True, misfit_theirs_ref, place_ref[0] ^ 1),
        ):
            home = holder ^ offset_of(t, holder % 2, 2 * blocks, flip)
            for x in range(own):
                a = x % 2
                spot = home * (own // 2) + x // 2
                for b in (0, 1):
                    for j in range(tiles):
                        for c, value in enumerate(split(ref[t, x, every(b, j), :])):
                            k = cls(a, b, c)
                            if flip:
                                residual[k, spot, tile(j)] = weight * value
                            else:
                                half_kappa[k, spot + 1, tile(j)] = 0.5 * value
        return carry

    lax.fori_loop(0, blocks, arrange, 0)

    z_low = jnp.where(lane % HALF > 0, 1.0, 0.0)
    z_high = jnp.where(lane % HALF < HALF - 1, 1.0, 0.0)
    y_low = [jnp.where(row > 0, 1.0, 0.0)] + [None] * (tiles - 1)
    y_high = [None] * (tiles - 1) + [jnp.where(row < TILE - 1, 1.0, 0.0)]

    def masked(mask, value):
        return value if mask is None else mask * value

    def coefficients(i, carry):
        x_low = jnp.where(i > 0, 1.0, 0.0)
        for j in range(tiles):
            kap = [half_kappa[k, i + 1, tile(j)] for k in range(8)]
            total = [shift for _ in range(8)]
            inside = [[] for _ in range(8)]
            outside = []
            cx, cy, cz = [], ([], []), ([], [])
            for p, q in pairs:
                for kind, low, high in (
                    (0, cls(0, p, q), cls(1, p, q)),
                    (1, cls(p, 0, q), cls(p, 1, q)),
                    (2, cls(p, q, 0), cls(p, q, 1)),
                ):
                    face = kap[low] + kap[high]
                    inner[4 * kind + 2 * p + q, i, tile(j)] = face
                    inside[low].append(face)
                    inside[high].append(face)

                low, high = cls(0, p, q), cls(1, p, q)
                minus = kap[low] + half_kappa[high, i, tile(j)]
                plus = kap[high] + half_kappa[low, i + 2, tile(j)]
                total[low] = total[low] + minus
                total[high] = total[high] + plus
                outside.append(minus + plus)
                minus = x_low * minus
                outer_x[2 * p + q, i, tile(j)] = minus
                cx.append(minus)

                low, high = cls(p, 0, q), cls(p, 1, q)
                minus = kap[low] + masked(
                    y_low[j],
                    before_row(lambda r: half_kappa[high, i + 1, tile(r)], j),
                )
                plus = kap[high] + masked(
                    y_high[j],
                    after_row(lambda r: half_kappa[low, i + 1, tile(r)], j),
                )
                total[low] = total[low] + minus
                total[high] = total[high] + plus
                outside.append(minus + plus)
                minus, plus = masked(y_low[j], minus), masked(y_high[j], plus)
                outer_y[2 * p + q, i, tile(j)] = minus
                outer_y[4 + 2 * p + q, i, tile(j)] = plus
                cy[0].append(minus)
                cy[1].append(plus)

                low, high = cls(p, q, 0), cls(p, q, 1)
                minus = kap[low] + z_low * roll(kap[high], 1, 1)
                plus = kap[high] + z_high * roll(kap[low], -1, 1)
                total[low] = total[low] + minus
                total[high] = total[high] + plus
                outside.append(minus + plus)
                minus, plus = z_low * minus, z_high * plus
                outer_z[2 * p + q, i, tile(j)] = minus
                outer_z[4 + 2 * p + q, i, tile(j)] = plus
                cz[0].append(minus)
                cz[1].append(plus)
            for k in range(8):
                within = sum(inside[k])
                inner_sum[k, i, tile(j)] = within
                diag = total[k] + within
                diagonal[k, i, tile(j)] = diag
                inverse = DAMPING / diag
                damped[k, i, tile(j)] = inverse
                scaled[k, i + 1, tile(j)] = inverse * residual[k, i, tile(j)]
            for at, part in enumerate((cx, cy[0], cy[1], cz[0], cz[1])):
                coarse_off[at, i, tile(j)] = tree_sum(part)
            coarse_damped[i, tile(j)] = DAMPING / (8.0 * shift + tree_sum(outside))
        return carry

    lax.fori_loop(0, coarse_x, coefficients, 0)

    def stencil(field, i, j):
        here = [field[k, i + 1, tile(j)] for k in range(8)]
        terms = [[] for _ in range(8)]
        for p, q in pairs:
            for kind, low, high in (
                (0, cls(0, p, q), cls(1, p, q)),
                (1, cls(p, 0, q), cls(p, 1, q)),
                (2, cls(p, q, 0), cls(p, q, 1)),
            ):
                face = inner[4 * kind + 2 * p + q, i, tile(j)]
                terms[low].append(face * here[high])
                terms[high].append(face * here[low])
            at = 2 * p + q
            low, high = cls(0, p, q), cls(1, p, q)
            terms[low].append(outer_x[at, i, tile(j)] * field[high, i, tile(j)])
            terms[high].append(outer_x[at, i + 1, tile(j)] * field[low, i + 2, tile(j)])
            low, high = cls(p, 0, q), cls(p, 1, q)
            side = before_row(lambda r: field[high, i + 1, tile(r)], j)
            terms[low].append(outer_y[at, i, tile(j)] * side)
            side = after_row(lambda r: field[low, i + 1, tile(r)], j)
            terms[high].append(outer_y[4 + at, i, tile(j)] * side)
            low, high = cls(p, q, 0), cls(p, q, 1)
            terms[low].append(outer_z[at, i, tile(j)] * roll(here[high], 1, 1))
            terms[high].append(outer_z[4 + at, i, tile(j)] * roll(here[low], -1, 1))
        return here, [tree_sum(part) for part in terms]

    def coarse_sides(field, i, j):
        here = field[i + 1, tile(j)]
        return here, (
            (field[i, tile(j)], field[i + 2, tile(j)]),
            (
                before_row(lambda r: field[i + 1, tile(r)], j),
                after_row(lambda r: field[i + 1, tile(r)], j),
            ),
            (roll(here, 1, 1), roll(here, -1, 1)),
        )

    def precondition(result, other):
        def down(i, carry):
            for j in range(tiles):
                res = [residual[k, i, tile(j)] for k in range(8)]
                _, sums = stencil(scaled, i, j)
                parts = [(2.0 - DAMPING) * res[k] + sums[k] for k in range(8)]
                for k in range(8):
                    partial[k, i, tile(j)] = parts[k]
                rhs = tree_sum(parts) - tree_sum(res)
                coarse_one[i + 1, tile(j)] = coarse_damped[i, tile(j)] * rhs
            return carry

        lax.fori_loop(0, coarse_x, down, 0, unroll=2)

        def smooth(i, carry):
            for j in range(tiles):
                here, sides = coarse_sides(coarse_one, i, j)
                total = coarse_off[0, i, tile(j)] * sides[0][0]
                total = total + coarse_off[0, i + 1, tile(j)] * sides[0][1]
                total = total + coarse_off[1, i, tile(j)] * sides[1][0]
                total = total + coarse_off[2, i, tile(j)] * sides[1][1]
                total = total + coarse_off[3, i, tile(j)] * sides[2][0]
                total = total + coarse_off[4, i, tile(j)] * sides[2][1]
                coarse_two[i + 1, tile(j)] = (2.0 - DAMPING) * here + coarse_damped[
                    i, tile(j)
                ] * total
            return carry

        lax.fori_loop(0, coarse_x, smooth, 0, unroll=8)

        def up(i, carry):
            gamma, cross = carry
            for j in range(tiles):
                here, sides = coarse_sides(coarse_two, i, j)
                kept = (1.0 - DAMPING) * here
                dots, crosses = [], []
                for a in (0, 1):
                    for b in (0, 1):
                        for c in (0, 1):
                            k = cls(a, b, c)
                            value = tree_sum(
                                [
                                    partial[k, i, tile(j)],
                                    inner_sum[k, i, tile(j)] * here,
                                    outer_x[2 * b + c, i + a, tile(j)] * sides[0][a],
                                    outer_y[4 * b + 2 * a + c, i, tile(j)] * sides[1][b],
                                    outer_z[4 * c + 2 * a + b, i, tile(j)] * sides[2][c],
                                ]
                            )
                            new = kept + damped[k, i, tile(j)] * value
                            result[k, i + 1, tile(j)] = new
                            dots.append(residual[k, i, tile(j)] * new)
                            if other is not None:
                                crosses.append(other[k, i, tile(j)] * new)
                gamma = gamma + tree_sum(dots)
                if other is not None:
                    cross = cross + tree_sum(crosses)
            return gamma, cross

        sums = lax.fori_loop(0, coarse_x, up, (zero, zero), unroll=2)
        return [slot_totals(part) for part in sums]

    def curvature(field, keep):
        def step(i, acc):
            for j in range(tiles):
                here, sums = stencil(field, i, j)
                dots = []
                for k in range(8):
                    value = diagonal[k, i, tile(j)] * here[k] - sums[k]
                    if keep:
                        image[k, i, tile(j)] = value
                    dots.append(here[k] * value)
                acc = acc + tree_sum(dots)
            return acc

        return slot_totals(lax.fori_loop(0, coarse_x, step, zero, unroll=2))

    gamma, _ = precondition(first_dir, None)
    curve = curvature(first_dir, True)
    step_one = gamma / curve

    def update(i, carry):
        for j in range(tiles):
            for k in range(8):
                new = residual[k, i, tile(j)] - step_one * image[k, i, tile(j)]
                residual[k, i, tile(j)] = new
                scaled[k, i + 1, tile(j)] = damped[k, i, tile(j)] * new
        return carry

    lax.fori_loop(0, coarse_x, update, 0, unroll=2)

    gamma_next, cross = precondition(second_dir, image)
    ratio = gamma_next / gamma
    step_two = gamma_next / (
        curvature(second_dir, False) + ratio * (2.0 * cross + ratio * curve)
    )
    step_first = step_one + step_two * ratio

    start = place_ref[0] * (own // 2)
    even = lane % 2 == 0
    for at in range(own + 2):
        a = (at + 1) % 2
        spot = start + (at + 1) // 2
        for b in (0, 1):
            for j in range(tiles):
                both = [
                    step_first * first_dir[cls(a, b, c), spot, tile(j)]
                    + step_two * second_dir[cls(a, b, c), spot, tile(j)]
                    for c in (0, 1)
                ]
                for slot in (0, 1):
                    source = lane // 2 + HALF * slot
                    planes[slot, at, every(b, j), :] = jnp.where(
                        even,
                        jnp.take_along_axis(both[0], source, axis=1),
                        jnp.take_along_axis(both[1], source, axis=1),
                    )

    full = (2 * rows, 2 * HALF)
    y_at = row_index(full)
    z_at = lane_index(full)

    def drop(value, axis, up):
        moved = roll(value, -1 if up else 1, axis)
        at = (y_at, z_at)[axis]
        edge = full[axis] - 1 if up else 0
        return value - jnp.where(at == edge, 0.0, moved)

    groups = share_ref.shape[0]
    chunk = share_ref.shape[2]
    for j in range(own):
        term = jnp.zeros(full, jnp.float32)
        for slot in (0, 1):
            here = planes[slot, j + 1]
            adjoint_ref[slot, j] = here
            f = state_ref[slot, j]
            f_low = state_ref[slot, j - 1] if j else before_ref[slot, 0]
            f_high = state_ref[slot, j + 1] if j + 1 < own else after_ref[slot, 0]
            term = term + (here - planes[slot, j + 2]) * (f - f_high)
            term = term + (here - planes[slot, j]) * (f - f_low)
            for axis in (0, 1):
                for up in (True, False):
                    term = term + drop(here, axis, up) * drop(f, axis, up)
        planes[0, j] = -0.5 * term
        for k in range(groups):
            at = lax.rem(place_ref[1] + k, groups) * chunk
            share_ref[k, j] = planes[0, j, pl.ds(pl.multiple_of(at, chunk), chunk), :]


def whole_grid(conductivity, misfit, forward_states, pole_shifts, pole_weights, pole_order):
    members, own, ny, nz = forward_states.shape
    groups = lax.axis_size("pole")
    place = jnp.stack([lax.axis_index("space"), lax.axis_index("pole")]).astype(jnp.int32)
    peers = lax.axis_size("space")
    up = [(i, i + 1) for i in range(peers - 1)]
    down = [(i + 1, i) for i in range(peers - 1)]
    halos = [(forward_states[:, own - 1 :], up), (forward_states[:, :1], down)]
    mine, theirs, halos = gather_blocks([conductivity, misfit], halos, "space")
    before, after = halos
    coarse_x, rows = peers * own // 2, ny // 2
    lanes = 2 * HALF

    def scratch(count, extent):
        return pltpu.VMEM((count, extent, rows, lanes), jnp.float32)

    smem = pl.BlockSpec(memory_space=pltpu.SMEM)
    vmem = pl.BlockSpec(memory_space=pltpu.VMEM)
    adjoint, share = pl.pallas_call(
        solve_kernel,
        out_shape=(
            jax.ShapeDtypeStruct(forward_states.shape, jnp.float32),
            jax.ShapeDtypeStruct((groups, own, ny // groups, nz), jnp.float32),
        ),
        in_specs=[smem] * 4 + [vmem] * 7,
        out_specs=(vmem, vmem),
        scratch_shapes=[
            scratch(8, coarse_x + 2),
            scratch(12, coarse_x),
            scratch(4, coarse_x + 1),
            scratch(8, coarse_x),
            scratch(8, coarse_x),
            scratch(8, coarse_x),
            scratch(8, coarse_x),
            scratch(8, coarse_x),
            scratch(5, coarse_x + 1),
            pltpu.VMEM((coarse_x, rows, lanes), jnp.float32),
            scratch(8, coarse_x),
            scratch(8, coarse_x + 2),
            scratch(8, coarse_x),
            scratch(8, coarse_x + 2),
            scratch(8, coarse_x + 2),
            scratch(8, coarse_x),
            pltpu.VMEM((coarse_x + 2, rows, lanes), jnp.float32),
            pltpu.VMEM((coarse_x + 2, rows, lanes), jnp.float32),
            pltpu.VMEM((members, own + 2, ny, nz), jnp.float32),
        ],
        compiler_params=pltpu.CompilerParams(vmem_limit_bytes=48 * 1024 * 1024),
        name="solve",
    )(
        place,
        pole_shifts,
        pole_weights,
        pole_order,
        *mine,
        *theirs,
        before,
        forward_states,
        after,
    )
    gradient = share[0]
    for k in range(1, groups):
        ring = [(i, (i + k) % groups) for i in range(groups)]
        gradient = gradient + lax.ppermute(share[k], "pole", ring)
    return adjoint, gradient


def plus_side(field, which_dim):
    extent = field.shape[which_dim]
    inner_part = lax.slice_in_dim(field, 1, extent, axis=which_dim)
    zero_plane = jnp.zeros_like(lax.slice_in_dim(field, 0, 1, axis=which_dim))
    return jnp.concatenate([inner_part, zero_plane], axis=which_dim)


def minus_side(field, which_dim):
    extent = field.shape[which_dim]
    inner_part = lax.slice_in_dim(field, 0, extent - 1, axis=which_dim)
    zero_plane = jnp.zeros_like(lax.slice_in_dim(field, 0, 1, axis=which_dim))
    return jnp.concatenate([zero_plane, inner_part], axis=which_dim)


def coarse_pick(faces, which_dim, offset):
    extent_x, extent_y, extent_z = faces.shape
    blocks = faces.reshape(extent_x // 2, 2, extent_y // 2, 2, extent_z // 2, 2)
    chosen = lax.index_in_dim(blocks, offset, axis=2 * which_dim + 1, keepdims=True)
    return jnp.sum(chosen, axis=(1, 3, 5))


def side_terms(field, plus_faces, minus_faces, widened):
    result = plus_faces[0] * (field - widened[:, 2:]) + minus_faces[0] * (field - widened[:, :-2])
    for which_dim in (1, 2):
        result = result + plus_faces[which_dim] * (field - plus_side(field, which_dim + 1))
        result = result + minus_faces[which_dim] * (field - minus_side(field, which_dim + 1))
    return result


def fine_image(field, plus_faces, minus_faces, shift_value):
    widened = extended(field, (("space", 1),), 1)
    return shift_value * field + side_terms(field, plus_faces, minus_faces, widened)


def coarse_image(field, plus_faces, minus_faces, shift_value):
    widened = extended(field, (("space", 1),), 1)
    return shift_value * field + side_terms(field, plus_faces, minus_faces, widened)


def restrict(field):
    members, extent_x, extent_y, extent_z = field.shape
    shaped = field.reshape(members, extent_x // 2, 2, extent_y // 2, 2, extent_z // 2, 2)
    return jnp.sum(shaped, axis=(2, 4, 6))


def prolong(field):
    return jnp.repeat(jnp.repeat(jnp.repeat(field, 2, axis=1), 2, axis=2), 2, axis=3)


def precondition(residual, fine, coarse):
    plus_faces, minus_faces, shift_value, diagonal = fine
    coarse_plus, coarse_minus, coarse_shift, coarse_diagonal = coarse
    smooth_one = DAMPING * residual / diagonal
    coarse_rhs = restrict(residual - fine_image(smooth_one, plus_faces, minus_faces, shift_value))
    coarse_one = DAMPING * coarse_rhs / coarse_diagonal
    coarse_two = (
        coarse_one
        + DAMPING
        * (coarse_rhs - coarse_image(coarse_one, coarse_plus, coarse_minus, coarse_shift))
        / coarse_diagonal
    )
    corrected = smooth_one + prolong(coarse_two)
    return (
        corrected
        + DAMPING
        * (residual - fine_image(corrected, plus_faces, minus_faces, shift_value))
        / diagonal
    )


def expand(values):
    return values.reshape(-1, 1, 1, 1)


def cell_sums(values):
    return jnp.sum(values, axis=(1, 2, 3))


def norm_sum(residual, precond):
    return lax.psum(cell_sums(residual * precond), "space")


def solve(rhs, fine, coarse):
    plus_faces, minus_faces, shift_value, diagonal = fine
    iterate = jnp.zeros_like(rhs)
    residual = rhs
    precond = precondition(residual, fine, coarse)
    gamma_now = norm_sum(residual, precond)
    search = precond
    for turn_index in range(ITERS):
        image_field = fine_image(search, plus_faces, minus_faces, shift_value)
        curve = lax.psum(cell_sums(search * image_field), "space")
        step_length = gamma_now / curve
        iterate = iterate + expand(step_length) * search
        if turn_index + 1 < ITERS:
            residual = residual - expand(step_length) * image_field
            precond = precondition(residual, fine, coarse)
            gamma_next = norm_sum(residual, precond)
            search = precond + expand(gamma_next / gamma_now) * search
            gamma_now = gamma_next
    return iterate


def divided(conductivity, misfit, forward_states, pole_shifts, pole_weights, pole_order):
    widened_kappa = extended(conductivity, (("space", 0),), 1)
    plus_faces = [
        0.5 * (conductivity + widened_kappa[2:]),
        0.5 * (conductivity + plus_side(conductivity, 1)),
        0.5 * (conductivity + plus_side(conductivity, 2)),
    ]
    minus_faces = [
        0.5 * (conductivity + widened_kappa[:-2]),
        0.5 * (conductivity + minus_side(conductivity, 1)),
        0.5 * (conductivity + minus_side(conductivity, 2)),
    ]
    base_diagonal = (
        plus_faces[0]
        + plus_faces[1]
        + plus_faces[2]
        + minus_faces[0]
        + minus_faces[1]
        + minus_faces[2]
    )
    coarse_plus = [coarse_pick(plus_faces[which_dim], which_dim, 1) for which_dim in range(3)]
    coarse_minus = [coarse_pick(minus_faces[which_dim], which_dim, 0) for which_dim in range(3)]
    coarse_base = (
        coarse_plus[0]
        + coarse_plus[1]
        + coarse_plus[2]
        + coarse_minus[0]
        + coarse_minus[1]
        + coarse_minus[2]
    )
    pole_index = jnp.arange(pole_shifts.shape[0], dtype=jnp.int32)
    matches = pole_order[:, None] == pole_index[None, :]
    shift_local = jnp.sum(jnp.where(matches, pole_shifts[None, :], 0.0), axis=1)
    weight_local = jnp.sum(jnp.where(matches, pole_weights[None, :], 0.0), axis=1)
    members = forward_states.shape[0]

    def solve_group(shift_part, weight_part):
        shift_value = expand(shift_part)
        fine = (plus_faces, minus_faces, shift_value, base_diagonal[None] + shift_value)
        coarse = (
            coarse_plus,
            coarse_minus,
            8.0 * shift_value,
            coarse_base[None] + 8.0 * shift_value,
        )
        return solve(expand(weight_part) * misfit[None], fine, coarse)

    adjoint_states = jnp.concatenate(
        [
            solve_group(shift_local[member : member + 1], weight_local[member : member + 1])
            for member in range(members)
        ],
        axis=0,
    )
    widened = extended(jnp.stack([adjoint_states, forward_states]), (("space", 2),), 1)
    term = (adjoint_states - widened[0, :, 2:]) * (forward_states - widened[1, :, 2:])
    term = term + (adjoint_states - widened[0, :, :-2]) * (forward_states - widened[1, :, :-2])
    for which_dim in (2, 3):
        term = term + (adjoint_states - plus_side(adjoint_states, which_dim)) * (
            forward_states - plus_side(forward_states, which_dim)
        )
        term = term + (adjoint_states - minus_side(adjoint_states, which_dim)) * (
            forward_states - minus_side(forward_states, which_dim)
        )
    local_term = -0.5 * jnp.sum(term, axis=0)
    gradient = lax.psum_scatter(local_term, "pole", scatter_dimension=1, tiled=True)
    return (adjoint_states, gradient)


def solution(mesh):
    in_specs = (
        P("space", None, None),
        P("space", None, None),
        P("pole", "space", None, None),
        P(),
        P(),
        P("pole"),
    )
    out_specs = (P("pole", "space", None, None), P("space", "pole", None))

    def body(conductivity, misfit, forward_states, *poles):
        nx = conductivity.shape[0] * lax.axis_size("space")
        _, ny, nz = conductivity.shape
        peers = lax.axis_size("space")
        small = nx * ny * nz <= REPLICATED_CELLS and forward_states.shape[0] == 2
        if small and nz == 2 * HALF and peers > 2 and peers & (peers - 1) == 0:
            return whole_grid(conductivity, misfit, forward_states, *poles)
        return divided(conductivity, misfit, forward_states, *poles)

    return jax.shard_map(
        body, mesh=mesh, in_specs=in_specs, out_specs=out_specs, check_vma=False
    )
```

```python
import functools

import jax
import jax.numpy as jnp
from jax import lax
from jax.experimental import pallas as pl
from jax.experimental.pallas import tpu as pltpu
from jax.sharding import PartitionSpec as P

ITERS = 2
DAMPING = 0.8
REPLICATED_CELLS = 32 * 64 * 128
HALF = 64
TILE = 8


def extended(array, sides, width):
    for axis, dim in sides:
        peers, length = (lax.axis_size(axis), array.shape[dim])
        up = [(i, (i + 1) % peers) for i in range(peers - 1)]
        down = [(j, i) for i, j in up]
        last = lax.slice_in_dim(array, length - width, length, axis=dim)
        leading = lax.slice_in_dim(array, 0, width, axis=dim)
        before = lax.ppermute(last, axis, up)
        after = lax.ppermute(leading, axis, down)
        array = jnp.concatenate([before, array, after], axis=dim)
    return array


def lane_index(shape):
    return lax.broadcasted_iota(jnp.int32, shape, len(shape) - 1)


def row_index(shape):
    return lax.broadcasted_iota(jnp.int32, shape, len(shape) - 2)


def roll(block, shift, axis):
    return pltpu.roll(block, shift % block.shape[axis], axis)


def tree_sum(values):
    while len(values) > 1:
        values = [sum(values[at : at + 2]) for at in range(0, len(values), 2)]
    return values[0]


def slot_totals(acc):
    line = jnp.sum(acc, axis=0, keepdims=True)
    lane = lane_index(line.shape)
    first = jnp.sum(jnp.where(lane < HALF, line, 0.0), axis=1, keepdims=True)
    second = jnp.sum(jnp.where(lane < HALF, 0.0, line), axis=1, keepdims=True)
    return jnp.where(lane < HALF, first, second)


def swap_masks(peers, flip):
    even = []
    mask = peers // 2
    while mask > 1:
        even.append(mask)
        mask //= 2
    odd = even[-1:] + even[:-1]
    return (odd, even) if flip else (even, odd)


def offset_of(t, parity, peers, flip):
    even, odd = swap_masks(peers, flip)
    offset = jnp.int32(0)
    for step, (mask_even, mask_odd) in enumerate(zip(even, odd)):
        mask = jnp.where(parity == 0, mask_even, mask_odd)
        offset = offset ^ (((t >> step) & 1) * mask)
    return offset


def gather_blocks(blocks, halos, axis):
    peers = lax.axis_size(axis)
    held = [block[None] for block in blocks]
    swaps = [list(zip(*swap_masks(peers, flip))) for flip in (False, True)]
    steps = len(swaps[0])
    for step in range(steps):
        if step == steps - 1:
            held[0], arrays = lax.optimization_barrier((held[0], [array for array, _ in halos]))
            halos = [lax.ppermute(array, axis, pairs) for array, (_, pairs) in zip(arrays, halos)]
        for at in (0, 1):
            masks = swaps[at][step]
            pairs = [(i, i ^ masks[i % 2]) for i in range(peers)]
            held[at] = jnp.concatenate([held[at], lax.ppermute(held[at], axis, pairs)], axis=0)
    other = [lax.ppermute(part, axis, [(i, i ^ 1) for i in range(peers)]) for part in held]
    return held, other, halos


def solve_kernel(
    place_ref,
    shifts_ref,
    weights_ref,
    order_ref,
    kappa_mine_ref,
    misfit_mine_ref,
    kappa_theirs_ref,
    misfit_theirs_ref,
    state_ref,
    far_ref,
    near_ref,
    adjoint_ref,
    share_ref,
    half_kappa,
    inner,
    outer_x,
    outer_y,
    outer_z,
    inner_sum,
    diagonal,
    damped,
    coarse_off,
    coarse_damped,
    residual,
    scaled,
    partial,
    first_dir,
    second_dir,
    image,
    coarse_one,
    coarse_two,
    planes,
):
    blocks, own, rows, _ = kappa_mine_ref.shape
    coarse_x = blocks * own
    rows = rows // 2
    tiles = rows // TILE
    shape = (TILE, 2 * HALF)
    lane = lane_index(shape)
    row = row_index(shape)
    slot0 = lane_index((1, 2 * HALF)) < HALF
    zero = jnp.zeros(shape, jnp.float32)

    def tile(j):
        return pl.ds(TILE * j, TILE)

    def every(b, j):
        return pl.ds(b + 2 * j, TILE, stride=2 * tiles)

    def pick(ref):
        return jnp.where(slot0, ref[order_ref[0]], ref[order_ref[1]])

    shift = pick(shifts_ref) + zero
    weight = pick(weights_ref) + zero

    def cls(a, b, c):
        return 4 * a + 2 * b + c

    pairs = [(p, q) for p in (0, 1) for q in (0, 1)]

    def before_row(load, j):
        return load(j - 1) if j else roll(load(tiles - 1), 1, 0)

    def after_row(load, j):
        return load(j + 1) if j + 1 < tiles else roll(load(0), -1, 0)

    for j in range(tiles):
        for ref in (half_kappa, scaled, first_dir, second_dir):
            for k in range(8):
                ref[k, 0, tile(j)] = zero
                ref[k, coarse_x + 1, tile(j)] = zero
        for ref in (coarse_one, coarse_two):
            ref[0, tile(j)] = zero
            ref[coarse_x + 1, tile(j)] = zero
        for k in range(4):
            outer_x[k, coarse_x, tile(j)] = zero
        coarse_off[0, coarse_x, tile(j)] = zero

    even_lane = 2 * (lane % HALF)

    def split(block):
        even = jnp.take_along_axis(block, even_lane, axis=1)
        odd = jnp.take_along_axis(block, even_lane + 1, axis=1)
        return even, odd

    def arrange(t, carry):
        for flip, ref, holder in (
            (False, kappa_mine_ref, place_ref[0]),
            (False, kappa_theirs_ref, place_ref[0] ^ 1),
            (True, misfit_mine_ref, place_ref[0]),
            (True, misfit_theirs_ref, place_ref[0] ^ 1),
        ):
            home = holder ^ offset_of(t, holder % 2, 2 * blocks, flip)
            for x in range(own):
                a = x % 2
                spot = home * (own // 2) + x // 2
                for b in (0, 1):
                    for j in range(tiles):
                        for c, value in enumerate(split(ref[t, x, every(b, j), :])):
                            k = cls(a, b, c)
                            if flip:
                                residual[k, spot, tile(j)] = weight * value
                            else:
                                half_kappa[k, spot + 1, tile(j)] = 0.5 * value
        return carry

    lax.fori_loop(0, blocks, arrange, 0)

    z_low = jnp.where(lane % HALF > 0, 1.0, 0.0)
    z_high = jnp.where(lane % HALF < HALF - 1, 1.0, 0.0)
    y_low = [jnp.where(row > 0, 1.0, 0.0)] + [None] * (tiles - 1)
    y_high = [None] * (tiles - 1) + [jnp.where(row < TILE - 1, 1.0, 0.0)]

    def masked(mask, value):
        return value if mask is None else mask * value

    def coefficients(i, carry):
        x_low = jnp.where(i > 0, 1.0, 0.0)
        for j in range(tiles):
            kap = [half_kappa[k, i + 1, tile(j)] for k in range(8)]
            total = [shift for _ in range(8)]
            inside = [[] for _ in range(8)]
            outside = []
            cx, cy, cz = [], ([], []), ([], [])
            for p, q in pairs:
                for kind, low, high in (
                    (0, cls(0, p, q), cls(1, p, q)),
                    (1, cls(p, 0, q), cls(p, 1, q)),
                    (2, cls(p, q, 0), cls(p, q, 1)),
                ):
                    face = kap[low] + kap[high]
                    inner[4 * kind + 2 * p + q, i, tile(j)] = face
                    inside[low].append(face)
                    inside[high].append(face)

                low, high = cls(0, p, q), cls(1, p, q)
                minus = kap[low] + half_kappa[high, i, tile(j)]
                plus = kap[high] + half_kappa[low, i + 2, tile(j)]
                total[low] = total[low] + minus
                total[high] = total[high] + plus
                outside.append(minus + plus)
                minus = x_low * minus
                outer_x[2 * p + q, i, tile(j)] = minus
                cx.append(minus)

                low, high = cls(p, 0, q), cls(p, 1, q)
                minus = kap[low] + masked(
                    y_low[j],
                    before_row(lambda r: half_kappa[high, i + 1, tile(r)], j),
                )
                plus = kap[high] + masked(
                    y_high[j],
                    after_row(lambda r: half_kappa[low, i + 1, tile(r)], j),
                )
                total[low] = total[low] + minus
                total[high] = total[high] + plus
                outside.append(minus + plus)
                minus, plus = masked(y_low[j], minus), masked(y_high[j], plus)
                outer_y[2 * p + q, i, tile(j)] = minus
                outer_y[4 + 2 * p + q, i, tile(j)] = plus
                cy[0].append(minus)
                cy[1].append(plus)

                low, high = cls(p, q, 0), cls(p, q, 1)
                minus = kap[low] + z_low * roll(kap[high], 1, 1)
                plus = kap[high] + z_high * roll(kap[low], -1, 1)
                total[low] = total[low] + minus
                total[high] = total[high] + plus
                outside.append(minus + plus)
                minus, plus = z_low * minus, z_high * plus
                outer_z[2 * p + q, i, tile(j)] = minus
                outer_z[4 + 2 * p + q, i, tile(j)] = plus
                cz[0].append(minus)
                cz[1].append(plus)
            for k in range(8):
                within = sum(inside[k])
                inner_sum[k, i, tile(j)] = within
                diag = total[k] + within
                diagonal[k, i, tile(j)] = diag
                inverse = DAMPING / diag
                damped[k, i, tile(j)] = inverse
                scaled[k, i + 1, tile(j)] = inverse * residual[k, i, tile(j)]
            for at, part in enumerate((cx, cy[0], cy[1], cz[0], cz[1])):
                coarse_off[at, i, tile(j)] = tree_sum(part)
            coarse_damped[i, tile(j)] = DAMPING / (8.0 * shift + tree_sum(outside))
        return carry

    lax.fori_loop(0, coarse_x, coefficients, 0)

    def stencil(field, i, j):
        here = [field[k, i + 1, tile(j)] for k in range(8)]
        terms = [[] for _ in range(8)]
        for p, q in pairs:
            for kind, low, high in (
                (0, cls(0, p, q), cls(1, p, q)),
                (1, cls(p, 0, q), cls(p, 1, q)),
                (2, cls(p, q, 0), cls(p, q, 1)),
            ):
                face = inner[4 * kind + 2 * p + q, i, tile(j)]
                terms[low].append(face * here[high])
                terms[high].append(face * here[low])
            at = 2 * p + q
            low, high = cls(0, p, q), cls(1, p, q)
            terms[low].append(outer_x[at, i, tile(j)] * field[high, i, tile(j)])
            terms[high].append(outer_x[at, i + 1, tile(j)] * field[low, i + 2, tile(j)])
            low, high = cls(p, 0, q), cls(p, 1, q)
            side = before_row(lambda r: field[high, i + 1, tile(r)], j)
            terms[low].append(outer_y[at, i, tile(j)] * side)
            side = after_row(lambda r: field[low, i + 1, tile(r)], j)
            terms[high].append(outer_y[4 + at, i, tile(j)] * side)
            low, high = cls(p, q, 0), cls(p, q, 1)
            terms[low].append(outer_z[at, i, tile(j)] * roll(here[high], 1, 1))
            terms[high].append(outer_z[4 + at, i, tile(j)] * roll(here[low], -1, 1))
        return here, [tree_sum(part) for part in terms]

    def coarse_sides(field, i, j):
        here = field[i + 1, tile(j)]
        return here, (
            (field[i, tile(j)], field[i + 2, tile(j)]),
            (
                before_row(lambda r: field[i + 1, tile(r)], j),
                after_row(lambda r: field[i + 1, tile(r)], j),
            ),
            (roll(here, 1, 1), roll(here, -1, 1)),
        )

    def precondition(result, other):
        def down(i, carry):
            for j in range(tiles):
                res = [residual[k, i, tile(j)] for k in range(8)]
                _, sums = stencil(scaled, i, j)
                parts = [(2.0 - DAMPING) * res[k] + sums[k] for k in range(8)]
                for k in range(8):
                    partial[k, i, tile(j)] = parts[k]
                rhs = tree_sum(parts) - tree_sum(res)
                coarse_one[i + 1, tile(j)] = coarse_damped[i, tile(j)] * rhs
            return carry

        lax.fori_loop(0, coarse_x, down, 0, unroll=2)

        def smooth(i, carry):
            for j in range(tiles):
                here, sides = coarse_sides(coarse_one, i, j)
                total = coarse_off[0, i, tile(j)] * sides[0][0]
                total = total + coarse_off[0, i + 1, tile(j)] * sides[0][1]
                total = total + coarse_off[1, i, tile(j)] * sides[1][0]
                total = total + coarse_off[2, i, tile(j)] * sides[1][1]
                total = total + coarse_off[3, i, tile(j)] * sides[2][0]
                total = total + coarse_off[4, i, tile(j)] * sides[2][1]
                coarse_two[i + 1, tile(j)] = (2.0 - DAMPING) * here + coarse_damped[
                    i, tile(j)
                ] * total
            return carry

        lax.fori_loop(0, coarse_x, smooth, 0, unroll=8)

        def up(i, carry):
            gamma, cross = carry
            for j in range(tiles):
                here, sides = coarse_sides(coarse_two, i, j)
                kept = (1.0 - DAMPING) * here
                dots, crosses = [], []
                for a in (0, 1):
                    for b in (0, 1):
                        for c in (0, 1):
                            k = cls(a, b, c)
                            value = tree_sum(
                                [
                                    partial[k, i, tile(j)],
                                    inner_sum[k, i, tile(j)] * here,
                                    outer_x[2 * b + c, i + a, tile(j)] * sides[0][a],
                                    outer_y[4 * b + 2 * a + c, i, tile(j)] * sides[1][b],
                                    outer_z[4 * c + 2 * a + b, i, tile(j)] * sides[2][c],
                                ]
                            )
                            new = kept + damped[k, i, tile(j)] * value
                            result[k, i + 1, tile(j)] = new
                            dots.append(residual[k, i, tile(j)] * new)
                            if other is not None:
                                crosses.append(other[k, i, tile(j)] * new)
                gamma = gamma + tree_sum(dots)
                if other is not None:
                    cross = cross + tree_sum(crosses)
            return gamma, cross

        sums = lax.fori_loop(0, coarse_x, up, (zero, zero), unroll=2)
        return [slot_totals(part) for part in sums]

    def curvature(field, keep):
        def step(i, acc):
            for j in range(tiles):
                here, sums = stencil(field, i, j)
                dots = []
                for k in range(8):
                    value = diagonal[k, i, tile(j)] * here[k] - sums[k]
                    if keep:
                        image[k, i, tile(j)] = value
                    dots.append(here[k] * value)
                acc = acc + tree_sum(dots)
            return acc

        return slot_totals(lax.fori_loop(0, coarse_x, step, zero, unroll=2))

    gamma, _ = precondition(first_dir, None)
    curve = curvature(first_dir, True)
    step_one = gamma / curve

    def update(i, carry):
        for j in range(tiles):
            for k in range(8):
                new = residual[k, i, tile(j)] - step_one * image[k, i, tile(j)]
                residual[k, i, tile(j)] = new
                scaled[k, i + 1, tile(j)] = damped[k, i, tile(j)] * new
        return carry

    lax.fori_loop(0, coarse_x, update, 0, unroll=2)

    gamma_next, cross = precondition(second_dir, image)
    ratio = gamma_next / gamma
    step_two = gamma_next / (
        curvature(second_dir, False) + ratio * (2.0 * cross + ratio * curve)
    )
    step_first = step_one + step_two * ratio

    start = place_ref[0] * (own // 2)
    even = lane % 2 == 0
    for at in range(own + 2):
        a = (at + 1) % 2
        spot = start + (at + 1) // 2
        for b in (0, 1):
            for j in range(tiles):
                both = [
                    step_first * first_dir[cls(a, b, c), spot, tile(j)]
                    + step_two * second_dir[cls(a, b, c), spot, tile(j)]
                    for c in (0, 1)
                ]
                for slot in (0, 1):
                    source = lane // 2 + HALF * slot
                    planes[slot, at, every(b, j), :] = jnp.where(
                        even,
                        jnp.take_along_axis(both[0], source, axis=1),
                        jnp.take_along_axis(both[1], source, axis=1),
                    )

    full = (2 * rows, 2 * HALF)
    y_at = row_index(full)
    z_at = lane_index(full)

    def drop(value, axis, up):
        moved = roll(value, -1 if up else 1, axis)
        at = (y_at, z_at)[axis]
        edge = full[axis] - 1 if up else 0
        return value - jnp.where(at == edge, 0.0, moved)

    is_even = place_ref[0] % 2 == 0
    groups = share_ref.shape[0]
    chunk = share_ref.shape[2]
    for j in range(own):
        term = jnp.zeros(full, jnp.float32)
        for slot in (0, 1):
            here = planes[slot, j + 1]
            adjoint_ref[slot, j] = here
            f = state_ref[slot, j]
            f_low = state_ref[slot, j - 1] if j else jnp.where(is_even, far_ref[slot, 0], near_ref[slot, 0])
            f_high = state_ref[slot, j + 1] if j + 1 < own else jnp.where(is_even, near_ref[slot, 0], far_ref[slot, 0])
            term = term + (here - planes[slot, j + 2]) * (f - f_high)
            term = term + (here - planes[slot, j]) * (f - f_low)
            for axis in (0, 1):
                for up in (True, False):
                    term = term + drop(here, axis, up) * drop(f, axis, up)
        planes[0, j] = -0.5 * term
        for k in range(groups):
            at = lax.rem(place_ref[1] + k, groups) * chunk
            share_ref[k, j] = planes[0, j, pl.ds(pl.multiple_of(at, chunk), chunk), :]


def whole_grid(conductivity, misfit, forward_states, pole_shifts, pole_weights, pole_order):
    members, own, ny, nz = forward_states.shape
    groups = lax.axis_size("pole")
    place = jnp.stack([lax.axis_index("space"), lax.axis_index("pole")]).astype(jnp.int32)
    peers = lax.axis_size("space")
    even = place[0] % 2 == 0
    first, last = forward_states[:, :1], forward_states[:, own - 1 :]
    near = [(i, i ^ 1) for i in range(peers)]
    far = [(i, i + 1 if i % 2 else i - 1) for i in range(1, peers - 1)]
    halos = [(jnp.where(even, first, last), far), (jnp.where(even, last, first), near)]
    mine, theirs, halos = gather_blocks([conductivity, misfit], halos, "space")
    far, near = halos
    coarse_x, rows = peers * own // 2, ny // 2
    lanes = 2 * HALF

    def scratch(count, extent):
        return pltpu.VMEM((count, extent, rows, lanes), jnp.float32)

    smem = pl.BlockSpec(memory_space=pltpu.SMEM)
    vmem = pl.BlockSpec(memory_space=pltpu.VMEM)
    adjoint, share = pl.pallas_call(
        solve_kernel,
        out_shape=(
            jax.ShapeDtypeStruct(forward_states.shape, jnp.float32),
            jax.ShapeDtypeStruct((groups, own, ny // groups, nz), jnp.float32),
        ),
        in_specs=[smem] * 4 + [vmem] * 7,
        out_specs=(vmem, vmem),
        scratch_shapes=[
            scratch(8, coarse_x + 2),
            scratch(12, coarse_x),
            scratch(4, coarse_x + 1),
            scratch(8, coarse_x),
            scratch(8, coarse_x),
            scratch(8, coarse_x),
            scratch(8, coarse_x),
            scratch(8, coarse_x),
            scratch(5, coarse_x + 1),
            pltpu.VMEM((coarse_x, rows, lanes), jnp.float32),
            scratch(8, coarse_x),
            scratch(8, coarse_x + 2),
            scratch(8, coarse_x),
            scratch(8, coarse_x + 2),
            scratch(8, coarse_x + 2),
            scratch(8, coarse_x),
            pltpu.VMEM((coarse_x + 2, rows, lanes), jnp.float32),
            pltpu.VMEM((coarse_x + 2, rows, lanes), jnp.float32),
            pltpu.VMEM((members, own + 2, ny, nz), jnp.float32),
        ],
        compiler_params=pltpu.CompilerParams(vmem_limit_bytes=48 * 1024 * 1024),
        name="solve",
    )(
        place,
        pole_shifts,
        pole_weights,
        pole_order,
        *mine,
        *theirs,
        forward_states,
        far,
        near,
    )
    gradient = share[0]
    for k in range(1, groups):
        ring = [(i, (i + k) % groups) for i in range(groups)]
        gradient = gradient + lax.ppermute(share[k], "pole", ring)
    return adjoint, gradient


def plus_side(field, which_dim):
    extent = field.shape[which_dim]
    inner_part = lax.slice_in_dim(field, 1, extent, axis=which_dim)
    zero_plane = jnp.zeros_like(lax.slice_in_dim(field, 0, 1, axis=which_dim))
    return jnp.concatenate([inner_part, zero_plane], axis=which_dim)


def minus_side(field, which_dim):
    extent = field.shape[which_dim]
    inner_part = lax.slice_in_dim(field, 0, extent - 1, axis=which_dim)
    zero_plane = jnp.zeros_like(lax.slice_in_dim(field, 0, 1, axis=which_dim))
    return jnp.concatenate([zero_plane, inner_part], axis=which_dim)


def coarse_pick(faces, which_dim, offset):
    extent_x, extent_y, extent_z = faces.shape
    blocks = faces.reshape(extent_x // 2, 2, extent_y // 2, 2, extent_z // 2, 2)
    chosen = lax.index_in_dim(blocks, offset, axis=2 * which_dim + 1, keepdims=True)
    return jnp.sum(chosen, axis=(1, 3, 5))


def side_terms(field, plus_faces, minus_faces, widened):
    result = plus_faces[0] * (field - widened[:, 2:]) + minus_faces[0] * (field - widened[:, :-2])
    for which_dim in (1, 2):
        result = result + plus_faces[which_dim] * (field - plus_side(field, which_dim + 1))
        result = result + minus_faces[which_dim] * (field - minus_side(field, which_dim + 1))
    return result


def fine_image(field, plus_faces, minus_faces, shift_value):
    widened = extended(field, (("space", 1),), 1)
    return shift_value * field + side_terms(field, plus_faces, minus_faces, widened)


def coarse_image(field, plus_faces, minus_faces, shift_value):
    widened = extended(field, (("space", 1),), 1)
    return shift_value * field + side_terms(field, plus_faces, minus_faces, widened)


def restrict(field):
    members, extent_x, extent_y, extent_z = field.shape
    shaped = field.reshape(members, extent_x // 2, 2, extent_y // 2, 2, extent_z // 2, 2)
    return jnp.sum(shaped, axis=(2, 4, 6))


def prolong(field):
    return jnp.repeat(jnp.repeat(jnp.repeat(field, 2, axis=1), 2, axis=2), 2, axis=3)


def precondition(residual, fine, coarse):
    plus_faces, minus_faces, shift_value, diagonal = fine
    coarse_plus, coarse_minus, coarse_shift, coarse_diagonal = coarse
    smooth_one = DAMPING * residual / diagonal
    coarse_rhs = restrict(residual - fine_image(smooth_one, plus_faces, minus_faces, shift_value))
    coarse_one = DAMPING * coarse_rhs / coarse_diagonal
    coarse_two = (
        coarse_one
        + DAMPING
        * (coarse_rhs - coarse_image(coarse_one, coarse_plus, coarse_minus, coarse_shift))
        / coarse_diagonal
    )
    corrected = smooth_one + prolong(coarse_two)
    return (
        corrected
        + DAMPING
        * (residual - fine_image(corrected, plus_faces, minus_faces, shift_value))
        / diagonal
    )


def expand(values):
    return values.reshape(-1, 1, 1, 1)


def cell_sums(values):
    return jnp.sum(values, axis=(1, 2, 3))


def norm_sum(residual, precond):
    return lax.psum(cell_sums(residual * precond), "space")


def solve(rhs, fine, coarse):
    plus_faces, minus_faces, shift_value, diagonal = fine
    iterate = jnp.zeros_like(rhs)
    residual = rhs
    precond = precondition(residual, fine, coarse)
    gamma_now = norm_sum(residual, precond)
    search = precond
    for turn_index in range(ITERS):
        image_field = fine_image(search, plus_faces, minus_faces, shift_value)
        curve = lax.psum(cell_sums(search * image_field), "space")
        step_length = gamma_now / curve
        iterate = iterate + expand(step_length) * search
        if turn_index + 1 < ITERS:
            residual = residual - expand(step_length) * image_field
            precond = precondition(residual, fine, coarse)
            gamma_next = norm_sum(residual, precond)
            search = precond + expand(gamma_next / gamma_now) * search
            gamma_now = gamma_next
    return iterate


def divided(conductivity, misfit, forward_states, pole_shifts, pole_weights, pole_order):
    widened_kappa = extended(conductivity, (("space", 0),), 1)
    plus_faces = [
        0.5 * (conductivity + widened_kappa[2:]),
        0.5 * (conductivity + plus_side(conductivity, 1)),
        0.5 * (conductivity + plus_side(conductivity, 2)),
    ]
    minus_faces = [
        0.5 * (conductivity + widened_kappa[:-2]),
        0.5 * (conductivity + minus_side(conductivity, 1)),
        0.5 * (conductivity + minus_side(conductivity, 2)),
    ]
    base_diagonal = (
        plus_faces[0]
        + plus_faces[1]
        + plus_faces[2]
        + minus_faces[0]
        + minus_faces[1]
        + minus_faces[2]
    )
    coarse_plus = [coarse_pick(plus_faces[which_dim], which_dim, 1) for which_dim in range(3)]
    coarse_minus = [coarse_pick(minus_faces[which_dim], which_dim, 0) for which_dim in range(3)]
    coarse_base = (
        coarse_plus[0]
        + coarse_plus[1]
        + coarse_plus[2]
        + coarse_minus[0]
        + coarse_minus[1]
        + coarse_minus[2]
    )
    pole_index = jnp.arange(pole_shifts.shape[0], dtype=jnp.int32)
    matches = pole_order[:, None] == pole_index[None, :]
    shift_local = jnp.sum(jnp.where(matches, pole_shifts[None, :], 0.0), axis=1)
    weight_local = jnp.sum(jnp.where(matches, pole_weights[None, :], 0.0), axis=1)
    members = forward_states.shape[0]

    def solve_group(shift_part, weight_part):
        shift_value = expand(shift_part)
        fine = (plus_faces, minus_faces, shift_value, base_diagonal[None] + shift_value)
        coarse = (
            coarse_plus,
            coarse_minus,
            8.0 * shift_value,
            coarse_base[None] + 8.0 * shift_value,
        )
        return solve(expand(weight_part) * misfit[None], fine, coarse)

    adjoint_states = jnp.concatenate(
        [
            solve_group(shift_local[member : member + 1], weight_local[member : member + 1])
            for member in range(members)
        ],
        axis=0,
    )
    widened = extended(jnp.stack([adjoint_states, forward_states]), (("space", 2),), 1)
    term = (adjoint_states - widened[0, :, 2:]) * (forward_states - widened[1, :, 2:])
    term = term + (adjoint_states - widened[0, :, :-2]) * (forward_states - widened[1, :, :-2])
    for which_dim in (2, 3):
        term = term + (adjoint_states - plus_side(adjoint_states, which_dim)) * (
            forward_states - plus_side(forward_states, which_dim)
        )
        term = term + (adjoint_states - minus_side(adjoint_states, which_dim)) * (
            forward_states - minus_side(forward_states, which_dim)
        )
    local_term = -0.5 * jnp.sum(term, axis=0)
    gradient = lax.psum_scatter(local_term, "pole", scatter_dimension=1, tiled=True)
    return (adjoint_states, gradient)


def solution(mesh):
    in_specs = (
        P("space", None, None),
        P("space", None, None),
        P("pole", "space", None, None),
        P(),
        P(),
        P("pole"),
    )
    out_specs = (P("pole", "space", None, None), P("space", "pole", None))

    def body(conductivity, misfit, forward_states, *poles):
        nx = conductivity.shape[0] * lax.axis_size("space")
        _, ny, nz = conductivity.shape
        peers = lax.axis_size("space")
        small = nx * ny * nz <= REPLICATED_CELLS and forward_states.shape[0] == 2
        if small and nz == 2 * HALF and peers > 2 and peers & (peers - 1) == 0:
            return whole_grid(conductivity, misfit, forward_states, *poles)
        return divided(conductivity, misfit, forward_states, *poles)

    return jax.shard_map(
        body, mesh=mesh, in_specs=in_specs, out_specs=out_specs, check_vma=False
    )
```

```python
import functools

import jax
import jax.numpy as jnp
from jax import lax
from jax.experimental import pallas as pl
from jax.experimental.pallas import tpu as pltpu
from jax.sharding import PartitionSpec as P

ITERS = 2
DAMPING = 0.8
REPLICATED_CELLS = 32 * 64 * 128
HALF = 64
TILE = 8


def extended(array, sides, width):
    for axis, dim in sides:
        peers, length = (lax.axis_size(axis), array.shape[dim])
        up = [(i, (i + 1) % peers) for i in range(peers - 1)]
        down = [(j, i) for i, j in up]
        last = lax.slice_in_dim(array, length - width, length, axis=dim)
        leading = lax.slice_in_dim(array, 0, width, axis=dim)
        before = lax.ppermute(last, axis, up)
        after = lax.ppermute(leading, axis, down)
        array = jnp.concatenate([before, array, after], axis=dim)
    return array


def lane_index(shape):
    return lax.broadcasted_iota(jnp.int32, shape, len(shape) - 1)


def row_index(shape):
    return lax.broadcasted_iota(jnp.int32, shape, len(shape) - 2)


def roll(block, shift, axis):
    return pltpu.roll(block, shift % block.shape[axis], axis)


def tree_sum(values):
    while len(values) > 1:
        values = [sum(values[at : at + 2]) for at in range(0, len(values), 2)]
    return values[0]


def slot_totals(acc):
    line = jnp.sum(acc, axis=0, keepdims=True)
    lane = lane_index(line.shape)
    first = jnp.sum(jnp.where(lane < HALF, line, 0.0), axis=1, keepdims=True)
    second = jnp.sum(jnp.where(lane < HALF, 0.0, line), axis=1, keepdims=True)
    return jnp.where(lane < HALF, first, second)


def swap_masks(peers, flip):
    even = []
    mask = peers // 2
    while mask > 1:
        even.append(mask)
        mask //= 2
    odd = even[-1:] + even[:-1]
    return (odd, even) if flip else (even, odd)


def offset_of(t, parity, peers, flip):
    even, odd = swap_masks(peers, flip)
    offset = jnp.int32(0)
    for step, (mask_even, mask_odd) in enumerate(zip(even, odd)):
        mask = jnp.where(parity == 0, mask_even, mask_odd)
        offset = offset ^ (((t >> step) & 1) * mask)
    return offset


def gather_blocks(blocks, halos, axis):
    peers = lax.axis_size(axis)
    own_half = lax.optimization_barrier(0.5 * blocks[0][None])
    held = [block[None] for block in blocks]
    halos = [lax.ppermute(array, axis, pairs) for array, pairs in halos]
    swaps = [list(zip(*swap_masks(peers, flip))) for flip in (False, True)]
    steps = len(swaps[0])
    for step in range(steps):
        if step == steps - 1:
            held[0], halos[0] = lax.optimization_barrier((held[0], halos[0]))
        for at in (0, 1):
            masks = swaps[at][step]
            pairs = [(i, i ^ masks[i % 2]) for i in range(peers)]
            arrived = lax.ppermute(held[at], axis, pairs)
            if step == 0 and at == 0:
                held[0], arrived = own_half, 0.5 * arrived
            held[at] = jnp.concatenate([held[at], arrived], axis=0)
    held[0], halos[1] = lax.optimization_barrier((held[0], halos[1]))
    other = [lax.ppermute(part, axis, [(i, i ^ 1) for i in range(peers)]) for part in held]
    return held, other, halos


def solve_kernel(
    place_ref,
    shifts_ref,
    weights_ref,
    order_ref,
    kappa_mine_ref,
    misfit_mine_ref,
    kappa_theirs_ref,
    misfit_theirs_ref,
    state_ref,
    far_ref,
    near_ref,
    adjoint_ref,
    share_ref,
    half_kappa,
    inner,
    outer_x,
    outer_y,
    outer_z,
    inner_sum,
    diagonal,
    damped,
    coarse_off,
    coarse_damped,
    residual,
    scaled,
    partial,
    first_dir,
    second_dir,
    image,
    coarse_one,
    coarse_two,
    planes,
):
    blocks, own, rows, _ = kappa_mine_ref.shape
    coarse_x = blocks * own
    rows = rows // 2
    tiles = rows // TILE
    shape = (TILE, 2 * HALF)
    lane = lane_index(shape)
    row = row_index(shape)
    slot0 = lane_index((1, 2 * HALF)) < HALF
    zero = jnp.zeros(shape, jnp.float32)

    def tile(j):
        return pl.ds(TILE * j, TILE)

    def every(b, j):
        return pl.ds(b + 2 * j, TILE, stride=2 * tiles)

    def pick(ref):
        return jnp.where(slot0, ref[order_ref[0]], ref[order_ref[1]])

    shift = pick(shifts_ref) + zero
    weight = pick(weights_ref) + zero

    def cls(a, b, c):
        return 4 * a + 2 * b + c

    pairs = [(p, q) for p in (0, 1) for q in (0, 1)]

    def before_row(load, j):
        return load(j - 1) if j else roll(load(tiles - 1), 1, 0)

    def after_row(load, j):
        return load(j + 1) if j + 1 < tiles else roll(load(0), -1, 0)

    for j in range(tiles):
        for ref in (half_kappa, scaled, first_dir, second_dir):
            for k in range(8):
                ref[k, 0, tile(j)] = zero
                ref[k, coarse_x + 1, tile(j)] = zero
        for ref in (coarse_one, coarse_two):
            ref[0, tile(j)] = zero
            ref[coarse_x + 1, tile(j)] = zero
        for k in range(4):
            outer_x[k, coarse_x, tile(j)] = zero
        coarse_off[0, coarse_x, tile(j)] = zero

    even_lane = 2 * (lane % HALF)

    def split(block):
        even = jnp.take_along_axis(block, even_lane, axis=1)
        odd = jnp.take_along_axis(block, even_lane + 1, axis=1)
        return even, odd

    def arrange(t, carry):
        for flip, ref, holder in (
            (False, kappa_mine_ref, place_ref[0]),
            (False, kappa_theirs_ref, place_ref[0] ^ 1),
            (True, misfit_mine_ref, place_ref[0]),
            (True, misfit_theirs_ref, place_ref[0] ^ 1),
        ):
            home = holder ^ offset_of(t, holder % 2, 2 * blocks, flip)
            for x in range(own):
                a = x % 2
                spot = home * (own // 2) + x // 2
                for b in (0, 1):
                    for j in range(tiles):
                        for c, value in enumerate(split(ref[t, x, every(b, j), :])):
                            k = cls(a, b, c)
                            if flip:
                                residual[k, spot, tile(j)] = weight * value
                            else:
                                half_kappa[k, spot + 1, tile(j)] = value
        return carry

    lax.fori_loop(0, blocks, arrange, 0)

    z_low = jnp.where(lane % HALF > 0, 1.0, 0.0)
    z_high = jnp.where(lane % HALF < HALF - 1, 1.0, 0.0)
    y_low = [jnp.where(row > 0, 1.0, 0.0)] + [None] * (tiles - 1)
    y_high = [None] * (tiles - 1) + [jnp.where(row < TILE - 1, 1.0, 0.0)]

    def masked(mask, value):
        return value if mask is None else mask * value

    def coefficients(i, carry):
        x_low = jnp.where(i > 0, 1.0, 0.0)
        for j in range(tiles):
            kap = [half_kappa[k, i + 1, tile(j)] for k in range(8)]
            total = [shift for _ in range(8)]
            inside = [[] for _ in range(8)]
            outside = []
            cx, cy, cz = [], ([], []), ([], [])
            for p, q in pairs:
                for kind, low, high in (
                    (0, cls(0, p, q), cls(1, p, q)),
                    (1, cls(p, 0, q), cls(p, 1, q)),
                    (2, cls(p, q, 0), cls(p, q, 1)),
                ):
                    face = kap[low] + kap[high]
                    inner[4 * kind + 2 * p + q, i, tile(j)] = face
                    inside[low].append(face)
                    inside[high].append(face)

                low, high = cls(0, p, q), cls(1, p, q)
                minus = kap[low] + half_kappa[high, i, tile(j)]
                plus = kap[high] + half_kappa[low, i + 2, tile(j)]
                total[low] = total[low] + minus
                total[high] = total[high] + plus
                outside.append(minus + plus)
                minus = x_low * minus
                outer_x[2 * p + q, i, tile(j)] = minus
                cx.append(minus)

                low, high = cls(p, 0, q), cls(p, 1, q)
                minus = kap[low] + masked(
                    y_low[j],
                    before_row(lambda r: half_kappa[high, i + 1, tile(r)], j),
                )
                plus = kap[high] + masked(
                    y_high[j],
                    after_row(lambda r: half_kappa[low, i + 1, tile(r)], j),
                )
                total[low] = total[low] + minus
                total[high] = total[high] + plus
                outside.append(minus + plus)
                minus, plus = masked(y_low[j], minus), masked(y_high[j], plus)
                outer_y[2 * p + q, i, tile(j)] = minus
                outer_y[4 + 2 * p + q, i, tile(j)] = plus
                cy[0].append(minus)
                cy[1].append(plus)

                low, high = cls(p, q, 0), cls(p, q, 1)
                minus = kap[low] + z_low * roll(kap[high], 1, 1)
                plus = kap[high] + z_high * roll(kap[low], -1, 1)
                total[low] = total[low] + minus
                total[high] = total[high] + plus
                outside.append(minus + plus)
                minus, plus = z_low * minus, z_high * plus
                outer_z[2 * p + q, i, tile(j)] = minus
                outer_z[4 + 2 * p + q, i, tile(j)] = plus
                cz[0].append(minus)
                cz[1].append(plus)
            for k in range(8):
                within = sum(inside[k])
                inner_sum[k, i, tile(j)] = within
                diag = total[k] + within
                diagonal[k, i, tile(j)] = diag
                inverse = DAMPING / diag
                damped[k, i, tile(j)] = inverse
                scaled[k, i + 1, tile(j)] = inverse * residual[k, i, tile(j)]
            for at, part in enumerate((cx, cy[0], cy[1], cz[0], cz[1])):
                coarse_off[at, i, tile(j)] = tree_sum(part)
            coarse_damped[i, tile(j)] = DAMPING / (8.0 * shift + tree_sum(outside))
        return carry

    lax.fori_loop(0, coarse_x, coefficients, 0)

    def stencil(field, i, j):
        here = [field[k, i + 1, tile(j)] for k in range(8)]
        terms = [[] for _ in range(8)]
        for p, q in pairs:
            for kind, low, high in (
                (0, cls(0, p, q), cls(1, p, q)),
                (1, cls(p, 0, q), cls(p, 1, q)),
                (2, cls(p, q, 0), cls(p, q, 1)),
            ):
                face = inner[4 * kind + 2 * p + q, i, tile(j)]
                terms[low].append(face * here[high])
                terms[high].append(face * here[low])
            at = 2 * p + q
            low, high = cls(0, p, q), cls(1, p, q)
            terms[low].append(outer_x[at, i, tile(j)] * field[high, i, tile(j)])
            terms[high].append(outer_x[at, i + 1, tile(j)] * field[low, i + 2, tile(j)])
            low, high = cls(p, 0, q), cls(p, 1, q)
            side = before_row(lambda r: field[high, i + 1, tile(r)], j)
            terms[low].append(outer_y[at, i, tile(j)] * side)
            side = after_row(lambda r: field[low, i + 1, tile(r)], j)
            terms[high].append(outer_y[4 + at, i, tile(j)] * side)
            low, high = cls(p, q, 0), cls(p, q, 1)
            terms[low].append(outer_z[at, i, tile(j)] * roll(here[high], 1, 1))
            terms[high].append(outer_z[4 + at, i, tile(j)] * roll(here[low], -1, 1))
        return here, [tree_sum(part) for part in terms]

    def coarse_sides(field, i, j):
        here = field[i + 1, tile(j)]
        return here, (
            (field[i, tile(j)], field[i + 2, tile(j)]),
            (
                before_row(lambda r: field[i + 1, tile(r)], j),
                after_row(lambda r: field[i + 1, tile(r)], j),
            ),
            (roll(here, 1, 1), roll(here, -1, 1)),
        )

    def precondition(result, other):
        def down(i, carry):
            for j in range(tiles):
                res = [residual[k, i, tile(j)] for k in range(8)]
                _, sums = stencil(scaled, i, j)
                parts = [(2.0 - DAMPING) * res[k] + sums[k] for k in range(8)]
                for k in range(8):
                    partial[k, i, tile(j)] = parts[k]
                rhs = tree_sum(parts) - tree_sum(res)
                coarse_one[i + 1, tile(j)] = coarse_damped[i, tile(j)] * rhs
            return carry

        lax.fori_loop(0, coarse_x, down, 0, unroll=2)

        def smooth(i, carry):
            for j in range(tiles):
                here, sides = coarse_sides(coarse_one, i, j)
                total = coarse_off[0, i, tile(j)] * sides[0][0]
                total = total + coarse_off[0, i + 1, tile(j)] * sides[0][1]
                total = total + coarse_off[1, i, tile(j)] * sides[1][0]
                total = total + coarse_off[2, i, tile(j)] * sides[1][1]
                total = total + coarse_off[3, i, tile(j)] * sides[2][0]
                total = total + coarse_off[4, i, tile(j)] * sides[2][1]
                coarse_two[i + 1, tile(j)] = (2.0 - DAMPING) * here + coarse_damped[
                    i, tile(j)
                ] * total
            return carry

        lax.fori_loop(0, coarse_x, smooth, 0, unroll=8)

        def up(i, carry):
            gamma, cross = carry
            for j in range(tiles):
                here, sides = coarse_sides(coarse_two, i, j)
                kept = (1.0 - DAMPING) * here
                dots, crosses = [], []
                for a in (0, 1):
                    for b in (0, 1):
                        for c in (0, 1):
                            k = cls(a, b, c)
                            value = tree_sum(
                                [
                                    partial[k, i, tile(j)],
                                    inner_sum[k, i, tile(j)] * here,
                                    outer_x[2 * b + c, i + a, tile(j)] * sides[0][a],
                                    outer_y[4 * b + 2 * a + c, i, tile(j)] * sides[1][b],
                                    outer_z[4 * c + 2 * a + b, i, tile(j)] * sides[2][c],
                                ]
                            )
                            new = kept + damped[k, i, tile(j)] * value
                            result[k, i + 1, tile(j)] = new
                            dots.append(residual[k, i, tile(j)] * new)
                            if other is not None:
                                crosses.append(other[k, i, tile(j)] * new)
                gamma = gamma + tree_sum(dots)
                if other is not None:
                    cross = cross + tree_sum(crosses)
            return gamma, cross

        sums = lax.fori_loop(0, coarse_x, up, (zero, zero), unroll=2)
        return [slot_totals(part) for part in sums]

    def curvature(field, keep):
        def step(i, acc):
            for j in range(tiles):
                here, sums = stencil(field, i, j)
                dots = []
                for k in range(8):
                    value = diagonal[k, i, tile(j)] * here[k] - sums[k]
                    if keep:
                        image[k, i, tile(j)] = value
                    dots.append(here[k] * value)
                acc = acc + tree_sum(dots)
            return acc

        return slot_totals(lax.fori_loop(0, coarse_x, step, zero, unroll=2))

    gamma, _ = precondition(first_dir, None)
    curve = curvature(first_dir, True)
    step_one = gamma / curve

    def update(i, carry):
        for j in range(tiles):
            for k in range(8):
                new = residual[k, i, tile(j)] - step_one * image[k, i, tile(j)]
                residual[k, i, tile(j)] = new
                scaled[k, i + 1, tile(j)] = damped[k, i, tile(j)] * new
        return carry

    lax.fori_loop(0, coarse_x, update, 0, unroll=2)

    gamma_next, cross = precondition(second_dir, image)
    ratio = gamma_next / gamma
    step_two = gamma_next / (
        curvature(second_dir, False) + ratio * (2.0 * cross + ratio * curve)
    )
    step_first = step_one + step_two * ratio

    start = place_ref[0] * (own // 2)
    even = lane % 2 == 0
    for at in range(own + 2):
        a = (at + 1) % 2
        spot = start + (at + 1) // 2
        for b in (0, 1):
            for j in range(tiles):
                both = [
                    step_first * first_dir[cls(a, b, c), spot, tile(j)]
                    + step_two * second_dir[cls(a, b, c), spot, tile(j)]
                    for c in (0, 1)
                ]
                for slot in (0, 1):
                    source = lane // 2 + HALF * slot
                    planes[slot, at, every(b, j), :] = jnp.where(
                        even,
                        jnp.take_along_axis(both[0], source, axis=1),
                        jnp.take_along_axis(both[1], source, axis=1),
                    )

    full = (2 * rows, 2 * HALF)
    y_at = row_index(full)
    z_at = lane_index(full)

    def drop(value, axis, up):
        moved = roll(value, -1 if up else 1, axis)
        at = (y_at, z_at)[axis]
        edge = full[axis] - 1 if up else 0
        return value - jnp.where(at == edge, 0.0, moved)

    is_even = place_ref[0] % 2 == 0
    groups = share_ref.shape[0]
    chunk = share_ref.shape[2]
    for j in range(own):
        term = jnp.zeros(full, jnp.float32)
        for slot in (0, 1):
            here = planes[slot, j + 1]
            adjoint_ref[slot, j] = here
            f = state_ref[slot, j]
            f_low = state_ref[slot, j - 1] if j else jnp.where(is_even, far_ref[slot, 0], near_ref[slot, 0])
            f_high = state_ref[slot, j + 1] if j + 1 < own else jnp.where(is_even, near_ref[slot, 0], far_ref[slot, 0])
            term = term + (here - planes[slot, j + 2]) * (f - f_high)
            term = term + (here - planes[slot, j]) * (f - f_low)
            for axis in (0, 1):
                for up in (True, False):
                    term = term + drop(here, axis, up) * drop(f, axis, up)
        planes[0, j] = -0.5 * term
        for k in range(groups):
            at = lax.rem(place_ref[1] + k, groups) * chunk
            share_ref[k, j] = planes[0, j, pl.ds(pl.multiple_of(at, chunk), chunk), :]


def whole_grid(conductivity, misfit, forward_states, pole_shifts, pole_weights, pole_order):
    members, own, ny, nz = forward_states.shape
    groups = lax.axis_size("pole")
    place = jnp.stack([lax.axis_index("space"), lax.axis_index("pole")]).astype(jnp.int32)
    peers = lax.axis_size("space")
    even = place[0] % 2 == 0
    first, last = forward_states[:, :1], forward_states[:, own - 1 :]
    near = [(i, i ^ 1) for i in range(peers)]
    far = [(i, i + 1 if i % 2 else i - 1) for i in range(1, peers - 1)]
    halos = [(jnp.where(even, first, last), far), (jnp.where(even, last, first), near)]
    mine, theirs, halos = gather_blocks([conductivity, misfit], halos, "space")
    far, near = halos
    coarse_x, rows = peers * own // 2, ny // 2
    lanes = 2 * HALF

    def scratch(count, extent):
        return pltpu.VMEM((count, extent, rows, lanes), jnp.float32)

    smem = pl.BlockSpec(memory_space=pltpu.SMEM)
    vmem = pl.BlockSpec(memory_space=pltpu.VMEM)
    adjoint, share = pl.pallas_call(
        solve_kernel,
        out_shape=(
            jax.ShapeDtypeStruct(forward_states.shape, jnp.float32),
            jax.ShapeDtypeStruct((groups, own, ny // groups, nz), jnp.float32),
        ),
        in_specs=[smem] * 4 + [vmem] * 7,
        out_specs=(vmem, vmem),
        scratch_shapes=[
            scratch(8, coarse_x + 2),
            scratch(12, coarse_x),
            scratch(4, coarse_x + 1),
            scratch(8, coarse_x),
            scratch(8, coarse_x),
            scratch(8, coarse_x),
            scratch(8, coarse_x),
            scratch(8, coarse_x),
            scratch(5, coarse_x + 1),
            pltpu.VMEM((coarse_x, rows, lanes), jnp.float32),
            scratch(8, coarse_x),
            scratch(8, coarse_x + 2),
            scratch(8, coarse_x),
            scratch(8, coarse_x + 2),
            scratch(8, coarse_x + 2),
            scratch(8, coarse_x),
            pltpu.VMEM((coarse_x + 2, rows, lanes), jnp.float32),
            pltpu.VMEM((coarse_x + 2, rows, lanes), jnp.float32),
            pltpu.VMEM((members, own + 2, ny, nz), jnp.float32),
        ],
        compiler_params=pltpu.CompilerParams(vmem_limit_bytes=48 * 1024 * 1024),
        name="solve",
    )(
        place,
        pole_shifts,
        pole_weights,
        pole_order,
        *mine,
        *theirs,
        forward_states,
        far,
        near,
    )
    gradient = share[0]
    for k in range(1, groups):
        ring = [(i, (i + k) % groups) for i in range(groups)]
        gradient = gradient + lax.ppermute(share[k], "pole", ring)
    return adjoint, gradient


def plus_side(field, which_dim):
    extent = field.shape[which_dim]
    inner_part = lax.slice_in_dim(field, 1, extent, axis=which_dim)
    zero_plane = jnp.zeros_like(lax.slice_in_dim(field, 0, 1, axis=which_dim))
    return jnp.concatenate([inner_part, zero_plane], axis=which_dim)


def minus_side(field, which_dim):
    extent = field.shape[which_dim]
    inner_part = lax.slice_in_dim(field, 0, extent - 1, axis=which_dim)
    zero_plane = jnp.zeros_like(lax.slice_in_dim(field, 0, 1, axis=which_dim))
    return jnp.concatenate([zero_plane, inner_part], axis=which_dim)


def coarse_pick(faces, which_dim, offset):
    extent_x, extent_y, extent_z = faces.shape
    blocks = faces.reshape(extent_x // 2, 2, extent_y // 2, 2, extent_z // 2, 2)
    chosen = lax.index_in_dim(blocks, offset, axis=2 * which_dim + 1, keepdims=True)
    return jnp.sum(chosen, axis=(1, 3, 5))


def side_terms(field, plus_faces, minus_faces, widened):
    result = plus_faces[0] * (field - widened[:, 2:]) + minus_faces[0] * (field - widened[:, :-2])
    for which_dim in (1, 2):
        result = result + plus_faces[which_dim] * (field - plus_side(field, which_dim + 1))
        result = result + minus_faces[which_dim] * (field - minus_side(field, which_dim + 1))
    return result


def fine_image(field, plus_faces, minus_faces, shift_value):
    widened = extended(field, (("space", 1),), 1)
    return shift_value * field + side_terms(field, plus_faces, minus_faces, widened)


def coarse_image(field, plus_faces, minus_faces, shift_value):
    widened = extended(field, (("space", 1),), 1)
    return shift_value * field + side_terms(field, plus_faces, minus_faces, widened)


def restrict(field):
    members, extent_x, extent_y, extent_z = field.shape
    shaped = field.reshape(members, extent_x // 2, 2, extent_y // 2, 2, extent_z // 2, 2)
    return jnp.sum(shaped, axis=(2, 4, 6))


def prolong(field):
    return jnp.repeat(jnp.repeat(jnp.repeat(field, 2, axis=1), 2, axis=2), 2, axis=3)


def precondition(residual, fine, coarse):
    plus_faces, minus_faces, shift_value, diagonal = fine
    coarse_plus, coarse_minus, coarse_shift, coarse_diagonal = coarse
    smooth_one = DAMPING * residual / diagonal
    coarse_rhs = restrict(residual - fine_image(smooth_one, plus_faces, minus_faces, shift_value))
    coarse_one = DAMPING * coarse_rhs / coarse_diagonal
    coarse_two = (
        coarse_one
        + DAMPING
        * (coarse_rhs - coarse_image(coarse_one, coarse_plus, coarse_minus, coarse_shift))
        / coarse_diagonal
    )
    corrected = smooth_one + prolong(coarse_two)
    return (
        corrected
        + DAMPING
        * (residual - fine_image(corrected, plus_faces, minus_faces, shift_value))
        / diagonal
    )


def expand(values):
    return values.reshape(-1, 1, 1, 1)


def cell_sums(values):
    return jnp.sum(values, axis=(1, 2, 3))


def norm_sum(residual, precond):
    return lax.psum(cell_sums(residual * precond), "space")


def solve(rhs, fine, coarse):
    plus_faces, minus_faces, shift_value, diagonal = fine
    iterate = jnp.zeros_like(rhs)
    residual = rhs
    precond = precondition(residual, fine, coarse)
    gamma_now = norm_sum(residual, precond)
    search = precond
    for turn_index in range(ITERS):
        image_field = fine_image(search, plus_faces, minus_faces, shift_value)
        curve = lax.psum(cell_sums(search * image_field), "space")
        step_length = gamma_now / curve
        iterate = iterate + expand(step_length) * search
        if turn_index + 1 < ITERS:
            residual = residual - expand(step_length) * image_field
            precond = precondition(residual, fine, coarse)
            gamma_next = norm_sum(residual, precond)
            search = precond + expand(gamma_next / gamma_now) * search
            gamma_now = gamma_next
    return iterate


def divided(conductivity, misfit, forward_states, pole_shifts, pole_weights, pole_order):
    widened_kappa = extended(conductivity, (("space", 0),), 1)
    plus_faces = [
        0.5 * (conductivity + widened_kappa[2:]),
        0.5 * (conductivity + plus_side(conductivity, 1)),
        0.5 * (conductivity + plus_side(conductivity, 2)),
    ]
    minus_faces = [
        0.5 * (conductivity + widened_kappa[:-2]),
        0.5 * (conductivity + minus_side(conductivity, 1)),
        0.5 * (conductivity + minus_side(conductivity, 2)),
    ]
    base_diagonal = (
        plus_faces[0]
        + plus_faces[1]
        + plus_faces[2]
        + minus_faces[0]
        + minus_faces[1]
        + minus_faces[2]
    )
    coarse_plus = [coarse_pick(plus_faces[which_dim], which_dim, 1) for which_dim in range(3)]
    coarse_minus = [coarse_pick(minus_faces[which_dim], which_dim, 0) for which_dim in range(3)]
    coarse_base = (
        coarse_plus[0]
        + coarse_plus[1]
        + coarse_plus[2]
        + coarse_minus[0]
        + coarse_minus[1]
        + coarse_minus[2]
    )
    pole_index = jnp.arange(pole_shifts.shape[0], dtype=jnp.int32)
    matches = pole_order[:, None] == pole_index[None, :]
    shift_local = jnp.sum(jnp.where(matches, pole_shifts[None, :], 0.0), axis=1)
    weight_local = jnp.sum(jnp.where(matches, pole_weights[None, :], 0.0), axis=1)
    members = forward_states.shape[0]

    def solve_group(shift_part, weight_part):
        shift_value = expand(shift_part)
        fine = (plus_faces, minus_faces, shift_value, base_diagonal[None] + shift_value)
        coarse = (
            coarse_plus,
            coarse_minus,
            8.0 * shift_value,
            coarse_base[None] + 8.0 * shift_value,
        )
        return solve(expand(weight_part) * misfit[None], fine, coarse)

    adjoint_states = jnp.concatenate(
        [
            solve_group(shift_local[member : member + 1], weight_local[member : member + 1])
            for member in range(members)
        ],
        axis=0,
    )
    widened = extended(jnp.stack([adjoint_states, forward_states]), (("space", 2),), 1)
    term = (adjoint_states - widened[0, :, 2:]) * (forward_states - widened[1, :, 2:])
    term = term + (adjoint_states - widened[0, :, :-2]) * (forward_states - widened[1, :, :-2])
    for which_dim in (2, 3):
        term = term + (adjoint_states - plus_side(adjoint_states, which_dim)) * (
            forward_states - plus_side(forward_states, which_dim)
        )
        term = term + (adjoint_states - minus_side(adjoint_states, which_dim)) * (
            forward_states - minus_side(forward_states, which_dim)
        )
    local_term = -0.5 * jnp.sum(term, axis=0)
    gradient = lax.psum_scatter(local_term, "pole", scatter_dimension=1, tiled=True)
    return (adjoint_states, gradient)


def solution(mesh):
    in_specs = (
        P("space", None, None),
        P("space", None, None),
        P("pole", "space", None, None),
        P(),
        P(),
        P("pole"),
    )
    out_specs = (P("pole", "space", None, None), P("space", "pole", None))

    def body(conductivity, misfit, forward_states, *poles):
        nx = conductivity.shape[0] * lax.axis_size("space")
        _, ny, nz = conductivity.shape
        peers = lax.axis_size("space")
        small = nx * ny * nz <= REPLICATED_CELLS and forward_states.shape[0] == 2
        if small and nz == 2 * HALF and peers > 2 and peers & (peers - 1) == 0:
            return whole_grid(conductivity, misfit, forward_states, *poles)
        return divided(conductivity, misfit, forward_states, *poles)

    return jax.shard_map(
        body, mesh=mesh, in_specs=in_specs, out_specs=out_specs, check_vma=False
    )
```

```python
import functools

import jax
import jax.numpy as jnp
from jax import lax
from jax.experimental import pallas as pl
from jax.experimental.pallas import tpu as pltpu
from jax.sharding import PartitionSpec as P

ITERS = 2
DAMPING = 0.8
REPLICATED_CELLS = 32 * 64 * 128
HALF = 64
TILE = 8


def extended(array, sides, width):
    for axis, dim in sides:
        peers, length = (lax.axis_size(axis), array.shape[dim])
        up = [(i, (i + 1) % peers) for i in range(peers - 1)]
        down = [(j, i) for i, j in up]
        last = lax.slice_in_dim(array, length - width, length, axis=dim)
        leading = lax.slice_in_dim(array, 0, width, axis=dim)
        before = lax.ppermute(last, axis, up)
        after = lax.ppermute(leading, axis, down)
        array = jnp.concatenate([before, array, after], axis=dim)
    return array


def lane_index(shape):
    return lax.broadcasted_iota(jnp.int32, shape, len(shape) - 1)


def row_index(shape):
    return lax.broadcasted_iota(jnp.int32, shape, len(shape) - 2)


def roll(block, shift, axis):
    return pltpu.roll(block, shift % block.shape[axis], axis)


def tree_sum(values):
    while len(values) > 1:
        values = [sum(values[at : at + 2]) for at in range(0, len(values), 2)]
    return values[0]


def grand_total(acc):
    line = jnp.sum(acc, axis=0, keepdims=True)
    return jnp.broadcast_to(jnp.sum(line, axis=1, keepdims=True), acc.shape)


def swap_masks(peers, flip):
    even = []
    mask = peers // 2
    while mask > 1:
        even.append(mask)
        mask //= 2
    odd = even[-1:] + even[:-1]
    return (odd, even) if flip else (even, odd)


def block_pair(u, holder, peers, flip):
    even, odd = swap_masks(peers, flip)
    parity = holder % 2
    top = jnp.where(parity == 0, even.index(peers // 2), odd.index(peers // 2))
    below = u & ((1 << top) - 1)
    base = ((u >> top) << (top + 1)) | below
    upper = jnp.where(holder >= peers // 2, 1, 0)
    first = base | (upper << top)
    second = base | ((1 - upper) << top)
    home = holder
    for step, (mask_even, mask_odd) in enumerate(zip(even, odd)):
        mask = jnp.where(parity == 0, mask_even, mask_odd)
        home = home ^ (((first >> step) & 1) * mask)
    return first, second, home


def gather_blocks(blocks, halos, axis):
    peers = lax.axis_size(axis)
    own_half = lax.optimization_barrier(0.5 * blocks[0][None])
    held = [block[None] for block in blocks]
    halos = [lax.ppermute(array, axis, pairs) for array, pairs in halos]
    swaps = [list(zip(*swap_masks(peers, flip))) for flip in (False, True)]
    steps = len(swaps[0])
    for step in range(steps):
        if step == steps - 1:
            held[0], halos[0] = lax.optimization_barrier((held[0], halos[0]))
        for at in (0, 1):
            masks = swaps[at][step]
            pairs = [(i, i ^ masks[i % 2]) for i in range(peers)]
            arrived = lax.ppermute(held[at], axis, pairs)
            if step == 0 and at == 0:
                held[0], arrived = own_half, 0.5 * arrived
            held[at] = jnp.concatenate([held[at], arrived], axis=0)
    held[0], halos[1] = lax.optimization_barrier((held[0], halos[1]))
    other = [lax.ppermute(part, axis, [(i, i ^ 1) for i in range(peers)]) for part in held]
    return held, other, halos


CLASSES = [(a, b, c) for a in (0, 1) for b in (0, 1) for c in (0, 1)]
PAIRS = [(p, q) for p in (0, 1) for q in (0, 1)]


def cls(a, b, c):
    return 4 * a + 2 * b + c


def inner_faces(p, q):
    return (
        (2 * p + q, cls(0, p, q), cls(1, p, q)),
        (4 + 2 * p + q, cls(p, 0, q), cls(p, 1, q)),
        (8 + 2 * p + q, cls(p, q, 0), cls(p, q, 1)),
    )


class Layout:
    def __init__(self, rows):
        self.tiles = rows // TILE
        self.lane = lane_index((TILE, 2 * HALF))
        self.row = row_index((TILE, 2 * HALF))
        self.left = self.lane < HALF
        self.zero = jnp.zeros((TILE, 2 * HALF), jnp.float32)

    def tile(self, j):
        return pl.ds(TILE * j, TILE)

    def every(self, b, j):
        return pl.ds(b + 2 * j, TILE, stride=2 * self.tiles)

    def row_before(self, load, j):
        return load(j - 1) if j else roll(load(self.tiles - 1), 1, 0)

    def row_after(self, load, j):
        return load(j + 1) if j + 1 < self.tiles else roll(load(0), -1, 0)

    def seam(self, ref, low, high):
        last = ref.shape[1] - 1
        for j in range(self.tiles):
            for k in low:
                moved = roll(ref[k, last - 1, self.tile(j)], HALF, 1)
                ref[k, 0, self.tile(j)] = jnp.where(self.left, 0.0, moved)
            for k in high:
                moved = roll(ref[k, 1, self.tile(j)], HALF, 1)
                ref[k, last, self.tile(j)] = jnp.where(self.left, moved, 0.0)

    def seam_fine(self, ref):
        count = ref.shape[0]
        self.seam(
            ref,
            [k for k in range(count) if k % 8 >= 4],
            [k for k in range(count) if k % 8 < 4],
        )

    def arrange(self, mine_ref, theirs_ref, place, flip, store):
        blocks, own, rows, _ = mine_ref.shape
        column = self.lane % HALF
        even_odd = 2 * column + jnp.where(self.left, 0, 1)
        odd_even = 2 * column + jnp.where(self.left, 1, 0)

        def pair(u, carry):
            for ref, holder in ((mine_ref, place), (theirs_ref, place ^ 1)):
                first, second, home = block_pair(u, holder, 2 * blocks, flip)
                for x in range(own):
                    spot = home * (own // 2) + x // 2
                    for b in (0, 1):
                        for j in range(self.tiles):
                            one = jnp.take_along_axis(
                                ref[first, x, self.every(b, j), :], even_odd, axis=1
                            )
                            two = jnp.take_along_axis(
                                ref[second, x, self.every(b, j), :], odd_even, axis=1
                            )
                            store(cls(x % 2, b, 0), spot, j, jnp.where(self.left, one, two))
                            odd = roll(jnp.where(self.left, two, one), HALF, 1)
                            store(cls(x % 2, b, 1), spot, j, odd)
            return carry

        lax.fori_loop(0, blocks // 2, pair, 0)


def setup_kernel(
    place_ref,
    shifts_ref,
    order_ref,
    mine_ref,
    theirs_ref,
    inner,
    outer_x,
    outer_y,
    outer_z,
    inner_sum,
    diagonal,
    damped,
    coarse_off,
    coarse_damped,
    half_kappa,
):
    half = inner.shape[1]
    at_ = Layout(inner.shape[2])
    tile, tiles = at_.tile, at_.tiles
    members = coarse_damped.shape[0]
    shifts = [shifts_ref[order_ref[slot]] for slot in range(members)]

    def keep(k, spot, j, value):
        half_kappa[k, spot + 1, tile(j)] = value

    at_.arrange(mine_ref, theirs_ref, place_ref[0], False, keep)
    at_.seam_fine(half_kappa)

    z_low = jnp.where(at_.lane % HALF > 0, 1.0, 0.0)
    z_high = jnp.where(at_.lane % HALF < HALF - 1, 1.0, 0.0)
    y_low = [jnp.where(at_.row > 0, 1.0, 0.0)] + [None] * (tiles - 1)
    y_high = [None] * (tiles - 1) + [jnp.where(at_.row < TILE - 1, 1.0, 0.0)]

    def masked(mask, value):
        return value if mask is None else mask * value

    def plane(i, carry):
        for j in range(tiles):
            kap = [half_kappa[k, i + 1, tile(j)] for k in range(8)]
            inside = [[] for _ in range(8)]
            outside = [[] for _ in range(8)]
            off = [[] for _ in range(5)]
            for p, q in PAIRS:
                for face_at, low, high in inner_faces(p, q):
                    face = kap[low] + kap[high]
                    inner[face_at, i, tile(j)] = face
                    inside[low].append(face)
                    inside[high].append(face)
                at = 2 * p + q

                low, high = cls(0, p, q), cls(1, p, q)
                minus = kap[low] + half_kappa[high, i, tile(j)]
                plus = kap[high] + half_kappa[low, i + 2, tile(j)]
                outside[low].append(minus)
                outside[high].append(plus)
                outer_x[at, i, tile(j)] = minus
                off[0].append(minus)

                low, high = cls(p, 0, q), cls(p, 1, q)
                side = at_.row_before(lambda r: half_kappa[high, i + 1, tile(r)], j)
                minus = kap[low] + masked(y_low[j], side)
                side = at_.row_after(lambda r: half_kappa[low, i + 1, tile(r)], j)
                plus = kap[high] + masked(y_high[j], side)
                outside[low].append(minus)
                outside[high].append(plus)
                minus, plus = masked(y_low[j], minus), masked(y_high[j], plus)
                outer_y[at, i, tile(j)] = minus
                outer_y[4 + at, i, tile(j)] = plus
                off[1].append(minus)
                off[2].append(plus)

                low, high = cls(p, q, 0), cls(p, q, 1)
                minus = kap[low] + z_low * roll(kap[high], 1, 1)
                plus = kap[high] + z_high * roll(kap[low], -1, 1)
                outside[low].append(minus)
                outside[high].append(plus)
                minus, plus = z_low * minus, z_high * plus
                outer_z[at, i, tile(j)] = minus
                outer_z[4 + at, i, tile(j)] = plus
                off[3].append(minus)
                off[4].append(plus)
            coarse_total = []
            for k in range(8):
                within, without = tree_sum(inside[k]), tree_sum(outside[k])
                inner_sum[k, i, tile(j)] = within
                base = within + without
                diagonal[k, i, tile(j)] = base
                coarse_total.append(without)
                for slot in range(members):
                    damped[8 * slot + k, i, tile(j)] = DAMPING / (base + shifts[slot])
            for at, part in enumerate(off):
                coarse_off[at, i, tile(j)] = tree_sum(part)
            total = tree_sum(coarse_total)
            for slot in range(members):
                coarse_damped[slot, i, tile(j)] = DAMPING / (total + 8.0 * shifts[slot])
        return carry

    lax.fori_loop(0, half, plane, 0)
    for j in range(tiles):
        part = []
        for p, q in PAIRS:
            face = half_kappa[cls(0, p, q), half + 1, tile(j)]
            face = face + half_kappa[cls(1, p, q), half, tile(j)]
            outer_x[2 * p + q, half, tile(j)] = face
            part.append(face)
        coarse_off[0, half, tile(j)] = tree_sum(part)


def solve_kernel(
    place_ref,
    shifts_ref,
    weights_ref,
    order_ref,
    mine_ref,
    theirs_ref,
    state_ref,
    far_ref,
    near_ref,
    inner,
    outer_x,
    outer_y,
    outer_z,
    inner_sum,
    diagonal,
    damped,
    coarse_off,
    coarse_damped,
    adjoint_ref,
    share_ref,
    residual,
    scaled,
    partial,
    first_dir,
    second_dir,
    image,
    coarse_one,
    coarse_two,
    planes,
):
    half, rows = inner.shape[1:3]
    at_ = Layout(rows)
    tile, tiles, zero = at_.tile, at_.tiles, at_.zero
    members = coarse_damped.shape[0]
    slots = range(members)
    shifts = [shifts_ref[order_ref[slot]] for slot in slots]
    weights = [weights_ref[order_ref[slot]] for slot in slots]

    def begin(k, spot, j, value):
        for slot in slots:
            at = 8 * slot + k
            res = weights[slot] * value
            residual[at, spot, tile(j)] = res
            scaled[at, spot + 1, tile(j)] = damped[at, spot, tile(j)] * res

    at_.arrange(mine_ref, theirs_ref, place_ref[0], True, begin)
    at_.seam_fine(scaled)

    def stencil(field, i, j):
        here = [[field[8 * s + k, i + 1, tile(j)] for k in range(8)] for s in slots]
        sums = [[None] * 8 for _ in slots]

        def add(s, k, value):
            sums[s][k] = value if sums[s][k] is None else sums[s][k] + value

        for p, q in PAIRS:
            at = 2 * p + q
            for face_at, low, high in inner_faces(p, q):
                face = inner[face_at, i, tile(j)]
                for s in slots:
                    add(s, low, face * here[s][high])
                    add(s, high, face * here[s][low])
            low, high = cls(0, p, q), cls(1, p, q)
            minus, plus = outer_x[at, i, tile(j)], outer_x[at, i + 1, tile(j)]
            for s in slots:
                add(s, low, minus * field[8 * s + high, i, tile(j)])
                add(s, high, plus * field[8 * s + low, i + 2, tile(j)])
            low, high = cls(p, 0, q), cls(p, 1, q)
            minus, plus = outer_y[at, i, tile(j)], outer_y[4 + at, i, tile(j)]
            for s in slots:
                side = at_.row_before(lambda r: field[8 * s + high, i + 1, tile(r)], j)
                add(s, low, minus * side)
                side = at_.row_after(lambda r: field[8 * s + low, i + 1, tile(r)], j)
                add(s, high, plus * side)
            low, high = cls(p, q, 0), cls(p, q, 1)
            minus, plus = outer_z[at, i, tile(j)], outer_z[4 + at, i, tile(j)]
            for s in slots:
                add(s, low, minus * roll(here[s][high], 1, 1))
                add(s, high, plus * roll(here[s][low], -1, 1))
        return here, sums

    def coarse_sides(field, s, i, j):
        here = field[s, i + 1, tile(j)]
        return here, (
            (field[s, i, tile(j)], field[s, i + 2, tile(j)]),
            (
                at_.row_before(lambda r: field[s, i + 1, tile(r)], j),
                at_.row_after(lambda r: field[s, i + 1, tile(r)], j),
            ),
            (roll(here, 1, 1), roll(here, -1, 1)),
        )

    def precondition(result, other):
        def down(i, carry):
            for j in range(tiles):
                _, sums = stencil(scaled, i, j)
                for s in slots:
                    rhs = None
                    for k in range(8):
                        res = residual[8 * s + k, i, tile(j)]
                        part = (2.0 - DAMPING) * res + sums[s][k]
                        partial[8 * s + k, i, tile(j)] = part
                        rhs = part - res if rhs is None else rhs + (part - res)
                    coarse_one[s, i + 1, tile(j)] = coarse_damped[s, i, tile(j)] * rhs
            return carry

        lax.fori_loop(0, half, down, 0)
        at_.seam(coarse_one, slots, slots)

        def smooth(i, carry):
            for j in range(tiles):
                faces = [coarse_off[0, i + 1, tile(j)]]
                faces += [coarse_off[at, i, tile(j)] for at in range(5)]
                for s in slots:
                    here, sides = coarse_sides(coarse_one, s, i, j)
                    total = faces[1] * sides[0][0] + faces[0] * sides[0][1]
                    total = total + (faces[2] * sides[1][0] + faces[3] * sides[1][1])
                    total = total + (faces[4] * sides[2][0] + faces[5] * sides[2][1])
                    coarse_two[s, i + 1, tile(j)] = (2.0 - DAMPING) * here + coarse_damped[
                        s, i, tile(j)
                    ] * total
            return carry

        lax.fori_loop(0, half, smooth, 0, unroll=4)
        at_.seam(coarse_two, slots, slots)

        def up(i, carry):
            carry = list(carry)
            for j in range(tiles):
                around = [coarse_sides(coarse_two, s, i, j) for s in slots]
                kept = [(1.0 - DAMPING) * around[s][0] for s in slots]
                for a, b, c in CLASSES:
                    k = cls(a, b, c)
                    faces = (
                        inner_sum[k, i, tile(j)],
                        outer_x[2 * b + c, i + a, tile(j)],
                        outer_y[4 * b + 2 * a + c, i, tile(j)],
                        outer_z[4 * c + 2 * a + b, i, tile(j)],
                    )
                    for s in slots:
                        at = 8 * s + k
                        here, sides = around[s]
                        value = partial[at, i, tile(j)] + faces[0] * here
                        value = value + (faces[1] * sides[0][a] + faces[2] * sides[1][b])
                        value = value + faces[3] * sides[2][c]
                        new = kept[s] + damped[at, i, tile(j)] * value
                        result[at, i + 1, tile(j)] = new
                        carry[s] = carry[s] + residual[at, i, tile(j)] * new
                        if other is not None:
                            into = members + s
                            carry[into] = carry[into] + other[at, i, tile(j)] * new
            return tuple(carry)

        count = members if other is None else 2 * members
        sums = lax.fori_loop(0, half, up, (zero,) * count)
        at_.seam_fine(result)
        return [grand_total(part) for part in sums]

    def curvature(field, keep):
        def step(i, carry):
            carry = list(carry)
            for j in range(tiles):
                here, sums = stencil(field, i, j)
                for k in range(8):
                    base = diagonal[k, i, tile(j)]
                    for s in slots:
                        value = (base + shifts[s]) * here[s][k] - sums[s][k]
                        if keep:
                            image[8 * s + k, i, tile(j)] = value
                        carry[s] = carry[s] + here[s][k] * value
            return tuple(carry)

        sums = lax.fori_loop(0, half, step, (zero,) * members)
        return [grand_total(part) for part in sums]

    gamma = precondition(first_dir, None)
    curve = curvature(first_dir, True)
    step_one = [gamma[s] / curve[s] for s in slots]

    def update(i, carry):
        for j in range(tiles):
            for s in slots:
                for k in range(8):
                    at = 8 * s + k
                    new = residual[at, i, tile(j)] - step_one[s] * image[at, i, tile(j)]
                    residual[at, i, tile(j)] = new
                    scaled[at, i + 1, tile(j)] = damped[at, i, tile(j)] * new
        return carry

    lax.fori_loop(0, half, update, 0)
    at_.seam_fine(scaled)

    sums = precondition(second_dir, image)
    gamma_next, cross = sums[:members], sums[members:]
    bend = curvature(second_dir, False)
    ratio = [gamma_next[s] / gamma[s] for s in slots]
    step_two = [
        gamma_next[s] / (bend[s] + ratio[s] * (2.0 * cross[s] + ratio[s] * curve[s]))
        for s in slots
    ]
    step_first = [step_one[s] + step_two[s] * ratio[s] for s in slots]

    own = adjoint_ref.shape[1]
    start = place_ref[0] * (own // 2)
    upper = jnp.where(start >= half, 1, 0)
    start = start - half * upper
    even = at_.lane % 2 == 0
    source = at_.lane // 2 + HALF * upper
    for at in range(own + 2):
        a = (at + 1) % 2
        spot = start + (at + 1) // 2
        for b in (0, 1):
            for j in range(tiles):
                for s in slots:
                    both = []
                    for c in (0, 1):
                        k = 8 * s + cls(a, b, c)
                        both.append(
                            step_first[s] * first_dir[k, spot, tile(j)]
                            + step_two[s] * second_dir[k, spot, tile(j)]
                        )
                    planes[s, at, at_.every(b, j), :] = jnp.where(
                        even,
                        jnp.take_along_axis(both[0], source, axis=1),
                        jnp.take_along_axis(both[1], source, axis=1),
                    )

    full = (2 * rows, 2 * HALF)
    y_at = row_index(full)
    z_at = lane_index(full)

    def drop(value, axis, up):
        moved = roll(value, -1 if up else 1, axis)
        at = (y_at, z_at)[axis]
        edge = full[axis] - 1 if up else 0
        return value - jnp.where(at == edge, 0.0, moved)

    is_even = place_ref[0] % 2 == 0
    groups = share_ref.shape[0]
    chunk = share_ref.shape[2]
    for j in range(own):
        term = jnp.zeros(full, jnp.float32)
        for s in slots:
            here = planes[s, j + 1]
            adjoint_ref[s, j] = here
            f = state_ref[s, j]
            if j:
                f_low = state_ref[s, j - 1]
            else:
                f_low = jnp.where(is_even, far_ref[s, 0], near_ref[s, 0])
            if j + 1 < own:
                f_high = state_ref[s, j + 1]
            else:
                f_high = jnp.where(is_even, near_ref[s, 0], far_ref[s, 0])
            term = term + (here - planes[s, j + 2]) * (f - f_high)
            term = term + (here - planes[s, j]) * (f - f_low)
            for axis in (0, 1):
                for up in (True, False):
                    term = term + drop(here, axis, up) * drop(f, axis, up)
        planes[0, j] = -0.5 * term
        for k in range(groups):
            at = lax.rem(place_ref[1] + k, groups) * chunk
            share_ref[k, j] = planes[0, j, pl.ds(pl.multiple_of(at, chunk), chunk), :]


def whole_grid(conductivity, misfit, forward_states, pole_shifts, pole_weights, pole_order):
    members, own, ny, nz = forward_states.shape
    groups = lax.axis_size("pole")
    place = jnp.stack([lax.axis_index("space"), lax.axis_index("pole")]).astype(jnp.int32)
    peers = lax.axis_size("space")
    even = place[0] % 2 == 0
    first, last = forward_states[:, :1], forward_states[:, own - 1 :]
    near = [(i, i ^ 1) for i in range(peers)]
    far = [(i, i + 1 if i % 2 else i - 1) for i in range(1, peers - 1)]
    halos = [(jnp.where(even, first, last), far), (jnp.where(even, last, first), near)]
    mine, theirs, halos = gather_blocks([conductivity, misfit], halos, "space")
    far, near = halos
    half, rows = peers * own // 4, ny // 2

    def field(count, extent):
        return (count, extent, rows, 2 * HALF)

    def held(*shape):
        return pltpu.VMEM(shape, jnp.float32)

    smem = pl.BlockSpec(memory_space=pltpu.SMEM)
    vmem = pl.BlockSpec(memory_space=pltpu.VMEM)
    shapes = [
        field(12, half),
        field(4, half + 1),
        field(8, half),
        field(8, half),
        field(8, half),
        field(8, half),
        field(8 * members, half),
        field(5, half + 1),
        field(members, half),
    ]
    coefficients = pl.pallas_call(
        setup_kernel,
        out_shape=[jax.ShapeDtypeStruct(shape, jnp.float32) for shape in shapes],
        in_specs=[smem] * 3 + [vmem] * 2,
        out_specs=[vmem] * len(shapes),
        scratch_shapes=[held(*field(8, half + 2))],
        compiler_params=pltpu.CompilerParams(vmem_limit_bytes=20 * 1024 * 1024),
        name="setup",
    )(place, pole_shifts, pole_order, mine[0], theirs[0])
    adjoint, share = pl.pallas_call(
        solve_kernel,
        out_shape=(
            jax.ShapeDtypeStruct(forward_states.shape, jnp.float32),
            jax.ShapeDtypeStruct((groups, own, ny // groups, nz), jnp.float32),
        ),
        in_specs=[smem] * 4 + [vmem] * (5 + len(shapes)),
        out_specs=(vmem, vmem),
        scratch_shapes=[
            held(*field(8 * members, half)),
            held(*field(8 * members, half + 2)),
            held(*field(8 * members, half)),
            held(*field(8 * members, half + 2)),
            held(*field(8 * members, half + 2)),
            held(*field(8 * members, half)),
            held(*field(members, half + 2)),
            held(*field(members, half + 2)),
            held(members, own + 2, ny, nz),
        ],
        compiler_params=pltpu.CompilerParams(vmem_limit_bytes=36 * 1024 * 1024),
        name="solve",
    )(
        place,
        pole_shifts,
        pole_weights,
        pole_order,
        mine[1],
        theirs[1],
        forward_states,
        far,
        near,
        *coefficients,
    )
    gradient = share[0]
    for k in range(1, groups):
        ring = [(i, (i + k) % groups) for i in range(groups)]
        gradient = gradient + lax.ppermute(share[k], "pole", ring)
    return adjoint, gradient


def plus_side(field, which_dim):
    extent = field.shape[which_dim]
    inner_part = lax.slice_in_dim(field, 1, extent, axis=which_dim)
    zero_plane = jnp.zeros_like(lax.slice_in_dim(field, 0, 1, axis=which_dim))
    return jnp.concatenate([inner_part, zero_plane], axis=which_dim)


def minus_side(field, which_dim):
    extent = field.shape[which_dim]
    inner_part = lax.slice_in_dim(field, 0, extent - 1, axis=which_dim)
    zero_plane = jnp.zeros_like(lax.slice_in_dim(field, 0, 1, axis=which_dim))
    return jnp.concatenate([zero_plane, inner_part], axis=which_dim)


def coarse_pick(faces, which_dim, offset):
    extent_x, extent_y, extent_z = faces.shape
    blocks = faces.reshape(extent_x // 2, 2, extent_y // 2, 2, extent_z // 2, 2)
    chosen = lax.index_in_dim(blocks, offset, axis=2 * which_dim + 1, keepdims=True)
    return jnp.sum(chosen, axis=(1, 3, 5))


def side_terms(field, plus_faces, minus_faces, widened):
    result = plus_faces[0] * (field - widened[:, 2:]) + minus_faces[0] * (field - widened[:, :-2])
    for which_dim in (1, 2):
        result = result + plus_faces[which_dim] * (field - plus_side(field, which_dim + 1))
        result = result + minus_faces[which_dim] * (field - minus_side(field, which_dim + 1))
    return result


def fine_image(field, plus_faces, minus_faces, shift_value):
    widened = extended(field, (("space", 1),), 1)
    return shift_value * field + side_terms(field, plus_faces, minus_faces, widened)


def coarse_image(field, plus_faces, minus_faces, shift_value):
    widened = extended(field, (("space", 1),), 1)
    return shift_value * field + side_terms(field, plus_faces, minus_faces, widened)


def restrict(field):
    members, extent_x, extent_y, extent_z = field.shape
    shaped = field.reshape(members, extent_x // 2, 2, extent_y // 2, 2, extent_z // 2, 2)
    return jnp.sum(shaped, axis=(2, 4, 6))


def prolong(field):
    return jnp.repeat(jnp.repeat(jnp.repeat(field, 2, axis=1), 2, axis=2), 2, axis=3)


def precondition(residual, fine, coarse):
    plus_faces, minus_faces, shift_value, diagonal = fine
    coarse_plus, coarse_minus, coarse_shift, coarse_diagonal = coarse
    smooth_one = DAMPING * residual / diagonal
    coarse_rhs = restrict(residual - fine_image(smooth_one, plus_faces, minus_faces, shift_value))
    coarse_one = DAMPING * coarse_rhs / coarse_diagonal
    coarse_two = (
        coarse_one
        + DAMPING
        * (coarse_rhs - coarse_image(coarse_one, coarse_plus, coarse_minus, coarse_shift))
        / coarse_diagonal
    )
    corrected = smooth_one + prolong(coarse_two)
    return (
        corrected
        + DAMPING
        * (residual - fine_image(corrected, plus_faces, minus_faces, shift_value))
        / diagonal
    )


def expand(values):
    return values.reshape(-1, 1, 1, 1)


def cell_sums(values):
    return jnp.sum(values, axis=(1, 2, 3))


def norm_sum(residual, precond):
    return lax.psum(cell_sums(residual * precond), "space")


def solve(rhs, fine, coarse):
    plus_faces, minus_faces, shift_value, diagonal = fine
    iterate = jnp.zeros_like(rhs)
    residual = rhs
    precond = precondition(residual, fine, coarse)
    gamma_now = norm_sum(residual, precond)
    search = precond
    for turn_index in range(ITERS):
        image_field = fine_image(search, plus_faces, minus_faces, shift_value)
        curve = lax.psum(cell_sums(search * image_field), "space")
        step_length = gamma_now / curve
        iterate = iterate + expand(step_length) * search
        if turn_index + 1 < ITERS:
            residual = residual - expand(step_length) * image_field
            precond = precondition(residual, fine, coarse)
            gamma_next = norm_sum(residual, precond)
            search = precond + expand(gamma_next / gamma_now) * search
            gamma_now = gamma_next
    return iterate


def divided(conductivity, misfit, forward_states, pole_shifts, pole_weights, pole_order):
    widened_kappa = extended(conductivity, (("space", 0),), 1)
    plus_faces = [
        0.5 * (conductivity + widened_kappa[2:]),
        0.5 * (conductivity + plus_side(conductivity, 1)),
        0.5 * (conductivity + plus_side(conductivity, 2)),
    ]
    minus_faces = [
        0.5 * (conductivity + widened_kappa[:-2]),
        0.5 * (conductivity + minus_side(conductivity, 1)),
        0.5 * (conductivity + minus_side(conductivity, 2)),
    ]
    base_diagonal = (
        plus_faces[0]
        + plus_faces[1]
        + plus_faces[2]
        + minus_faces[0]
        + minus_faces[1]
        + minus_faces[2]
    )
    coarse_plus = [coarse_pick(plus_faces[which_dim], which_dim, 1) for which_dim in range(3)]
    coarse_minus = [coarse_pick(minus_faces[which_dim], which_dim, 0) for which_dim in range(3)]
    coarse_base = (
        coarse_plus[0]
        + coarse_plus[1]
        + coarse_plus[2]
        + coarse_minus[0]
        + coarse_minus[1]
        + coarse_minus[2]
    )
    pole_index = jnp.arange(pole_shifts.shape[0], dtype=jnp.int32)
    matches = pole_order[:, None] == pole_index[None, :]
    shift_local = jnp.sum(jnp.where(matches, pole_shifts[None, :], 0.0), axis=1)
    weight_local = jnp.sum(jnp.where(matches, pole_weights[None, :], 0.0), axis=1)
    members = forward_states.shape[0]

    def solve_group(shift_part, weight_part):
        shift_value = expand(shift_part)
        fine = (plus_faces, minus_faces, shift_value, base_diagonal[None] + shift_value)
        coarse = (
            coarse_plus,
            coarse_minus,
            8.0 * shift_value,
            coarse_base[None] + 8.0 * shift_value,
        )
        return solve(expand(weight_part) * misfit[None], fine, coarse)

    adjoint_states = jnp.concatenate(
        [
            solve_group(shift_local[member : member + 1], weight_local[member : member + 1])
            for member in range(members)
        ],
        axis=0,
    )
    widened = extended(jnp.stack([adjoint_states, forward_states]), (("space", 2),), 1)
    term = (adjoint_states - widened[0, :, 2:]) * (forward_states - widened[1, :, 2:])
    term = term + (adjoint_states - widened[0, :, :-2]) * (forward_states - widened[1, :, :-2])
    for which_dim in (2, 3):
        term = term + (adjoint_states - plus_side(adjoint_states, which_dim)) * (
            forward_states - plus_side(forward_states, which_dim)
        )
        term = term + (adjoint_states - minus_side(adjoint_states, which_dim)) * (
            forward_states - minus_side(forward_states, which_dim)
        )
    local_term = -0.5 * jnp.sum(term, axis=0)
    gradient = lax.psum_scatter(local_term, "pole", scatter_dimension=1, tiled=True)
    return (adjoint_states, gradient)


def solution(mesh):
    in_specs = (
        P("space", None, None),
        P("space", None, None),
        P("pole", "space", None, None),
        P(),
        P(),
        P("pole"),
    )
    out_specs = (P("pole", "space", None, None), P("space", "pole", None))

    def body(conductivity, misfit, forward_states, *poles):
        nx = conductivity.shape[0] * lax.axis_size("space")
        _, ny, nz = conductivity.shape
        peers = lax.axis_size("space")
        small = nx * ny * nz <= REPLICATED_CELLS and conductivity.shape[0] % 2 == 0
        if small and nz == 2 * HALF and peers > 2 and peers & (peers - 1) == 0:
            return whole_grid(conductivity, misfit, forward_states, *poles)
        return divided(conductivity, misfit, forward_states, *poles)

    return jax.shard_map(
        body, mesh=mesh, in_specs=in_specs, out_specs=out_specs, check_vma=False
    )
```

```python
import functools

import jax
import jax.numpy as jnp
from jax import lax
from jax.experimental import pallas as pl
from jax.experimental.pallas import tpu as pltpu
from jax.sharding import PartitionSpec as P

ITERS = 2
DAMPING = 0.8
REPLICATED_CELLS = 32 * 64 * 128
HALF = 64
TILE = 8


def extended(array, sides, width):
    for axis, dim in sides:
        peers, length = (lax.axis_size(axis), array.shape[dim])
        up = [(i, (i + 1) % peers) for i in range(peers - 1)]
        down = [(j, i) for i, j in up]
        last = lax.slice_in_dim(array, length - width, length, axis=dim)
        leading = lax.slice_in_dim(array, 0, width, axis=dim)
        before = lax.ppermute(last, axis, up)
        after = lax.ppermute(leading, axis, down)
        array = jnp.concatenate([before, array, after], axis=dim)
    return array


def lane_index(shape):
    return lax.broadcasted_iota(jnp.int32, shape, len(shape) - 1)


def row_index(shape):
    return lax.broadcasted_iota(jnp.int32, shape, len(shape) - 2)


def roll(block, shift, axis):
    return pltpu.roll(block, shift % block.shape[axis], axis)


def tree_sum(values):
    while len(values) > 1:
        values = [sum(values[at : at + 2]) for at in range(0, len(values), 2)]
    return values[0]


def grand_total(acc):
    line = jnp.sum(acc, axis=0, keepdims=True)
    return jnp.broadcast_to(jnp.sum(line, axis=1, keepdims=True), acc.shape)


def swap_masks(peers, flip):
    even = []
    mask = peers // 2
    while mask > 1:
        even.append(mask)
        mask //= 2
    odd = even[-1:] + even[:-1]
    return (odd, even) if flip else (even, odd)


def block_pair(u, holder, peers, flip):
    even, odd = swap_masks(peers, flip)
    parity = holder % 2
    top = jnp.where(parity == 0, even.index(peers // 2), odd.index(peers // 2))
    below = u & ((1 << top) - 1)
    base = ((u >> top) << (top + 1)) | below
    upper = jnp.where(holder >= peers // 2, 1, 0)
    first = base | (upper << top)
    second = base | ((1 - upper) << top)
    home = holder
    for step, (mask_even, mask_odd) in enumerate(zip(even, odd)):
        mask = jnp.where(parity == 0, mask_even, mask_odd)
        home = home ^ (((first >> step) & 1) * mask)
    return first, second, home


def gather_blocks(blocks, states, axis):
    peers = lax.axis_size(axis)
    even = lax.axis_index(axis) % 2 == 0
    swap = [(i, i ^ 1) for i in range(peers)]
    own_half = lax.optimization_barrier(0.5 * blocks[0][None])
    held = [block[None] for block in blocks]
    edge = jnp.where(even, states[:, :1], states[:, -1:])
    over = [(i, i + 1 if i % 2 else i - 1) for i in range(1, peers - 1)]
    far = lax.ppermute(edge, axis, over)
    swaps = [list(zip(*swap_masks(peers, flip))) for flip in (False, True)]
    steps = len(swaps[0])
    for step in range(steps):
        if step == steps - 1:
            held[0], far = lax.optimization_barrier((held[0], far))
            given = jnp.concatenate([states, far], axis=1)
            near = lax.ppermute(jnp.where(even, given[1], given[0]), axis, swap)
        for at in (0, 1):
            masks = swaps[at][step]
            pairs = [(i, i ^ masks[i % 2]) for i in range(peers)]
            arrived = lax.ppermute(held[at], axis, pairs)
            if step == 0 and at == 0:
                held[0], arrived = own_half, 0.5 * arrived
            held[at] = jnp.concatenate([held[at], arrived], axis=0)
    held[0], near = lax.optimization_barrier((held[0], near))
    other = [lax.ppermute(part, axis, swap) for part in held]
    return held, other, far, near


CLASSES = [(a, b, c) for a in (0, 1) for b in (0, 1) for c in (0, 1)]
PAIRS = [(p, q) for p in (0, 1) for q in (0, 1)]


def cls(a, b, c):
    return 4 * a + 2 * b + c


def inner_faces(p, q):
    return (
        (2 * p + q, cls(0, p, q), cls(1, p, q)),
        (4 + 2 * p + q, cls(p, 0, q), cls(p, 1, q)),
        (8 + 2 * p + q, cls(p, q, 0), cls(p, q, 1)),
    )


class Layout:
    def __init__(self, rows):
        self.tiles = rows // TILE
        self.lane = lane_index((TILE, 2 * HALF))
        self.row = row_index((TILE, 2 * HALF))
        self.left = self.lane < HALF
        self.zero = jnp.zeros((TILE, 2 * HALF), jnp.float32)

    def tile(self, j):
        return pl.ds(TILE * j, TILE)

    def every(self, b, j):
        return pl.ds(b + 2 * j, TILE, stride=2 * self.tiles)

    def row_before(self, load, j):
        return load(j - 1) if j else roll(load(self.tiles - 1), 1, 0)

    def row_after(self, load, j):
        return load(j + 1) if j + 1 < self.tiles else roll(load(0), -1, 0)

    def seam(self, ref, low, high):
        last = ref.shape[1] - 1
        for j in range(self.tiles):
            for k in low:
                moved = roll(ref[k, last - 1, self.tile(j)], HALF, 1)
                ref[k, 0, self.tile(j)] = jnp.where(self.left, 0.0, moved)
            for k in high:
                moved = roll(ref[k, 1, self.tile(j)], HALF, 1)
                ref[k, last, self.tile(j)] = jnp.where(self.left, moved, 0.0)

    def seam_fine(self, ref):
        count = ref.shape[0]
        self.seam(
            ref,
            [k for k in range(count) if k % 8 >= 4],
            [k for k in range(count) if k % 8 < 4],
        )

    def arrange(self, mine_ref, theirs_ref, place, flip, store):
        blocks, own, rows, _ = mine_ref.shape
        column = self.lane % HALF
        even_odd = 2 * column + jnp.where(self.left, 0, 1)
        odd_even = 2 * column + jnp.where(self.left, 1, 0)

        def pair(u, carry):
            for ref, holder in ((mine_ref, place), (theirs_ref, place ^ 1)):
                first, second, home = block_pair(u, holder, 2 * blocks, flip)
                for x in range(own):
                    spot = home * (own // 2) + x // 2
                    for b in (0, 1):
                        for j in range(self.tiles):
                            one = jnp.take_along_axis(
                                ref[first, x, self.every(b, j), :], even_odd, axis=1
                            )
                            two = jnp.take_along_axis(
                                ref[second, x, self.every(b, j), :], odd_even, axis=1
                            )
                            store(cls(x % 2, b, 0), spot, j, jnp.where(self.left, one, two))
                            odd = roll(jnp.where(self.left, two, one), HALF, 1)
                            store(cls(x % 2, b, 1), spot, j, odd)
            return carry

        lax.fori_loop(0, blocks // 2, pair, 0)


def setup_kernel(
    place_ref,
    shifts_ref,
    order_ref,
    mine_ref,
    theirs_ref,
    inner,
    outer_x,
    outer_y,
    outer_z,
    inner_sum,
    diagonal,
    damped,
    coarse_off,
    coarse_damped,
    half_kappa,
):
    half = inner.shape[1]
    at_ = Layout(inner.shape[2])
    tile, tiles = at_.tile, at_.tiles
    shift = shifts_ref[order_ref[place_ref[0] % 2]]

    def keep(k, spot, j, value):
        half_kappa[k, spot + 1, tile(j)] = value

    at_.arrange(mine_ref, theirs_ref, place_ref[0], False, keep)
    at_.seam_fine(half_kappa)

    z_low = jnp.where(at_.lane % HALF > 0, 1.0, 0.0)
    z_high = jnp.where(at_.lane % HALF < HALF - 1, 1.0, 0.0)
    y_low = [jnp.where(at_.row > 0, 1.0, 0.0)] + [None] * (tiles - 1)
    y_high = [None] * (tiles - 1) + [jnp.where(at_.row < TILE - 1, 1.0, 0.0)]

    def masked(mask, value):
        return value if mask is None else mask * value

    def plane(i, carry):
        for j in range(tiles):
            kap = [half_kappa[k, i + 1, tile(j)] for k in range(8)]
            inside = [[] for _ in range(8)]
            outside = [[] for _ in range(8)]
            off = [[] for _ in range(5)]
            for p, q in PAIRS:
                for face_at, low, high in inner_faces(p, q):
                    face = kap[low] + kap[high]
                    inner[face_at, i, tile(j)] = face
                    inside[low].append(face)
                    inside[high].append(face)
                at = 2 * p + q

                low, high = cls(0, p, q), cls(1, p, q)
                minus = kap[low] + half_kappa[high, i, tile(j)]
                plus = kap[high] + half_kappa[low, i + 2, tile(j)]
                outside[low].append(minus)
                outside[high].append(plus)
                outer_x[at, i, tile(j)] = minus
                off[0].append(minus)

                low, high = cls(p, 0, q), cls(p, 1, q)
                side = at_.row_before(lambda r: half_kappa[high, i + 1, tile(r)], j)
                minus = kap[low] + masked(y_low[j], side)
                side = at_.row_after(lambda r: half_kappa[low, i + 1, tile(r)], j)
                plus = kap[high] + masked(y_high[j], side)
                outside[low].append(minus)
                outside[high].append(plus)
                minus, plus = masked(y_low[j], minus), masked(y_high[j], plus)
                outer_y[at, i, tile(j)] = minus
                outer_y[4 + at, i, tile(j)] = plus
                off[1].append(minus)
                off[2].append(plus)

                low, high = cls(p, q, 0), cls(p, q, 1)
                minus = kap[low] + z_low * roll(kap[high], 1, 1)
                plus = kap[high] + z_high * roll(kap[low], -1, 1)
                outside[low].append(minus)
                outside[high].append(plus)
                minus, plus = z_low * minus, z_high * plus
                outer_z[at, i, tile(j)] = minus
                outer_z[4 + at, i, tile(j)] = plus
                off[3].append(minus)
                off[4].append(plus)
            coarse_total = []
            for k in range(8):
                within, without = tree_sum(inside[k]), tree_sum(outside[k])
                inner_sum[k, i, tile(j)] = within
                base = within + without + shift
                diagonal[k, i, tile(j)] = base
                coarse_total.append(without)
                damped[k, i, tile(j)] = DAMPING / base
            for at, part in enumerate(off):
                coarse_off[at, i, tile(j)] = tree_sum(part)
            coarse_damped[i, tile(j)] = DAMPING / (tree_sum(coarse_total) + 8.0 * shift)
        return carry

    lax.fori_loop(0, half, plane, 0)
    for j in range(tiles):
        part = []
        for p, q in PAIRS:
            face = half_kappa[cls(0, p, q), half + 1, tile(j)]
            face = face + half_kappa[cls(1, p, q), half, tile(j)]
            outer_x[2 * p + q, half, tile(j)] = face
            part.append(face)
        coarse_off[0, half, tile(j)] = tree_sum(part)


def solve_kernel(
    place_ref,
    weights_ref,
    order_ref,
    mine_ref,
    theirs_ref,
    state_ref,
    far_ref,
    near_ref,
    inner,
    outer_x,
    outer_y,
    outer_z,
    inner_sum,
    diagonal,
    damped,
    coarse_off,
    coarse_damped,
    adjoint_ref,
    share_ref,
    residual,
    scaled,
    partial,
    first_dir,
    second_dir,
    image,
    coarse_one,
    coarse_two,
    planes,
):
    half, rows = inner.shape[1:3]
    at_ = Layout(rows)
    tile, tiles, zero = at_.tile, at_.tiles, at_.zero
    core = place_ref[0] % 2
    weight = weights_ref[order_ref[core]]

    def begin(k, spot, j, value):
        res = weight * value
        residual[k, spot, tile(j)] = res
        scaled[k, spot + 1, tile(j)] = damped[k, spot, tile(j)] * res

    at_.arrange(mine_ref, theirs_ref, place_ref[0], True, begin)
    at_.seam_fine(scaled)

    def stencil(field, i, j, both):
        here = [field[k, i + 1, tile(j)] for k in range(8)]
        terms = [[] for _ in range(8)]
        for p, q in PAIRS:
            at = 2 * p + q
            for face_at, low, high in inner_faces(p, q):
                face = inner[face_at, i, tile(j)]
                terms[low].append(face * here[high])
                if both:
                    terms[high].append(face * here[low])
            low, high = cls(0, p, q), cls(1, p, q)
            terms[low].append(outer_x[at, i, tile(j)] * field[high, i, tile(j)])
            if both:
                side = field[low, i + 2, tile(j)]
                terms[high].append(outer_x[at, i + 1, tile(j)] * side)
            low, high = cls(p, 0, q), cls(p, 1, q)
            side = at_.row_before(lambda r: field[high, i + 1, tile(r)], j)
            terms[low].append(outer_y[at, i, tile(j)] * side)
            if both:
                side = at_.row_after(lambda r: field[low, i + 1, tile(r)], j)
                terms[high].append(outer_y[4 + at, i, tile(j)] * side)
            low, high = cls(p, q, 0), cls(p, q, 1)
            terms[low].append(outer_z[at, i, tile(j)] * roll(here[high], 1, 1))
            if both:
                terms[high].append(outer_z[4 + at, i, tile(j)] * roll(here[low], -1, 1))
        return here, [tree_sum(part) if part else None for part in terms]

    def coarse_sides(field, i, j):
        here = field[0, i + 1, tile(j)]
        return here, (
            (field[0, i, tile(j)], field[0, i + 2, tile(j)]),
            (
                at_.row_before(lambda r: field[0, i + 1, tile(r)], j),
                at_.row_after(lambda r: field[0, i + 1, tile(r)], j),
            ),
            (roll(here, 1, 1), roll(here, -1, 1)),
        )

    def precondition(result, other):
        def down(i, carry):
            for j in range(tiles):
                res = [residual[k, i, tile(j)] for k in range(8)]
                _, sums = stencil(scaled, i, j, True)
                parts = [(2.0 - DAMPING) * res[k] + sums[k] for k in range(8)]
                for k in range(8):
                    partial[k, i, tile(j)] = parts[k]
                rhs = tree_sum(parts) - tree_sum(res)
                coarse_one[0, i + 1, tile(j)] = coarse_damped[i, tile(j)] * rhs
            return carry

        lax.fori_loop(0, half, down, 0, unroll=2)
        at_.seam(coarse_one, [0], [0])

        def smooth(i, carry):
            for j in range(tiles):
                here, sides = coarse_sides(coarse_one, i, j)
                total = coarse_off[0, i, tile(j)] * sides[0][0]
                total = total + coarse_off[0, i + 1, tile(j)] * sides[0][1]
                more = coarse_off[1, i, tile(j)] * sides[1][0]
                more = more + coarse_off[2, i, tile(j)] * sides[1][1]
                most = coarse_off[3, i, tile(j)] * sides[2][0]
                most = most + coarse_off[4, i, tile(j)] * sides[2][1]
                coarse_two[0, i + 1, tile(j)] = (2.0 - DAMPING) * here + coarse_damped[
                    i, tile(j)
                ] * (total + more + most)
            return carry

        lax.fori_loop(0, half, smooth, 0, unroll=8)
        at_.seam(coarse_two, [0], [0])

        def up(i, carry):
            gamma, cross = carry
            for j in range(tiles):
                here, sides = coarse_sides(coarse_two, i, j)
                kept = (1.0 - DAMPING) * here
                dots, crosses = [], []
                for a, b, c in CLASSES:
                    k = cls(a, b, c)
                    value = tree_sum(
                        [
                            partial[k, i, tile(j)],
                            inner_sum[k, i, tile(j)] * here,
                            outer_x[2 * b + c, i + a, tile(j)] * sides[0][a],
                            outer_y[4 * b + 2 * a + c, i, tile(j)] * sides[1][b],
                            outer_z[4 * c + 2 * a + b, i, tile(j)] * sides[2][c],
                        ]
                    )
                    new = kept + damped[k, i, tile(j)] * value
                    result[k, i + 1, tile(j)] = new
                    dots.append(residual[k, i, tile(j)] * new)
                    if other is not None:
                        crosses.append(other[k, i, tile(j)] * new)
                gamma = gamma + tree_sum(dots)
                if other is not None:
                    cross = cross + tree_sum(crosses)
            return gamma, cross

        sums = lax.fori_loop(0, half, up, (zero, zero), unroll=2)
        at_.seam_fine(result)
        return [grand_total(part) for part in sums]

    gamma, _ = precondition(first_dir, None)

    def apply(i, acc):
        for j in range(tiles):
            here, sums = stencil(first_dir, i, j, True)
            dots = []
            for k in range(8):
                value = diagonal[k, i, tile(j)] * here[k] - sums[k]
                image[k, i, tile(j)] = value
                dots.append(here[k] * value)
            acc = acc + tree_sum(dots)
        return acc

    curve = grand_total(lax.fori_loop(0, half, apply, zero, unroll=2))
    step_one = gamma / curve

    def update(i, carry):
        for j in range(tiles):
            for k in range(8):
                new = residual[k, i, tile(j)] - step_one * image[k, i, tile(j)]
                residual[k, i, tile(j)] = new
                scaled[k, i + 1, tile(j)] = damped[k, i, tile(j)] * new
        return carry

    lax.fori_loop(0, half, update, 0, unroll=2)
    at_.seam_fine(scaled)

    gamma_next, cross = precondition(second_dir, image)

    def bend(i, carry):
        own_part, face_part = carry
        for j in range(tiles):
            here, sums = stencil(second_dir, i, j, False)
            own_part = own_part + tree_sum(
                [here[k] * (diagonal[k, i, tile(j)] * here[k]) for k in range(8)]
            )
            face_part = face_part + tree_sum([here[k] * sums[k] for k in range(7)])
        return own_part, face_part

    own_part, face_part = lax.fori_loop(0, half, bend, (zero, zero), unroll=2)
    ratio = gamma_next / gamma
    curve_next = grand_total(own_part - 2.0 * face_part)
    step_two = gamma_next / (curve_next + ratio * (2.0 * cross + ratio * curve))
    step_first = step_one + step_two * ratio

    _, own, ny, nz = adjoint_ref.shape
    start = (place_ref[0] - core) * (own // 2)
    upper = jnp.where(start >= half, 1, 0)
    start = start - half * upper
    even = at_.lane % 2 == 0
    source = at_.lane // 2 + HALF * upper
    for at in range(2 * own + 2):
        a = (at + 1) % 2
        spot = start + (at + 1) // 2
        for b in (0, 1):
            for j in range(tiles):
                both = [
                    step_first * first_dir[cls(a, b, c), spot, tile(j)]
                    + step_two * second_dir[cls(a, b, c), spot, tile(j)]
                    for c in (0, 1)
                ]
                planes[at, at_.every(b, j), :] = jnp.where(
                    even,
                    jnp.take_along_axis(both[0], source, axis=1),
                    jnp.take_along_axis(both[1], source, axis=1),
                )

    full = (ny, nz)
    y_at = row_index(full)
    z_at = lane_index(full)

    def drop(value, axis, up):
        moved = roll(value, -1 if up else 1, axis)
        at = (y_at, z_at)[axis]
        edge = full[axis] - 1 if up else 0
        return value - jnp.where(at == edge, 0.0, moved)

    is_even = core == 0
    state = [jnp.where(is_even, far_ref[core, 0], near_ref[own])]
    state += [jnp.where(is_even, state_ref[core, x], near_ref[x]) for x in range(own)]
    state += [jnp.where(is_even, near_ref[x], state_ref[core, x]) for x in range(own)]
    state += [jnp.where(is_even, near_ref[own], far_ref[core, 0])]
    groups = share_ref.shape[0]
    chunk = share_ref.shape[3]
    for owner in (0, 1):
        target = jnp.where(core == owner, 0, 1)
        for x in range(own):
            j = owner * own + x + 1
            here, f = planes[j], state[j]
            adjoint_ref[target, x] = here
            term = (here - planes[j + 1]) * (f - state[j + 1])
            term = term + (here - planes[j - 1]) * (f - state[j - 1])
            for axis in (0, 1):
                for up in (True, False):
                    term = term + drop(here, axis, up) * drop(f, axis, up)
            planes[2 * own + 2 + x] = -0.5 * term
            for k in range(groups):
                at = pl.multiple_of(lax.rem(place_ref[1] + k, groups) * chunk, chunk)
                share_ref[k, target, x] = planes[2 * own + 2 + x, pl.ds(at, chunk), :]


def whole_grid(conductivity, misfit, forward_states, pole_shifts, pole_weights, pole_order):
    members, own, ny, nz = forward_states.shape
    groups = lax.axis_size("pole")
    place = jnp.stack([lax.axis_index("space"), lax.axis_index("pole")]).astype(jnp.int32)
    peers = lax.axis_size("space")
    mine, theirs, far, near = gather_blocks([conductivity, misfit], forward_states, "space")
    half, rows = peers * own // 4, ny // 2

    def field(count, extent):
        return (count, extent, rows, 2 * HALF)

    def held(*shape):
        return pltpu.VMEM(shape, jnp.float32)

    smem = pl.BlockSpec(memory_space=pltpu.SMEM)
    vmem = pl.BlockSpec(memory_space=pltpu.VMEM)
    shapes = [
        field(12, half),
        field(4, half + 1),
        field(8, half),
        field(8, half),
        field(8, half),
        field(8, half),
        field(8, half),
        field(5, half + 1),
        (half, rows, 2 * HALF),
    ]
    coefficients = pl.pallas_call(
        setup_kernel,
        out_shape=[jax.ShapeDtypeStruct(shape, jnp.float32) for shape in shapes],
        in_specs=[smem] * 3 + [vmem] * 2,
        out_specs=[vmem] * len(shapes),
        scratch_shapes=[held(*field(8, half + 2))],
        compiler_params=pltpu.CompilerParams(vmem_limit_bytes=6 * 1024 * 1024),
        name="setup",
    )(place, pole_shifts, pole_order, mine[0], theirs[0])
    adjoint, share = pl.pallas_call(
        solve_kernel,
        out_shape=(
            jax.ShapeDtypeStruct((2, own, ny, nz), jnp.float32),
            jax.ShapeDtypeStruct((groups, 2, own, ny // groups, nz), jnp.float32),
        ),
        in_specs=[smem] * 3 + [vmem] * (5 + len(shapes)),
        out_specs=(vmem, vmem),
        scratch_shapes=[
            held(*field(8, half)),
            held(*field(8, half + 2)),
            held(*field(8, half)),
            held(*field(8, half + 2)),
            held(*field(8, half + 2)),
            held(*field(8, half)),
            held(*field(1, half + 2)),
            held(*field(1, half + 2)),
            held(3 * own + 2, ny, nz),
        ],
        compiler_params=pltpu.CompilerParams(vmem_limit_bytes=12 * 1024 * 1024),
        name="solve",
    )(
        place,
        pole_weights,
        pole_order,
        mine[1],
        theirs[1],
        forward_states,
        far,
        near,
        *coefficients,
    )

    gradient = share[0, 0]
    for k in range(groups):
        for side in (0, 1):
            if k or side:
                pairs = [
                    (i * peers + j, (i + k) % groups * peers + (j ^ side))
                    for i in range(groups)
                    for j in range(peers)
                ]
                gradient = gradient + lax.ppermute(share[k, side], ("pole", "space"), pairs)
    swap = [(i, i ^ 1) for i in range(peers)]
    partner = lax.ppermute(adjoint[1], "space", swap)
    even = place[0] % 2 == 0
    adjoint_states = jnp.stack(
        [jnp.where(even, adjoint[0], partner), jnp.where(even, partner, adjoint[0])]
    )
    return adjoint_states, gradient


def plus_side(field, which_dim):
    extent = field.shape[which_dim]
    inner_part = lax.slice_in_dim(field, 1, extent, axis=which_dim)
    zero_plane = jnp.zeros_like(lax.slice_in_dim(field, 0, 1, axis=which_dim))
    return jnp.concatenate([inner_part, zero_plane], axis=which_dim)


def minus_side(field, which_dim):
    extent = field.shape[which_dim]
    inner_part = lax.slice_in_dim(field, 0, extent - 1, axis=which_dim)
    zero_plane = jnp.zeros_like(lax.slice_in_dim(field, 0, 1, axis=which_dim))
    return jnp.concatenate([zero_plane, inner_part], axis=which_dim)


def coarse_pick(faces, which_dim, offset):
    extent_x, extent_y, extent_z = faces.shape
    blocks = faces.reshape(extent_x // 2, 2, extent_y // 2, 2, extent_z // 2, 2)
    chosen = lax.index_in_dim(blocks, offset, axis=2 * which_dim + 1, keepdims=True)
    return jnp.sum(chosen, axis=(1, 3, 5))


def side_terms(field, plus_faces, minus_faces, widened):
    result = plus_faces[0] * (field - widened[:, 2:]) + minus_faces[0] * (field - widened[:, :-2])
    for which_dim in (1, 2):
        result = result + plus_faces[which_dim] * (field - plus_side(field, which_dim + 1))
        result = result + minus_faces[which_dim] * (field - minus_side(field, which_dim + 1))
    return result


def fine_image(field, plus_faces, minus_faces, shift_value):
    widened = extended(field, (("space", 1),), 1)
    return shift_value * field + side_terms(field, plus_faces, minus_faces, widened)


def coarse_image(field, plus_faces, minus_faces, shift_value):
    widened = extended(field, (("space", 1),), 1)
    return shift_value * field + side_terms(field, plus_faces, minus_faces, widened)


def restrict(field):
    members, extent_x, extent_y, extent_z = field.shape
    shaped = field.reshape(members, extent_x // 2, 2, extent_y // 2, 2, extent_z // 2, 2)
    return jnp.sum(shaped, axis=(2, 4, 6))


def prolong(field):
    return jnp.repeat(jnp.repeat(jnp.repeat(field, 2, axis=1), 2, axis=2), 2, axis=3)


def precondition(residual, fine, coarse):
    plus_faces, minus_faces, shift_value, diagonal = fine
    coarse_plus, coarse_minus, coarse_shift, coarse_diagonal = coarse
    smooth_one = DAMPING * residual / diagonal
    coarse_rhs = restrict(residual - fine_image(smooth_one, plus_faces, minus_faces, shift_value))
    coarse_one = DAMPING * coarse_rhs / coarse_diagonal
    coarse_two = (
        coarse_one
        + DAMPING
        * (coarse_rhs - coarse_image(coarse_one, coarse_plus, coarse_minus, coarse_shift))
        / coarse_diagonal
    )
    corrected = smooth_one + prolong(coarse_two)
    return (
        corrected
        + DAMPING
        * (residual - fine_image(corrected, plus_faces, minus_faces, shift_value))
        / diagonal
    )


def expand(values):
    return values.reshape(-1, 1, 1, 1)


def cell_sums(values):
    return jnp.sum(values, axis=(1, 2, 3))


def norm_sum(residual, precond):
    return lax.psum(cell_sums(residual * precond), "space")


def solve(rhs, fine, coarse):
    plus_faces, minus_faces, shift_value, diagonal = fine
    iterate = jnp.zeros_like(rhs)
    residual = rhs
    precond = precondition(residual, fine, coarse)
    gamma_now = norm_sum(residual, precond)
    search = precond
    for turn_index in range(ITERS):
        image_field = fine_image(search, plus_faces, minus_faces, shift_value)
        curve = lax.psum(cell_sums(search * image_field), "space")
        step_length = gamma_now / curve
        iterate = iterate + expand(step_length) * search
        if turn_index + 1 < ITERS:
            residual = residual - expand(step_length) * image_field
            precond = precondition(residual, fine, coarse)
            gamma_next = norm_sum(residual, precond)
            search = precond + expand(gamma_next / gamma_now) * search
            gamma_now = gamma_next
    return iterate


def divided(conductivity, misfit, forward_states, pole_shifts, pole_weights, pole_order):
    widened_kappa = extended(conductivity, (("space", 0),), 1)
    plus_faces = [
        0.5 * (conductivity + widened_kappa[2:]),
        0.5 * (conductivity + plus_side(conductivity, 1)),
        0.5 * (conductivity + plus_side(conductivity, 2)),
    ]
    minus_faces = [
        0.5 * (conductivity + widened_kappa[:-2]),
        0.5 * (conductivity + minus_side(conductivity, 1)),
        0.5 * (conductivity + minus_side(conductivity, 2)),
    ]
    base_diagonal = (
        plus_faces[0]
        + plus_faces[1]
        + plus_faces[2]
        + minus_faces[0]
        + minus_faces[1]
        + minus_faces[2]
    )
    coarse_plus = [coarse_pick(plus_faces[which_dim], which_dim, 1) for which_dim in range(3)]
    coarse_minus = [coarse_pick(minus_faces[which_dim], which_dim, 0) for which_dim in range(3)]
    coarse_base = (
        coarse_plus[0]
        + coarse_plus[1]
        + coarse_plus[2]
        + coarse_minus[0]
        + coarse_minus[1]
        + coarse_minus[2]
    )
    pole_index = jnp.arange(pole_shifts.shape[0], dtype=jnp.int32)
    matches = pole_order[:, None] == pole_index[None, :]
    shift_local = jnp.sum(jnp.where(matches, pole_shifts[None, :], 0.0), axis=1)
    weight_local = jnp.sum(jnp.where(matches, pole_weights[None, :], 0.0), axis=1)
    members = forward_states.shape[0]

    def solve_group(shift_part, weight_part):
        shift_value = expand(shift_part)
        fine = (plus_faces, minus_faces, shift_value, base_diagonal[None] + shift_value)
        coarse = (
            coarse_plus,
            coarse_minus,
            8.0 * shift_value,
            coarse_base[None] + 8.0 * shift_value,
        )
        return solve(expand(weight_part) * misfit[None], fine, coarse)

    adjoint_states = jnp.concatenate(
        [
            solve_group(shift_local[member : member + 1], weight_local[member : member + 1])
            for member in range(members)
        ],
        axis=0,
    )
    widened = extended(jnp.stack([adjoint_states, forward_states]), (("space", 2),), 1)
    term = (adjoint_states - widened[0, :, 2:]) * (forward_states - widened[1, :, 2:])
    term = term + (adjoint_states - widened[0, :, :-2]) * (forward_states - widened[1, :, :-2])
    for which_dim in (2, 3):
        term = term + (adjoint_states - plus_side(adjoint_states, which_dim)) * (
            forward_states - plus_side(forward_states, which_dim)
        )
        term = term + (adjoint_states - minus_side(adjoint_states, which_dim)) * (
            forward_states - minus_side(forward_states, which_dim)
        )
    local_term = -0.5 * jnp.sum(term, axis=0)
    gradient = lax.psum_scatter(local_term, "pole", scatter_dimension=1, tiled=True)
    return (adjoint_states, gradient)


def solution(mesh):
    in_specs = (
        P("space", None, None),
        P("space", None, None),
        P("pole", "space", None, None),
        P(),
        P(),
        P("pole"),
    )
    out_specs = (P("pole", "space", None, None), P("space", "pole", None))

    def body(conductivity, misfit, forward_states, *poles):
        nx = conductivity.shape[0] * lax.axis_size("space")
        _, ny, nz = conductivity.shape
        peers = lax.axis_size("space")
        small = nx * ny * nz <= REPLICATED_CELLS and forward_states.shape[:2] == (2, 2)
        if small and nz == 2 * HALF and peers > 2 and peers & (peers - 1) == 0:
            return whole_grid(conductivity, misfit, forward_states, *poles)
        return divided(conductivity, misfit, forward_states, *poles)

    return jax.shard_map(
        body, mesh=mesh, in_specs=in_specs, out_specs=out_specs, check_vma=False
    )
```

```python
import functools

import jax
import jax.numpy as jnp
from jax import lax
from jax.experimental import pallas as pl
from jax.experimental.pallas import tpu as pltpu
from jax.sharding import PartitionSpec as P

ITERS = 2
DAMPING = 0.8
REPLICATED_CELLS = 32 * 64 * 128
HALF = 64
TILE = 8
UNROLL = 8


def extended(array, sides, width):
    for axis, dim in sides:
        peers, length = (lax.axis_size(axis), array.shape[dim])
        up = [(i, (i + 1) % peers) for i in range(peers - 1)]
        down = [(j, i) for i, j in up]
        last = lax.slice_in_dim(array, length - width, length, axis=dim)
        leading = lax.slice_in_dim(array, 0, width, axis=dim)
        before = lax.ppermute(last, axis, up)
        after = lax.ppermute(leading, axis, down)
        array = jnp.concatenate([before, array, after], axis=dim)
    return array


def lane_index(shape):
    return lax.broadcasted_iota(jnp.int32, shape, len(shape) - 1)


def row_index(shape):
    return lax.broadcasted_iota(jnp.int32, shape, len(shape) - 2)


def roll(block, shift, axis):
    return pltpu.roll(block, shift % block.shape[axis], axis)


def inverse(value):
    guess = pl.reciprocal(value, approx=True)
    return guess * (2.0 - value * guess)


def tree_sum(values):
    while len(values) > 1:
        values = [sum(values[at : at + 2]) for at in range(0, len(values), 2)]
    return values[0]


def grand_total(acc):
    line = jnp.sum(acc, axis=0, keepdims=True)
    return jnp.broadcast_to(jnp.sum(line, axis=1, keepdims=True), acc.shape)


def swap_masks(peers, flip):
    even = []
    mask = peers // 2
    while mask > 1:
        even.append(mask)
        mask //= 2
    odd = even[-1:] + even[:-1]
    return (odd, even) if flip else (even, odd)


def block_pair(u, holder, peers, flip):
    even, odd = swap_masks(peers, flip)
    parity = holder % 2
    top = jnp.where(parity == 0, even.index(peers // 2), odd.index(peers // 2))
    below = u & ((1 << top) - 1)
    base = ((u >> top) << (top + 1)) | below
    upper = jnp.where(holder >= peers // 2, 1, 0)
    first = base | (upper << top)
    second = base | ((1 - upper) << top)
    home = holder
    for step, (mask_even, mask_odd) in enumerate(zip(even, odd)):
        mask = jnp.where(parity == 0, mask_even, mask_odd)
        home = home ^ (((first >> step) & 1) * mask)
    return first, second, home


def prepare_kernel(place_ref, kappa_ref, misfit_ref, state_ref, half_ref, own_ref, held_ref, edge_ref):
    half_ref[0] = 0.5 * kappa_ref[...]
    own_ref[0] = misfit_ref[...]
    held_ref[...] = state_ref[...]
    even = place_ref[0] % 2 == 0
    last = state_ref.shape[1] - 1
    for slot in (0, 1):
        edge_ref[slot, 0] = jnp.where(even, state_ref[slot, 0], state_ref[slot, last])


def gather_blocks(place, kappa, misfit, states, axis):
    peers = lax.axis_size(axis)
    even = place[0] % 2 == 0
    swap = [(i, i ^ 1) for i in range(peers)]
    smem = pl.BlockSpec(memory_space=pltpu.SMEM)
    vmem = pl.BlockSpec(memory_space=pltpu.VMEM)
    shapes = [(1, *kappa.shape), (1, *misfit.shape), states.shape, (2, 1, *states.shape[2:])]
    half, own, states, edge = pl.pallas_call(
        prepare_kernel,
        out_shape=[jax.ShapeDtypeStruct(shape, jnp.float32) for shape in shapes],
        in_specs=[smem] + [vmem] * 3,
        out_specs=[vmem] * 4,
        compiler_params=pltpu.CompilerParams(vmem_limit_bytes=2 * 1024 * 1024),
        name="prepare",
    )(place, kappa, misfit, states)
    over = [(i, i + 1 if i % 2 else i - 1) for i in range(1, peers - 1)]
    far = lax.ppermute(edge, axis, over)
    swaps = [list(zip(*swap_masks(peers, flip))) for flip in (False, True)]
    steps = len(swaps[0])
    held = [kappa[None], misfit[None]]
    for step in range(steps):
        if step == steps - 1:
            held[0], far = lax.optimization_barrier((held[0], far))
            given = jnp.concatenate([states, far], axis=1)
            near = lax.ppermute(jnp.where(even, given[1], given[0]), axis, swap)
        for at in (0, 1):
            masks = swaps[at][step]
            pairs = [(i, i ^ masks[i % 2]) for i in range(peers)]
            arrived = lax.ppermute(held[at], axis, pairs)
            if step == 0:
                held[at] = (half, own)[at]
                arrived = (0.5, 1.0)[at] * arrived
            held[at] = jnp.concatenate([held[at], arrived], axis=0)
    held[0], near = lax.optimization_barrier((held[0], near))
    other = [lax.ppermute(part, axis, swap) for part in held]
    return held, other, states, far, near


CLASSES = [(a, b, c) for a in (0, 1) for b in (0, 1) for c in (0, 1)]
PAIRS = [(p, q) for p in (0, 1) for q in (0, 1)]


def cls(a, b, c):
    return 4 * a + 2 * b + c


def inner_faces(p, q):
    return (
        (2 * p + q, cls(0, p, q), cls(1, p, q)),
        (4 + 2 * p + q, cls(p, 0, q), cls(p, 1, q)),
        (8 + 2 * p + q, cls(p, q, 0), cls(p, q, 1)),
    )


class Layout:
    def __init__(self, rows):
        self.tiles = rows // TILE
        self.lane = lane_index((TILE, 2 * HALF))
        self.row = row_index((TILE, 2 * HALF))
        self.left = self.lane < HALF
        self.zero = jnp.zeros((TILE, 2 * HALF), jnp.float32)

    def tile(self, j):
        return pl.ds(TILE * j, TILE)

    def every(self, b, j):
        return pl.ds(b + 2 * j, TILE, stride=2 * self.tiles)

    def row_before(self, load, j):
        return load(j - 1) if j else roll(load(self.tiles - 1), 1, 0)

    def row_after(self, load, j):
        return load(j + 1) if j + 1 < self.tiles else roll(load(0), -1, 0)

    def seam(self, ref, low, high):
        last = ref.shape[1] - 1
        for j in range(self.tiles):
            for k in low:
                moved = roll(ref[k, last - 1, self.tile(j)], HALF, 1)
                ref[k, 0, self.tile(j)] = jnp.where(self.left, 0.0, moved)
            for k in high:
                moved = roll(ref[k, 1, self.tile(j)], HALF, 1)
                ref[k, last, self.tile(j)] = jnp.where(self.left, moved, 0.0)

    def seam_fine(self, ref):
        count = ref.shape[0]
        self.seam(
            ref,
            [k for k in range(count) if k % 8 >= 4],
            [k for k in range(count) if k % 8 < 4],
        )

    def arrange(self, mine_ref, theirs_ref, place, flip, store):
        blocks, own, rows, _ = mine_ref.shape
        column = self.lane % HALF
        even_odd = 2 * column + jnp.where(self.left, 0, 1)
        odd_even = 2 * column + jnp.where(self.left, 1, 0)

        def pair(u, carry):
            for ref, holder in ((mine_ref, place), (theirs_ref, place ^ 1)):
                first, second, home = block_pair(u, holder, 2 * blocks, flip)
                for x in range(own):
                    spot = home * (own // 2) + x // 2
                    for b in (0, 1):
                        for j in range(self.tiles):
                            one = jnp.take_along_axis(
                                ref[first, x, self.every(b, j), :], even_odd, axis=1
                            )
                            two = jnp.take_along_axis(
                                ref[second, x, self.every(b, j), :], odd_even, axis=1
                            )
                            store(cls(x % 2, b, 0), spot, j, jnp.where(self.left, one, two))
                            odd = roll(jnp.where(self.left, two, one), HALF, 1)
                            store(cls(x % 2, b, 1), spot, j, odd)
            return carry

        lax.fori_loop(0, blocks // 2, pair, 0)


def setup_kernel(
    place_ref,
    shifts_ref,
    order_ref,
    mine_ref,
    theirs_ref,
    inner,
    outer_x,
    outer_y,
    outer_z,
    inner_sum,
    diagonal,
    damped,
    coarse_off,
    coarse_damped,
    half_kappa,
):
    half = inner.shape[1]
    at_ = Layout(inner.shape[2])
    tile, tiles = at_.tile, at_.tiles
    shift = shifts_ref[order_ref[place_ref[0] % 2]]

    def keep(k, spot, j, value):
        half_kappa[k, spot + 1, tile(j)] = value

    at_.arrange(mine_ref, theirs_ref, place_ref[0], False, keep)
    at_.seam_fine(half_kappa)

    z_low = jnp.where(at_.lane % HALF > 0, 1.0, 0.0)
    z_high = jnp.where(at_.lane % HALF < HALF - 1, 1.0, 0.0)
    y_low = [jnp.where(at_.row > 0, 1.0, 0.0)] + [None] * (tiles - 1)
    y_high = [None] * (tiles - 1) + [jnp.where(at_.row < TILE - 1, 1.0, 0.0)]

    def masked(mask, value):
        return value if mask is None else mask * value

    def plane(i, carry):
        for j in range(tiles):
            kap = [half_kappa[k, i + 1, tile(j)] for k in range(8)]
            inside = [[] for _ in range(8)]
            outside = [[] for _ in range(8)]
            off = [[] for _ in range(5)]
            for p, q in PAIRS:
                for face_at, low, high in inner_faces(p, q):
                    face = kap[low] + kap[high]
                    inner[face_at, i, tile(j)] = face
                    inside[low].append(face)
                    inside[high].append(face)
                at = 2 * p + q

                low, high = cls(0, p, q), cls(1, p, q)
                minus = kap[low] + half_kappa[high, i, tile(j)]
                plus = kap[high] + half_kappa[low, i + 2, tile(j)]
                outside[low].append(minus)
                outside[high].append(plus)
                outer_x[at, i, tile(j)] = minus
                off[0].append(minus)

                low, high = cls(p, 0, q), cls(p, 1, q)
                side = at_.row_before(lambda r: half_kappa[high, i + 1, tile(r)], j)
                minus = kap[low] + masked(y_low[j], side)
                side = at_.row_after(lambda r: half_kappa[low, i + 1, tile(r)], j)
                plus = kap[high] + masked(y_high[j], side)
                outside[low].append(minus)
                outside[high].append(plus)
                minus, plus = masked(y_low[j], minus), masked(y_high[j], plus)
                outer_y[at, i, tile(j)] = minus
                outer_y[4 + at, i, tile(j)] = plus
                off[1].append(minus)
                off[2].append(plus)

                low, high = cls(p, q, 0), cls(p, q, 1)
                minus = kap[low] + z_low * roll(kap[high], 1, 1)
                plus = kap[high] + z_high * roll(kap[low], -1, 1)
                outside[low].append(minus)
                outside[high].append(plus)
                minus, plus = z_low * minus, z_high * plus
                outer_z[at, i, tile(j)] = minus
                outer_z[4 + at, i, tile(j)] = plus
                off[3].append(minus)
                off[4].append(plus)
            coarse_total = []
            for k in range(8):
                within, without = tree_sum(inside[k]), tree_sum(outside[k])
                inner_sum[k, i, tile(j)] = within
                base = within + without + shift
                diagonal[k, i, tile(j)] = base
                coarse_total.append(without)
                damped[k, i, tile(j)] = DAMPING * inverse(base)
            for at, part in enumerate(off):
                coarse_off[at, i, tile(j)] = tree_sum(part)
            coarse_damped[i, tile(j)] = DAMPING * inverse(tree_sum(coarse_total) + 8.0 * shift)
        return carry

    lax.fori_loop(0, half, plane, 0)
    for j in range(tiles):
        part = []
        for p, q in PAIRS:
            face = half_kappa[cls(0, p, q), half + 1, tile(j)]
            face = face + half_kappa[cls(1, p, q), half, tile(j)]
            outer_x[2 * p + q, half, tile(j)] = face
            part.append(face)
        coarse_off[0, half, tile(j)] = tree_sum(part)


def solve_kernel(
    place_ref,
    weights_ref,
    order_ref,
    mine_ref,
    theirs_ref,
    state_ref,
    far_ref,
    near_ref,
    inner,
    outer_x,
    outer_y,
    outer_z,
    inner_sum,
    diagonal,
    damped,
    coarse_off,
    coarse_damped,
    adjoint_ref,
    keep_ref,
    partner_ref,
    send_ref,
    residual,
    scaled,
    partial,
    first_dir,
    second_dir,
    image,
    coarse_one,
    coarse_two,
    planes,
):
    half, rows = inner.shape[1:3]
    at_ = Layout(rows)
    tile, tiles, zero = at_.tile, at_.tiles, at_.zero
    core = place_ref[0] % 2
    weight = weights_ref[order_ref[core]]

    def begin(k, spot, j, value):
        res = weight * value
        residual[k, spot, tile(j)] = res
        scaled[k, spot + 1, tile(j)] = damped[k, spot, tile(j)] * res

    at_.arrange(mine_ref, theirs_ref, place_ref[0], True, begin)
    at_.seam_fine(scaled)

    def stencil(field, i, j, both):
        here = [field[k, i + 1, tile(j)] for k in range(8)]
        terms = [[] for _ in range(8)]
        for p, q in PAIRS:
            at = 2 * p + q
            for face_at, low, high in inner_faces(p, q):
                face = inner[face_at, i, tile(j)]
                terms[low].append(face * here[high])
                if both:
                    terms[high].append(face * here[low])
            low, high = cls(0, p, q), cls(1, p, q)
            terms[low].append(outer_x[at, i, tile(j)] * field[high, i, tile(j)])
            if both:
                side = field[low, i + 2, tile(j)]
                terms[high].append(outer_x[at, i + 1, tile(j)] * side)
            low, high = cls(p, 0, q), cls(p, 1, q)
            side = at_.row_before(lambda r: field[high, i + 1, tile(r)], j)
            terms[low].append(outer_y[at, i, tile(j)] * side)
            if both:
                side = at_.row_after(lambda r: field[low, i + 1, tile(r)], j)
                terms[high].append(outer_y[4 + at, i, tile(j)] * side)
            low, high = cls(p, q, 0), cls(p, q, 1)
            terms[low].append(outer_z[at, i, tile(j)] * roll(here[high], 1, 1))
            if both:
                terms[high].append(outer_z[4 + at, i, tile(j)] * roll(here[low], -1, 1))
        return here, [tree_sum(part) if part else None for part in terms]

    def coarse_sides(field, i, j):
        here = field[0, i + 1, tile(j)]
        return here, (
            (field[0, i, tile(j)], field[0, i + 2, tile(j)]),
            (
                at_.row_before(lambda r: field[0, i + 1, tile(r)], j),
                at_.row_after(lambda r: field[0, i + 1, tile(r)], j),
            ),
            (roll(here, 1, 1), roll(here, -1, 1)),
        )

    def precondition(result, other):
        def down(i, carry):
            for j in range(tiles):
                res = [residual[k, i, tile(j)] for k in range(8)]
                _, sums = stencil(scaled, i, j, True)
                parts = [(2.0 - DAMPING) * res[k] + sums[k] for k in range(8)]
                for k in range(8):
                    partial[k, i, tile(j)] = parts[k]
                rhs = tree_sum(parts) - tree_sum(res)
                coarse_one[0, i + 1, tile(j)] = coarse_damped[i, tile(j)] * rhs
            return carry

        lax.fori_loop(0, half, down, 0, unroll=UNROLL)
        at_.seam(coarse_one, [0], [0])

        def smooth(i, carry):
            for j in range(tiles):
                here, sides = coarse_sides(coarse_one, i, j)
                total = coarse_off[0, i, tile(j)] * sides[0][0]
                total = total + coarse_off[0, i + 1, tile(j)] * sides[0][1]
                more = coarse_off[1, i, tile(j)] * sides[1][0]
                more = more + coarse_off[2, i, tile(j)] * sides[1][1]
                most = coarse_off[3, i, tile(j)] * sides[2][0]
                most = most + coarse_off[4, i, tile(j)] * sides[2][1]
                coarse_two[0, i + 1, tile(j)] = (2.0 - DAMPING) * here + coarse_damped[
                    i, tile(j)
                ] * (total + more + most)
            return carry

        lax.fori_loop(0, half, smooth, 0, unroll=UNROLL)
        at_.seam(coarse_two, [0], [0])

        def up(i, carry):
            gamma, cross = carry
            for j in range(tiles):
                here, sides = coarse_sides(coarse_two, i, j)
                kept = (1.0 - DAMPING) * here
                dots, crosses = [], []
                for a, b, c in CLASSES:
                    k = cls(a, b, c)
                    value = tree_sum(
                        [
                            partial[k, i, tile(j)],
                            inner_sum[k, i, tile(j)] * here,
                            outer_x[2 * b + c, i + a, tile(j)] * sides[0][a],
                            outer_y[4 * b + 2 * a + c, i, tile(j)] * sides[1][b],
                            outer_z[4 * c + 2 * a + b, i, tile(j)] * sides[2][c],
                        ]
                    )
                    new = kept + damped[k, i, tile(j)] * value
                    result[k, i + 1, tile(j)] = new
                    dots.append(residual[k, i, tile(j)] * new)
                    if other is not None:
                        crosses.append(other[k, i, tile(j)] * new)
                gamma = gamma + tree_sum(dots)
                if other is not None:
                    cross = cross + tree_sum(crosses)
            return gamma, cross

        sums = lax.fori_loop(0, half, up, (zero, zero), unroll=UNROLL)
        at_.seam_fine(result)
        return [grand_total(part) for part in sums]

    gamma, _ = precondition(first_dir, None)

    def apply(i, acc):
        for j in range(tiles):
            here, sums = stencil(first_dir, i, j, True)
            dots = []
            for k in range(8):
                value = diagonal[k, i, tile(j)] * here[k] - sums[k]
                image[k, i, tile(j)] = value
                dots.append(here[k] * value)
            acc = acc + tree_sum(dots)
        return acc

    curve = grand_total(lax.fori_loop(0, half, apply, zero, unroll=UNROLL))
    step_one = gamma / curve

    def update(i, carry):
        for j in range(tiles):
            for k in range(8):
                new = residual[k, i, tile(j)] - step_one * image[k, i, tile(j)]
                residual[k, i, tile(j)] = new
                scaled[k, i + 1, tile(j)] = damped[k, i, tile(j)] * new
        return carry

    lax.fori_loop(0, half, update, 0, unroll=UNROLL)
    at_.seam_fine(scaled)

    gamma_next, cross = precondition(second_dir, image)

    def bend(i, carry):
        own_part, face_part = carry
        for j in range(tiles):
            here, sums = stencil(second_dir, i, j, False)
            own_part = own_part + tree_sum(
                [here[k] * (diagonal[k, i, tile(j)] * here[k]) for k in range(8)]
            )
            face_part = face_part + tree_sum([here[k] * sums[k] for k in range(7)])
        return own_part, face_part

    own_part, face_part = lax.fori_loop(0, half, bend, (zero, zero), unroll=UNROLL)
    ratio = gamma_next / gamma
    curve_next = grand_total(own_part - 2.0 * face_part)
    step_two = gamma_next / (curve_next + ratio * (2.0 * cross + ratio * curve))
    step_first = step_one + step_two * ratio

    own, ny, nz = adjoint_ref.shape
    start = (place_ref[0] - core) * (own // 2)
    upper = jnp.where(start >= half, 1, 0)
    start = start - half * upper
    even = at_.lane % 2 == 0
    source = at_.lane // 2 + HALF * upper
    for at in range(2 * own + 2):
        a = (at + 1) % 2
        spot = start + (at + 1) // 2
        for b in (0, 1):
            for j in range(tiles):
                both = [
                    step_first * first_dir[cls(a, b, c), spot, tile(j)]
                    + step_two * second_dir[cls(a, b, c), spot, tile(j)]
                    for c in (0, 1)
                ]
                planes[at, at_.every(b, j), :] = jnp.where(
                    even,
                    jnp.take_along_axis(both[0], source, axis=1),
                    jnp.take_along_axis(both[1], source, axis=1),
                )

    full = (ny, nz)
    y_at = row_index(full)
    z_at = lane_index(full)

    def drop(value, axis, up):
        moved = roll(value, -1 if up else 1, axis)
        at = (y_at, z_at)[axis]
        edge = full[axis] - 1 if up else 0
        return value - jnp.where(at == edge, 0.0, moved)

    is_even = core == 0
    state = [jnp.where(is_even, far_ref[core, 0], near_ref[own])]
    state += [jnp.where(is_even, state_ref[core, x], near_ref[x]) for x in range(own)]
    state += [jnp.where(is_even, near_ref[x], state_ref[core, x]) for x in range(own)]
    state += [jnp.where(is_even, near_ref[own], far_ref[core, 0])]
    terms = 2 * own + 2
    for x in range(2 * own):
        here, f = planes[x + 1], state[x + 1]
        term = (here - planes[x + 2]) * (f - state[x + 2])
        term = term + (here - planes[x]) * (f - state[x])
        for axis in (0, 1):
            for up in (True, False):
                term = term + drop(here, axis, up) * drop(f, axis, up)
        planes[terms + x] = -0.5 * term

    groups = send_ref.shape[0] + 1
    chunk = keep_ref.shape[1]
    for x in range(own):
        mine, other = core * own + x, (1 - core) * own + x
        adjoint_ref[x] = planes[1 + mine]
        partner_ref[x, :ny] = planes[1 + other]
        for k in range(groups):
            at = pl.multiple_of(lax.rem(place_ref[1] + k, groups) * chunk, chunk)
            for side, plane in enumerate((mine, other)):
                share = planes[terms + plane, pl.ds(at, chunk), :]
                if k:
                    send_ref[k - 1, side, x] = share
                elif side:
                    partner_ref[x, ny:] = share
                else:
                    keep_ref[x] = share


def whole_grid(conductivity, misfit, forward_states, pole_shifts, pole_weights, pole_order):
    members, own, ny, nz = forward_states.shape
    groups = lax.axis_size("pole")
    place = jnp.stack([lax.axis_index("space"), lax.axis_index("pole")]).astype(jnp.int32)
    peers = lax.axis_size("space")
    mine, theirs, states, far, near = gather_blocks(
        place, conductivity, misfit, forward_states, "space"
    )
    half, rows = peers * own // 4, ny // 2

    def field(count, extent):
        return (count, extent, rows, 2 * HALF)

    def held(*shape):
        return pltpu.VMEM(shape, jnp.float32)

    smem = pl.BlockSpec(memory_space=pltpu.SMEM)
    vmem = pl.BlockSpec(memory_space=pltpu.VMEM)
    shapes = [
        field(12, half),
        field(4, half + 1),
        field(8, half),
        field(8, half),
        field(8, half),
        field(8, half),
        field(8, half),
        field(5, half + 1),
        (half, rows, 2 * HALF),
    ]
    coefficients = pl.pallas_call(
        setup_kernel,
        out_shape=[jax.ShapeDtypeStruct(shape, jnp.float32) for shape in shapes],
        in_specs=[smem] * 3 + [vmem] * 2,
        out_specs=[vmem] * len(shapes),
        scratch_shapes=[held(*field(8, half + 2))],
        compiler_params=pltpu.CompilerParams(vmem_limit_bytes=6 * 1024 * 1024),
        name="setup",
    )(place, pole_shifts, pole_order, mine[0], theirs[0])
    chunk = ny // groups
    adjoint, gradient, partner, send = pl.pallas_call(
        solve_kernel,
        out_shape=[
            jax.ShapeDtypeStruct((own, ny, nz), jnp.float32),
            jax.ShapeDtypeStruct((own, chunk, nz), jnp.float32),
            jax.ShapeDtypeStruct((own, ny + chunk, nz), jnp.float32),
            jax.ShapeDtypeStruct((groups - 1, 2, own, chunk, nz), jnp.float32),
        ],
        in_specs=[smem] * 3 + [vmem] * (5 + len(shapes)),
        out_specs=[vmem] * 4,
        scratch_shapes=[
            held(*field(8, half)),
            held(*field(8, half + 2)),
            held(*field(8, half)),
            held(*field(8, half + 2)),
            held(*field(8, half + 2)),
            held(*field(8, half)),
            held(*field(1, half + 2)),
            held(*field(1, half + 2)),
            held(4 * own + 2, ny, nz),
        ],
        compiler_params=pltpu.CompilerParams(vmem_limit_bytes=12 * 1024 * 1024),
        name="solve",
    )(
        place,
        pole_weights,
        pole_order,
        mine[1],
        theirs[1],
        states,
        far,
        near,
        *coefficients,
    )

    arrived = lax.ppermute(partner, "space", [(i, i ^ 1) for i in range(peers)])
    shares = []
    for k in range(1, groups):
        for side in (0, 1):
            pairs = [
                (i * peers + j, (i + k) % groups * peers + (j ^ side))
                for i in range(groups)
                for j in range(peers)
            ]
            shares.append(lax.ppermute(send[k - 1, side], ("pole", "space"), pairs))
    even = place[0] % 2 == 0
    theirs = arrived[:, :ny]
    adjoint_states = jnp.stack(
        [jnp.where(even, adjoint, theirs), jnp.where(even, theirs, adjoint)]
    )
    adjoint_states, arrived = lax.optimization_barrier((adjoint_states, arrived))
    return adjoint_states, gradient + arrived[:, ny:] + sum(shares)


def plus_side(field, which_dim):
    extent = field.shape[which_dim]
    inner_part = lax.slice_in_dim(field, 1, extent, axis=which_dim)
    zero_plane = jnp.zeros_like(lax.slice_in_dim(field, 0, 1, axis=which_dim))
    return jnp.concatenate([inner_part, zero_plane], axis=which_dim)


def minus_side(field, which_dim):
    extent = field.shape[which_dim]
    inner_part = lax.slice_in_dim(field, 0, extent - 1, axis=which_dim)
    zero_plane = jnp.zeros_like(lax.slice_in_dim(field, 0, 1, axis=which_dim))
    return jnp.concatenate([zero_plane, inner_part], axis=which_dim)


def coarse_pick(faces, which_dim, offset):
    extent_x, extent_y, extent_z = faces.shape
    blocks = faces.reshape(extent_x // 2, 2, extent_y // 2, 2, extent_z // 2, 2)
    chosen = lax.index_in_dim(blocks, offset, axis=2 * which_dim + 1, keepdims=True)
    return jnp.sum(chosen, axis=(1, 3, 5))


def side_terms(field, plus_faces, minus_faces, widened):
    result = plus_faces[0] * (field - widened[:, 2:]) + minus_faces[0] * (field - widened[:, :-2])
    for which_dim in (1, 2):
        result = result + plus_faces[which_dim] * (field - plus_side(field, which_dim + 1))
        result = result + minus_faces[which_dim] * (field - minus_side(field, which_dim + 1))
    return result


def fine_image(field, plus_faces, minus_faces, shift_value):
    widened = extended(field, (("space", 1),), 1)
    return shift_value * field + side_terms(field, plus_faces, minus_faces, widened)


def coarse_image(field, plus_faces, minus_faces, shift_value):
    widened = extended(field, (("space", 1),), 1)
    return shift_value * field + side_terms(field, plus_faces, minus_faces, widened)


def restrict(field):
    members, extent_x, extent_y, extent_z = field.shape
    shaped = field.reshape(members, extent_x // 2, 2, extent_y // 2, 2, extent_z // 2, 2)
    return jnp.sum(shaped, axis=(2, 4, 6))


def prolong(field):
    return jnp.repeat(jnp.repeat(jnp.repeat(field, 2, axis=1), 2, axis=2), 2, axis=3)


def precondition(residual, fine, coarse):
    plus_faces, minus_faces, shift_value, diagonal = fine
    coarse_plus, coarse_minus, coarse_shift, coarse_diagonal = coarse
    smooth_one = DAMPING * residual / diagonal
    coarse_rhs = restrict(residual - fine_image(smooth_one, plus_faces, minus_faces, shift_value))
    coarse_one = DAMPING * coarse_rhs / coarse_diagonal
    coarse_two = (
        coarse_one
        + DAMPING
        * (coarse_rhs - coarse_image(coarse_one, coarse_plus, coarse_minus, coarse_shift))
        / coarse_diagonal
    )
    corrected = smooth_one + prolong(coarse_two)
    return (
        corrected
        + DAMPING
        * (residual - fine_image(corrected, plus_faces, minus_faces, shift_value))
        / diagonal
    )


def expand(values):
    return values.reshape(-1, 1, 1, 1)


def cell_sums(values):
    return jnp.sum(values, axis=(1, 2, 3))


def norm_sum(residual, precond):
    return lax.psum(cell_sums(residual * precond), "space")


def solve(rhs, fine, coarse):
    plus_faces, minus_faces, shift_value, diagonal = fine
    iterate = jnp.zeros_like(rhs)
    residual = rhs
    precond = precondition(residual, fine, coarse)
    gamma_now = norm_sum(residual, precond)
    search = precond
    for turn_index in range(ITERS):
        image_field = fine_image(search, plus_faces, minus_faces, shift_value)
        curve = lax.psum(cell_sums(search * image_field), "space")
        step_length = gamma_now / curve
        iterate = iterate + expand(step_length) * search
        if turn_index + 1 < ITERS:
            residual = residual - expand(step_length) * image_field
            precond = precondition(residual, fine, coarse)
            gamma_next = norm_sum(residual, precond)
            search = precond + expand(gamma_next / gamma_now) * search
            gamma_now = gamma_next
    return iterate


def divided(conductivity, misfit, forward_states, pole_shifts, pole_weights, pole_order):
    widened_kappa = extended(conductivity, (("space", 0),), 1)
    plus_faces = [
        0.5 * (conductivity + widened_kappa[2:]),
        0.5 * (conductivity + plus_side(conductivity, 1)),
        0.5 * (conductivity + plus_side(conductivity, 2)),
    ]
    minus_faces = [
        0.5 * (conductivity + widened_kappa[:-2]),
        0.5 * (conductivity + minus_side(conductivity, 1)),
        0.5 * (conductivity + minus_side(conductivity, 2)),
    ]
    base_diagonal = (
        plus_faces[0]
        + plus_faces[1]
        + plus_faces[2]
        + minus_faces[0]
        + minus_faces[1]
        + minus_faces[2]
    )
    coarse_plus = [coarse_pick(plus_faces[which_dim], which_dim, 1) for which_dim in range(3)]
    coarse_minus = [coarse_pick(minus_faces[which_dim], which_dim, 0) for which_dim in range(3)]
    coarse_base = (
        coarse_plus[0]
        + coarse_plus[1]
        + coarse_plus[2]
        + coarse_minus[0]
        + coarse_minus[1]
        + coarse_minus[2]
    )
    pole_index = jnp.arange(pole_shifts.shape[0], dtype=jnp.int32)
    matches = pole_order[:, None] == pole_index[None, :]
    shift_local = jnp.sum(jnp.where(matches, pole_shifts[None, :], 0.0), axis=1)
    weight_local = jnp.sum(jnp.where(matches, pole_weights[None, :], 0.0), axis=1)
    members = forward_states.shape[0]

    def solve_group(shift_part, weight_part):
        shift_value = expand(shift_part)
        fine = (plus_faces, minus_faces, shift_value, base_diagonal[None] + shift_value)
        coarse = (
            coarse_plus,
            coarse_minus,
            8.0 * shift_value,
            coarse_base[None] + 8.0 * shift_value,
        )
        return solve(expand(weight_part) * misfit[None], fine, coarse)

    adjoint_states = jnp.concatenate(
        [
            solve_group(shift_local[member : member + 1], weight_local[member : member + 1])
            for member in range(members)
        ],
        axis=0,
    )
    widened = extended(jnp.stack([adjoint_states, forward_states]), (("space", 2),), 1)
    term = (adjoint_states - widened[0, :, 2:]) * (forward_states - widened[1, :, 2:])
    term = term + (adjoint_states - widened[0, :, :-2]) * (forward_states - widened[1, :, :-2])
    for which_dim in (2, 3):
        term = term + (adjoint_states - plus_side(adjoint_states, which_dim)) * (
            forward_states - plus_side(forward_states, which_dim)
        )
        term = term + (adjoint_states - minus_side(adjoint_states, which_dim)) * (
            forward_states - minus_side(forward_states, which_dim)
        )
    local_term = -0.5 * jnp.sum(term, axis=0)
    gradient = lax.psum_scatter(local_term, "pole", scatter_dimension=1, tiled=True)
    return (adjoint_states, gradient)


def solution(mesh):
    in_specs = (
        P("space", None, None),
        P("space", None, None),
        P("pole", "space", None, None),
        P(),
        P(),
        P("pole"),
    )
    out_specs = (P("pole", "space", None, None), P("space", "pole", None))

    def body(conductivity, misfit, forward_states, *poles):
        nx = conductivity.shape[0] * lax.axis_size("space")
        _, ny, nz = conductivity.shape
        peers = lax.axis_size("space")
        small = nx * ny * nz <= REPLICATED_CELLS and forward_states.shape[:2] == (2, 2)
        if small and nz == 2 * HALF and peers > 2 and peers & (peers - 1) == 0:
            return whole_grid(conductivity, misfit, forward_states, *poles)
        return divided(conductivity, misfit, forward_states, *poles)

    return jax.shard_map(
        body, mesh=mesh, in_specs=in_specs, out_specs=out_specs, check_vma=False
    )
```

```python
import functools

import jax
import jax.numpy as jnp
from jax import lax
from jax.experimental import pallas as pl
from jax.experimental.pallas import tpu as pltpu
from jax.sharding import PartitionSpec as P

ITERS = 2
DAMPING = 0.8
REPLICATED_CELLS = 32 * 64 * 128
HALF = 64
TILE = 8
UNROLL = 2


def extended(array, sides, width):
    for axis, dim in sides:
        peers, length = (lax.axis_size(axis), array.shape[dim])
        up = [(i, (i + 1) % peers) for i in range(peers - 1)]
        down = [(j, i) for i, j in up]
        last = lax.slice_in_dim(array, length - width, length, axis=dim)
        leading = lax.slice_in_dim(array, 0, width, axis=dim)
        before = lax.ppermute(last, axis, up)
        after = lax.ppermute(leading, axis, down)
        array = jnp.concatenate([before, array, after], axis=dim)
    return array


def lane_index(shape):
    return lax.broadcasted_iota(jnp.int32, shape, len(shape) - 1)


def row_index(shape):
    return lax.broadcasted_iota(jnp.int32, shape, len(shape) - 2)


def roll(block, shift, axis):
    return pltpu.roll(block, shift % block.shape[axis], axis)


def inverse(value):
    guess = pl.reciprocal(value, approx=True)
    return guess * (2.0 - value * guess)


def tree_sum(values):
    while len(values) > 1:
        values = [sum(values[at : at + 2]) for at in range(0, len(values), 2)]
    return values[0]


def grand_total(acc):
    line = jnp.sum(acc, axis=0, keepdims=True)
    return jnp.broadcast_to(jnp.sum(line, axis=1, keepdims=True), acc.shape)


def swap_masks(peers, flip):
    falling = []
    mask = peers // 2
    while mask > 1:
        falling.append(mask)
        mask //= 2
    if flip:
        return falling[::-1], falling[:1] + falling[:0:-1]
    return falling, falling[-1:] + falling[:-1]


def block_pair(u, holder, peers, flip):
    even, odd = swap_masks(peers, flip)
    parity = holder % 2
    top = jnp.where(parity == 0, even.index(peers // 2), odd.index(peers // 2))
    below = u & ((1 << top) - 1)
    base = ((u >> top) << (top + 1)) | below
    upper = jnp.where(holder >= peers // 2, 1, 0)
    first = base | (upper << top)
    second = base | ((1 - upper) << top)
    home = holder
    for step, (mask_even, mask_odd) in enumerate(zip(even, odd)):
        mask = jnp.where(parity == 0, mask_even, mask_odd)
        home = home ^ (((first >> step) & 1) * mask)
    return first, second, home


def prepare_kernel(kappa_ref, misfit_ref, kappa_out, misfit_out):
    kappa_out[0] = kappa_ref[...]
    misfit_out[0] = misfit_ref[...]


def gather_blocks(place, kappa, misfit, states, axis):
    peers = lax.axis_size(axis)
    even = place[0] % 2 == 0
    swap = [(i, i ^ 1) for i in range(peers)]
    vmem = pl.BlockSpec(memory_space=pltpu.VMEM)
    own = pl.pallas_call(
        prepare_kernel,
        out_shape=[jax.ShapeDtypeStruct((1, *kappa.shape), jnp.float32)] * 2,
        in_specs=[vmem] * 2,
        out_specs=[vmem] * 2,
        compiler_params=pltpu.CompilerParams(vmem_limit_bytes=1024 * 1024),
        name="prepare",
    )(kappa, misfit)
    over = [(i, i + 1 if i % 2 else i - 1) for i in range(1, peers - 1)]
    swaps = [list(zip(*swap_masks(peers, flip))) for flip in (False, True)]
    steps = len(swaps[0])
    held = [kappa[None], misfit[None]]
    for step in range(steps):
        if step == steps - 1:
            held[0], far = lax.optimization_barrier((held[0], far))
            given = jnp.concatenate([states, far], axis=1)
            near = lax.ppermute(jnp.where(even, given[1], given[0]), axis, swap)
        for at in (0, 1):
            masks = swaps[at][step]
            pairs = [(i, i ^ masks[i % 2]) for i in range(peers)]
            arrived = lax.ppermute(held[at], axis, pairs)
            mine = held[at] if step else own[at]
            held[at] = jnp.concatenate([mine, arrived], axis=0)
        if step == 0:
            held[1], states = lax.optimization_barrier((held[1], states))
            edge = jnp.where(even, states[:, :1], states[:, -1:])
            far = lax.ppermute(edge, axis, over)
    held[0], near = lax.optimization_barrier((held[0], near))
    other = [lax.ppermute(part, axis, swap) for part in held]
    return held, other, states, far, near


CLASSES = [(a, b, c) for a in (0, 1) for b in (0, 1) for c in (0, 1)]
PAIRS = [(p, q) for p in (0, 1) for q in (0, 1)]


def cls(a, b, c):
    return 4 * a + 2 * b + c


def inner_faces(p, q):
    return (
        (2 * p + q, cls(0, p, q), cls(1, p, q)),
        (4 + 2 * p + q, cls(p, 0, q), cls(p, 1, q)),
        (8 + 2 * p + q, cls(p, q, 0), cls(p, q, 1)),
    )


class Layout:
    def __init__(self, rows):
        self.tiles = rows // TILE
        self.lane = lane_index((TILE, 2 * HALF))
        self.row = row_index((TILE, 2 * HALF))
        self.left = self.lane < HALF
        self.zero = jnp.zeros((TILE, 2 * HALF), jnp.float32)

    def tile(self, j):
        return pl.ds(TILE * j, TILE)

    def every(self, b, j):
        return pl.ds(b + 2 * j, TILE, stride=2 * self.tiles)

    def row_before(self, load, j):
        return load(j - 1) if j else roll(load(self.tiles - 1), 1, 0)

    def row_after(self, load, j):
        return load(j + 1) if j + 1 < self.tiles else roll(load(0), -1, 0)

    def seam(self, ref, low, high):
        last = ref.shape[1] - 1
        for j in range(self.tiles):
            for k in low:
                moved = roll(ref[k, last - 1, self.tile(j)], HALF, 1)
                ref[k, 0, self.tile(j)] = jnp.where(self.left, 0.0, moved)
            for k in high:
                moved = roll(ref[k, 1, self.tile(j)], HALF, 1)
                ref[k, last, self.tile(j)] = jnp.where(self.left, moved, 0.0)

    def seam_fine(self, ref):
        count = ref.shape[0]
        self.seam(
            ref,
            [k for k in range(count) if k % 8 >= 4],
            [k for k in range(count) if k % 8 < 4],
        )

    def arrange(self, mine_ref, theirs_ref, place, flip, store):
        blocks, own, rows, _ = mine_ref.shape
        column = self.lane % HALF
        even_odd = 2 * column + jnp.where(self.left, 0, 1)
        odd_even = 2 * column + jnp.where(self.left, 1, 0)

        def pair(u, carry):
            for ref, holder in ((mine_ref, place), (theirs_ref, place ^ 1)):
                first, second, home = block_pair(u, holder, 2 * blocks, flip)
                for x in range(own):
                    spot = home * (own // 2) + x // 2
                    for b in (0, 1):
                        for j in range(self.tiles):
                            one = jnp.take_along_axis(
                                ref[first, x, self.every(b, j), :], even_odd, axis=1
                            )
                            two = jnp.take_along_axis(
                                ref[second, x, self.every(b, j), :], odd_even, axis=1
                            )
                            store(cls(x % 2, b, 0), spot, j, jnp.where(self.left, one, two))
                            odd = roll(jnp.where(self.left, two, one), HALF, 1)
                            store(cls(x % 2, b, 1), spot, j, odd)
            return carry

        lax.fori_loop(0, blocks // 2, pair, 0)


def setup_kernel(
    place_ref,
    shifts_ref,
    order_ref,
    mine_ref,
    theirs_ref,
    inner,
    outer_x,
    outer_y,
    outer_z,
    inner_sum,
    diagonal,
    damped,
    coarse_off,
    coarse_damped,
    half_kappa,
):
    half = inner.shape[1]
    at_ = Layout(inner.shape[2])
    tile, tiles = at_.tile, at_.tiles
    shift = shifts_ref[order_ref[place_ref[0] % 2]]

    def keep(k, spot, j, value):
        half_kappa[k, spot + 1, tile(j)] = 0.5 * value

    at_.arrange(mine_ref, theirs_ref, place_ref[0], False, keep)
    at_.seam_fine(half_kappa)

    z_low = jnp.where(at_.lane % HALF > 0, 1.0, 0.0)
    z_high = jnp.where(at_.lane % HALF < HALF - 1, 1.0, 0.0)
    y_low = [jnp.where(at_.row > 0, 1.0, 0.0)] + [None] * (tiles - 1)
    y_high = [None] * (tiles - 1) + [jnp.where(at_.row < TILE - 1, 1.0, 0.0)]

    def masked(mask, value):
        return value if mask is None else mask * value

    def plane(i, carry):
        for j in range(tiles):
            kap = [half_kappa[k, i + 1, tile(j)] for k in range(8)]
            inside = [[] for _ in range(8)]
            outside = [[] for _ in range(8)]
            off = [[] for _ in range(5)]
            for p, q in PAIRS:
                for face_at, low, high in inner_faces(p, q):
                    face = kap[low] + kap[high]
                    inner[face_at, i, tile(j)] = face
                    inside[low].append(face)
                    inside[high].append(face)
                at = 2 * p + q

                low, high = cls(0, p, q), cls(1, p, q)
                minus = kap[low] + half_kappa[high, i, tile(j)]
                plus = kap[high] + half_kappa[low, i + 2, tile(j)]
                outside[low].append(minus)
                outside[high].append(plus)
                outer_x[at, i, tile(j)] = minus
                off[0].append(minus)

                low, high = cls(p, 0, q), cls(p, 1, q)
                side = at_.row_before(lambda r: half_kappa[high, i + 1, tile(r)], j)
                minus = kap[low] + masked(y_low[j], side)
                side = at_.row_after(lambda r: half_kappa[low, i + 1, tile(r)], j)
                plus = kap[high] + masked(y_high[j], side)
                outside[low].append(minus)
                outside[high].append(plus)
                minus, plus = masked(y_low[j], minus), masked(y_high[j], plus)
                outer_y[at, i, tile(j)] = minus
                outer_y[4 + at, i, tile(j)] = plus
                off[1].append(minus)
                off[2].append(plus)

                low, high = cls(p, q, 0), cls(p, q, 1)
                minus = kap[low] + z_low * roll(kap[high], 1, 1)
                plus = kap[high] + z_high * roll(kap[low], -1, 1)
                outside[low].append(minus)
                outside[high].append(plus)
                minus, plus = z_low * minus, z_high * plus
                outer_z[at, i, tile(j)] = minus
                outer_z[4 + at, i, tile(j)] = plus
                off[3].append(minus)
                off[4].append(plus)
            coarse_total = []
            for k in range(8):
                within, without = tree_sum(inside[k]), tree_sum(outside[k])
                inner_sum[k, i, tile(j)] = within
                base = within + without + shift
                diagonal[k, i, tile(j)] = base
                coarse_total.append(without)
                damped[k, i, tile(j)] = DAMPING * inverse(base)
            for at, part in enumerate(off):
                coarse_off[at, i, tile(j)] = tree_sum(part)
            coarse_damped[i, tile(j)] = DAMPING * inverse(tree_sum(coarse_total) + 8.0 * shift)
        return carry

    lax.fori_loop(0, half, plane, 0)
    for j in range(tiles):
        part = []
        for p, q in PAIRS:
            face = half_kappa[cls(0, p, q), half + 1, tile(j)]
            face = face + half_kappa[cls(1, p, q), half, tile(j)]
            outer_x[2 * p + q, half, tile(j)] = face
            part.append(face)
        coarse_off[0, half, tile(j)] = tree_sum(part)


def solve_kernel(
    place_ref,
    weights_ref,
    order_ref,
    mine_ref,
    theirs_ref,
    state_ref,
    far_ref,
    near_ref,
    inner,
    outer_x,
    outer_y,
    outer_z,
    inner_sum,
    diagonal,
    damped,
    coarse_off,
    coarse_damped,
    adjoint_ref,
    keep_ref,
    partner_ref,
    send_ref,
    residual,
    scaled,
    partial,
    first_dir,
    second_dir,
    image,
    coarse_one,
    coarse_two,
    planes,
):
    half, rows = inner.shape[1:3]
    at_ = Layout(rows)
    tile, tiles, zero = at_.tile, at_.tiles, at_.zero
    core = place_ref[0] % 2
    weight = weights_ref[order_ref[core]]

    def begin(k, spot, j, value):
        res = weight * value
        residual[k, spot, tile(j)] = res
        scaled[k, spot + 1, tile(j)] = damped[k, spot, tile(j)] * res

    at_.arrange(mine_ref, theirs_ref, place_ref[0], True, begin)
    at_.seam_fine(scaled)

    def rows_of(field, i):
        cache = {}

        def load(k, j):
            if (k, j) not in cache:
                cache[k, j] = field[k, i + 1, tile(j)]
            return cache[k, j]

        return load

    def stencil(field, load, i, j, both):
        here = [load(k, j) for k in range(8)]
        terms = [[] for _ in range(8)]
        for p, q in PAIRS:
            at = 2 * p + q
            for face_at, low, high in inner_faces(p, q):
                face = inner[face_at, i, tile(j)]
                terms[low].append(face * here[high])
                if both:
                    terms[high].append(face * here[low])
            low, high = cls(0, p, q), cls(1, p, q)
            terms[low].append(outer_x[at, i, tile(j)] * field[high, i, tile(j)])
            if both:
                side = field[low, i + 2, tile(j)]
                terms[high].append(outer_x[at, i + 1, tile(j)] * side)
            low, high = cls(p, 0, q), cls(p, 1, q)
            side = at_.row_before(lambda r: load(high, r), j)
            terms[low].append(outer_y[at, i, tile(j)] * side)
            if both:
                side = at_.row_after(lambda r: load(low, r), j)
                terms[high].append(outer_y[4 + at, i, tile(j)] * side)
            low, high = cls(p, q, 0), cls(p, q, 1)
            terms[low].append(outer_z[at, i, tile(j)] * roll(here[high], 1, 1))
            if both:
                terms[high].append(outer_z[4 + at, i, tile(j)] * roll(here[low], -1, 1))
        return here, [tree_sum(part) if part else None for part in terms]

    def coarse_sides(field, i, j):
        here = field[0, i + 1, tile(j)]
        return here, (
            (field[0, i, tile(j)], field[0, i + 2, tile(j)]),
            (
                at_.row_before(lambda r: field[0, i + 1, tile(r)], j),
                at_.row_after(lambda r: field[0, i + 1, tile(r)], j),
            ),
            (roll(here, 1, 1), roll(here, -1, 1)),
        )

    def precondition(result, other):
        def down(i, carry):
            load = rows_of(scaled, i)
            for j in range(tiles):
                res = [residual[k, i, tile(j)] for k in range(8)]
                _, sums = stencil(scaled, load, i, j, True)
                parts = [(2.0 - DAMPING) * res[k] + sums[k] for k in range(8)]
                for k in range(8):
                    partial[k, i, tile(j)] = parts[k]
                rhs = tree_sum(parts) - tree_sum(res)
                coarse_one[0, i + 1, tile(j)] = coarse_damped[i, tile(j)] * rhs
            return carry

        lax.fori_loop(0, half, down, 0, unroll=UNROLL)
        at_.seam(coarse_one, [0], [0])

        def smooth(i, carry):
            for j in range(tiles):
                here, sides = coarse_sides(coarse_one, i, j)
                total = coarse_off[0, i, tile(j)] * sides[0][0]
                total = total + coarse_off[0, i + 1, tile(j)] * sides[0][1]
                more = coarse_off[1, i, tile(j)] * sides[1][0]
                more = more + coarse_off[2, i, tile(j)] * sides[1][1]
                most = coarse_off[3, i, tile(j)] * sides[2][0]
                most = most + coarse_off[4, i, tile(j)] * sides[2][1]
                coarse_two[0, i + 1, tile(j)] = (2.0 - DAMPING) * here + coarse_damped[
                    i, tile(j)
                ] * (total + more + most)
            return carry

        lax.fori_loop(0, half, smooth, 0, unroll=UNROLL)
        at_.seam(coarse_two, [0], [0])

        def up(i, carry):
            gamma, cross = carry
            for j in range(tiles):
                here, sides = coarse_sides(coarse_two, i, j)
                kept = (1.0 - DAMPING) * here
                dots, crosses = [], []
                for a, b, c in CLASSES:
                    k = cls(a, b, c)
                    value = tree_sum(
                        [
                            partial[k, i, tile(j)],
                            inner_sum[k, i, tile(j)] * here,
                            outer_x[2 * b + c, i + a, tile(j)] * sides[0][a],
                            outer_y[4 * b + 2 * a + c, i, tile(j)] * sides[1][b],
                            outer_z[4 * c + 2 * a + b, i, tile(j)] * sides[2][c],
                        ]
                    )
                    new = kept + damped[k, i, tile(j)] * value
                    result[k, i + 1, tile(j)] = new
                    dots.append(residual[k, i, tile(j)] * new)
                    if other is not None:
                        crosses.append(other[k, i, tile(j)] * new)
                gamma = gamma + tree_sum(dots)
                if other is not None:
                    cross = cross + tree_sum(crosses)
            return gamma, cross

        sums = lax.fori_loop(0, half, up, (zero, zero), unroll=UNROLL)
        at_.seam_fine(result)
        return [grand_total(part) for part in sums]

    gamma, _ = precondition(first_dir, None)

    def apply(i, acc):
        load = rows_of(first_dir, i)
        for j in range(tiles):
            here, sums = stencil(first_dir, load, i, j, True)
            dots = []
            for k in range(8):
                value = diagonal[k, i, tile(j)] * here[k] - sums[k]
                image[k, i, tile(j)] = value
                dots.append(here[k] * value)
            acc = acc + tree_sum(dots)
        return acc

    curve = grand_total(lax.fori_loop(0, half, apply, zero, unroll=UNROLL))
    step_one = gamma / curve

    def update(i, carry):
        for j in range(tiles):
            for k in range(8):
                new = residual[k, i, tile(j)] - step_one * image[k, i, tile(j)]
                residual[k, i, tile(j)] = new
                scaled[k, i + 1, tile(j)] = damped[k, i, tile(j)] * new
        return carry

    lax.fori_loop(0, half, update, 0, unroll=UNROLL)
    at_.seam_fine(scaled)

    gamma_next, cross = precondition(second_dir, image)

    def bend(i, carry):
        own_part, face_part = carry
        load = rows_of(second_dir, i)
        for j in range(tiles):
            here, sums = stencil(second_dir, load, i, j, False)
            own_part = own_part + tree_sum(
                [here[k] * (diagonal[k, i, tile(j)] * here[k]) for k in range(8)]
            )
            face_part = face_part + tree_sum([here[k] * sums[k] for k in range(7)])
        return own_part, face_part

    own_part, face_part = lax.fori_loop(0, half, bend, (zero, zero), unroll=UNROLL)
    ratio = gamma_next / gamma
    curve_next = grand_total(own_part - 2.0 * face_part)
    step_two = gamma_next / (curve_next + ratio * (2.0 * cross + ratio * curve))
    step_first = step_one + step_two * ratio

    own, ny, nz = adjoint_ref.shape
    start = (place_ref[0] - core) * (own // 2)
    upper = jnp.where(start >= half, 1, 0)
    start = start - half * upper
    even = at_.lane % 2 == 0
    source = at_.lane // 2 + HALF * upper
    for at in range(2 * own + 2):
        a = (at + 1) % 2
        spot = start + (at + 1) // 2
        for b in (0, 1):
            for j in range(tiles):
                both = [
                    step_first * first_dir[cls(a, b, c), spot, tile(j)]
                    + step_two * second_dir[cls(a, b, c), spot, tile(j)]
                    for c in (0, 1)
                ]
                planes[at, at_.every(b, j), :] = jnp.where(
                    even,
                    jnp.take_along_axis(both[0], source, axis=1),
                    jnp.take_along_axis(both[1], source, axis=1),
                )

    full = (ny, nz)
    y_at = row_index(full)
    z_at = lane_index(full)

    def drop(value, axis, up):
        moved = roll(value, -1 if up else 1, axis)
        at = (y_at, z_at)[axis]
        edge = full[axis] - 1 if up else 0
        return value - jnp.where(at == edge, 0.0, moved)

    is_even = core == 0
    state = [jnp.where(is_even, far_ref[core, 0], near_ref[own])]
    state += [jnp.where(is_even, state_ref[core, x], near_ref[x]) for x in range(own)]
    state += [jnp.where(is_even, near_ref[x], state_ref[core, x]) for x in range(own)]
    state += [jnp.where(is_even, near_ref[own], far_ref[core, 0])]
    terms = 2 * own + 2
    for x in range(2 * own):
        here, f = planes[x + 1], state[x + 1]
        term = (here - planes[x + 2]) * (f - state[x + 2])
        term = term + (here - planes[x]) * (f - state[x])
        for axis in (0, 1):
            for up in (True, False):
                term = term + drop(here, axis, up) * drop(f, axis, up)
        planes[terms + x] = -0.5 * term

    groups = send_ref.shape[0] + 1
    chunk = keep_ref.shape[1]
    for x in range(own):
        mine, other = core * own + x, (1 - core) * own + x
        adjoint_ref[x] = planes[1 + mine]
        partner_ref[x, :ny] = planes[1 + other]
        for k in range(groups):
            at = pl.multiple_of(lax.rem(place_ref[1] + k, groups) * chunk, chunk)
            for side, plane in enumerate((mine, other)):
                share = planes[terms + plane, pl.ds(at, chunk), :]
                if k:
                    send_ref[k - 1, side, x] = share
                elif side:
                    partner_ref[x, ny:] = share
                else:
                    keep_ref[x] = share


def whole_grid(conductivity, misfit, forward_states, pole_shifts, pole_weights, pole_order):
    members, own, ny, nz = forward_states.shape
    groups = lax.axis_size("pole")
    place = jnp.stack([lax.axis_index("space"), lax.axis_index("pole")]).astype(jnp.int32)
    peers = lax.axis_size("space")
    mine, theirs, states, far, near = gather_blocks(
        place, conductivity, misfit, forward_states, "space"
    )
    half, rows = peers * own // 4, ny // 2

    def field(count, extent):
        return (count, extent, rows, 2 * HALF)

    def held(*shape):
        return pltpu.VMEM(shape, jnp.float32)

    smem = pl.BlockSpec(memory_space=pltpu.SMEM)
    vmem = pl.BlockSpec(memory_space=pltpu.VMEM)
    shapes = [
        field(12, half),
        field(4, half + 1),
        field(8, half),
        field(8, half),
        field(8, half),
        field(8, half),
        field(8, half),
        field(5, half + 1),
        (half, rows, 2 * HALF),
    ]
    coefficients = pl.pallas_call(
        setup_kernel,
        out_shape=[jax.ShapeDtypeStruct(shape, jnp.float32) for shape in shapes],
        in_specs=[smem] * 3 + [vmem] * 2,
        out_specs=[vmem] * len(shapes),
        scratch_shapes=[held(*field(8, half + 2))],
        compiler_params=pltpu.CompilerParams(vmem_limit_bytes=6 * 1024 * 1024),
        name="setup",
    )(place, pole_shifts, pole_order, mine[0], theirs[0])
    chunk = ny // groups
    adjoint, gradient, partner, send = pl.pallas_call(
        solve_kernel,
        out_shape=[
            jax.ShapeDtypeStruct((own, ny, nz), jnp.float32),
            jax.ShapeDtypeStruct((own, chunk, nz), jnp.float32),
            jax.ShapeDtypeStruct((own, ny + chunk, nz), jnp.float32),
            jax.ShapeDtypeStruct((groups - 1, 2, own, chunk, nz), jnp.float32),
        ],
        in_specs=[smem] * 3 + [vmem] * (5 + len(shapes)),
        out_specs=[vmem] * 4,
        scratch_shapes=[
            held(*field(8, half)),
            held(*field(8, half + 2)),
            held(*field(8, half)),
            held(*field(8, half + 2)),
            held(*field(8, half + 2)),
            held(*field(8, half)),
            held(*field(1, half + 2)),
            held(*field(1, half + 2)),
            held(4 * own + 2, ny, nz),
        ],
        compiler_params=pltpu.CompilerParams(vmem_limit_bytes=12 * 1024 * 1024),
        name="solve",
    )(
        place,
        pole_weights,
        pole_order,
        mine[1],
        theirs[1],
        states,
        far,
        near,
        *coefficients,
    )

    arrived = lax.ppermute(partner, "space", [(i, i ^ 1) for i in range(peers)])
    shares = []
    for k in range(1, groups):
        for side in (0, 1):
            pairs = [
                (i * peers + j, (i + k) % groups * peers + (j ^ side))
                for i in range(groups)
                for j in range(peers)
            ]
            shares.append(lax.ppermute(send[k - 1, side], ("pole", "space"), pairs))
    even = place[0] % 2 == 0
    theirs = arrived[:, :ny]
    adjoint_states = jnp.stack(
        [jnp.where(even, adjoint, theirs), jnp.where(even, theirs, adjoint)]
    )
    adjoint_states, arrived = lax.optimization_barrier((adjoint_states, arrived))
    return adjoint_states, gradient + arrived[:, ny:] + sum(shares)


def plus_side(field, which_dim):
    extent = field.shape[which_dim]
    inner_part = lax.slice_in_dim(field, 1, extent, axis=which_dim)
    zero_plane = jnp.zeros_like(lax.slice_in_dim(field, 0, 1, axis=which_dim))
    return jnp.concatenate([inner_part, zero_plane], axis=which_dim)


def minus_side(field, which_dim):
    extent = field.shape[which_dim]
    inner_part = lax.slice_in_dim(field, 0, extent - 1, axis=which_dim)
    zero_plane = jnp.zeros_like(lax.slice_in_dim(field, 0, 1, axis=which_dim))
    return jnp.concatenate([zero_plane, inner_part], axis=which_dim)


def coarse_pick(faces, which_dim, offset):
    extent_x, extent_y, extent_z = faces.shape
    blocks = faces.reshape(extent_x // 2, 2, extent_y // 2, 2, extent_z // 2, 2)
    chosen = lax.index_in_dim(blocks, offset, axis=2 * which_dim + 1, keepdims=True)
    return jnp.sum(chosen, axis=(1, 3, 5))


def side_terms(field, plus_faces, minus_faces, widened):
    result = plus_faces[0] * (field - widened[:, 2:]) + minus_faces[0] * (field - widened[:, :-2])
    for which_dim in (1, 2):
        result = result + plus_faces[which_dim] * (field - plus_side(field, which_dim + 1))
        result = result + minus_faces[which_dim] * (field - minus_side(field, which_dim + 1))
    return result


def fine_image(field, plus_faces, minus_faces, shift_value):
    widened = extended(field, (("space", 1),), 1)
    return shift_value * field + side_terms(field, plus_faces, minus_faces, widened)


def coarse_image(field, plus_faces, minus_faces, shift_value):
    widened = extended(field, (("space", 1),), 1)
    return shift_value * field + side_terms(field, plus_faces, minus_faces, widened)


def restrict(field):
    members, extent_x, extent_y, extent_z = field.shape
    shaped = field.reshape(members, extent_x // 2, 2, extent_y // 2, 2, extent_z // 2, 2)
    return jnp.sum(shaped, axis=(2, 4, 6))


def prolong(field):
    return jnp.repeat(jnp.repeat(jnp.repeat(field, 2, axis=1), 2, axis=2), 2, axis=3)


def precondition(residual, fine, coarse):
    plus_faces, minus_faces, shift_value, diagonal = fine
    coarse_plus, coarse_minus, coarse_shift, coarse_diagonal = coarse
    smooth_one = DAMPING * residual / diagonal
    coarse_rhs = restrict(residual - fine_image(smooth_one, plus_faces, minus_faces, shift_value))
    coarse_one = DAMPING * coarse_rhs / coarse_diagonal
    coarse_two = (
        coarse_one
        + DAMPING
        * (coarse_rhs - coarse_image(coarse_one, coarse_plus, coarse_minus, coarse_shift))
        / coarse_diagonal
    )
    corrected = smooth_one + prolong(coarse_two)
    return (
        corrected
        + DAMPING
        * (residual - fine_image(corrected, plus_faces, minus_faces, shift_value))
        / diagonal
    )


def expand(values):
    return values.reshape(-1, 1, 1, 1)


def cell_sums(values):
    return jnp.sum(values, axis=(1, 2, 3))


def norm_sum(residual, precond):
    return lax.psum(cell_sums(residual * precond), "space")


def solve(rhs, fine, coarse):
    plus_faces, minus_faces, shift_value, diagonal = fine
    iterate = jnp.zeros_like(rhs)
    residual = rhs
    precond = precondition(residual, fine, coarse)
    gamma_now = norm_sum(residual, precond)
    search = precond
    for turn_index in range(ITERS):
        image_field = fine_image(search, plus_faces, minus_faces, shift_value)
        curve = lax.psum(cell_sums(search * image_field), "space")
        step_length = gamma_now / curve
        iterate = iterate + expand(step_length) * search
        if turn_index + 1 < ITERS:
            residual = residual - expand(step_length) * image_field
            precond = precondition(residual, fine, coarse)
            gamma_next = norm_sum(residual, precond)
            search = precond + expand(gamma_next / gamma_now) * search
            gamma_now = gamma_next
    return iterate


def divided(conductivity, misfit, forward_states, pole_shifts, pole_weights, pole_order):
    widened_kappa = extended(conductivity, (("space", 0),), 1)
    plus_faces = [
        0.5 * (conductivity + widened_kappa[2:]),
        0.5 * (conductivity + plus_side(conductivity, 1)),
        0.5 * (conductivity + plus_side(conductivity, 2)),
    ]
    minus_faces = [
        0.5 * (conductivity + widened_kappa[:-2]),
        0.5 * (conductivity + minus_side(conductivity, 1)),
        0.5 * (conductivity + minus_side(conductivity, 2)),
    ]
    base_diagonal = (
        plus_faces[0]
        + plus_faces[1]
        + plus_faces[2]
        + minus_faces[0]
        + minus_faces[1]
        + minus_faces[2]
    )
    coarse_plus = [coarse_pick(plus_faces[which_dim], which_dim, 1) for which_dim in range(3)]
    coarse_minus = [coarse_pick(minus_faces[which_dim], which_dim, 0) for which_dim in range(3)]
    coarse_base = (
        coarse_plus[0]
        + coarse_plus[1]
        + coarse_plus[2]
        + coarse_minus[0]
        + coarse_minus[1]
        + coarse_minus[2]
    )
    pole_index = jnp.arange(pole_shifts.shape[0], dtype=jnp.int32)
    matches = pole_order[:, None] == pole_index[None, :]
    shift_local = jnp.sum(jnp.where(matches, pole_shifts[None, :], 0.0), axis=1)
    weight_local = jnp.sum(jnp.where(matches, pole_weights[None, :], 0.0), axis=1)
    members = forward_states.shape[0]

    def solve_group(shift_part, weight_part):
        shift_value = expand(shift_part)
        fine = (plus_faces, minus_faces, shift_value, base_diagonal[None] + shift_value)
        coarse = (
            coarse_plus,
            coarse_minus,
            8.0 * shift_value,
            coarse_base[None] + 8.0 * shift_value,
        )
        return solve(expand(weight_part) * misfit[None], fine, coarse)

    adjoint_states = jnp.concatenate(
        [
            solve_group(shift_local[member : member + 1], weight_local[member : member + 1])
            for member in range(members)
        ],
        axis=0,
    )
    widened = extended(jnp.stack([adjoint_states, forward_states]), (("space", 2),), 1)
    term = (adjoint_states - widened[0, :, 2:]) * (forward_states - widened[1, :, 2:])
    term = term + (adjoint_states - widened[0, :, :-2]) * (forward_states - widened[1, :, :-2])
    for which_dim in (2, 3):
        term = term + (adjoint_states - plus_side(adjoint_states, which_dim)) * (
            forward_states - plus_side(forward_states, which_dim)
        )
        term = term + (adjoint_states - minus_side(adjoint_states, which_dim)) * (
            forward_states - minus_side(forward_states, which_dim)
        )
    local_term = -0.5 * jnp.sum(term, axis=0)
    gradient = lax.psum_scatter(local_term, "pole", scatter_dimension=1, tiled=True)
    return (adjoint_states, gradient)


def solution(mesh):
    in_specs = (
        P("space", None, None),
        P("space", None, None),
        P("pole", "space", None, None),
        P(),
        P(),
        P("pole"),
    )
    out_specs = (P("pole", "space", None, None), P("space", "pole", None))

    def body(conductivity, misfit, forward_states, *poles):
        nx = conductivity.shape[0] * lax.axis_size("space")
        _, ny, nz = conductivity.shape
        peers = lax.axis_size("space")
        small = nx * ny * nz <= REPLICATED_CELLS and forward_states.shape[:2] == (2, 2)
        if small and nz == 2 * HALF and peers > 2 and peers & (peers - 1) == 0:
            return whole_grid(conductivity, misfit, forward_states, *poles)
        return divided(conductivity, misfit, forward_states, *poles)

    return jax.shard_map(
        body, mesh=mesh, in_specs=in_specs, out_specs=out_specs, check_vma=False
    )
```

```python
import functools

import jax
import jax.numpy as jnp
from jax import lax
from jax.experimental import pallas as pl
from jax.experimental.pallas import tpu as pltpu
from jax.sharding import PartitionSpec as P

ITERS = 2
DAMPING = 0.8
REPLICATED_CELLS = 32 * 64 * 128
HALF = 64
TILE = 8
UNROLL = 2


def extended(array, sides, width):
    for axis, dim in sides:
        peers, length = (lax.axis_size(axis), array.shape[dim])
        up = [(i, (i + 1) % peers) for i in range(peers - 1)]
        down = [(j, i) for i, j in up]
        last = lax.slice_in_dim(array, length - width, length, axis=dim)
        leading = lax.slice_in_dim(array, 0, width, axis=dim)
        before = lax.ppermute(last, axis, up)
        after = lax.ppermute(leading, axis, down)
        array = jnp.concatenate([before, array, after], axis=dim)
    return array


def lane_index(shape):
    return lax.broadcasted_iota(jnp.int32, shape, len(shape) - 1)


def row_index(shape):
    return lax.broadcasted_iota(jnp.int32, shape, len(shape) - 2)


def roll(block, shift, axis):
    return pltpu.roll(block, shift % block.shape[axis], axis)


def inverse(value):
    guess = pl.reciprocal(value, approx=True)
    return guess * (2.0 - value * guess)


def tree_sum(values):
    while len(values) > 1:
        values = [sum(values[at : at + 2]) for at in range(0, len(values), 2)]
    return values[0]


def grand_total(acc):
    line = jnp.sum(acc, axis=0, keepdims=True)
    return jnp.broadcast_to(jnp.sum(line, axis=1, keepdims=True), acc.shape)


def swap_masks(peers, flip):
    falling = []
    mask = peers // 2
    while mask > 1:
        falling.append(mask)
        mask //= 2
    if flip:
        return falling[::-1], falling[:1] + falling[:0:-1]
    return falling, falling[-1:] + falling[:-1]


def block_pair(u, holder, peers, flip):
    even, odd = swap_masks(peers, flip)
    parity = holder % 2
    top = jnp.where(parity == 0, even.index(peers // 2), odd.index(peers // 2))
    below = u & ((1 << top) - 1)
    base = ((u >> top) << (top + 1)) | below
    upper = jnp.where(holder >= peers // 2, 1, 0)
    first = base | (upper << top)
    second = base | ((1 - upper) << top)
    home = holder
    for step, (mask_even, mask_odd) in enumerate(zip(even, odd)):
        mask = jnp.where(parity == 0, mask_even, mask_odd)
        home = home ^ (((first >> step) & 1) * mask)
    return first, second, home


def prepare_kernel(kappa_ref, misfit_ref, kappa_out, misfit_out):
    kappa_out[...] = kappa_ref[...]
    misfit_out[...] = misfit_ref[...]


def join_kernel(place_ref, *refs, masks, peers):
    place = place_ref[0]
    at_ = Layout(refs[0].shape[1] // 2)
    for at, (even, odd) in enumerate(masks):
        partner = place ^ jnp.where(place % 2 == 0, even, odd)
        for t, (ref, holder) in enumerate(((refs[at], place), (refs[2 + at], partner))):
            at_.deal(ref, refs[4 + at].at[t], jnp.where(holder >= peers // 2, 1, 0))


def gather_blocks(place, blocks, states, axis):
    peers = lax.axis_size(axis)
    even = place[0] % 2 == 0
    swap = [(i, i ^ 1) for i in range(peers)]
    over = [(i, i + 1 if i % 2 else i - 1) for i in range(1, peers - 1)]
    smem = pl.BlockSpec(memory_space=pltpu.SMEM)
    vmem = pl.BlockSpec(memory_space=pltpu.VMEM)
    swaps = [list(zip(*swap_masks(peers, flip))) for flip in (False, True)]
    own = pl.pallas_call(
        prepare_kernel,
        out_shape=[jax.ShapeDtypeStruct(block.shape, jnp.float32) for block in blocks],
        in_specs=[vmem] * 2,
        out_specs=[vmem] * 2,
        compiler_params=pltpu.CompilerParams(vmem_limit_bytes=1024 * 1024),
        name="prepare",
    )(*blocks)
    held = list(blocks)
    for step in range(len(swaps[0])):
        arrived = []
        for at in (0, 1):
            masks = swaps[at][step]
            pairs = [(i, i ^ masks[i % 2]) for i in range(peers)]
            arrived.append(lax.ppermute(held[at], axis, pairs))
        if step:
            held = [jnp.concatenate(pair, axis=0) for pair in zip(held, arrived)]
            continue
        masks = [swaps[at][0] for at in (0, 1)]
        shape = jax.ShapeDtypeStruct((2, *blocks[0].shape), jnp.float32)
        held[:] = pl.pallas_call(
            functools.partial(join_kernel, masks=masks, peers=peers),
            out_shape=[shape] * 2,
            in_specs=[smem] + [vmem] * 4,
            out_specs=[vmem] * 2,
            compiler_params=pltpu.CompilerParams(vmem_limit_bytes=1024 * 1024),
            name="join",
        )(place, *own, *arrived)
        held[1], states = lax.optimization_barrier((held[1], states))
        far = lax.ppermute(jnp.where(even, states[:, :1], states[:, -1:]), axis, over)
    held[1], far = lax.optimization_barrier((held[1], far))
    given = jnp.concatenate([states, far], axis=1)
    near = lax.ppermute(jnp.where(even, given[1], given[0]), axis, swap)
    other = [lax.ppermute(part, axis, swap) for part in held]
    return held, other, far, near


CLASSES = [(a, b, c) for a in (0, 1) for b in (0, 1) for c in (0, 1)]
PAIRS = [(p, q) for p in (0, 1) for q in (0, 1)]


def cls(a, b, c):
    return 4 * a + 2 * b + c


def inner_faces(p, q):
    return (
        (2 * p + q, cls(0, p, q), cls(1, p, q)),
        (4 + 2 * p + q, cls(p, 0, q), cls(p, 1, q)),
        (8 + 2 * p + q, cls(p, q, 0), cls(p, q, 1)),
    )


class Layout:
    def __init__(self, rows):
        self.tiles = rows // TILE
        self.lane = lane_index((TILE, 2 * HALF))
        self.row = row_index((TILE, 2 * HALF))
        self.left = self.lane < HALF
        self.zero = jnp.zeros((TILE, 2 * HALF), jnp.float32)

    def tile(self, j):
        return pl.ds(TILE * j, TILE)

    def every(self, b, j):
        return pl.ds(b + 2 * j, TILE, stride=2 * self.tiles)

    def row_before(self, load, j):
        return load(j - 1) if j else roll(load(self.tiles - 1), 1, 0)

    def row_after(self, load, j):
        return load(j + 1) if j + 1 < self.tiles else roll(load(0), -1, 0)

    def seam(self, ref, low, high):
        last = ref.shape[1] - 1
        for j in range(self.tiles):
            for k in low:
                moved = roll(ref[k, last - 1, self.tile(j)], HALF, 1)
                ref[k, 0, self.tile(j)] = jnp.where(self.left, 0.0, moved)
            for k in high:
                moved = roll(ref[k, 1, self.tile(j)], HALF, 1)
                ref[k, last, self.tile(j)] = jnp.where(self.left, moved, 0.0)

    def seam_fine(self, ref):
        count = ref.shape[0]
        self.seam(
            ref,
            [k for k in range(count) if k % 8 >= 4],
            [k for k in range(count) if k % 8 < 4],
        )

    def dealt(self, b, j):
        return pl.ds(TILE * (self.tiles * b + j), TILE)

    def deal(self, block_ref, out_ref, upper):
        odd = jnp.where(self.left, upper, 1 - upper)
        column = 2 * (self.lane % HALF) + odd
        for x in range(block_ref.shape[0]):
            for b in (0, 1):
                for j in range(self.tiles):
                    rows = block_ref[x, self.every(b, j), :]
                    out_ref[x, self.dealt(b, j), :] = jnp.take_along_axis(rows, column, axis=1)

    def arrange(self, mine_ref, theirs_ref, place, flip, store):
        blocks, own = mine_ref.shape[:2]

        def pair(u, carry):
            for ref, holder in ((mine_ref, place), (theirs_ref, place ^ 1)):
                first, second, home = block_pair(u, holder, 2 * blocks, flip)
                for x in range(own):
                    spot = home * (own // 2) + x // 2
                    for b in (0, 1):
                        for j in range(self.tiles):
                            one = ref[first, x, self.dealt(b, j), :]
                            two = ref[second, x, self.dealt(b, j), :]
                            store(cls(x % 2, b, 0), spot, j, jnp.where(self.left, one, two))
                            odd = roll(jnp.where(self.left, two, one), HALF, 1)
                            store(cls(x % 2, b, 1), spot, j, odd)
            return carry

        lax.fori_loop(0, blocks // 2, pair, 0)


def setup_kernel(
    place_ref,
    shifts_ref,
    order_ref,
    mine_ref,
    theirs_ref,
    inner,
    outer_x,
    outer_y,
    outer_z,
    inner_sum,
    diagonal,
    damped,
    coarse_off,
    coarse_damped,
    half_kappa,
):
    half = inner.shape[1]
    at_ = Layout(inner.shape[2])
    tile, tiles = at_.tile, at_.tiles
    shift = shifts_ref[order_ref[place_ref[0] % 2]]

    def keep(k, spot, j, value):
        half_kappa[k, spot + 1, tile(j)] = 0.5 * value

    at_.arrange(mine_ref, theirs_ref, place_ref[0], False, keep)
    at_.seam_fine(half_kappa)

    z_low = jnp.where(at_.lane % HALF > 0, 1.0, 0.0)
    z_high = jnp.where(at_.lane % HALF < HALF - 1, 1.0, 0.0)
    y_low = [jnp.where(at_.row > 0, 1.0, 0.0)] + [None] * (tiles - 1)
    y_high = [None] * (tiles - 1) + [jnp.where(at_.row < TILE - 1, 1.0, 0.0)]

    def masked(mask, value):
        return value if mask is None else mask * value

    def plane(i, carry):
        for j in range(tiles):
            kap = [half_kappa[k, i + 1, tile(j)] for k in range(8)]
            inside = [[] for _ in range(8)]
            outside = [[] for _ in range(8)]
            off = [[] for _ in range(5)]
            for p, q in PAIRS:
                for face_at, low, high in inner_faces(p, q):
                    face = kap[low] + kap[high]
                    inner[face_at, i, tile(j)] = face
                    inside[low].append(face)
                    inside[high].append(face)
                at = 2 * p + q

                low, high = cls(0, p, q), cls(1, p, q)
                minus = kap[low] + half_kappa[high, i, tile(j)]
                plus = kap[high] + half_kappa[low, i + 2, tile(j)]
                outside[low].append(minus)
                outside[high].append(plus)
                outer_x[at, i, tile(j)] = minus
                off[0].append(minus)

                low, high = cls(p, 0, q), cls(p, 1, q)
                side = at_.row_before(lambda r: half_kappa[high, i + 1, tile(r)], j)
                minus = kap[low] + masked(y_low[j], side)
                side = at_.row_after(lambda r: half_kappa[low, i + 1, tile(r)], j)
                plus = kap[high] + masked(y_high[j], side)
                outside[low].append(minus)
                outside[high].append(plus)
                minus, plus = masked(y_low[j], minus), masked(y_high[j], plus)
                outer_y[at, i, tile(j)] = minus
                off[1].append(minus)
                off[2].append(plus)

                low, high = cls(p, q, 0), cls(p, q, 1)
                minus = kap[low] + z_low * roll(kap[high], 1, 1)
                plus = kap[high] + z_high * roll(kap[low], -1, 1)
                outside[low].append(minus)
                outside[high].append(plus)
                minus, plus = z_low * minus, z_high * plus
                outer_z[at, i, tile(j)] = minus
                outer_z[4 + at, i, tile(j)] = plus
                off[3].append(minus)
                off[4].append(plus)
            coarse_total = []
            for k in range(8):
                within, without = tree_sum(inside[k]), tree_sum(outside[k])
                inner_sum[k, i, tile(j)] = within
                base = within + without + shift
                diagonal[k, i, tile(j)] = base
                coarse_total.append(without)
                damped[k, i, tile(j)] = DAMPING * inverse(base)
            for at, part in enumerate(off):
                coarse_off[at, i, tile(j)] = tree_sum(part)
            coarse_damped[i, tile(j)] = DAMPING * inverse(tree_sum(coarse_total) + 8.0 * shift)
        return carry

    lax.fori_loop(0, half, plane, 0)
    for j in range(tiles):
        part = []
        for p, q in PAIRS:
            face = half_kappa[cls(0, p, q), half + 1, tile(j)]
            face = face + half_kappa[cls(1, p, q), half, tile(j)]
            outer_x[2 * p + q, half, tile(j)] = face
            part.append(face)
        coarse_off[0, half, tile(j)] = tree_sum(part)


def solve_kernel(
    place_ref,
    weights_ref,
    order_ref,
    mine_ref,
    theirs_ref,
    state_ref,
    far_ref,
    near_ref,
    inner,
    outer_x,
    outer_y,
    outer_z,
    inner_sum,
    diagonal,
    damped,
    coarse_off,
    coarse_damped,
    adjoint_ref,
    keep_ref,
    partner_ref,
    send_ref,
    residual,
    scaled,
    partial,
    first_dir,
    second_dir,
    image,
    coarse_one,
    coarse_two,
    planes,
):
    half, rows = inner.shape[1:3]
    at_ = Layout(rows)
    tile, tiles, zero = at_.tile, at_.tiles, at_.zero
    core = place_ref[0] % 2
    weight = weights_ref[order_ref[core]]

    def begin(k, spot, j, value):
        res = weight * value
        residual[k, spot, tile(j)] = res
        scaled[k, spot + 1, tile(j)] = damped[k, spot, tile(j)] * res

    at_.arrange(mine_ref, theirs_ref, place_ref[0], True, begin)
    at_.seam_fine(scaled)

    def rows_of(ref, i):
        cache = {}

        def load(k, j, step):
            if abs(j - step) > 1:
                return ref[k, i, tile(j)]
            if (k, j) not in cache:
                cache[k, j] = ref[k, i, tile(j)]
            return cache[k, j]

        def get(k, j):
            return load(k, j, j)

        def before(k, j):
            return at_.row_before(lambda r: load(k, r, j), j)

        def after(k, j):
            return at_.row_after(lambda r: load(k, r, j), j)

        return get, before, after

    def stencil(field, i, both):
        get, before, after = rows_of(field, i + 1)
        face_get, _, face_after = rows_of(outer_y, i)
        for j in range(tiles):
            here = [get(k, j) for k in range(8)]
            terms = [[] for _ in range(8)]
            for p, q in PAIRS:
                at = 2 * p + q
                for face_at, low, high in inner_faces(p, q):
                    face = inner[face_at, i, tile(j)]
                    terms[low].append(face * here[high])
                    if both:
                        terms[high].append(face * here[low])
                low, high = cls(0, p, q), cls(1, p, q)
                terms[low].append(outer_x[at, i, tile(j)] * field[high, i, tile(j)])
                if both:
                    side = field[low, i + 2, tile(j)]
                    terms[high].append(outer_x[at, i + 1, tile(j)] * side)
                low, high = cls(p, 0, q), cls(p, 1, q)
                terms[low].append(face_get(at, j) * before(high, j))
                if both:
                    terms[high].append(face_after(at, j) * after(low, j))
                low, high = cls(p, q, 0), cls(p, q, 1)
                terms[low].append(outer_z[at, i, tile(j)] * roll(here[high], 1, 1))
                if both:
                    terms[high].append(outer_z[4 + at, i, tile(j)] * roll(here[low], -1, 1))
            yield j, here, [tree_sum(part) if part else None for part in terms]

    def coarse_sides(field, i, j):
        here = field[0, i + 1, tile(j)]
        return here, (
            (field[0, i, tile(j)], field[0, i + 2, tile(j)]),
            (
                at_.row_before(lambda r: field[0, i + 1, tile(r)], j),
                at_.row_after(lambda r: field[0, i + 1, tile(r)], j),
            ),
            (roll(here, 1, 1), roll(here, -1, 1)),
        )

    def precondition(result, other):
        def down(i, carry):
            for j, _, sums in stencil(scaled, i, True):
                res = [residual[k, i, tile(j)] for k in range(8)]
                parts = [(2.0 - DAMPING) * res[k] + sums[k] for k in range(8)]
                for k in range(8):
                    partial[k, i, tile(j)] = parts[k]
                rhs = tree_sum(parts) - tree_sum(res)
                coarse_one[0, i + 1, tile(j)] = coarse_damped[i, tile(j)] * rhs
            return carry

        lax.fori_loop(0, half, down, 0, unroll=UNROLL)
        at_.seam(coarse_one, [0], [0])

        def smooth(i, carry):
            for j in range(tiles):
                here, sides = coarse_sides(coarse_one, i, j)
                total = coarse_off[0, i, tile(j)] * sides[0][0]
                total = total + coarse_off[0, i + 1, tile(j)] * sides[0][1]
                more = coarse_off[1, i, tile(j)] * sides[1][0]
                more = more + coarse_off[2, i, tile(j)] * sides[1][1]
                most = coarse_off[3, i, tile(j)] * sides[2][0]
                most = most + coarse_off[4, i, tile(j)] * sides[2][1]
                coarse_two[0, i + 1, tile(j)] = (2.0 - DAMPING) * here + coarse_damped[
                    i, tile(j)
                ] * (total + more + most)
            return carry

        lax.fori_loop(0, half, smooth, 0, unroll=UNROLL)
        at_.seam(coarse_two, [0], [0])

        def up(i, carry):
            gamma, cross = carry
            face_get, _, face_after = rows_of(outer_y, i)
            for j in range(tiles):
                here, sides = coarse_sides(coarse_two, i, j)
                kept = (1.0 - DAMPING) * here
                dots, crosses = [], []
                for a, b, c in CLASSES:
                    k = cls(a, b, c)
                    value = tree_sum(
                        [
                            partial[k, i, tile(j)],
                            inner_sum[k, i, tile(j)] * here,
                            outer_x[2 * b + c, i + a, tile(j)] * sides[0][a],
                            (face_after if b else face_get)(2 * a + c, j) * sides[1][b],
                            outer_z[4 * c + 2 * a + b, i, tile(j)] * sides[2][c],
                        ]
                    )
                    new = kept + damped[k, i, tile(j)] * value
                    result[k, i + 1, tile(j)] = new
                    dots.append(residual[k, i, tile(j)] * new)
                    if other is not None:
                        crosses.append(other[k, i, tile(j)] * new)
                gamma = gamma + tree_sum(dots)
                if other is not None:
                    cross = cross + tree_sum(crosses)
            return gamma, cross

        sums = lax.fori_loop(0, half, up, (zero, zero), unroll=UNROLL)
        at_.seam_fine(result)
        return [grand_total(part) for part in sums]

    gamma, _ = precondition(first_dir, None)

    def apply(i, acc):
        for j, here, sums in stencil(first_dir, i, True):
            dots = []
            for k in range(8):
                value = diagonal[k, i, tile(j)] * here[k] - sums[k]
                image[k, i, tile(j)] = value
                dots.append(here[k] * value)
            acc = acc + tree_sum(dots)
        return acc

    curve = grand_total(lax.fori_loop(0, half, apply, zero, unroll=UNROLL))
    step_one = gamma / curve

    def update(i, carry):
        for j in range(tiles):
            for k in range(8):
                new = residual[k, i, tile(j)] - step_one * image[k, i, tile(j)]
                residual[k, i, tile(j)] = new
                scaled[k, i + 1, tile(j)] = damped[k, i, tile(j)] * new
        return carry

    lax.fori_loop(0, half, update, 0, unroll=UNROLL)
    at_.seam_fine(scaled)

    gamma_next, cross = precondition(second_dir, image)

    def bend(i, carry):
        own_part, face_part = carry
        for j, here, sums in stencil(second_dir, i, False):
            own_part = own_part + tree_sum(
                [here[k] * (diagonal[k, i, tile(j)] * here[k]) for k in range(8)]
            )
            face_part = face_part + tree_sum([here[k] * sums[k] for k in range(7)])
        return own_part, face_part

    own_part, face_part = lax.fori_loop(0, half, bend, (zero, zero), unroll=UNROLL)
    ratio = gamma_next / gamma
    curve_next = grand_total(own_part - 2.0 * face_part)
    step_two = gamma_next / (curve_next + ratio * (2.0 * cross + ratio * curve))
    step_first = step_one + step_two * ratio

    own, ny, nz = adjoint_ref.shape
    start = (place_ref[0] - core) * (own // 2)
    upper = jnp.where(start >= half, 1, 0)
    start = start - half * upper
    even = at_.lane % 2 == 0
    source = at_.lane // 2 + HALF * upper
    for at in range(2 * own + 2):
        a = (at + 1) % 2
        spot = start + (at + 1) // 2
        for b in (0, 1):
            for j in range(tiles):
                both = [
                    step_first * first_dir[cls(a, b, c), spot, tile(j)]
                    + step_two * second_dir[cls(a, b, c), spot, tile(j)]
                    for c in (0, 1)
                ]
                planes[at, at_.every(b, j), :] = jnp.where(
                    even,
                    jnp.take_along_axis(both[0], source, axis=1),
                    jnp.take_along_axis(both[1], source, axis=1),
                )

    full = (ny, nz)
    y_at = row_index(full)
    z_at = lane_index(full)

    def drop(value, axis, up):
        moved = roll(value, -1 if up else 1, axis)
        at = (y_at, z_at)[axis]
        edge = full[axis] - 1 if up else 0
        return value - jnp.where(at == edge, 0.0, moved)

    is_even = core == 0
    state = [jnp.where(is_even, far_ref[core, 0], near_ref[own])]
    state += [jnp.where(is_even, state_ref[core, x], near_ref[x]) for x in range(own)]
    state += [jnp.where(is_even, near_ref[x], state_ref[core, x]) for x in range(own)]
    state += [jnp.where(is_even, near_ref[own], far_ref[core, 0])]
    terms = 2 * own + 2
    for x in range(2 * own):
        here, f = planes[x + 1], state[x + 1]
        term = (here - planes[x + 2]) * (f - state[x + 2])
        term = term + (here - planes[x]) * (f - state[x])
        for axis in (0, 1):
            for up in (True, False):
                term = term + drop(here, axis, up) * drop(f, axis, up)
        planes[terms + x] = -0.5 * term

    groups = send_ref.shape[0] + 1
    chunk = keep_ref.shape[1]
    for x in range(own):
        mine, other = core * own + x, (1 - core) * own + x
        adjoint_ref[x] = planes[1 + mine]
        partner_ref[x, :ny] = planes[1 + other]
        for k in range(groups):
            at = pl.multiple_of(lax.rem(place_ref[1] + k, groups) * chunk, chunk)
            for side, plane in enumerate((mine, other)):
                share = planes[terms + plane, pl.ds(at, chunk), :]
                if k:
                    send_ref[k - 1, side, x] = share
                elif side:
                    partner_ref[x, ny:] = share
                else:
                    keep_ref[x] = share


def whole_grid(conductivity, misfit, forward_states, pole_shifts, pole_weights, pole_order):
    members, own, ny, nz = forward_states.shape
    groups = lax.axis_size("pole")
    place = jnp.stack([lax.axis_index("space"), lax.axis_index("pole")]).astype(jnp.int32)
    peers = lax.axis_size("space")
    mine, theirs, far, near = gather_blocks(
        place, [conductivity, misfit], forward_states, "space"
    )
    half, rows = peers * own // 4, ny // 2

    def field(count, extent):
        return (count, extent, rows, 2 * HALF)

    def held(*shape):
        return pltpu.VMEM(shape, jnp.float32)

    smem = pl.BlockSpec(memory_space=pltpu.SMEM)
    vmem = pl.BlockSpec(memory_space=pltpu.VMEM)
    shapes = [
        field(12, half),
        field(4, half + 1),
        field(4, half),
        field(8, half),
        field(8, half),
        field(8, half),
        field(8, half),
        field(5, half + 1),
        (half, rows, 2 * HALF),
    ]
    coefficients = pl.pallas_call(
        setup_kernel,
        out_shape=[jax.ShapeDtypeStruct(shape, jnp.float32) for shape in shapes],
        in_specs=[smem] * 3 + [vmem] * 2,
        out_specs=[vmem] * len(shapes),
        scratch_shapes=[held(*field(8, half + 2))],
        compiler_params=pltpu.CompilerParams(vmem_limit_bytes=6 * 1024 * 1024),
        name="setup",
    )(place, pole_shifts, pole_order, mine[0], theirs[0])
    chunk = ny // groups
    adjoint, gradient, partner, send = pl.pallas_call(
        solve_kernel,
        out_shape=[
            jax.ShapeDtypeStruct((own, ny, nz), jnp.float32),
            jax.ShapeDtypeStruct((own, chunk, nz), jnp.float32),
            jax.ShapeDtypeStruct((own, ny + chunk, nz), jnp.float32),
            jax.ShapeDtypeStruct((groups - 1, 2, own, chunk, nz), jnp.float32),
        ],
        in_specs=[smem] * 3 + [vmem] * (5 + len(shapes)),
        out_specs=[vmem] * 4,
        scratch_shapes=[
            held(*field(8, half)),
            held(*field(8, half + 2)),
            held(*field(8, half)),
            held(*field(8, half + 2)),
            held(*field(8, half + 2)),
            held(*field(8, half)),
            held(*field(1, half + 2)),
            held(*field(1, half + 2)),
            held(4 * own + 2, ny, nz),
        ],
        compiler_params=pltpu.CompilerParams(vmem_limit_bytes=12 * 1024 * 1024),
        name="solve",
    )(
        place,
        pole_weights,
        pole_order,
        mine[1],
        theirs[1],
        forward_states,
        far,
        near,
        *coefficients,
    )

    arrived = lax.ppermute(partner, "space", [(i, i ^ 1) for i in range(peers)])
    shares = []
    for k in range(1, groups):
        for side in (0, 1):
            pairs = [
                (i * peers + j, (i + k) % groups * peers + (j ^ side))
                for i in range(groups)
                for j in range(peers)
            ]
            shares.append(lax.ppermute(send[k - 1, side], ("pole", "space"), pairs))
    even = place[0] % 2 == 0
    theirs = arrived[:, :ny]
    adjoint_states = jnp.stack(
        [jnp.where(even, adjoint, theirs), jnp.where(even, theirs, adjoint)]
    )
    adjoint_states, arrived = lax.optimization_barrier((adjoint_states, arrived))
    return adjoint_states, gradient + arrived[:, ny:] + sum(shares)


def plus_side(field, which_dim):
    extent = field.shape[which_dim]
    inner_part = lax.slice_in_dim(field, 1, extent, axis=which_dim)
    zero_plane = jnp.zeros_like(lax.slice_in_dim(field, 0, 1, axis=which_dim))
    return jnp.concatenate([inner_part, zero_plane], axis=which_dim)


def minus_side(field, which_dim):
    extent = field.shape[which_dim]
    inner_part = lax.slice_in_dim(field, 0, extent - 1, axis=which_dim)
    zero_plane = jnp.zeros_like(lax.slice_in_dim(field, 0, 1, axis=which_dim))
    return jnp.concatenate([zero_plane, inner_part], axis=which_dim)


def coarse_pick(faces, which_dim, offset):
    extent_x, extent_y, extent_z = faces.shape
    blocks = faces.reshape(extent_x // 2, 2, extent_y // 2, 2, extent_z // 2, 2)
    chosen = lax.index_in_dim(blocks, offset, axis=2 * which_dim + 1, keepdims=True)
    return jnp.sum(chosen, axis=(1, 3, 5))


def side_terms(field, plus_faces, minus_faces, widened):
    result = plus_faces[0] * (field - widened[:, 2:]) + minus_faces[0] * (field - widened[:, :-2])
    for which_dim in (1, 2):
        result = result + plus_faces[which_dim] * (field - plus_side(field, which_dim + 1))
        result = result + minus_faces[which_dim] * (field - minus_side(field, which_dim + 1))
    return result


def fine_image(field, plus_faces, minus_faces, shift_value):
    widened = extended(field, (("space", 1),), 1)
    return shift_value * field + side_terms(field, plus_faces, minus_faces, widened)


def coarse_image(field, plus_faces, minus_faces, shift_value):
    widened = extended(field, (("space", 1),), 1)
    return shift_value * field + side_terms(field, plus_faces, minus_faces, widened)


def restrict(field):
    members, extent_x, extent_y, extent_z = field.shape
    shaped = field.reshape(members, extent_x // 2, 2, extent_y // 2, 2, extent_z // 2, 2)
    return jnp.sum(shaped, axis=(2, 4, 6))


def prolong(field):
    return jnp.repeat(jnp.repeat(jnp.repeat(field, 2, axis=1), 2, axis=2), 2, axis=3)


def precondition(residual, fine, coarse):
    plus_faces, minus_faces, shift_value, diagonal = fine
    coarse_plus, coarse_minus, coarse_shift, coarse_diagonal = coarse
    smooth_one = DAMPING * residual / diagonal
    coarse_rhs = restrict(residual - fine_image(smooth_one, plus_faces, minus_faces, shift_value))
    coarse_one = DAMPING * coarse_rhs / coarse_diagonal
    coarse_two = (
        coarse_one
        + DAMPING
        * (coarse_rhs - coarse_image(coarse_one, coarse_plus, coarse_minus, coarse_shift))
        / coarse_diagonal
    )
    corrected = smooth_one + prolong(coarse_two)
    return (
        corrected
        + DAMPING
        * (residual - fine_image(corrected, plus_faces, minus_faces, shift_value))
        / diagonal
    )


def expand(values):
    return values.reshape(-1, 1, 1, 1)


def cell_sums(values):
    return jnp.sum(values, axis=(1, 2, 3))


def norm_sum(residual, precond):
    return lax.psum(cell_sums(residual * precond), "space")


def solve(rhs, fine, coarse):
    plus_faces, minus_faces, shift_value, diagonal = fine
    iterate = jnp.zeros_like(rhs)
    residual = rhs
    precond = precondition(residual, fine, coarse)
    gamma_now = norm_sum(residual, precond)
    search = precond
    for turn_index in range(ITERS):
        image_field = fine_image(search, plus_faces, minus_faces, shift_value)
        curve = lax.psum(cell_sums(search * image_field), "space")
        step_length = gamma_now / curve
        iterate = iterate + expand(step_length) * search
        if turn_index + 1 < ITERS:
            residual = residual - expand(step_length) * image_field
            precond = precondition(residual, fine, coarse)
            gamma_next = norm_sum(residual, precond)
            search = precond + expand(gamma_next / gamma_now) * search
            gamma_now = gamma_next
    return iterate


def divided(conductivity, misfit, forward_states, pole_shifts, pole_weights, pole_order):
    widened_kappa = extended(conductivity, (("space", 0),), 1)
    plus_faces = [
        0.5 * (conductivity + widened_kappa[2:]),
        0.5 * (conductivity + plus_side(conductivity, 1)),
        0.5 * (conductivity + plus_side(conductivity, 2)),
    ]
    minus_faces = [
        0.5 * (conductivity + widened_kappa[:-2]),
        0.5 * (conductivity + minus_side(conductivity, 1)),
        0.5 * (conductivity + minus_side(conductivity, 2)),
    ]
    base_diagonal = (
        plus_faces[0]
        + plus_faces[1]
        + plus_faces[2]
        + minus_faces[0]
        + minus_faces[1]
        + minus_faces[2]
    )
    coarse_plus = [coarse_pick(plus_faces[which_dim], which_dim, 1) for which_dim in range(3)]
    coarse_minus = [coarse_pick(minus_faces[which_dim], which_dim, 0) for which_dim in range(3)]
    coarse_base = (
        coarse_plus[0]
        + coarse_plus[1]
        + coarse_plus[2]
        + coarse_minus[0]
        + coarse_minus[1]
        + coarse_minus[2]
    )
    pole_index = jnp.arange(pole_shifts.shape[0], dtype=jnp.int32)
    matches = pole_order[:, None] == pole_index[None, :]
    shift_local = jnp.sum(jnp.where(matches, pole_shifts[None, :], 0.0), axis=1)
    weight_local = jnp.sum(jnp.where(matches, pole_weights[None, :], 0.0), axis=1)
    members = forward_states.shape[0]

    def solve_group(shift_part, weight_part):
        shift_value = expand(shift_part)
        fine = (plus_faces, minus_faces, shift_value, base_diagonal[None] + shift_value)
        coarse = (
            coarse_plus,
            coarse_minus,
            8.0 * shift_value,
            coarse_base[None] + 8.0 * shift_value,
        )
        return solve(expand(weight_part) * misfit[None], fine, coarse)

    adjoint_states = jnp.concatenate(
        [
            solve_group(shift_local[member : member + 1], weight_local[member : member + 1])
            for member in range(members)
        ],
        axis=0,
    )
    widened = extended(jnp.stack([adjoint_states, forward_states]), (("space", 2),), 1)
    term = (adjoint_states - widened[0, :, 2:]) * (forward_states - widened[1, :, 2:])
    term = term + (adjoint_states - widened[0, :, :-2]) * (forward_states - widened[1, :, :-2])
    for which_dim in (2, 3):
        term = term + (adjoint_states - plus_side(adjoint_states, which_dim)) * (
            forward_states - plus_side(forward_states, which_dim)
        )
        term = term + (adjoint_states - minus_side(adjoint_states, which_dim)) * (
            forward_states - minus_side(forward_states, which_dim)
        )
    local_term = -0.5 * jnp.sum(term, axis=0)
    gradient = lax.psum_scatter(local_term, "pole", scatter_dimension=1, tiled=True)
    return (adjoint_states, gradient)


def solution(mesh):
    in_specs = (
        P("space", None, None),
        P("space", None, None),
        P("pole", "space", None, None),
        P(),
        P(),
        P("pole"),
    )
    out_specs = (P("pole", "space", None, None), P("space", "pole", None))

    def body(conductivity, misfit, forward_states, *poles):
        nx = conductivity.shape[0] * lax.axis_size("space")
        _, ny, nz = conductivity.shape
        peers = lax.axis_size("space")
        small = nx * ny * nz <= REPLICATED_CELLS and forward_states.shape[:2] == (2, 2)
        if small and nz == 2 * HALF and peers > 2 and peers & (peers - 1) == 0:
            return whole_grid(conductivity, misfit, forward_states, *poles)
        return divided(conductivity, misfit, forward_states, *poles)

    return jax.shard_map(
        body, mesh=mesh, in_specs=in_specs, out_specs=out_specs, check_vma=False
    )
```

```python
import functools

import jax
import jax.numpy as jnp
from jax import lax
from jax.experimental import pallas as pl
from jax.experimental.pallas import tpu as pltpu
from jax.sharding import PartitionSpec as P

ITERS = 2
DAMPING = 0.8
REPLICATED_CELLS = 32 * 64 * 128
HALF = 64
TILE = 8
UNROLL = 8
SETUP_FLOPS = 40 * REPLICATED_CELLS
SETUP_BYTES = 10 * 1024 * 1024


def extended(array, sides, width):
    for axis, dim in sides:
        peers, length = (lax.axis_size(axis), array.shape[dim])
        up = [(i, (i + 1) % peers) for i in range(peers - 1)]
        down = [(j, i) for i, j in up]
        last = lax.slice_in_dim(array, length - width, length, axis=dim)
        leading = lax.slice_in_dim(array, 0, width, axis=dim)
        before = lax.ppermute(last, axis, up)
        after = lax.ppermute(leading, axis, down)
        array = jnp.concatenate([before, array, after], axis=dim)
    return array


def lane_index(shape):
    return lax.broadcasted_iota(jnp.int32, shape, len(shape) - 1)


def row_index(shape):
    return lax.broadcasted_iota(jnp.int32, shape, len(shape) - 2)


def roll(block, shift, axis):
    return pltpu.roll(block, shift % block.shape[axis], axis)


def inverse(value):
    guess = pl.reciprocal(value, approx=True)
    return guess * (2.0 - value * guess)


def tree_sum(values):
    while len(values) > 1:
        values = [sum(values[at : at + 2]) for at in range(0, len(values), 2)]
    return values[0]


def grand_total(acc):
    line = jnp.sum(acc, axis=0, keepdims=True)
    return jnp.broadcast_to(jnp.sum(line, axis=1, keepdims=True), acc.shape)


def swap_masks(peers, flip):
    falling = []
    mask = peers // 2
    while mask > 1:
        falling.append(mask)
        mask //= 2
    rotated = falling[-1:] + falling[:-1]
    return (rotated, falling) if flip else (falling, rotated)


def block_pair(u, holder, peers, flip):
    even, odd = swap_masks(peers, flip)
    parity = holder % 2
    top = jnp.where(parity == 0, even.index(peers // 2), odd.index(peers // 2))
    below = u & ((1 << top) - 1)
    base = ((u >> top) << (top + 1)) | below
    upper = jnp.where(holder >= peers // 2, 1, 0)
    first = base | (upper << top)
    second = base | ((1 - upper) << top)
    home = holder
    for step, (mask_even, mask_odd) in enumerate(zip(even, odd)):
        mask = jnp.where(parity == 0, mask_even, mask_odd)
        home = home ^ (((first >> step) & 1) * mask)
    return first, second, home


def prepare_kernel(kappa_ref, misfit_ref, kappa_out, misfit_out):
    kappa_out[...] = kappa_ref[...]
    misfit_out[...] = misfit_ref[...]


def join_kernel(place_ref, *refs, masks, peers):
    place = place_ref[0]
    at_ = Layout(refs[0].shape[1] // 2)
    for at, (even, odd) in enumerate(masks):
        partner = place ^ jnp.where(place % 2 == 0, even, odd)
        for t, (ref, holder) in enumerate(((refs[at], place), (refs[2 + at], partner))):
            at_.deal(ref, refs[4 + at].at[t], jnp.where(holder >= peers // 2, 1, 0))


def gather_blocks(place, blocks, states, axis):
    peers = lax.axis_size(axis)
    even = place[0] % 2 == 0
    swap = [(i, i ^ 1) for i in range(peers)]
    over = [(i, i + 1 if i % 2 else i - 1) for i in range(1, peers - 1)]
    smem = pl.BlockSpec(memory_space=pltpu.SMEM)
    vmem = pl.BlockSpec(memory_space=pltpu.VMEM)
    swaps = [list(zip(*swap_masks(peers, flip))) for flip in (False, True)]
    own = pl.pallas_call(
        prepare_kernel,
        out_shape=[jax.ShapeDtypeStruct(block.shape, jnp.float32) for block in blocks],
        in_specs=[vmem] * 2,
        out_specs=[vmem] * 2,
        compiler_params=pltpu.CompilerParams(vmem_limit_bytes=1024 * 1024),
        name="prepare",
    )(*blocks)
    held = list(blocks)
    for step in range(len(swaps[0])):
        arrived = []
        for at in (0, 1):
            masks = swaps[at][step]
            pairs = [(i, i ^ masks[i % 2]) for i in range(peers)]
            arrived.append(lax.ppermute(held[at], axis, pairs))
        if step:
            held = [jnp.concatenate(pair, axis=0) for pair in zip(held, arrived)]
            continue
        masks = [swaps[at][0] for at in (0, 1)]
        shape = jax.ShapeDtypeStruct((2, *blocks[0].shape), jnp.float32)
        held[:] = pl.pallas_call(
            functools.partial(join_kernel, masks=masks, peers=peers),
            out_shape=[shape] * 2,
            in_specs=[smem] + [vmem] * 4,
            out_specs=[vmem] * 2,
            compiler_params=pltpu.CompilerParams(vmem_limit_bytes=1024 * 1024),
            name="join",
        )(place, *own, *arrived)
        held[1], states = lax.optimization_barrier((held[1], states))
        far = lax.ppermute(jnp.where(even, states[:, :1], states[:, -1:]), axis, over)
    given = jnp.concatenate([states, far], axis=1)
    near = lax.ppermute(jnp.where(even, given[1], given[0]), axis, swap)
    return held, lambda part: lax.ppermute(part, axis, swap), far, near


CLASSES = [(a, b, c) for a in (0, 1) for b in (0, 1) for c in (0, 1)]
PAIRS = [(p, q) for p in (0, 1) for q in (0, 1)]


def cls(a, b, c):
    return 4 * a + 2 * b + c


def inner_faces(p, q):
    return (
        (2 * p + q, cls(0, p, q), cls(1, p, q)),
        (4 + 2 * p + q, cls(p, 0, q), cls(p, 1, q)),
        (8 + 2 * p + q, cls(p, q, 0), cls(p, q, 1)),
    )


class Layout:
    def __init__(self, rows):
        self.tiles = rows // TILE
        self.lane = lane_index((TILE, 2 * HALF))
        self.row = row_index((TILE, 2 * HALF))
        self.left = self.lane < HALF
        self.zero = jnp.zeros((TILE, 2 * HALF), jnp.float32)

    def tile(self, j):
        return pl.ds(TILE * j, TILE)

    def every(self, b, j):
        return pl.ds(b + 2 * j, TILE, stride=2 * self.tiles)

    def row_before(self, load, j):
        return load(j - 1) if j else roll(load(self.tiles - 1), 1, 0)

    def row_after(self, load, j):
        return load(j + 1) if j + 1 < self.tiles else roll(load(0), -1, 0)

    def seam(self, ref, low, high):
        last = ref.shape[1] - 1
        for j in range(self.tiles):
            for k in low:
                moved = roll(ref[k, last - 1, self.tile(j)], HALF, 1)
                ref[k, 0, self.tile(j)] = jnp.where(self.left, 0.0, moved)
            for k in high:
                moved = roll(ref[k, 1, self.tile(j)], HALF, 1)
                ref[k, last, self.tile(j)] = jnp.where(self.left, moved, 0.0)

    def seam_fine(self, ref):
        count = ref.shape[0]
        self.seam(
            ref,
            [k for k in range(count) if k % 8 >= 4],
            [k for k in range(count) if k % 8 < 4],
        )

    def dealt(self, b, j):
        return pl.ds(TILE * (self.tiles * b + j), TILE)

    def deal(self, block_ref, out_ref, upper):
        odd = jnp.where(self.left, upper, 1 - upper)
        column = 2 * (self.lane % HALF) + odd
        for x in range(block_ref.shape[0]):
            for b in (0, 1):
                for j in range(self.tiles):
                    rows = block_ref[x, self.every(b, j), :]
                    out_ref[x, self.dealt(b, j), :] = jnp.take_along_axis(rows, column, axis=1)

    def arrange(self, mine_ref, theirs_ref, place, flip, store):
        blocks, own = mine_ref.shape[:2]

        def pair(u, carry):
            for ref, holder in ((mine_ref, place), (theirs_ref, place ^ 1)):
                first, second, home = block_pair(u, holder, 2 * blocks, flip)
                for x in range(own):
                    spot = home * (own // 2) + x // 2
                    for b in (0, 1):
                        for j in range(self.tiles):
                            one = ref[first, x, self.dealt(b, j), :]
                            two = ref[second, x, self.dealt(b, j), :]
                            store(cls(x % 2, b, 0), spot, j, jnp.where(self.left, one, two))
                            odd = roll(jnp.where(self.left, two, one), HALF, 1)
                            store(cls(x % 2, b, 1), spot, j, odd)
            return carry

        lax.fori_loop(0, blocks // 2, pair, 0)


def setup_kernel(
    place_ref,
    shifts_ref,
    order_ref,
    mine_ref,
    theirs_ref,
    inner,
    outer_x,
    outer_y,
    outer_z,
    inner_sum,
    diagonal,
    damped,
    coarse_off,
    coarse_damped,
    half_kappa,
):
    half = inner.shape[1]
    at_ = Layout(inner.shape[2])
    tile, tiles = at_.tile, at_.tiles
    shift = shifts_ref[order_ref[place_ref[0] % 2]]

    def keep(k, spot, j, value):
        half_kappa[k, spot + 1, tile(j)] = 0.5 * value

    at_.arrange(mine_ref, theirs_ref, place_ref[0], False, keep)
    at_.seam_fine(half_kappa)

    z_low = jnp.where(at_.lane % HALF > 0, 1.0, 0.0)
    z_high = jnp.where(at_.lane % HALF < HALF - 1, 1.0, 0.0)
    y_low = [jnp.where(at_.row > 0, 1.0, 0.0)] + [None] * (tiles - 1)
    y_high = [None] * (tiles - 1) + [jnp.where(at_.row < TILE - 1, 1.0, 0.0)]

    def masked(mask, value):
        return value if mask is None else mask * value

    def plane(i, carry):
        for j in range(tiles):
            kap = [half_kappa[k, i + 1, tile(j)] for k in range(8)]
            inside = [[] for _ in range(8)]
            outside = [[] for _ in range(8)]
            off = [[] for _ in range(5)]
            for p, q in PAIRS:
                for face_at, low, high in inner_faces(p, q):
                    face = kap[low] + kap[high]
                    inner[face_at, i, tile(j)] = face
                    inside[low].append(face)
                    inside[high].append(face)
                at = 2 * p + q

                low, high = cls(0, p, q), cls(1, p, q)
                minus = kap[low] + half_kappa[high, i, tile(j)]
                plus = kap[high] + half_kappa[low, i + 2, tile(j)]
                outside[low].append(minus)
                outside[high].append(plus)
                outer_x[at, i, tile(j)] = minus
                off[0].append(minus)

                low, high = cls(p, 0, q), cls(p, 1, q)
                side = at_.row_before(lambda r: half_kappa[high, i + 1, tile(r)], j)
                minus = kap[low] + masked(y_low[j], side)
                side = at_.row_after(lambda r: half_kappa[low, i + 1, tile(r)], j)
                plus = kap[high] + masked(y_high[j], side)
                outside[low].append(minus)
                outside[high].append(plus)
                minus, plus = masked(y_low[j], minus), masked(y_high[j], plus)
                outer_y[at, i, tile(j)] = minus
                off[1].append(minus)
                off[2].append(plus)

                low, high = cls(p, q, 0), cls(p, q, 1)
                minus = kap[low] + z_low * roll(kap[high], 1, 1)
                plus = kap[high] + z_high * roll(kap[low], -1, 1)
                outside[low].append(minus)
                outside[high].append(plus)
                minus, plus = z_low * minus, z_high * plus
                outer_z[at, i, tile(j)] = minus
                outer_z[4 + at, i, tile(j)] = plus
                off[3].append(minus)
                off[4].append(plus)
            coarse_total = []
            for k in range(8):
                within, without = tree_sum(inside[k]), tree_sum(outside[k])
                inner_sum[k, i, tile(j)] = within
                base = within + without + shift
                diagonal[k, i, tile(j)] = base
                coarse_total.append(without)
                damped[k, i, tile(j)] = DAMPING * inverse(base)
            for at, part in enumerate(off):
                coarse_off[at, i, tile(j)] = tree_sum(part)
            coarse_damped[i, tile(j)] = DAMPING * inverse(tree_sum(coarse_total) + 8.0 * shift)
        return carry

    lax.fori_loop(0, half, plane, 0, unroll=UNROLL)
    for j in range(tiles):
        part = []
        for p, q in PAIRS:
            face = half_kappa[cls(0, p, q), half + 1, tile(j)]
            face = face + half_kappa[cls(1, p, q), half, tile(j)]
            outer_x[2 * p + q, half, tile(j)] = face
            part.append(face)
        coarse_off[0, half, tile(j)] = tree_sum(part)


def solve_kernel(
    place_ref,
    weights_ref,
    order_ref,
    mine_ref,
    theirs_ref,
    state_ref,
    far_ref,
    near_ref,
    inner,
    outer_x,
    outer_y,
    outer_z,
    inner_sum,
    diagonal,
    damped,
    coarse_off,
    coarse_damped,
    adjoint_ref,
    keep_ref,
    partner_ref,
    send_ref,
    residual,
    scaled,
    partial,
    first_dir,
    second_dir,
    image,
    coarse_one,
    coarse_two,
    planes,
):
    half, rows = inner.shape[1:3]
    at_ = Layout(rows)
    tile, tiles, zero = at_.tile, at_.tiles, at_.zero
    core = place_ref[0] % 2
    weight = weights_ref[order_ref[core]]

    def begin(k, spot, j, value):
        res = weight * value
        residual[k, spot, tile(j)] = res
        scaled[k, spot + 1, tile(j)] = damped[k, spot, tile(j)] * res

    at_.arrange(mine_ref, theirs_ref, place_ref[0], True, begin)
    at_.seam_fine(scaled)

    def rows_of(ref, i):
        cache = {}

        def load(k, j, step):
            if abs(j - step) > 1:
                return ref[k, i, tile(j)]
            if (k, j) not in cache:
                cache[k, j] = ref[k, i, tile(j)]
            return cache[k, j]

        def get(k, j):
            return load(k, j, j)

        def before(k, j):
            return at_.row_before(lambda r: load(k, r, j), j)

        def after(k, j):
            return at_.row_after(lambda r: load(k, r, j), j)

        return get, before, after

    def stencil(field, i, both):
        get, before, after = rows_of(field, i + 1)
        face_get, _, face_after = rows_of(outer_y, i)
        for j in range(tiles):
            here = [get(k, j) for k in range(8)]
            terms = [[] for _ in range(8)]
            for p, q in PAIRS:
                at = 2 * p + q
                for face_at, low, high in inner_faces(p, q):
                    face = inner[face_at, i, tile(j)]
                    terms[low].append(face * here[high])
                    if both:
                        terms[high].append(face * here[low])
                low, high = cls(0, p, q), cls(1, p, q)
                terms[low].append(outer_x[at, i, tile(j)] * field[high, i, tile(j)])
                if both:
                    side = field[low, i + 2, tile(j)]
                    terms[high].append(outer_x[at, i + 1, tile(j)] * side)
                low, high = cls(p, 0, q), cls(p, 1, q)
                terms[low].append(face_get(at, j) * before(high, j))
                if both:
                    terms[high].append(face_after(at, j) * after(low, j))
                low, high = cls(p, q, 0), cls(p, q, 1)
                terms[low].append(outer_z[at, i, tile(j)] * roll(here[high], 1, 1))
                if both:
                    terms[high].append(outer_z[4 + at, i, tile(j)] * roll(here[low], -1, 1))
            yield j, here, [tree_sum(part) if part else None for part in terms]

    def coarse_sides(field, i, j):
        here = field[0, i + 1, tile(j)]
        return here, (
            (field[0, i, tile(j)], field[0, i + 2, tile(j)]),
            (
                at_.row_before(lambda r: field[0, i + 1, tile(r)], j),
                at_.row_after(lambda r: field[0, i + 1, tile(r)], j),
            ),
            (roll(here, 1, 1), roll(here, -1, 1)),
        )

    def precondition(result, other):
        def down(i, carry):
            for j, _, sums in stencil(scaled, i, True):
                res = [residual[k, i, tile(j)] for k in range(8)]
                parts = [(2.0 - DAMPING) * res[k] + sums[k] for k in range(8)]
                for k in range(8):
                    partial[k, i, tile(j)] = parts[k]
                rhs = tree_sum(parts) - tree_sum(res)
                coarse_one[0, i + 1, tile(j)] = coarse_damped[i, tile(j)] * rhs
            return carry

        lax.fori_loop(0, half, down, 0, unroll=UNROLL)
        at_.seam(coarse_one, [0], [0])

        def smooth(i, carry):
            for j in range(tiles):
                here, sides = coarse_sides(coarse_one, i, j)
                total = coarse_off[0, i, tile(j)] * sides[0][0]
                total = total + coarse_off[0, i + 1, tile(j)] * sides[0][1]
                more = coarse_off[1, i, tile(j)] * sides[1][0]
                more = more + coarse_off[2, i, tile(j)] * sides[1][1]
                most = coarse_off[3, i, tile(j)] * sides[2][0]
                most = most + coarse_off[4, i, tile(j)] * sides[2][1]
                coarse_two[0, i + 1, tile(j)] = (2.0 - DAMPING) * here + coarse_damped[
                    i, tile(j)
                ] * (total + more + most)
            return carry

        lax.fori_loop(0, half, smooth, 0, unroll=UNROLL)
        at_.seam(coarse_two, [0], [0])

        def up(i, carry):
            gamma, cross = carry
            face_get, _, face_after = rows_of(outer_y, i)
            for j in range(tiles):
                here, sides = coarse_sides(coarse_two, i, j)
                kept = (1.0 - DAMPING) * here
                dots, crosses = [], []
                for a, b, c in CLASSES:
                    k = cls(a, b, c)
                    value = tree_sum(
                        [
                            partial[k, i, tile(j)],
                            inner_sum[k, i, tile(j)] * here,
                            outer_x[2 * b + c, i + a, tile(j)] * sides[0][a],
                            (face_after if b else face_get)(2 * a + c, j) * sides[1][b],
                            outer_z[4 * c + 2 * a + b, i, tile(j)] * sides[2][c],
                        ]
                    )
                    new = kept + damped[k, i, tile(j)] * value
                    result[k, i + 1, tile(j)] = new
                    dots.append(residual[k, i, tile(j)] * new)
                    if other is not None:
                        crosses.append(other[k, i, tile(j)] * new)
                gamma = gamma + tree_sum(dots)
                if other is not None:
                    cross = cross + tree_sum(crosses)
            return gamma, cross

        sums = lax.fori_loop(0, half, up, (zero, zero), unroll=UNROLL)
        at_.seam_fine(result)
        return [grand_total(part) for part in sums]

    gamma, _ = precondition(first_dir, None)

    def apply(i, acc):
        for j, here, sums in stencil(first_dir, i, True):
            dots = []
            for k in range(8):
                value = diagonal[k, i, tile(j)] * here[k] - sums[k]
                image[k, i, tile(j)] = value
                dots.append(here[k] * value)
            acc = acc + tree_sum(dots)
        return acc

    curve = grand_total(lax.fori_loop(0, half, apply, zero, unroll=UNROLL))
    step_one = gamma / curve

    def update(i, carry):
        for j in range(tiles):
            for k in range(8):
                new = residual[k, i, tile(j)] - step_one * image[k, i, tile(j)]
                residual[k, i, tile(j)] = new
                scaled[k, i + 1, tile(j)] = damped[k, i, tile(j)] * new
        return carry

    lax.fori_loop(0, half, update, 0, unroll=UNROLL)
    at_.seam_fine(scaled)

    gamma_next, cross = precondition(second_dir, image)

    def bend(i, carry):
        own_part, face_part = carry
        for j, here, sums in stencil(second_dir, i, False):
            own_part = own_part + tree_sum(
                [here[k] * (diagonal[k, i, tile(j)] * here[k]) for k in range(8)]
            )
            face_part = face_part + tree_sum([here[k] * sums[k] for k in range(7)])
        return own_part, face_part

    own_part, face_part = lax.fori_loop(0, half, bend, (zero, zero), unroll=UNROLL)
    ratio = gamma_next / gamma
    curve_next = grand_total(own_part - 2.0 * face_part)
    step_two = gamma_next / (curve_next + ratio * (2.0 * cross + ratio * curve))
    step_first = step_one + step_two * ratio

    own, ny, nz = adjoint_ref.shape
    start = (place_ref[0] - core) * (own // 2)
    upper = jnp.where(start >= half, 1, 0)
    start = start - half * upper
    even = at_.lane % 2 == 0
    source = at_.lane // 2 + HALF * upper
    for at in range(2 * own + 2):
        a = (at + 1) % 2
        spot = start + (at + 1) // 2
        for b in (0, 1):
            for j in range(tiles):
                both = [
                    step_first * first_dir[cls(a, b, c), spot, tile(j)]
                    + step_two * second_dir[cls(a, b, c), spot, tile(j)]
                    for c in (0, 1)
                ]
                planes[at, at_.every(b, j), :] = jnp.where(
                    even,
                    jnp.take_along_axis(both[0], source, axis=1),
                    jnp.take_along_axis(both[1], source, axis=1),
                )

    full = (ny, nz)
    y_at = row_index(full)
    z_at = lane_index(full)

    def drop(value, axis, up):
        moved = roll(value, -1 if up else 1, axis)
        at = (y_at, z_at)[axis]
        edge = full[axis] - 1 if up else 0
        return value - jnp.where(at == edge, 0.0, moved)

    is_even = core == 0
    state = [jnp.where(is_even, far_ref[core, 0], near_ref[own])]
    state += [jnp.where(is_even, state_ref[core, x], near_ref[x]) for x in range(own)]
    state += [jnp.where(is_even, near_ref[x], state_ref[core, x]) for x in range(own)]
    state += [jnp.where(is_even, near_ref[own], far_ref[core, 0])]
    terms = 2 * own + 2
    for x in range(2 * own):
        here, f = planes[x + 1], state[x + 1]
        term = (here - planes[x + 2]) * (f - state[x + 2])
        term = term + (here - planes[x]) * (f - state[x])
        for axis in (0, 1):
            for up in (True, False):
                term = term + drop(here, axis, up) * drop(f, axis, up)
        planes[terms + x] = -0.5 * term

    groups = send_ref.shape[0] + 1
    chunk = keep_ref.shape[1]
    for x in range(own):
        mine, other = core * own + x, (1 - core) * own + x
        adjoint_ref[x] = planes[1 + mine]
        partner_ref[x, :ny] = planes[1 + other]
        for k in range(groups):
            at = pl.multiple_of(lax.rem(place_ref[1] + k, groups) * chunk, chunk)
            for side, plane in enumerate((mine, other)):
                share = planes[terms + plane, pl.ds(at, chunk), :]
                if k:
                    send_ref[k - 1, side, x] = share
                elif side:
                    partner_ref[x, ny:] = share
                else:
                    keep_ref[x] = share


def whole_grid(conductivity, misfit, forward_states, pole_shifts, pole_weights, pole_order):
    members, own, ny, nz = forward_states.shape
    groups = lax.axis_size("pole")
    place = jnp.stack([lax.axis_index("space"), lax.axis_index("pole")]).astype(jnp.int32)
    peers = lax.axis_size("space")
    mine, fetch, far, near = gather_blocks(
        place, [conductivity, misfit], forward_states, "space"
    )
    half, rows = peers * own // 4, ny // 2

    def field(count, extent):
        return (count, extent, rows, 2 * HALF)

    def held(*shape):
        return pltpu.VMEM(shape, jnp.float32)

    smem = pl.BlockSpec(memory_space=pltpu.SMEM)
    vmem = pl.BlockSpec(memory_space=pltpu.VMEM)
    shapes = [
        field(12, half),
        field(4, half + 1),
        field(4, half),
        field(8, half),
        field(8, half),
        field(8, half),
        field(8, half),
        field(5, half + 1),
        (half, rows, 2 * HALF),
    ]
    coefficients = pl.pallas_call(
        setup_kernel,
        out_shape=[jax.ShapeDtypeStruct(shape, jnp.float32) for shape in shapes],
        in_specs=[smem] * 3 + [vmem] * 2,
        out_specs=[vmem] * len(shapes),
        scratch_shapes=[held(*field(8, half + 2))],
        compiler_params=pltpu.CompilerParams(vmem_limit_bytes=6 * 1024 * 1024),
        cost_estimate=pl.CostEstimate(
            flops=SETUP_FLOPS, bytes_accessed=SETUP_BYTES, transcendentals=0
        ),
        name="setup",
    )(place, pole_shifts, pole_order, mine[0], fetch(mine[0]))
    coefficients, source, far = lax.optimization_barrier((coefficients, mine[1], far))
    chunk = ny // groups
    adjoint, gradient, partner, send = pl.pallas_call(
        solve_kernel,
        out_shape=[
            jax.ShapeDtypeStruct((own, ny, nz), jnp.float32),
            jax.ShapeDtypeStruct((own, chunk, nz), jnp.float32),
            jax.ShapeDtypeStruct((own, ny + chunk, nz), jnp.float32),
            jax.ShapeDtypeStruct((groups - 1, 2, own, chunk, nz), jnp.float32),
        ],
        in_specs=[smem] * 3 + [vmem] * (5 + len(shapes)),
        out_specs=[vmem] * 4,
        scratch_shapes=[
            held(*field(8, half)),
            held(*field(8, half + 2)),
            held(*field(8, half)),
            held(*field(8, half + 2)),
            held(*field(8, half + 2)),
            held(*field(8, half)),
            held(*field(1, half + 2)),
            held(*field(1, half + 2)),
            held(4 * own + 2, ny, nz),
        ],
        compiler_params=pltpu.CompilerParams(vmem_limit_bytes=12 * 1024 * 1024),
        name="solve",
    )(
        place,
        pole_weights,
        pole_order,
        source,
        fetch(source),
        forward_states,
        far,
        near,
        *coefficients,
    )

    arrived = lax.ppermute(partner, "space", [(i, i ^ 1) for i in range(peers)])
    shares = []
    for k in range(1, groups):
        for side in (0, 1):
            pairs = [
                (i * peers + j, (i + k) % groups * peers + (j ^ side))
                for i in range(groups)
                for j in range(peers)
            ]
            shares.append(lax.ppermute(send[k - 1, side], ("pole", "space"), pairs))
    even = place[0] % 2 == 0
    theirs = arrived[:, :ny]
    adjoint_states = jnp.stack(
        [jnp.where(even, adjoint, theirs), jnp.where(even, theirs, adjoint)]
    )
    adjoint_states, arrived = lax.optimization_barrier((adjoint_states, arrived))
    return adjoint_states, gradient + arrived[:, ny:] + sum(shares)


def plus_side(field, which_dim):
    extent = field.shape[which_dim]
    inner_part = lax.slice_in_dim(field, 1, extent, axis=which_dim)
    zero_plane = jnp.zeros_like(lax.slice_in_dim(field, 0, 1, axis=which_dim))
    return jnp.concatenate([inner_part, zero_plane], axis=which_dim)


def minus_side(field, which_dim):
    extent = field.shape[which_dim]
    inner_part = lax.slice_in_dim(field, 0, extent - 1, axis=which_dim)
    zero_plane = jnp.zeros_like(lax.slice_in_dim(field, 0, 1, axis=which_dim))
    return jnp.concatenate([zero_plane, inner_part], axis=which_dim)


def coarse_pick(faces, which_dim, offset):
    extent_x, extent_y, extent_z = faces.shape
    blocks = faces.reshape(extent_x // 2, 2, extent_y // 2, 2, extent_z // 2, 2)
    chosen = lax.index_in_dim(blocks, offset, axis=2 * which_dim + 1, keepdims=True)
    return jnp.sum(chosen, axis=(1, 3, 5))


def side_terms(field, plus_faces, minus_faces, widened):
    result = plus_faces[0] * (field - widened[:, 2:]) + minus_faces[0] * (field - widened[:, :-2])
    for which_dim in (1, 2):
        result = result + plus_faces[which_dim] * (field - plus_side(field, which_dim + 1))
        result = result + minus_faces[which_dim] * (field - minus_side(field, which_dim + 1))
    return result


def fine_image(field, plus_faces, minus_faces, shift_value):
    widened = extended(field, (("space", 1),), 1)
    return shift_value * field + side_terms(field, plus_faces, minus_faces, widened)


def coarse_image(field, plus_faces, minus_faces, shift_value):
    widened = extended(field, (("space", 1),), 1)
    return shift_value * field + side_terms(field, plus_faces, minus_faces, widened)


def restrict(field):
    members, extent_x, extent_y, extent_z = field.shape
    shaped = field.reshape(members, extent_x // 2, 2, extent_y // 2, 2, extent_z // 2, 2)
    return jnp.sum(shaped, axis=(2, 4, 6))


def prolong(field):
    return jnp.repeat(jnp.repeat(jnp.repeat(field, 2, axis=1), 2, axis=2), 2, axis=3)


def precondition(residual, fine, coarse):
    plus_faces, minus_faces, shift_value, diagonal = fine
    coarse_plus, coarse_minus, coarse_shift, coarse_diagonal = coarse
    smooth_one = DAMPING * residual / diagonal
    coarse_rhs = restrict(residual - fine_image(smooth_one, plus_faces, minus_faces, shift_value))
    coarse_one = DAMPING * coarse_rhs / coarse_diagonal
    coarse_two = (
        coarse_one
        + DAMPING
        * (coarse_rhs - coarse_image(coarse_one, coarse_plus, coarse_minus, coarse_shift))
        / coarse_diagonal
    )
    corrected = smooth_one + prolong(coarse_two)
    return (
        corrected
        + DAMPING
        * (residual - fine_image(corrected, plus_faces, minus_faces, shift_value))
        / diagonal
    )


def expand(values):
    return values.reshape(-1, 1, 1, 1)


def cell_sums(values):
    return jnp.sum(values, axis=(1, 2, 3))


def norm_sum(residual, precond):
    return lax.psum(cell_sums(residual * precond), "space")


def solve(rhs, fine, coarse):
    plus_faces, minus_faces, shift_value, diagonal = fine
    iterate = jnp.zeros_like(rhs)
    residual = rhs
    precond = precondition(residual, fine, coarse)
    gamma_now = norm_sum(residual, precond)
    search = precond
    for turn_index in range(ITERS):
        image_field = fine_image(search, plus_faces, minus_faces, shift_value)
        curve = lax.psum(cell_sums(search * image_field), "space")
        step_length = gamma_now / curve
        iterate = iterate + expand(step_length) * search
        if turn_index + 1 < ITERS:
            residual = residual - expand(step_length) * image_field
            precond = precondition(residual, fine, coarse)
            gamma_next = norm_sum(residual, precond)
            search = precond + expand(gamma_next / gamma_now) * search
            gamma_now = gamma_next
    return iterate


def divided(conductivity, misfit, forward_states, pole_shifts, pole_weights, pole_order):
    widened_kappa = extended(conductivity, (("space", 0),), 1)
    plus_faces = [
        0.5 * (conductivity + widened_kappa[2:]),
        0.5 * (conductivity + plus_side(conductivity, 1)),
        0.5 * (conductivity + plus_side(conductivity, 2)),
    ]
    minus_faces = [
        0.5 * (conductivity + widened_kappa[:-2]),
        0.5 * (conductivity + minus_side(conductivity, 1)),
        0.5 * (conductivity + minus_side(conductivity, 2)),
    ]
    base_diagonal = (
        plus_faces[0]
        + plus_faces[1]
        + plus_faces[2]
        + minus_faces[0]
        + minus_faces[1]
        + minus_faces[2]
    )
    coarse_plus = [coarse_pick(plus_faces[which_dim], which_dim, 1) for which_dim in range(3)]
    coarse_minus = [coarse_pick(minus_faces[which_dim], which_dim, 0) for which_dim in range(3)]
    coarse_base = (
        coarse_plus[0]
        + coarse_plus[1]
        + coarse_plus[2]
        + coarse_minus[0]
        + coarse_minus[1]
        + coarse_minus[2]
    )
    pole_index = jnp.arange(pole_shifts.shape[0], dtype=jnp.int32)
    matches = pole_order[:, None] == pole_index[None, :]
    shift_local = jnp.sum(jnp.where(matches, pole_shifts[None, :], 0.0), axis=1)
    weight_local = jnp.sum(jnp.where(matches, pole_weights[None, :], 0.0), axis=1)
    members = forward_states.shape[0]

    def solve_group(shift_part, weight_part):
        shift_value = expand(shift_part)
        fine = (plus_faces, minus_faces, shift_value, base_diagonal[None] + shift_value)
        coarse = (
            coarse_plus,
            coarse_minus,
            8.0 * shift_value,
            coarse_base[None] + 8.0 * shift_value,
        )
        return solve(expand(weight_part) * misfit[None], fine, coarse)

    adjoint_states = jnp.concatenate(
        [
            solve_group(shift_local[member : member + 1], weight_local[member : member + 1])
            for member in range(members)
        ],
        axis=0,
    )
    widened = extended(jnp.stack([adjoint_states, forward_states]), (("space", 2),), 1)
    term = (adjoint_states - widened[0, :, 2:]) * (forward_states - widened[1, :, 2:])
    term = term + (adjoint_states - widened[0, :, :-2]) * (forward_states - widened[1, :, :-2])
    for which_dim in (2, 3):
        term = term + (adjoint_states - plus_side(adjoint_states, which_dim)) * (
            forward_states - plus_side(forward_states, which_dim)
        )
        term = term + (adjoint_states - minus_side(adjoint_states, which_dim)) * (
            forward_states - minus_side(forward_states, which_dim)
        )
    local_term = -0.5 * jnp.sum(term, axis=0)
    gradient = lax.psum_scatter(local_term, "pole", scatter_dimension=1, tiled=True)
    return (adjoint_states, gradient)


def solution(mesh):
    in_specs = (
        P("space", None, None),
        P("space", None, None),
        P("pole", "space", None, None),
        P(),
        P(),
        P("pole"),
    )
    out_specs = (P("pole", "space", None, None), P("space", "pole", None))

    def body(conductivity, misfit, forward_states, *poles):
        nx = conductivity.shape[0] * lax.axis_size("space")
        _, ny, nz = conductivity.shape
        peers = lax.axis_size("space")
        small = nx * ny * nz <= REPLICATED_CELLS and forward_states.shape[:2] == (2, 2)
        if small and nz == 2 * HALF and peers > 2 and peers & (peers - 1) == 0:
            return whole_grid(conductivity, misfit, forward_states, *poles)
        return divided(conductivity, misfit, forward_states, *poles)

    return jax.shard_map(
        body, mesh=mesh, in_specs=in_specs, out_specs=out_specs, check_vma=False
    )
```

```python
import functools

import jax
import jax.numpy as jnp
from jax import lax
from jax.experimental import pallas as pl
from jax.experimental.pallas import tpu as pltpu
from jax.sharding import PartitionSpec as P

ITERS = 2
DAMPING = 0.8
KEPT = 2.0 - DAMPING
REPLICATED_CELLS = 32 * 64 * 128
HALF = 64
TILE = 8
UNROLL = 8


def extended(array, sides, width):
    for axis, dim in sides:
        peers, length = (lax.axis_size(axis), array.shape[dim])
        up = [(i, (i + 1) % peers) for i in range(peers - 1)]
        down = [(j, i) for i, j in up]
        last = lax.slice_in_dim(array, length - width, length, axis=dim)
        leading = lax.slice_in_dim(array, 0, width, axis=dim)
        before = lax.ppermute(last, axis, up)
        after = lax.ppermute(leading, axis, down)
        array = jnp.concatenate([before, array, after], axis=dim)
    return array


def lane_index(shape):
    return lax.broadcasted_iota(jnp.int32, shape, len(shape) - 1)


def row_index(shape):
    return lax.broadcasted_iota(jnp.int32, shape, len(shape) - 2)


def roll(block, shift, axis):
    return pltpu.roll(block, shift % block.shape[axis], axis)


def inverse(value):
    guess = pl.reciprocal(value, approx=True)
    return guess * (2.0 - value * guess)


def tree_sum(values):
    while len(values) > 1:
        values = [sum(values[at : at + 2]) for at in range(0, len(values), 2)]
    return values[0]


def grand_total(acc):
    line = jnp.sum(acc, axis=0, keepdims=True)
    return jnp.broadcast_to(jnp.sum(line, axis=1, keepdims=True), acc.shape)


def swap_masks(peers, flip):
    falling = []
    mask = peers // 2
    while mask > 1:
        falling.append(mask)
        mask //= 2
    if flip:
        return falling[::-1], falling[:1] + falling[:0:-1]
    return falling, falling[-1:] + falling[:-1]


def block_pair(u, holder, peers, flip):
    even, odd = swap_masks(peers, flip)
    parity = holder % 2
    top = jnp.where(parity == 0, even.index(peers // 2), odd.index(peers // 2))
    below = u & ((1 << top) - 1)
    base = ((u >> top) << (top + 1)) | below
    upper = jnp.where(holder >= peers // 2, 1, 0)
    first = base | (upper << top)
    second = base | ((1 - upper) << top)
    home = holder
    for step, (mask_even, mask_odd) in enumerate(zip(even, odd)):
        mask = jnp.where(parity == 0, mask_even, mask_odd)
        home = home ^ (((first >> step) & 1) * mask)
    return first, second, home


def prepare_kernel(place_ref, kappa_ref, misfit_ref, kappa_out, misfit_out, *, peers):
    at_ = Layout(kappa_ref.shape[1] // 2)
    upper = jnp.where(place_ref[0] >= peers // 2, 1, 0)
    at_.deal(kappa_ref, kappa_out, upper)
    at_.deal(misfit_ref, misfit_out, upper)


def join_kernel(place_ref, *refs, masks, peers):
    place = place_ref[0]
    at_ = Layout(refs[0].shape[1] // 2)
    for at, (even, odd) in enumerate(masks):
        partner = place ^ jnp.where(place % 2 == 0, even, odd)
        refs[4 + at][0] = refs[at][...]
        at_.deal(refs[2 + at], refs[4 + at].at[1], jnp.where(partner >= peers // 2, 1, 0))


def gather_blocks(place, blocks, states, axis):
    peers = lax.axis_size(axis)
    even = place[0] % 2 == 0
    swap = [(i, i ^ 1) for i in range(peers)]
    over = [(i, i + 1 if i % 2 else i - 1) for i in range(1, peers - 1)]
    smem = pl.BlockSpec(memory_space=pltpu.SMEM)
    vmem = pl.BlockSpec(memory_space=pltpu.VMEM)
    swaps = [list(zip(*swap_masks(peers, flip))) for flip in (False, True)]
    own = pl.pallas_call(
        functools.partial(prepare_kernel, peers=peers),
        out_shape=[jax.ShapeDtypeStruct(block.shape, jnp.float32) for block in blocks],
        in_specs=[smem] + [vmem] * 2,
        out_specs=[vmem] * 2,
        compiler_params=pltpu.CompilerParams(vmem_limit_bytes=1024 * 1024),
        name="prepare",
    )(place, *blocks)
    held = list(blocks)
    for step in range(len(swaps[0])):
        arrived = []
        for at in (0, 1):
            masks = swaps[at][step]
            pairs = [(i, i ^ masks[i % 2]) for i in range(peers)]
            arrived.append(lax.ppermute(held[at], axis, pairs))
        if step:
            held = [jnp.concatenate(pair, axis=0) for pair in zip(held, arrived)]
            continue
        masks = [swaps[at][0] for at in (0, 1)]
        shape = jax.ShapeDtypeStruct((2, *blocks[0].shape), jnp.float32)
        held[:] = pl.pallas_call(
            functools.partial(join_kernel, masks=masks, peers=peers),
            out_shape=[shape] * 2,
            in_specs=[smem] + [vmem] * 4,
            out_specs=[vmem] * 2,
            compiler_params=pltpu.CompilerParams(vmem_limit_bytes=1024 * 1024),
            name="join",
        )(place, *own, *arrived)
        held[1], states = lax.optimization_barrier((held[1], states))
        far = lax.ppermute(jnp.where(even, states[:, :1], states[:, -1:]), axis, over)
    held[1], far = lax.optimization_barrier((held[1], far))
    given = jnp.concatenate([states, far], axis=1)
    near = lax.ppermute(jnp.where(even, given[1], given[0]), axis, swap)
    other = [lax.ppermute(part, axis, swap) for part in held]
    return held, other, far, near


CLASSES = [(a, b, c) for a in (0, 1) for b in (0, 1) for c in (0, 1)]
PAIRS = [(p, q) for p in (0, 1) for q in (0, 1)]


def cls(a, b, c):
    return 4 * a + 2 * b + c


def inner_faces(p, q):
    return (
        (2 * p + q, cls(0, p, q), cls(1, p, q)),
        (4 + 2 * p + q, cls(p, 0, q), cls(p, 1, q)),
        (8 + 2 * p + q, cls(p, q, 0), cls(p, q, 1)),
    )


class Layout:
    def __init__(self, rows):
        self.tiles = rows // TILE
        self.lane = lane_index((TILE, 2 * HALF))
        self.row = row_index((TILE, 2 * HALF))
        self.left = self.lane < HALF
        self.zero = jnp.zeros((TILE, 2 * HALF), jnp.float32)

    def tile(self, j):
        return pl.ds(TILE * j, TILE)

    def every(self, b, j):
        return pl.ds(b + 2 * j, TILE, stride=2 * self.tiles)

    def row_before(self, load, j):
        return load(j - 1) if j else roll(load(self.tiles - 1), 1, 0)

    def row_after(self, load, j):
        return load(j + 1) if j + 1 < self.tiles else roll(load(0), -1, 0)

    def seam(self, ref, low, high):
        last = ref.shape[1] - 1
        for j in range(self.tiles):
            for k in low:
                moved = roll(ref[k, last - 1, self.tile(j)], HALF, 1)
                ref[k, 0, self.tile(j)] = jnp.where(self.left, 0.0, moved)
            for k in high:
                moved = roll(ref[k, 1, self.tile(j)], HALF, 1)
                ref[k, last, self.tile(j)] = jnp.where(self.left, moved, 0.0)

    def seam_fine(self, ref):
        count = ref.shape[0]
        self.seam(
            ref,
            [k for k in range(count) if k % 8 >= 4],
            [k for k in range(count) if k % 8 < 4],
        )

    def dealt(self, b, j):
        return pl.ds(TILE * (self.tiles * b + j), TILE)

    def deal(self, block_ref, out_ref, upper):
        odd = jnp.where(self.left, upper, 1 - upper)
        column = 2 * (self.lane % HALF) + odd
        for x in range(block_ref.shape[0]):
            for b in (0, 1):
                for j in range(self.tiles):
                    rows = block_ref[x, self.every(b, j), :]
                    out_ref[x, self.dealt(b, j), :] = jnp.take_along_axis(rows, column, axis=1)

    def arrange(self, mine_ref, theirs_ref, place, flip, store):
        blocks, own = mine_ref.shape[:2]

        def pair(u, carry):
            for ref, holder in ((mine_ref, place), (theirs_ref, place ^ 1)):
                first, second, home = block_pair(u, holder, 2 * blocks, flip)
                for x in range(own):
                    spot = home * (own // 2) + x // 2
                    for b in (0, 1):
                        for j in range(self.tiles):
                            one = ref[first, x, self.dealt(b, j), :]
                            two = ref[second, x, self.dealt(b, j), :]
                            store(cls(x % 2, b, 0), spot, j, jnp.where(self.left, one, two))
                            odd = roll(jnp.where(self.left, two, one), HALF, 1)
                            store(cls(x % 2, b, 1), spot, j, odd)
            return carry

        lax.fori_loop(0, blocks // 2, pair, 0)


def setup_kernel(
    place_ref,
    shifts_ref,
    order_ref,
    mine_ref,
    theirs_ref,
    inner,
    outer_x,
    outer_y,
    outer_z,
    inner_sum,
    diagonal,
    damped,
    coarse_off,
    coarse_damped,
    half_kappa,
):
    half = inner.shape[1]
    at_ = Layout(inner.shape[2])
    tile, tiles = at_.tile, at_.tiles
    shift = shifts_ref[order_ref[place_ref[0] % 2]]

    def keep(k, spot, j, value):
        half_kappa[k, spot + 1, tile(j)] = 0.5 * value

    at_.arrange(mine_ref, theirs_ref, place_ref[0], False, keep)
    at_.seam_fine(half_kappa)

    z_low = jnp.where(at_.lane % HALF > 0, 1.0, 0.0)
    z_high = jnp.where(at_.lane % HALF < HALF - 1, 1.0, 0.0)
    y_low = [jnp.where(at_.row > 0, 1.0, 0.0)] + [None] * (tiles - 1)
    y_high = [None] * (tiles - 1) + [jnp.where(at_.row < TILE - 1, 1.0, 0.0)]

    def masked(mask, value):
        return value if mask is None else mask * value

    def plane(i, carry):
        for j in range(tiles):
            kap = [half_kappa[k, i + 1, tile(j)] for k in range(8)]
            inside = [[] for _ in range(8)]
            outside = [[] for _ in range(8)]
            off = [[] for _ in range(5)]
            for p, q in PAIRS:
                for face_at, low, high in inner_faces(p, q):
                    face = kap[low] + kap[high]
                    inner[face_at, i, tile(j)] = face
                    inside[low].append(face)
                    inside[high].append(face)
                at = 2 * p + q

                low, high = cls(0, p, q), cls(1, p, q)
                minus = kap[low] + half_kappa[high, i, tile(j)]
                plus = kap[high] + half_kappa[low, i + 2, tile(j)]
                outside[low].append(minus)
                outside[high].append(plus)
                outer_x[at, i, tile(j)] = minus
                off[0].append(minus)

                low, high = cls(p, 0, q), cls(p, 1, q)
                side = at_.row_before(lambda r: half_kappa[high, i + 1, tile(r)], j)
                minus = kap[low] + masked(y_low[j], side)
                side = at_.row_after(lambda r: half_kappa[low, i + 1, tile(r)], j)
                plus = kap[high] + masked(y_high[j], side)
                outside[low].append(minus)
                outside[high].append(plus)
                minus, plus = masked(y_low[j], minus), masked(y_high[j], plus)
                outer_y[at, i, tile(j)] = minus
                off[1].append(minus)
                off[2].append(plus)

                low, high = cls(p, q, 0), cls(p, q, 1)
                minus = kap[low] + z_low * roll(kap[high], 1, 1)
                plus = kap[high] + z_high * roll(kap[low], -1, 1)
                outside[low].append(minus)
                outside[high].append(plus)
                minus, plus = z_low * minus, z_high * plus
                outer_z[at, i, tile(j)] = minus
                outer_z[4 + at, i, tile(j)] = plus
                off[3].append(minus)
                off[4].append(plus)
            coarse_total = []
            for k in range(8):
                within, without = tree_sum(inside[k]), tree_sum(outside[k])
                inner_sum[k, i, tile(j)] = within
                base = within + without + shift
                diagonal[k, i, tile(j)] = base
                coarse_total.append(without)
                damped[k, i, tile(j)] = (DAMPING / KEPT) * inverse(base)
            for at, part in enumerate(off):
                coarse_off[at, i, tile(j)] = tree_sum(part)
            coarse_damped[i, tile(j)] = DAMPING * inverse(tree_sum(coarse_total) + 8.0 * shift)
        return carry

    lax.fori_loop(0, half, plane, 0, unroll=UNROLL)
    for j in range(tiles):
        part = []
        for p, q in PAIRS:
            face = half_kappa[cls(0, p, q), half + 1, tile(j)]
            face = face + half_kappa[cls(1, p, q), half, tile(j)]
            outer_x[2 * p + q, half, tile(j)] = face
            part.append(face)
        coarse_off[0, half, tile(j)] = tree_sum(part)


def solve_kernel(
    place_ref,
    weights_ref,
    order_ref,
    mine_ref,
    theirs_ref,
    state_ref,
    far_ref,
    near_ref,
    inner,
    outer_x,
    outer_y,
    outer_z,
    inner_sum,
    diagonal,
    damped,
    coarse_off,
    coarse_damped,
    adjoint_ref,
    keep_ref,
    partner_ref,
    send_ref,
    residual,
    scaled,
    partial,
    first_dir,
    second_dir,
    image,
    coarse_one,
    coarse_two,
    planes,
):
    half, rows = inner.shape[1:3]
    at_ = Layout(rows)
    tile, tiles, zero = at_.tile, at_.tiles, at_.zero
    core = place_ref[0] % 2
    weight = weights_ref[order_ref[core]]

    def begin(k, spot, j, value):
        res = (KEPT * weight) * value
        residual[k, spot, tile(j)] = res
        scaled[k, spot + 1, tile(j)] = damped[k, spot, tile(j)] * res

    at_.arrange(mine_ref, theirs_ref, place_ref[0], True, begin)
    at_.seam_fine(scaled)

    def rows_of(ref, i):
        cache = {}

        def load(k, j, step):
            if abs(j - step) > 1:
                return ref[k, i, tile(j)]
            if (k, j) not in cache:
                cache[k, j] = ref[k, i, tile(j)]
            return cache[k, j]

        def get(k, j):
            return load(k, j, j)

        def before(k, j):
            return at_.row_before(lambda r: load(k, r, j), j)

        def after(k, j):
            return at_.row_after(lambda r: load(k, r, j), j)

        return get, before, after

    def stencil(field, i, both):
        get, before, after = rows_of(field, i + 1)
        face_get, _, face_after = rows_of(outer_y, i)
        for j in range(tiles):
            here = [get(k, j) for k in range(8)]
            terms = [[] for _ in range(8)]
            for p, q in PAIRS:
                at = 2 * p + q
                for face_at, low, high in inner_faces(p, q):
                    face = inner[face_at, i, tile(j)]
                    terms[low].append(face * here[high])
                    if both:
                        terms[high].append(face * here[low])
                low, high = cls(0, p, q), cls(1, p, q)
                terms[low].append(outer_x[at, i, tile(j)] * field[high, i, tile(j)])
                if both:
                    side = field[low, i + 2, tile(j)]
                    terms[high].append(outer_x[at, i + 1, tile(j)] * side)
                low, high = cls(p, 0, q), cls(p, 1, q)
                terms[low].append(face_get(at, j) * before(high, j))
                if both:
                    terms[high].append(face_after(at, j) * after(low, j))
                low, high = cls(p, q, 0), cls(p, q, 1)
                terms[low].append(outer_z[at, i, tile(j)] * roll(here[high], 1, 1))
                if both:
                    terms[high].append(outer_z[4 + at, i, tile(j)] * roll(here[low], -1, 1))
            yield j, here, [tree_sum(part) if part else None for part in terms]

    def coarse_sides(field, i, j):
        here = field[0, i + 1, tile(j)]
        return here, (
            (field[0, i, tile(j)], field[0, i + 2, tile(j)]),
            (
                at_.row_before(lambda r: field[0, i + 1, tile(r)], j),
                at_.row_after(lambda r: field[0, i + 1, tile(r)], j),
            ),
            (roll(here, 1, 1), roll(here, -1, 1)),
        )

    def precondition(result):
        def down(i, carry):
            for j, _, sums in stencil(scaled, i, True):
                res = [residual[k, i, tile(j)] for k in range(8)]
                parts = [res[k] + sums[k] for k in range(8)]
                for k in range(8):
                    partial[k, i, tile(j)] = parts[k]
                rhs = tree_sum(parts) - (1.0 / KEPT) * tree_sum(res)
                coarse_one[0, i + 1, tile(j)] = coarse_damped[i, tile(j)] * rhs
            return carry

        lax.fori_loop(0, half, down, 0, unroll=UNROLL)
        at_.seam(coarse_one, [0], [0])

        def smooth(i, carry):
            for j in range(tiles):
                here, sides = coarse_sides(coarse_one, i, j)
                total = coarse_off[0, i, tile(j)] * sides[0][0]
                total = total + coarse_off[0, i + 1, tile(j)] * sides[0][1]
                more = coarse_off[1, i, tile(j)] * sides[1][0]
                more = more + coarse_off[2, i, tile(j)] * sides[1][1]
                most = coarse_off[3, i, tile(j)] * sides[2][0]
                most = most + coarse_off[4, i, tile(j)] * sides[2][1]
                coarse_two[0, i + 1, tile(j)] = KEPT * here + coarse_damped[
                    i, tile(j)
                ] * (total + more + most)
            return carry

        lax.fori_loop(0, half, smooth, 0, unroll=UNROLL)
        at_.seam(coarse_two, [0], [0])

        def up(i, gamma):
            face_get, _, face_after = rows_of(outer_y, i)
            for j in range(tiles):
                here, sides = coarse_sides(coarse_two, i, j)
                kept = ((1.0 - DAMPING) / KEPT) * here
                dots = []
                for a, b, c in CLASSES:
                    k = cls(a, b, c)
                    value = tree_sum(
                        [
                            partial[k, i, tile(j)],
                            inner_sum[k, i, tile(j)] * here,
                            outer_x[2 * b + c, i + a, tile(j)] * sides[0][a],
                            (face_after if b else face_get)(2 * a + c, j) * sides[1][b],
                            outer_z[4 * c + 2 * a + b, i, tile(j)] * sides[2][c],
                        ]
                    )
                    new = kept + damped[k, i, tile(j)] * value
                    result[k, i + 1, tile(j)] = new
                    dots.append(residual[k, i, tile(j)] * new)
                gamma = gamma + tree_sum(dots)
            return gamma

        gamma = lax.fori_loop(0, half, up, zero, unroll=UNROLL)
        at_.seam_fine(result)
        return grand_total(gamma)

    gamma = precondition(first_dir)

    def apply(i, acc):
        for j, here, sums in stencil(first_dir, i, True):
            dots = []
            for k in range(8):
                value = diagonal[k, i, tile(j)] * here[k] - sums[k]
                image[k, i, tile(j)] = value
                dots.append(here[k] * value)
            acc = acc + tree_sum(dots)
        return acc

    curve = grand_total(lax.fori_loop(0, half, apply, zero, unroll=UNROLL))
    step_one = gamma / curve

    def update(i, carry):
        for j in range(tiles):
            for k in range(8):
                new = residual[k, i, tile(j)] - step_one * image[k, i, tile(j)]
                residual[k, i, tile(j)] = new
                scaled[k, i + 1, tile(j)] = damped[k, i, tile(j)] * new
        return carry

    lax.fori_loop(0, half, update, 0, unroll=UNROLL)
    at_.seam_fine(scaled)

    gamma_next = precondition(second_dir)

    def bend(i, carry):
        own_part, face_part = carry
        for j, here, sums in stencil(second_dir, i, False):
            own_part = own_part + tree_sum(
                [here[k] * (diagonal[k, i, tile(j)] * here[k]) for k in range(8)]
            )
            face_part = face_part + tree_sum([here[k] * sums[k] for k in range(7)])
        return own_part, face_part

    own_part, face_part = lax.fori_loop(0, half, bend, (zero, zero), unroll=UNROLL)
    ratio = gamma_next / gamma
    curve_next = grand_total(own_part - 2.0 * face_part)
    step_two = gamma_next / (curve_next - ratio * ratio * curve)
    step_first = (step_one + step_two * ratio) * (1.0 / KEPT)
    step_two = step_two * (1.0 / KEPT)

    own, ny, nz = adjoint_ref.shape
    start = (place_ref[0] - core) * (own // 2)
    upper = jnp.where(start >= half, 1, 0)
    start = start - half * upper
    even = at_.lane % 2 == 0
    source = at_.lane // 2 + HALF * upper
    for at in range(2 * own + 2):
        a = (at + 1) % 2
        spot = start + (at + 1) // 2
        for b in (0, 1):
            for j in range(tiles):
                both = [
                    step_first * first_dir[cls(a, b, c), spot, tile(j)]
                    + step_two * second_dir[cls(a, b, c), spot, tile(j)]
                    for c in (0, 1)
                ]
                planes[at, at_.every(b, j), :] = jnp.where(
                    even,
                    jnp.take_along_axis(both[0], source, axis=1),
                    jnp.take_along_axis(both[1], source, axis=1),
                )

    full = (ny, nz)
    y_at = row_index(full)
    z_at = lane_index(full)

    def drop(value, axis, up):
        moved = roll(value, -1 if up else 1, axis)
        at = (y_at, z_at)[axis]
        edge = full[axis] - 1 if up else 0
        return value - jnp.where(at == edge, 0.0, moved)

    is_even = core == 0
    state = [jnp.where(is_even, far_ref[core, 0], near_ref[own])]
    state += [jnp.where(is_even, state_ref[core, x], near_ref[x]) for x in range(own)]
    state += [jnp.where(is_even, near_ref[x], state_ref[core, x]) for x in range(own)]
    state += [jnp.where(is_even, near_ref[own], far_ref[core, 0])]
    terms = 2 * own + 2
    for x in range(2 * own):
        here, f = planes[x + 1], state[x + 1]
        term = (here - planes[x + 2]) * (f - state[x + 2])
        term = term + (here - planes[x]) * (f - state[x])
        for axis in (0, 1):
            for up in (True, False):
                term = term + drop(here, axis, up) * drop(f, axis, up)
        planes[terms + x] = -0.5 * term

    groups = send_ref.shape[0] + 1
    chunk = keep_ref.shape[1]
    for x in range(own):
        mine, other = core * own + x, (1 - core) * own + x
        adjoint_ref[x] = planes[1 + mine]
        partner_ref[x, :ny] = planes[1 + other]
        for k in range(groups):
            at = pl.multiple_of(lax.rem(place_ref[1] + k, groups) * chunk, chunk)
            for side, plane in enumerate((mine, other)):
                share = planes[terms + plane, pl.ds(at, chunk), :]
                if k:
                    send_ref[k - 1, side, x] = share
                elif side:
                    partner_ref[x, ny:] = share
                else:
                    keep_ref[x] = share


def whole_grid(conductivity, misfit, forward_states, pole_shifts, pole_weights, pole_order):
    members, own, ny, nz = forward_states.shape
    groups = lax.axis_size("pole")
    place = jnp.stack([lax.axis_index("space"), lax.axis_index("pole")]).astype(jnp.int32)
    peers = lax.axis_size("space")
    mine, theirs, far, near = gather_blocks(
        place, [conductivity, misfit], forward_states, "space"
    )
    half, rows = peers * own // 4, ny // 2

    def field(count, extent):
        return (count, extent, rows, 2 * HALF)

    def held(*shape):
        return pltpu.VMEM(shape, jnp.float32)

    smem = pl.BlockSpec(memory_space=pltpu.SMEM)
    vmem = pl.BlockSpec(memory_space=pltpu.VMEM)
    shapes = [
        field(12, half),
        field(4, half + 1),
        field(4, half),
        field(8, half),
        field(8, half),
        field(8, half),
        field(8, half),
        field(5, half + 1),
        (half, rows, 2 * HALF),
    ]
    coefficients = pl.pallas_call(
        setup_kernel,
        out_shape=[jax.ShapeDtypeStruct(shape, jnp.float32) for shape in shapes],
        in_specs=[smem] * 3 + [vmem] * 2,
        out_specs=[vmem] * len(shapes),
        scratch_shapes=[held(*field(8, half + 2))],
        compiler_params=pltpu.CompilerParams(vmem_limit_bytes=6 * 1024 * 1024),
        name="setup",
    )(place, pole_shifts, pole_order, mine[0], theirs[0])
    chunk = ny // groups
    adjoint, gradient, partner, send = pl.pallas_call(
        solve_kernel,
        out_shape=[
            jax.ShapeDtypeStruct((own, ny, nz), jnp.float32),
            jax.ShapeDtypeStruct((own, chunk, nz), jnp.float32),
            jax.ShapeDtypeStruct((own, ny + chunk, nz), jnp.float32),
            jax.ShapeDtypeStruct((groups - 1, 2, own, chunk, nz), jnp.float32),
        ],
        in_specs=[smem] * 3 + [vmem] * (5 + len(shapes)),
        out_specs=[vmem] * 4,
        scratch_shapes=[
            held(*field(8, half)),
            held(*field(8, half + 2)),
            held(*field(8, half)),
            held(*field(8, half + 2)),
            held(*field(8, half + 2)),
            held(*field(8, half)),
            held(*field(1, half + 2)),
            held(*field(1, half + 2)),
            held(4 * own + 2, ny, nz),
        ],
        compiler_params=pltpu.CompilerParams(vmem_limit_bytes=12 * 1024 * 1024),
        name="solve",
    )(
        place,
        pole_weights,
        pole_order,
        mine[1],
        theirs[1],
        forward_states,
        far,
        near,
        *coefficients,
    )

    arrived = lax.ppermute(partner, "space", [(i, i ^ 1) for i in range(peers)])
    shares = []
    for k in range(1, groups):
        for side in (0, 1):
            pairs = [
                (i * peers + j, (i + k) % groups * peers + (j ^ side))
                for i in range(groups)
                for j in range(peers)
            ]
            shares.append(lax.ppermute(send[k - 1, side], ("pole", "space"), pairs))
    even = place[0] % 2 == 0
    theirs = arrived[:, :ny]
    adjoint_states = jnp.stack(
        [jnp.where(even, adjoint, theirs), jnp.where(even, theirs, adjoint)]
    )
    adjoint_states, arrived = lax.optimization_barrier((adjoint_states, arrived))
    return adjoint_states, gradient + arrived[:, ny:] + sum(shares)


def plus_side(field, which_dim):
    extent = field.shape[which_dim]
    inner_part = lax.slice_in_dim(field, 1, extent, axis=which_dim)
    zero_plane = jnp.zeros_like(lax.slice_in_dim(field, 0, 1, axis=which_dim))
    return jnp.concatenate([inner_part, zero_plane], axis=which_dim)


def minus_side(field, which_dim):
    extent = field.shape[which_dim]
    inner_part = lax.slice_in_dim(field, 0, extent - 1, axis=which_dim)
    zero_plane = jnp.zeros_like(lax.slice_in_dim(field, 0, 1, axis=which_dim))
    return jnp.concatenate([zero_plane, inner_part], axis=which_dim)


def coarse_pick(faces, which_dim, offset):
    extent_x, extent_y, extent_z = faces.shape
    blocks = faces.reshape(extent_x // 2, 2, extent_y // 2, 2, extent_z // 2, 2)
    chosen = lax.index_in_dim(blocks, offset, axis=2 * which_dim + 1, keepdims=True)
    return jnp.sum(chosen, axis=(1, 3, 5))


def side_terms(field, plus_faces, minus_faces, widened):
    result = plus_faces[0] * (field - widened[:, 2:]) + minus_faces[0] * (field - widened[:, :-2])
    for which_dim in (1, 2):
        result = result + plus_faces[which_dim] * (field - plus_side(field, which_dim + 1))
        result = result + minus_faces[which_dim] * (field - minus_side(field, which_dim + 1))
    return result


def fine_image(field, plus_faces, minus_faces, shift_value):
    widened = extended(field, (("space", 1),), 1)
    return shift_value * field + side_terms(field, plus_faces, minus_faces, widened)


def coarse_image(field, plus_faces, minus_faces, shift_value):
    widened = extended(field, (("space", 1),), 1)
    return shift_value * field + side_terms(field, plus_faces, minus_faces, widened)


def restrict(field):
    members, extent_x, extent_y, extent_z = field.shape
    shaped = field.reshape(members, extent_x // 2, 2, extent_y // 2, 2, extent_z // 2, 2)
    return jnp.sum(shaped, axis=(2, 4, 6))


def prolong(field):
    return jnp.repeat(jnp.repeat(jnp.repeat(field, 2, axis=1), 2, axis=2), 2, axis=3)


def precondition(residual, fine, coarse):
    plus_faces, minus_faces, shift_value, diagonal = fine
    coarse_plus, coarse_minus, coarse_shift, coarse_diagonal = coarse
    smooth_one = DAMPING * residual / diagonal
    coarse_rhs = restrict(residual - fine_image(smooth_one, plus_faces, minus_faces, shift_value))
    coarse_one = DAMPING * coarse_rhs / coarse_diagonal
    coarse_two = (
        coarse_one
        + DAMPING
        * (coarse_rhs - coarse_image(coarse_one, coarse_plus, coarse_minus, coarse_shift))
        / coarse_diagonal
    )
    corrected = smooth_one + prolong(coarse_two)
    return (
        corrected
        + DAMPING
        * (residual - fine_image(corrected, plus_faces, minus_faces, shift_value))
        / diagonal
    )


def expand(values):
    return values.reshape(-1, 1, 1, 1)


def cell_sums(values):
    return jnp.sum(values, axis=(1, 2, 3))


def norm_sum(residual, precond):
    return lax.psum(cell_sums(residual * precond), "space")


def solve(rhs, fine, coarse):
    plus_faces, minus_faces, shift_value, diagonal = fine
    iterate = jnp.zeros_like(rhs)
    residual = rhs
    precond = precondition(residual, fine, coarse)
    gamma_now = norm_sum(residual, precond)
    search = precond
    for turn_index in range(ITERS):
        image_field = fine_image(search, plus_faces, minus_faces, shift_value)
        curve = lax.psum(cell_sums(search * image_field), "space")
        step_length = gamma_now / curve
        iterate = iterate + expand(step_length) * search
        if turn_index + 1 < ITERS:
            residual = residual - expand(step_length) * image_field
            precond = precondition(residual, fine, coarse)
            gamma_next = norm_sum(residual, precond)
            search = precond + expand(gamma_next / gamma_now) * search
            gamma_now = gamma_next
    return iterate


def divided(conductivity, misfit, forward_states, pole_shifts, pole_weights, pole_order):
    widened_kappa = extended(conductivity, (("space", 0),), 1)
    plus_faces = [
        0.5 * (conductivity + widened_kappa[2:]),
        0.5 * (conductivity + plus_side(conductivity, 1)),
        0.5 * (conductivity + plus_side(conductivity, 2)),
    ]
    minus_faces = [
        0.5 * (conductivity + widened_kappa[:-2]),
        0.5 * (conductivity + minus_side(conductivity, 1)),
        0.5 * (conductivity + minus_side(conductivity, 2)),
    ]
    base_diagonal = (
        plus_faces[0]
        + plus_faces[1]
        + plus_faces[2]
        + minus_faces[0]
        + minus_faces[1]
        + minus_faces[2]
    )
    coarse_plus = [coarse_pick(plus_faces[which_dim], which_dim, 1) for which_dim in range(3)]
    coarse_minus = [coarse_pick(minus_faces[which_dim], which_dim, 0) for which_dim in range(3)]
    coarse_base = (
        coarse_plus[0]
        + coarse_plus[1]
        + coarse_plus[2]
        + coarse_minus[0]
        + coarse_minus[1]
        + coarse_minus[2]
    )
    pole_index = jnp.arange(pole_shifts.shape[0], dtype=jnp.int32)
    matches = pole_order[:, None] == pole_index[None, :]
    shift_local = jnp.sum(jnp.where(matches, pole_shifts[None, :], 0.0), axis=1)
    weight_local = jnp.sum(jnp.where(matches, pole_weights[None, :], 0.0), axis=1)
    members = forward_states.shape[0]

    def solve_group(shift_part, weight_part):
        shift_value = expand(shift_part)
        fine = (plus_faces, minus_faces, shift_value, base_diagonal[None] + shift_value)
        coarse = (
            coarse_plus,
            coarse_minus,
            8.0 * shift_value,
            coarse_base[None] + 8.0 * shift_value,
        )
        return solve(expand(weight_part) * misfit[None], fine, coarse)

    adjoint_states = jnp.concatenate(
        [
            solve_group(shift_local[member : member + 1], weight_local[member : member + 1])
            for member in range(members)
        ],
        axis=0,
    )
    widened = extended(jnp.stack([adjoint_states, forward_states]), (("space", 2),), 1)
    term = (adjoint_states - widened[0, :, 2:]) * (forward_states - widened[1, :, 2:])
    term = term + (adjoint_states - widened[0, :, :-2]) * (forward_states - widened[1, :, :-2])
    for which_dim in (2, 3):
        term = term + (adjoint_states - plus_side(adjoint_states, which_dim)) * (
            forward_states - plus_side(forward_states, which_dim)
        )
        term = term + (adjoint_states - minus_side(adjoint_states, which_dim)) * (
            forward_states - minus_side(forward_states, which_dim)
        )
    local_term = -0.5 * jnp.sum(term, axis=0)
    gradient = lax.psum_scatter(local_term, "pole", scatter_dimension=1, tiled=True)
    return (adjoint_states, gradient)


def solution(mesh):
    in_specs = (
        P("space", None, None),
        P("space", None, None),
        P("pole", "space", None, None),
        P(),
        P(),
        P("pole"),
    )
    out_specs = (P("pole", "space", None, None), P("space", "pole", None))

    def body(conductivity, misfit, forward_states, *poles):
        nx = conductivity.shape[0] * lax.axis_size("space")
        _, ny, nz = conductivity.shape
        peers = lax.axis_size("space")
        small = nx * ny * nz <= REPLICATED_CELLS and forward_states.shape[:2] == (2, 2)
        if small and nz == 2 * HALF and peers > 2 and peers & (peers - 1) == 0:
            return whole_grid(conductivity, misfit, forward_states, *poles)
        return divided(conductivity, misfit, forward_states, *poles)

    return jax.shard_map(
        body, mesh=mesh, in_specs=in_specs, out_specs=out_specs, check_vma=False
    )
```

```python
import functools

import jax
import jax.numpy as jnp
from jax import lax
from jax.experimental import pallas as pl
from jax.experimental.pallas import tpu as pltpu
from jax.sharding import PartitionSpec as P

ITERS = 2
DAMPING = 0.8
KEPT = 2.0 - DAMPING
REPLICATED_CELLS = 32 * 64 * 128
HALF = 64
TILE = 8
UNROLL = 8


def extended(array, sides, width):
    for axis, dim in sides:
        peers, length = (lax.axis_size(axis), array.shape[dim])
        up = [(i, (i + 1) % peers) for i in range(peers - 1)]
        down = [(j, i) for i, j in up]
        last = lax.slice_in_dim(array, length - width, length, axis=dim)
        leading = lax.slice_in_dim(array, 0, width, axis=dim)
        before = lax.ppermute(last, axis, up)
        after = lax.ppermute(leading, axis, down)
        array = jnp.concatenate([before, array, after], axis=dim)
    return array


def lane_index(shape):
    return lax.broadcasted_iota(jnp.int32, shape, len(shape) - 1)


def row_index(shape):
    return lax.broadcasted_iota(jnp.int32, shape, len(shape) - 2)


def roll(block, shift, axis):
    return pltpu.roll(block, shift % block.shape[axis], axis)


def inverse(value):
    guess = pl.reciprocal(value, approx=True)
    return guess * (2.0 - value * guess)


def tree_sum(values):
    while len(values) > 1:
        values = [sum(values[at : at + 2]) for at in range(0, len(values), 2)]
    return values[0]


def grand_total(acc):
    line = jnp.sum(acc, axis=0, keepdims=True)
    return jnp.broadcast_to(jnp.sum(line, axis=1, keepdims=True), acc.shape)


def swap_masks(peers, flip):
    falling = []
    mask = peers // 2
    while mask > 1:
        falling.append(mask)
        mask //= 2
    if flip:
        return falling[::-1], falling[:1] + falling[:0:-1]
    return falling, falling[-1:] + falling[:-1]


def block_pair(u, holder, peers, flip):
    even, odd = swap_masks(peers, flip)
    parity = holder % 2
    top = jnp.where(parity == 0, even.index(peers // 2), odd.index(peers // 2))
    below = u & ((1 << top) - 1)
    base = ((u >> top) << (top + 1)) | below
    upper = jnp.where(holder >= peers // 2, 1, 0)
    first = base | (upper << top)
    second = base | ((1 - upper) << top)
    home = holder
    for step, (mask_even, mask_odd) in enumerate(zip(even, odd)):
        mask = jnp.where(parity == 0, mask_even, mask_odd)
        home = home ^ (((first >> step) & 1) * mask)
    return first, second, home


def prepare_kernel(kappa_ref, misfit_ref, kappa_out, misfit_out, *, axis, peers):
    at_ = Layout(kappa_ref.shape[1] // 2)
    upper = jnp.where(lax.axis_index(axis) >= peers // 2, 1, 0)
    at_.deal(kappa_ref, kappa_out, upper)
    at_.deal(misfit_ref, misfit_out, upper)


def join_kernel(*refs, masks, axis, peers):
    place = lax.axis_index(axis)
    at_ = Layout(refs[0].shape[1] // 2)
    for at, (even, odd) in enumerate(masks):
        partner = place ^ jnp.where(place % 2 == 0, even, odd)
        refs[4 + at][0] = refs[at][...]
        at_.deal(refs[2 + at], refs[4 + at].at[1], jnp.where(partner >= peers // 2, 1, 0))


def gather_blocks(blocks, states, axis):
    peers = lax.axis_size(axis)
    even = lax.axis_index(axis) % 2 == 0
    swap = [(i, i ^ 1) for i in range(peers)]
    over = [(i, i + 1 if i % 2 else i - 1) for i in range(1, peers - 1)]
    vmem = pl.BlockSpec(memory_space=pltpu.VMEM)
    swaps = [list(zip(*swap_masks(peers, flip))) for flip in (False, True)]
    own = pl.pallas_call(
        functools.partial(prepare_kernel, axis=axis, peers=peers),
        out_shape=[jax.ShapeDtypeStruct(block.shape, jnp.float32) for block in blocks],
        in_specs=[vmem] * 2,
        out_specs=[vmem] * 2,
        compiler_params=pltpu.CompilerParams(vmem_limit_bytes=1024 * 1024),
        name="prepare",
    )(*blocks)
    held = list(blocks)
    for step in range(len(swaps[0])):
        arrived = []
        for at in (0, 1):
            masks = swaps[at][step]
            pairs = [(i, i ^ masks[i % 2]) for i in range(peers)]
            arrived.append(lax.ppermute(held[at], axis, pairs))
        if step:
            held = [jnp.concatenate(pair, axis=0) for pair in zip(held, arrived)]
            continue
        masks = [swaps[at][0] for at in (0, 1)]
        shape = jax.ShapeDtypeStruct((2, *blocks[0].shape), jnp.float32)
        held[:] = pl.pallas_call(
            functools.partial(join_kernel, masks=masks, axis=axis, peers=peers),
            out_shape=[shape] * 2,
            in_specs=[vmem] * 4,
            out_specs=[vmem] * 2,
            compiler_params=pltpu.CompilerParams(vmem_limit_bytes=1024 * 1024),
            name="join",
        )(*own, *arrived)
        held[1], states = lax.optimization_barrier((held[1], states))
        far = lax.ppermute(jnp.where(even, states[:, :1], states[:, -1:]), axis, over)
    held[1], far = lax.optimization_barrier((held[1], far))
    given = jnp.concatenate([states, far], axis=1)
    near = lax.ppermute(jnp.where(even, given[1], given[0]), axis, swap)
    other = [lax.ppermute(part, axis, swap) for part in held]
    return held, other, far, near


CLASSES = [(a, b, c) for a in (0, 1) for b in (0, 1) for c in (0, 1)]
PAIRS = [(p, q) for p in (0, 1) for q in (0, 1)]


def cls(a, b, c):
    return 4 * a + 2 * b + c


def inner_faces(p, q):
    return (
        (2 * p + q, cls(0, p, q), cls(1, p, q)),
        (4 + 2 * p + q, cls(p, 0, q), cls(p, 1, q)),
        (8 + 2 * p + q, cls(p, q, 0), cls(p, q, 1)),
    )


class Layout:
    def __init__(self, rows):
        self.tiles = rows // TILE
        self.lane = lane_index((TILE, 2 * HALF))
        self.row = row_index((TILE, 2 * HALF))
        self.left = self.lane < HALF
        self.zero = jnp.zeros((TILE, 2 * HALF), jnp.float32)

    def tile(self, j):
        return pl.ds(TILE * j, TILE)

    def every(self, b, j):
        return pl.ds(b + 2 * j, TILE, stride=2 * self.tiles)

    def row_before(self, load, j):
        return load(j - 1) if j else roll(load(self.tiles - 1), 1, 0)

    def row_after(self, load, j):
        return load(j + 1) if j + 1 < self.tiles else roll(load(0), -1, 0)

    def seam(self, ref, low, high):
        last = ref.shape[1] - 1
        for j in range(self.tiles):
            for k in low:
                moved = roll(ref[k, last - 1, self.tile(j)], HALF, 1)
                ref[k, 0, self.tile(j)] = jnp.where(self.left, 0.0, moved)
            for k in high:
                moved = roll(ref[k, 1, self.tile(j)], HALF, 1)
                ref[k, last, self.tile(j)] = jnp.where(self.left, moved, 0.0)

    def seam_fine(self, ref):
        count = ref.shape[0]
        self.seam(
            ref,
            [k for k in range(count) if k % 8 >= 4],
            [k for k in range(count) if k % 8 < 4],
        )

    def dealt(self, b, j):
        return pl.ds(TILE * (self.tiles * b + j), TILE)

    def deal(self, block_ref, out_ref, upper):
        odd = jnp.where(self.left, upper, 1 - upper)
        column = 2 * (self.lane % HALF) + odd
        for x in range(block_ref.shape[0]):
            for b in (0, 1):
                for j in range(self.tiles):
                    rows = block_ref[x, self.every(b, j), :]
                    out_ref[x, self.dealt(b, j), :] = jnp.take_along_axis(rows, column, axis=1)

    def arrange(self, mine_ref, theirs_ref, place, flip, store):
        blocks, own = mine_ref.shape[:2]

        def pair(u, carry):
            for ref, holder in ((mine_ref, place), (theirs_ref, place ^ 1)):
                first, second, home = block_pair(u, holder, 2 * blocks, flip)
                for x in range(own):
                    spot = home * (own // 2) + x // 2
                    for b in (0, 1):
                        for j in range(self.tiles):
                            one = ref[first, x, self.dealt(b, j), :]
                            two = ref[second, x, self.dealt(b, j), :]
                            store(cls(x % 2, b, 0), spot, j, jnp.where(self.left, one, two))
                            odd = roll(jnp.where(self.left, two, one), HALF, 1)
                            store(cls(x % 2, b, 1), spot, j, odd)
            return carry

        lax.fori_loop(0, blocks // 2, pair, 0)


def setup_kernel(
    pole_ref,
    mine_ref,
    theirs_ref,
    inner,
    outer_x,
    outer_y,
    outer_z,
    inner_sum,
    diagonal,
    damped,
    coarse_off,
    coarse_damped,
    half_kappa,
):
    half = inner.shape[1]
    at_ = Layout(inner.shape[2])
    tile, tiles = at_.tile, at_.tiles
    shift = pole_ref[0] + at_.zero

    def keep(k, spot, j, value):
        half_kappa[k, spot + 1, tile(j)] = 0.5 * value

    at_.arrange(mine_ref, theirs_ref, lax.axis_index("space"), False, keep)
    at_.seam_fine(half_kappa)

    z_low = jnp.where(at_.lane % HALF > 0, 1.0, 0.0)
    z_high = jnp.where(at_.lane % HALF < HALF - 1, 1.0, 0.0)
    y_low = [jnp.where(at_.row > 0, 1.0, 0.0)] + [None] * (tiles - 1)
    y_high = [None] * (tiles - 1) + [jnp.where(at_.row < TILE - 1, 1.0, 0.0)]

    def masked(mask, value):
        return value if mask is None else mask * value

    def plane(i, carry):
        for j in range(tiles):
            kap = [half_kappa[k, i + 1, tile(j)] for k in range(8)]
            inside = [[] for _ in range(8)]
            outside = [[] for _ in range(8)]
            off = [[] for _ in range(5)]
            for p, q in PAIRS:
                for face_at, low, high in inner_faces(p, q):
                    face = kap[low] + kap[high]
                    inner[face_at, i, tile(j)] = face
                    inside[low].append(face)
                    inside[high].append(face)
                at = 2 * p + q

                low, high = cls(0, p, q), cls(1, p, q)
                minus = kap[low] + half_kappa[high, i, tile(j)]
                plus = kap[high] + half_kappa[low, i + 2, tile(j)]
                outside[low].append(minus)
                outside[high].append(plus)
                outer_x[at, i, tile(j)] = minus
                off[0].append(minus)

                low, high = cls(p, 0, q), cls(p, 1, q)
                side = at_.row_before(lambda r: half_kappa[high, i + 1, tile(r)], j)
                minus = kap[low] + masked(y_low[j], side)
                side = at_.row_after(lambda r: half_kappa[low, i + 1, tile(r)], j)
                plus = kap[high] + masked(y_high[j], side)
                outside[low].append(minus)
                outside[high].append(plus)
                minus, plus = masked(y_low[j], minus), masked(y_high[j], plus)
                outer_y[at, i, tile(j)] = minus
                off[1].append(minus)
                off[2].append(plus)

                low, high = cls(p, q, 0), cls(p, q, 1)
                minus = kap[low] + z_low * roll(kap[high], 1, 1)
                plus = kap[high] + z_high * roll(kap[low], -1, 1)
                outside[low].append(minus)
                outside[high].append(plus)
                minus, plus = z_low * minus, z_high * plus
                outer_z[at, i, tile(j)] = minus
                outer_z[4 + at, i, tile(j)] = plus
                off[3].append(minus)
                off[4].append(plus)
            coarse_total = []
            for k in range(8):
                within, without = tree_sum(inside[k]), tree_sum(outside[k])
                inner_sum[k, i, tile(j)] = within
                base = within + without + shift
                diagonal[k, i, tile(j)] = base
                coarse_total.append(without)
                damped[k, i, tile(j)] = (DAMPING / KEPT) * inverse(base)
            for at, part in enumerate(off):
                coarse_off[at, i, tile(j)] = tree_sum(part)
            coarse_damped[i, tile(j)] = DAMPING * inverse(tree_sum(coarse_total) + 8.0 * shift)
        return carry

    lax.fori_loop(0, half, plane, 0, unroll=UNROLL)
    for j in range(tiles):
        part = []
        for p, q in PAIRS:
            face = half_kappa[cls(0, p, q), half + 1, tile(j)]
            face = face + half_kappa[cls(1, p, q), half, tile(j)]
            outer_x[2 * p + q, half, tile(j)] = face
            part.append(face)
        coarse_off[0, half, tile(j)] = tree_sum(part)


def solve_kernel(
    pole_ref,
    mine_ref,
    theirs_ref,
    state_ref,
    far_ref,
    near_ref,
    inner,
    outer_x,
    outer_y,
    outer_z,
    inner_sum,
    diagonal,
    damped,
    coarse_off,
    coarse_damped,
    adjoint_ref,
    keep_ref,
    partner_ref,
    send_ref,
    residual,
    scaled,
    partial,
    first_dir,
    second_dir,
    image,
    coarse_one,
    coarse_two,
    planes,
):
    half, rows = inner.shape[1:3]
    at_ = Layout(rows)
    tile, tiles, zero = at_.tile, at_.tiles, at_.zero
    place = lax.axis_index("space")
    core = place % 2
    weight = KEPT * pole_ref[1] + zero

    def begin(k, spot, j, value):
        res = weight * value
        residual[k, spot, tile(j)] = res
        scaled[k, spot + 1, tile(j)] = damped[k, spot, tile(j)] * res

    at_.arrange(mine_ref, theirs_ref, place, True, begin)
    at_.seam_fine(scaled)

    def rows_of(ref, i):
        cache = {}

        def load(k, j, step):
            if abs(j - step) > 1:
                return ref[k, i, tile(j)]
            if (k, j) not in cache:
                cache[k, j] = ref[k, i, tile(j)]
            return cache[k, j]

        def get(k, j):
            return load(k, j, j)

        def before(k, j):
            return at_.row_before(lambda r: load(k, r, j), j)

        def after(k, j):
            return at_.row_after(lambda r: load(k, r, j), j)

        return get, before, after

    def stencil(field, i, both):
        get, before, after = rows_of(field, i + 1)
        face_get, _, face_after = rows_of(outer_y, i)
        for j in range(tiles):
            here = [get(k, j) for k in range(8)]
            terms = [[] for _ in range(8)]
            for p, q in PAIRS:
                at = 2 * p + q
                for face_at, low, high in inner_faces(p, q):
                    face = inner[face_at, i, tile(j)]
                    terms[low].append(face * here[high])
                    if both:
                        terms[high].append(face * here[low])
                low, high = cls(0, p, q), cls(1, p, q)
                terms[low].append(outer_x[at, i, tile(j)] * field[high, i, tile(j)])
                if both:
                    side = field[low, i + 2, tile(j)]
                    terms[high].append(outer_x[at, i + 1, tile(j)] * side)
                low, high = cls(p, 0, q), cls(p, 1, q)
                terms[low].append(face_get(at, j) * before(high, j))
                if both:
                    terms[high].append(face_after(at, j) * after(low, j))
                low, high = cls(p, q, 0), cls(p, q, 1)
                terms[low].append(outer_z[at, i, tile(j)] * roll(here[high], 1, 1))
                if both:
                    terms[high].append(outer_z[4 + at, i, tile(j)] * roll(here[low], -1, 1))
            yield j, here, [tree_sum(part) if part else None for part in terms]

    def coarse_sides(field, i, j):
        here = field[0, i + 1, tile(j)]
        return here, (
            (field[0, i, tile(j)], field[0, i + 2, tile(j)]),
            (
                at_.row_before(lambda r: field[0, i + 1, tile(r)], j),
                at_.row_after(lambda r: field[0, i + 1, tile(r)], j),
            ),
            (roll(here, 1, 1), roll(here, -1, 1)),
        )

    def precondition(result):
        def down(i, carry):
            for j, _, sums in stencil(scaled, i, True):
                res = [residual[k, i, tile(j)] for k in range(8)]
                parts = [res[k] + sums[k] for k in range(8)]
                for k in range(8):
                    partial[k, i, tile(j)] = parts[k]
                rhs = tree_sum(parts) - (1.0 / KEPT) * tree_sum(res)
                coarse_one[0, i + 1, tile(j)] = coarse_damped[i, tile(j)] * rhs
            return carry

        lax.fori_loop(0, half, down, 0, unroll=UNROLL)
        at_.seam(coarse_one, [0], [0])

        def smooth(i, carry):
            for j in range(tiles):
                here, sides = coarse_sides(coarse_one, i, j)
                total = coarse_off[0, i, tile(j)] * sides[0][0]
                total = total + coarse_off[0, i + 1, tile(j)] * sides[0][1]
                more = coarse_off[1, i, tile(j)] * sides[1][0]
                more = more + coarse_off[2, i, tile(j)] * sides[1][1]
                most = coarse_off[3, i, tile(j)] * sides[2][0]
                most = most + coarse_off[4, i, tile(j)] * sides[2][1]
                coarse_two[0, i + 1, tile(j)] = KEPT * here + coarse_damped[
                    i, tile(j)
                ] * (total + more + most)
            return carry

        lax.fori_loop(0, half, smooth, 0, unroll=UNROLL)
        at_.seam(coarse_two, [0], [0])

        def up(i, gamma):
            face_get, _, face_after = rows_of(outer_y, i)
            for j in range(tiles):
                here, sides = coarse_sides(coarse_two, i, j)
                kept = ((1.0 - DAMPING) / KEPT) * here
                dots = []
                for a, b, c in CLASSES:
                    k = cls(a, b, c)
                    value = tree_sum(
                        [
                            partial[k, i, tile(j)],
                            inner_sum[k, i, tile(j)] * here,
                            outer_x[2 * b + c, i + a, tile(j)] * sides[0][a],
                            (face_after if b else face_get)(2 * a + c, j) * sides[1][b],
                            outer_z[4 * c + 2 * a + b, i, tile(j)] * sides[2][c],
                        ]
                    )
                    new = kept + damped[k, i, tile(j)] * value
                    result[k, i + 1, tile(j)] = new
                    dots.append(residual[k, i, tile(j)] * new)
                gamma = gamma + tree_sum(dots)
            return gamma

        gamma = lax.fori_loop(0, half, up, zero, unroll=UNROLL)
        at_.seam_fine(result)
        return grand_total(gamma)

    gamma = precondition(first_dir)

    def apply(i, acc):
        for j, here, sums in stencil(first_dir, i, True):
            dots = []
            for k in range(8):
                value = diagonal[k, i, tile(j)] * here[k] - sums[k]
                image[k, i, tile(j)] = value
                dots.append(here[k] * value)
            acc = acc + tree_sum(dots)
        return acc

    curve = grand_total(lax.fori_loop(0, half, apply, zero, unroll=UNROLL))
    step_one = gamma / curve

    def update(i, carry):
        for j in range(tiles):
            for k in range(8):
                new = residual[k, i, tile(j)] - step_one * image[k, i, tile(j)]
                residual[k, i, tile(j)] = new
                scaled[k, i + 1, tile(j)] = damped[k, i, tile(j)] * new
        return carry

    lax.fori_loop(0, half, update, 0, unroll=UNROLL)
    at_.seam_fine(scaled)

    gamma_next = precondition(second_dir)

    def bend(i, carry):
        own_part, face_part = carry
        for j, here, sums in stencil(second_dir, i, False):
            own_part = own_part + tree_sum(
                [here[k] * (diagonal[k, i, tile(j)] * here[k]) for k in range(8)]
            )
            face_part = face_part + tree_sum([here[k] * sums[k] for k in range(7)])
        return own_part, face_part

    own_part, face_part = lax.fori_loop(0, half, bend, (zero, zero), unroll=UNROLL)
    ratio = gamma_next / gamma
    curve_next = grand_total(own_part - 2.0 * face_part)
    step_two = gamma_next / (curve_next - ratio * ratio * curve)
    step_first = (step_one + step_two * ratio) * (1.0 / KEPT)
    step_two = step_two * (1.0 / KEPT)

    own, ny, nz = adjoint_ref.shape
    start = (place - core) * (own // 2)
    upper = jnp.where(start >= half, 1, 0)
    start = start - half * upper
    even = at_.lane % 2 == 0
    source = at_.lane // 2 + HALF * upper
    for at in range(2 * own + 2):
        a = (at + 1) % 2
        spot = start + (at + 1) // 2
        for b in (0, 1):
            for j in range(tiles):
                both = [
                    step_first * first_dir[cls(a, b, c), spot, tile(j)]
                    + step_two * second_dir[cls(a, b, c), spot, tile(j)]
                    for c in (0, 1)
                ]
                planes[at, at_.every(b, j), :] = jnp.where(
                    even,
                    jnp.take_along_axis(both[0], source, axis=1),
                    jnp.take_along_axis(both[1], source, axis=1),
                )

    full = (ny, nz)
    y_at = row_index(full)
    z_at = lane_index(full)

    def drop(value, axis, up):
        moved = roll(value, -1 if up else 1, axis)
        at = (y_at, z_at)[axis]
        edge = full[axis] - 1 if up else 0
        return value - jnp.where(at == edge, 0.0, moved)

    is_even = core == 0
    state = [jnp.where(is_even, far_ref[core, 0], near_ref[own])]
    state += [jnp.where(is_even, state_ref[core, x], near_ref[x]) for x in range(own)]
    state += [jnp.where(is_even, near_ref[x], state_ref[core, x]) for x in range(own)]
    state += [jnp.where(is_even, near_ref[own], far_ref[core, 0])]
    terms = 2 * own + 2
    for x in range(2 * own):
        here, f = planes[x + 1], state[x + 1]
        term = (here - planes[x + 2]) * (f - state[x + 2])
        term = term + (here - planes[x]) * (f - state[x])
        for axis in (0, 1):
            for up in (True, False):
                term = term + drop(here, axis, up) * drop(f, axis, up)
        planes[terms + x] = -0.5 * term

    groups = send_ref.shape[0] + 1
    chunk = keep_ref.shape[1]
    for x in range(own):
        mine, other = core * own + x, (1 - core) * own + x
        adjoint_ref[x] = planes[1 + mine]
        partner_ref[x, :ny] = planes[1 + other]
        for k in range(groups):
            at = pl.multiple_of(lax.rem(lax.axis_index("pole") + k, groups) * chunk, chunk)
            for side, plane in enumerate((mine, other)):
                share = planes[terms + plane, pl.ds(at, chunk), :]
                if k:
                    send_ref[k - 1, side, x] = share
                elif side:
                    partner_ref[x, ny:] = share
                else:
                    keep_ref[x] = share


def whole_grid(conductivity, misfit, forward_states, pole_shifts, pole_weights, pole_order):
    members, own, ny, nz = forward_states.shape
    groups = lax.axis_size("pole")
    peers = lax.axis_size("space")
    even = lax.axis_index("space") % 2 == 0
    pole = jnp.where(even, pole_order[0], pole_order[1])
    chosen = jnp.arange(pole_shifts.shape[0], dtype=jnp.int32) == pole
    scalars = jnp.sum(jnp.where(chosen, jnp.stack([pole_shifts, pole_weights]), 0.0), axis=1)
    scalars = jnp.broadcast_to(scalars[:, None, None], (2, 1, nz))
    mine, theirs, far, near = gather_blocks([conductivity, misfit], forward_states, "space")
    half, rows = peers * own // 4, ny // 2

    def field(count, extent):
        return (count, extent, rows, 2 * HALF)

    def held(*shape):
        return pltpu.VMEM(shape, jnp.float32)

    vmem = pl.BlockSpec(memory_space=pltpu.VMEM)
    shapes = [
        field(12, half),
        field(4, half + 1),
        field(4, half),
        field(8, half),
        field(8, half),
        field(8, half),
        field(8, half),
        field(5, half + 1),
        (half, rows, 2 * HALF),
    ]
    coefficients = pl.pallas_call(
        setup_kernel,
        out_shape=[jax.ShapeDtypeStruct(shape, jnp.float32) for shape in shapes],
        in_specs=[vmem] * 3,
        out_specs=[vmem] * len(shapes),
        scratch_shapes=[held(*field(8, half + 2))],
        compiler_params=pltpu.CompilerParams(vmem_limit_bytes=6 * 1024 * 1024),
        name="setup",
    )(scalars, mine[0], theirs[0])
    chunk = ny // groups
    adjoint, gradient, partner, send = pl.pallas_call(
        solve_kernel,
        out_shape=[
            jax.ShapeDtypeStruct((own, ny, nz), jnp.float32),
            jax.ShapeDtypeStruct((own, chunk, nz), jnp.float32),
            jax.ShapeDtypeStruct((own, ny + chunk, nz), jnp.float32),
            jax.ShapeDtypeStruct((groups - 1, 2, own, chunk, nz), jnp.float32),
        ],
        in_specs=[vmem] * (6 + len(shapes)),
        out_specs=[vmem] * 4,
        scratch_shapes=[
            held(*field(8, half)),
            held(*field(8, half + 2)),
            held(*field(8, half)),
            held(*field(8, half + 2)),
            held(*field(8, half + 2)),
            held(*field(8, half)),
            held(*field(1, half + 2)),
            held(*field(1, half + 2)),
            held(4 * own + 2, ny, nz),
        ],
        compiler_params=pltpu.CompilerParams(vmem_limit_bytes=12 * 1024 * 1024),
        name="solve",
    )(
        scalars,
        mine[1],
        theirs[1],
        forward_states,
        far,
        near,
        *coefficients,
    )

    arrived = lax.ppermute(partner, "space", [(i, i ^ 1) for i in range(peers)])
    shares = []
    for k in range(1, groups):
        for side in (0, 1):
            pairs = [
                (i * peers + j, (i + k) % groups * peers + (j ^ side))
                for i in range(groups)
                for j in range(peers)
            ]
            shares.append(lax.ppermute(send[k - 1, side], ("pole", "space"), pairs))
    theirs = arrived[:, :ny]
    adjoint_states = jnp.stack(
        [jnp.where(even, adjoint, theirs), jnp.where(even, theirs, adjoint)]
    )
    adjoint_states, arrived = lax.optimization_barrier((adjoint_states, arrived))
    return adjoint_states, gradient + arrived[:, ny:] + sum(shares)


def plus_side(field, which_dim):
    extent = field.shape[which_dim]
    inner_part = lax.slice_in_dim(field, 1, extent, axis=which_dim)
    zero_plane = jnp.zeros_like(lax.slice_in_dim(field, 0, 1, axis=which_dim))
    return jnp.concatenate([inner_part, zero_plane], axis=which_dim)


def minus_side(field, which_dim):
    extent = field.shape[which_dim]
    inner_part = lax.slice_in_dim(field, 0, extent - 1, axis=which_dim)
    zero_plane = jnp.zeros_like(lax.slice_in_dim(field, 0, 1, axis=which_dim))
    return jnp.concatenate([zero_plane, inner_part], axis=which_dim)


def coarse_pick(faces, which_dim, offset):
    extent_x, extent_y, extent_z = faces.shape
    blocks = faces.reshape(extent_x // 2, 2, extent_y // 2, 2, extent_z // 2, 2)
    chosen = lax.index_in_dim(blocks, offset, axis=2 * which_dim + 1, keepdims=True)
    return jnp.sum(chosen, axis=(1, 3, 5))


def side_terms(field, plus_faces, minus_faces, widened):
    result = plus_faces[0] * (field - widened[:, 2:]) + minus_faces[0] * (field - widened[:, :-2])
    for which_dim in (1, 2):
        result = result + plus_faces[which_dim] * (field - plus_side(field, which_dim + 1))
        result = result + minus_faces[which_dim] * (field - minus_side(field, which_dim + 1))
    return result


def fine_image(field, plus_faces, minus_faces, shift_value):
    widened = extended(field, (("space", 1),), 1)
    return shift_value * field + side_terms(field, plus_faces, minus_faces, widened)


def coarse_image(field, plus_faces, minus_faces, shift_value):
    widened = extended(field, (("space", 1),), 1)
    return shift_value * field + side_terms(field, plus_faces, minus_faces, widened)


def restrict(field):
    members, extent_x, extent_y, extent_z = field.shape
    shaped = field.reshape(members, extent_x // 2, 2, extent_y // 2, 2, extent_z // 2, 2)
    return jnp.sum(shaped, axis=(2, 4, 6))


def prolong(field):
    return jnp.repeat(jnp.repeat(jnp.repeat(field, 2, axis=1), 2, axis=2), 2, axis=3)


def precondition(residual, fine, coarse):
    plus_faces, minus_faces, shift_value, diagonal = fine
    coarse_plus, coarse_minus, coarse_shift, coarse_diagonal = coarse
    smooth_one = DAMPING * residual / diagonal
    coarse_rhs = restrict(residual - fine_image(smooth_one, plus_faces, minus_faces, shift_value))
    coarse_one = DAMPING * coarse_rhs / coarse_diagonal
    coarse_two = (
        coarse_one
        + DAMPING
        * (coarse_rhs - coarse_image(coarse_one, coarse_plus, coarse_minus, coarse_shift))
        / coarse_diagonal
    )
    corrected = smooth_one + prolong(coarse_two)
    return (
        corrected
        + DAMPING
        * (residual - fine_image(corrected, plus_faces, minus_faces, shift_value))
        / diagonal
    )


def expand(values):
    return values.reshape(-1, 1, 1, 1)


def cell_sums(values):
    return jnp.sum(values, axis=(1, 2, 3))


def norm_sum(residual, precond):
    return lax.psum(cell_sums(residual * precond), "space")


def solve(rhs, fine, coarse):
    plus_faces, minus_faces, shift_value, diagonal = fine
    iterate = jnp.zeros_like(rhs)
    residual = rhs
    precond = precondition(residual, fine, coarse)
    gamma_now = norm_sum(residual, precond)
    search = precond
    for turn_index in range(ITERS):
        image_field = fine_image(search, plus_faces, minus_faces, shift_value)
        curve = lax.psum(cell_sums(search * image_field), "space")
        step_length = gamma_now / curve
        iterate = iterate + expand(step_length) * search
        if turn_index + 1 < ITERS:
            residual = residual - expand(step_length) * image_field
            precond = precondition(residual, fine, coarse)
            gamma_next = norm_sum(residual, precond)
            search = precond + expand(gamma_next / gamma_now) * search
            gamma_now = gamma_next
    return iterate


def divided(conductivity, misfit, forward_states, pole_shifts, pole_weights, pole_order):
    widened_kappa = extended(conductivity, (("space", 0),), 1)
    plus_faces = [
        0.5 * (conductivity + widened_kappa[2:]),
        0.5 * (conductivity + plus_side(conductivity, 1)),
        0.5 * (conductivity + plus_side(conductivity, 2)),
    ]
    minus_faces = [
        0.5 * (conductivity + widened_kappa[:-2]),
        0.5 * (conductivity + minus_side(conductivity, 1)),
        0.5 * (conductivity + minus_side(conductivity, 2)),
    ]
    base_diagonal = (
        plus_faces[0]
        + plus_faces[1]
        + plus_faces[2]
        + minus_faces[0]
        + minus_faces[1]
        + minus_faces[2]
    )
    coarse_plus = [coarse_pick(plus_faces[which_dim], which_dim, 1) for which_dim in range(3)]
    coarse_minus = [coarse_pick(minus_faces[which_dim], which_dim, 0) for which_dim in range(3)]
    coarse_base = (
        coarse_plus[0]
        + coarse_plus[1]
        + coarse_plus[2]
        + coarse_minus[0]
        + coarse_minus[1]
        + coarse_minus[2]
    )
    pole_index = jnp.arange(pole_shifts.shape[0], dtype=jnp.int32)
    matches = pole_order[:, None] == pole_index[None, :]
    shift_local = jnp.sum(jnp.where(matches, pole_shifts[None, :], 0.0), axis=1)
    weight_local = jnp.sum(jnp.where(matches, pole_weights[None, :], 0.0), axis=1)
    members = forward_states.shape[0]

    def solve_group(shift_part, weight_part):
        shift_value = expand(shift_part)
        fine = (plus_faces, minus_faces, shift_value, base_diagonal[None] + shift_value)
        coarse = (
            coarse_plus,
            coarse_minus,
            8.0 * shift_value,
            coarse_base[None] + 8.0 * shift_value,
        )
        return solve(expand(weight_part) * misfit[None], fine, coarse)

    adjoint_states = jnp.concatenate(
        [
            solve_group(shift_local[member : member + 1], weight_local[member : member + 1])
            for member in range(members)
        ],
        axis=0,
    )
    widened = extended(jnp.stack([adjoint_states, forward_states]), (("space", 2),), 1)
    term = (adjoint_states - widened[0, :, 2:]) * (forward_states - widened[1, :, 2:])
    term = term + (adjoint_states - widened[0, :, :-2]) * (forward_states - widened[1, :, :-2])
    for which_dim in (2, 3):
        term = term + (adjoint_states - plus_side(adjoint_states, which_dim)) * (
            forward_states - plus_side(forward_states, which_dim)
        )
        term = term + (adjoint_states - minus_side(adjoint_states, which_dim)) * (
            forward_states - minus_side(forward_states, which_dim)
        )
    local_term = -0.5 * jnp.sum(term, axis=0)
    gradient = lax.psum_scatter(local_term, "pole", scatter_dimension=1, tiled=True)
    return (adjoint_states, gradient)


def solution(mesh):
    in_specs = (
        P("space", None, None),
        P("space", None, None),
        P("pole", "space", None, None),
        P(),
        P(),
        P("pole"),
    )
    out_specs = (P("pole", "space", None, None), P("space", "pole", None))

    def body(conductivity, misfit, forward_states, *poles):
        nx = conductivity.shape[0] * lax.axis_size("space")
        _, ny, nz = conductivity.shape
        peers = lax.axis_size("space")
        small = nx * ny * nz <= REPLICATED_CELLS and forward_states.shape[:2] == (2, 2)
        if small and nz == 2 * HALF and peers > 2 and peers & (peers - 1) == 0:
            return whole_grid(conductivity, misfit, forward_states, *poles)
        return divided(conductivity, misfit, forward_states, *poles)

    return jax.shard_map(
        body, mesh=mesh, in_specs=in_specs, out_specs=out_specs, check_vma=False
    )
```

```python
import functools

import jax
import jax.numpy as jnp
from jax import lax
from jax.experimental import pallas as pl
from jax.experimental.pallas import tpu as pltpu
from jax.sharding import PartitionSpec as P

ITERS = 2
DAMPING = 0.8
KEPT = 2.0 - DAMPING
REPLICATED_CELLS = 32 * 64 * 128
HALF = 64
TILE = 8
UNROLL = 8


def extended(array, sides, width):
    for axis, dim in sides:
        peers, length = (lax.axis_size(axis), array.shape[dim])
        up = [(i, (i + 1) % peers) for i in range(peers - 1)]
        down = [(j, i) for i, j in up]
        last = lax.slice_in_dim(array, length - width, length, axis=dim)
        leading = lax.slice_in_dim(array, 0, width, axis=dim)
        before = lax.ppermute(last, axis, up)
        after = lax.ppermute(leading, axis, down)
        array = jnp.concatenate([before, array, after], axis=dim)
    return array


def lane_index(shape):
    return lax.broadcasted_iota(jnp.int32, shape, len(shape) - 1)


def row_index(shape):
    return lax.broadcasted_iota(jnp.int32, shape, len(shape) - 2)


def roll(block, shift, axis):
    return pltpu.roll(block, shift % block.shape[axis], axis)


def inverse(value):
    guess = pl.reciprocal(value, approx=True)
    return guess * (2.0 - value * guess)


def tree_sum(values):
    while len(values) > 1:
        values = [sum(values[at : at + 2]) for at in range(0, len(values), 2)]
    return values[0]


def grand_total(acc):
    line = jnp.sum(acc, axis=0, keepdims=True)
    return jnp.broadcast_to(jnp.sum(line, axis=1, keepdims=True), acc.shape)


def swap_masks(peers, flip):
    falling = []
    mask = peers // 2
    while mask > 1:
        falling.append(mask)
        mask //= 2
    if flip:
        return falling[::-1], falling[:1] + falling[:0:-1]
    return falling, falling[-1:] + falling[:-1]


def block_pair(u, holder, peers, flip):
    even, odd = swap_masks(peers, flip)
    parity = holder % 2
    top = jnp.where(parity == 0, even.index(peers // 2), odd.index(peers // 2))
    below = u & ((1 << top) - 1)
    base = ((u >> top) << (top + 1)) | below
    upper = jnp.where(holder >= peers // 2, 1, 0)
    first = base | (upper << top)
    second = base | ((1 - upper) << top)
    home = holder
    for step, (mask_even, mask_odd) in enumerate(zip(even, odd)):
        mask = jnp.where(parity == 0, mask_even, mask_odd)
        home = home ^ (((first >> step) & 1) * mask)
    return first, second, home


def prepare_kernel(kappa_ref, misfit_ref, kappa_out, misfit_out, *, axis, peers):
    at_ = Layout(kappa_ref.shape[1] // 2)
    upper = jnp.where(lax.axis_index(axis) >= peers // 2, 1, 0)
    at_.deal(kappa_ref, kappa_out, upper)
    at_.deal(misfit_ref, misfit_out, upper)


def join_kernel(*refs, masks, axis, peers):
    place = lax.axis_index(axis)
    at_ = Layout(refs[0].shape[1] // 2)
    for at, (even, odd) in enumerate(masks):
        partner = place ^ jnp.where(place % 2 == 0, even, odd)
        refs[4 + at][0] = refs[at][...]
        at_.deal(refs[2 + at], refs[4 + at].at[1], jnp.where(partner >= peers // 2, 1, 0))


def gather_blocks(blocks, states, axis):
    peers = lax.axis_size(axis)
    even = lax.axis_index(axis) % 2 == 0
    swap = [(i, i ^ 1) for i in range(peers)]
    over = [(i, i + 1 if i % 2 else i - 1) for i in range(1, peers - 1)]
    vmem = pl.BlockSpec(memory_space=pltpu.VMEM)
    swaps = [list(zip(*swap_masks(peers, flip))) for flip in (False, True)]
    own = pl.pallas_call(
        functools.partial(prepare_kernel, axis=axis, peers=peers),
        out_shape=[jax.ShapeDtypeStruct(block.shape, jnp.float32) for block in blocks],
        in_specs=[vmem] * 2,
        out_specs=[vmem] * 2,
        compiler_params=pltpu.CompilerParams(vmem_limit_bytes=1024 * 1024),
        name="prepare",
    )(*blocks)
    held = list(blocks)
    for step in range(len(swaps[0])):
        arrived = []
        for at in (0, 1):
            masks = swaps[at][step]
            pairs = [(i, i ^ masks[i % 2]) for i in range(peers)]
            arrived.append(lax.ppermute(held[at], axis, pairs))
        if step:
            held = [jnp.concatenate(pair, axis=0) for pair in zip(held, arrived)]
            continue
        masks = [swaps[at][0] for at in (0, 1)]
        shape = jax.ShapeDtypeStruct((2, *blocks[0].shape), jnp.float32)
        held[:] = pl.pallas_call(
            functools.partial(join_kernel, masks=masks, axis=axis, peers=peers),
            out_shape=[shape] * 2,
            in_specs=[vmem] * 4,
            out_specs=[vmem] * 2,
            compiler_params=pltpu.CompilerParams(vmem_limit_bytes=1024 * 1024),
            name="join",
        )(*own, *arrived)
        held[1], states = lax.optimization_barrier((held[1], states))
        far = lax.ppermute(jnp.where(even, states[:, :1], states[:, -1:]), axis, over)
    other = [lax.ppermute(part, axis, swap) for part in held]

    def fetch_near(after):
        late, states_late, far_late = lax.optimization_barrier((after, states, far))
        given = jnp.concatenate([states_late, far_late], axis=1)
        return late, lax.ppermute(jnp.where(even, given[1], given[0]), axis, swap)

    return held, other, far, fetch_near


CLASSES = [(a, b, c) for a in (0, 1) for b in (0, 1) for c in (0, 1)]
PAIRS = [(p, q) for p in (0, 1) for q in (0, 1)]


def cls(a, b, c):
    return 4 * a + 2 * b + c


def inner_faces(p, q):
    return (
        (2 * p + q, cls(0, p, q), cls(1, p, q)),
        (4 + 2 * p + q, cls(p, 0, q), cls(p, 1, q)),
        (8 + 2 * p + q, cls(p, q, 0), cls(p, q, 1)),
    )


class Layout:
    def __init__(self, rows):
        self.tiles = rows // TILE
        self.lane = lane_index((TILE, 2 * HALF))
        self.row = row_index((TILE, 2 * HALF))
        self.left = self.lane < HALF
        self.zero = jnp.zeros((TILE, 2 * HALF), jnp.float32)

    def tile(self, j):
        return pl.ds(TILE * j, TILE)

    def every(self, b, j):
        return pl.ds(b + 2 * j, TILE, stride=2 * self.tiles)

    def row_before(self, load, j):
        return load(j - 1) if j else roll(load(self.tiles - 1), 1, 0)

    def row_after(self, load, j):
        return load(j + 1) if j + 1 < self.tiles else roll(load(0), -1, 0)

    def seam(self, ref, low, high):
        last = ref.shape[1] - 1
        for j in range(self.tiles):
            for k in low:
                moved = roll(ref[k, last - 1, self.tile(j)], HALF, 1)
                ref[k, 0, self.tile(j)] = jnp.where(self.left, 0.0, moved)
            for k in high:
                moved = roll(ref[k, 1, self.tile(j)], HALF, 1)
                ref[k, last, self.tile(j)] = jnp.where(self.left, moved, 0.0)

    def seam_fine(self, ref):
        count = ref.shape[0]
        self.seam(
            ref,
            [k for k in range(count) if k % 8 >= 4],
            [k for k in range(count) if k % 8 < 4],
        )

    def dealt(self, b, j):
        return pl.ds(TILE * (self.tiles * b + j), TILE)

    def deal(self, block_ref, out_ref, upper):
        odd = jnp.where(self.left, upper, 1 - upper)
        column = 2 * (self.lane % HALF) + odd
        for x in range(block_ref.shape[0]):
            for b in (0, 1):
                for j in range(self.tiles):
                    rows = block_ref[x, self.every(b, j), :]
                    out_ref[x, self.dealt(b, j), :] = jnp.take_along_axis(rows, column, axis=1)

    def arrange(self, mine_ref, theirs_ref, place, flip, store):
        blocks, own = mine_ref.shape[:2]

        def pair(u, carry):
            for ref, holder in ((mine_ref, place), (theirs_ref, place ^ 1)):
                first, second, home = block_pair(u, holder, 2 * blocks, flip)
                for x in range(own):
                    spot = home * (own // 2) + x // 2
                    for b in (0, 1):
                        for j in range(self.tiles):
                            one = ref[first, x, self.dealt(b, j), :]
                            two = ref[second, x, self.dealt(b, j), :]
                            store(cls(x % 2, b, 0), spot, j, jnp.where(self.left, one, two))
                            odd = roll(jnp.where(self.left, two, one), HALF, 1)
                            store(cls(x % 2, b, 1), spot, j, odd)
            return carry

        lax.fori_loop(0, blocks // 2, pair, 0)


def setup_kernel(
    order_ref,
    shifts_ref,
    weights_ref,
    mine_ref,
    theirs_ref,
    inner,
    outer_x,
    outer_y,
    outer_z,
    inner_sum,
    diagonal,
    damped,
    coarse_off,
    coarse_damped,
    chosen,
    half_kappa,
):
    half = inner.shape[1]
    at_ = Layout(inner.shape[2])
    tile, tiles = at_.tile, at_.tiles
    place = lax.axis_index("space")
    pole = jnp.where(place % 2 == 0, order_ref[:, 0:1], order_ref[:, 1:2])
    taken = lane_index(shifts_ref.shape) == pole
    shift = jnp.sum(jnp.where(taken, shifts_ref[...], 0.0), axis=1, keepdims=True)
    weight = jnp.sum(jnp.where(taken, weights_ref[...], 0.0), axis=1, keepdims=True)
    shift = jnp.broadcast_to(shift, at_.zero.shape)
    chosen[...] = jnp.broadcast_to(weight, at_.zero.shape)

    def keep(k, spot, j, value):
        half_kappa[k, spot + 1, tile(j)] = 0.5 * value

    at_.arrange(mine_ref, theirs_ref, place, False, keep)
    at_.seam_fine(half_kappa)

    z_low = jnp.where(at_.lane % HALF > 0, 1.0, 0.0)
    z_high = jnp.where(at_.lane % HALF < HALF - 1, 1.0, 0.0)
    y_low = [jnp.where(at_.row > 0, 1.0, 0.0)] + [None] * (tiles - 1)
    y_high = [None] * (tiles - 1) + [jnp.where(at_.row < TILE - 1, 1.0, 0.0)]

    def masked(mask, value):
        return value if mask is None else mask * value

    def plane(i, carry):
        for j in range(tiles):
            kap = [half_kappa[k, i + 1, tile(j)] for k in range(8)]
            inside = [[] for _ in range(8)]
            outside = [[] for _ in range(8)]
            off = [[] for _ in range(5)]
            for p, q in PAIRS:
                for face_at, low, high in inner_faces(p, q):
                    face = kap[low] + kap[high]
                    inner[face_at, i, tile(j)] = face
                    inside[low].append(face)
                    inside[high].append(face)
                at = 2 * p + q

                low, high = cls(0, p, q), cls(1, p, q)
                minus = kap[low] + half_kappa[high, i, tile(j)]
                plus = kap[high] + half_kappa[low, i + 2, tile(j)]
                outside[low].append(minus)
                outside[high].append(plus)
                outer_x[at, i, tile(j)] = minus
                off[0].append(minus)

                low, high = cls(p, 0, q), cls(p, 1, q)
                side = at_.row_before(lambda r: half_kappa[high, i + 1, tile(r)], j)
                minus = kap[low] + masked(y_low[j], side)
                side = at_.row_after(lambda r: half_kappa[low, i + 1, tile(r)], j)
                plus = kap[high] + masked(y_high[j], side)
                outside[low].append(minus)
                outside[high].append(plus)
                minus, plus = masked(y_low[j], minus), masked(y_high[j], plus)
                outer_y[at, i, tile(j)] = minus
                off[1].append(minus)
                off[2].append(plus)

                low, high = cls(p, q, 0), cls(p, q, 1)
                minus = kap[low] + z_low * roll(kap[high], 1, 1)
                plus = kap[high] + z_high * roll(kap[low], -1, 1)
                outside[low].append(minus)
                outside[high].append(plus)
                minus, plus = z_low * minus, z_high * plus
                outer_z[at, i, tile(j)] = minus
                outer_z[4 + at, i, tile(j)] = plus
                off[3].append(minus)
                off[4].append(plus)
            coarse_total = []
            for k in range(8):
                within, without = tree_sum(inside[k]), tree_sum(outside[k])
                inner_sum[k, i, tile(j)] = within
                base = within + without + shift
                diagonal[k, i, tile(j)] = base
                coarse_total.append(without)
                damped[k, i, tile(j)] = (DAMPING / KEPT) * inverse(base)
            for at, part in enumerate(off):
                coarse_off[at, i, tile(j)] = tree_sum(part)
            coarse_damped[i, tile(j)] = DAMPING * inverse(tree_sum(coarse_total) + 8.0 * shift)
        return carry

    lax.fori_loop(0, half, plane, 0, unroll=UNROLL)
    for j in range(tiles):
        part = []
        for p, q in PAIRS:
            face = half_kappa[cls(0, p, q), half + 1, tile(j)]
            face = face + half_kappa[cls(1, p, q), half, tile(j)]
            outer_x[2 * p + q, half, tile(j)] = face
            part.append(face)
        coarse_off[0, half, tile(j)] = tree_sum(part)


def solve_kernel(
    mine_ref,
    theirs_ref,
    inner,
    outer_x,
    outer_y,
    outer_z,
    inner_sum,
    diagonal,
    damped,
    coarse_off,
    coarse_damped,
    chosen,
    planes,
    residual,
    scaled,
    partial,
    first_dir,
    second_dir,
    image,
    coarse_one,
    coarse_two,
    *,
    own,
):
    half, rows = inner.shape[1:3]
    at_ = Layout(rows)
    tile, tiles, zero = at_.tile, at_.tiles, at_.zero
    place = lax.axis_index("space")
    core = place % 2
    weight = KEPT * chosen[...]

    def begin(k, spot, j, value):
        res = weight * value
        residual[k, spot, tile(j)] = res
        scaled[k, spot + 1, tile(j)] = damped[k, spot, tile(j)] * res

    at_.arrange(mine_ref, theirs_ref, place, True, begin)
    at_.seam_fine(scaled)

    def rows_of(ref, i):
        cache = {}

        def load(k, j, step):
            if abs(j - step) > 1:
                return ref[k, i, tile(j)]
            if (k, j) not in cache:
                cache[k, j] = ref[k, i, tile(j)]
            return cache[k, j]

        def get(k, j):
            return load(k, j, j)

        def before(k, j):
            return at_.row_before(lambda r: load(k, r, j), j)

        def after(k, j):
            return at_.row_after(lambda r: load(k, r, j), j)

        return get, before, after

    def stencil(field, i, both):
        get, before, after = rows_of(field, i + 1)
        face_get, _, face_after = rows_of(outer_y, i)
        for j in range(tiles):
            here = [get(k, j) for k in range(8)]
            terms = [[] for _ in range(8)]
            for p, q in PAIRS:
                at = 2 * p + q
                for face_at, low, high in inner_faces(p, q):
                    face = inner[face_at, i, tile(j)]
                    terms[low].append(face * here[high])
                    if both:
                        terms[high].append(face * here[low])
                low, high = cls(0, p, q), cls(1, p, q)
                terms[low].append(outer_x[at, i, tile(j)] * field[high, i, tile(j)])
                if both:
                    side = field[low, i + 2, tile(j)]
                    terms[high].append(outer_x[at, i + 1, tile(j)] * side)
                low, high = cls(p, 0, q), cls(p, 1, q)
                terms[low].append(face_get(at, j) * before(high, j))
                if both:
                    terms[high].append(face_after(at, j) * after(low, j))
                low, high = cls(p, q, 0), cls(p, q, 1)
                terms[low].append(outer_z[at, i, tile(j)] * roll(here[high], 1, 1))
                if both:
                    terms[high].append(outer_z[4 + at, i, tile(j)] * roll(here[low], -1, 1))
            yield j, here, [tree_sum(part) if part else None for part in terms]

    def coarse_sides(field, i, j):
        here = field[0, i + 1, tile(j)]
        return here, (
            (field[0, i, tile(j)], field[0, i + 2, tile(j)]),
            (
                at_.row_before(lambda r: field[0, i + 1, tile(r)], j),
                at_.row_after(lambda r: field[0, i + 1, tile(r)], j),
            ),
            (roll(here, 1, 1), roll(here, -1, 1)),
        )

    def precondition(result):
        def down(i, carry):
            for j, _, sums in stencil(scaled, i, True):
                res = [residual[k, i, tile(j)] for k in range(8)]
                parts = [res[k] + sums[k] for k in range(8)]
                for k in range(8):
                    partial[k, i, tile(j)] = parts[k]
                rhs = tree_sum(parts) - (1.0 / KEPT) * tree_sum(res)
                coarse_one[0, i + 1, tile(j)] = coarse_damped[i, tile(j)] * rhs
            return carry

        lax.fori_loop(0, half, down, 0, unroll=UNROLL)
        at_.seam(coarse_one, [0], [0])

        def smooth(i, carry):
            for j in range(tiles):
                here, sides = coarse_sides(coarse_one, i, j)
                total = coarse_off[0, i, tile(j)] * sides[0][0]
                total = total + coarse_off[0, i + 1, tile(j)] * sides[0][1]
                more = coarse_off[1, i, tile(j)] * sides[1][0]
                more = more + coarse_off[2, i, tile(j)] * sides[1][1]
                most = coarse_off[3, i, tile(j)] * sides[2][0]
                most = most + coarse_off[4, i, tile(j)] * sides[2][1]
                coarse_two[0, i + 1, tile(j)] = KEPT * here + coarse_damped[
                    i, tile(j)
                ] * (total + more + most)
            return carry

        lax.fori_loop(0, half, smooth, 0, unroll=UNROLL)
        at_.seam(coarse_two, [0], [0])

        def up(i, gamma):
            face_get, _, face_after = rows_of(outer_y, i)
            for j in range(tiles):
                here, sides = coarse_sides(coarse_two, i, j)
                kept = ((1.0 - DAMPING) / KEPT) * here
                dots = []
                for a, b, c in CLASSES:
                    k = cls(a, b, c)
                    value = tree_sum(
                        [
                            partial[k, i, tile(j)],
                            inner_sum[k, i, tile(j)] * here,
                            outer_x[2 * b + c, i + a, tile(j)] * sides[0][a],
                            (face_after if b else face_get)(2 * a + c, j) * sides[1][b],
                            outer_z[4 * c + 2 * a + b, i, tile(j)] * sides[2][c],
                        ]
                    )
                    new = kept + damped[k, i, tile(j)] * value
                    result[k, i + 1, tile(j)] = new
                    dots.append(residual[k, i, tile(j)] * new)
                gamma = gamma + tree_sum(dots)
            return gamma

        gamma = lax.fori_loop(0, half, up, zero, unroll=UNROLL)
        at_.seam_fine(result)
        return grand_total(gamma)

    gamma = precondition(first_dir)

    def apply(i, acc):
        for j, here, sums in stencil(first_dir, i, True):
            dots = []
            for k in range(8):
                value = diagonal[k, i, tile(j)] * here[k] - sums[k]
                image[k, i, tile(j)] = value
                dots.append(here[k] * value)
            acc = acc + tree_sum(dots)
        return acc

    curve = grand_total(lax.fori_loop(0, half, apply, zero, unroll=UNROLL))
    step_one = gamma / curve

    def update(i, carry):
        for j in range(tiles):
            for k in range(8):
                new = residual[k, i, tile(j)] - step_one * image[k, i, tile(j)]
                residual[k, i, tile(j)] = new
                scaled[k, i + 1, tile(j)] = damped[k, i, tile(j)] * new
        return carry

    lax.fori_loop(0, half, update, 0, unroll=UNROLL)
    at_.seam_fine(scaled)

    gamma_next = precondition(second_dir)

    def bend(i, carry):
        own_part, face_part = carry
        for j, here, sums in stencil(second_dir, i, False):
            own_part = own_part + tree_sum(
                [here[k] * (diagonal[k, i, tile(j)] * here[k]) for k in range(8)]
            )
            face_part = face_part + tree_sum([here[k] * sums[k] for k in range(7)])
        return own_part, face_part

    own_part, face_part = lax.fori_loop(0, half, bend, (zero, zero), unroll=UNROLL)
    ratio = gamma_next / gamma
    curve_next = grand_total(own_part - 2.0 * face_part)
    step_two = gamma_next / (curve_next - ratio * ratio * curve)
    step_first = (step_one + step_two * ratio) * (1.0 / KEPT)
    step_two = step_two * (1.0 / KEPT)

    start = (place - core) * (own // 2)
    upper = jnp.where(start >= half, 1, 0)
    start = start - half * upper
    even = at_.lane % 2 == 0
    source = at_.lane // 2 + HALF * upper
    for at in range(2 * own + 2):
        a = (at + 1) % 2
        spot = start + (at + 1) // 2
        for b in (0, 1):
            for j in range(tiles):
                both = [
                    step_first * first_dir[cls(a, b, c), spot, tile(j)]
                    + step_two * second_dir[cls(a, b, c), spot, tile(j)]
                    for c in (0, 1)
                ]
                planes[at, at_.every(b, j), :] = jnp.where(
                    even,
                    jnp.take_along_axis(both[0], source, axis=1),
                    jnp.take_along_axis(both[1], source, axis=1),
                )


def finish_kernel(planes_ref, state_ref, far_ref, near_ref, adjoint_ref, keep_ref, partner_ref, send_ref, terms):
    own, ny, nz = adjoint_ref.shape
    core = lax.axis_index("space") % 2
    full = (ny, nz)
    y_at = row_index(full)
    z_at = lane_index(full)

    def drop(value, axis, up):
        moved = roll(value, -1 if up else 1, axis)
        at = (y_at, z_at)[axis]
        edge = full[axis] - 1 if up else 0
        return value - jnp.where(at == edge, 0.0, moved)

    is_even = core == 0
    state = [jnp.where(is_even, far_ref[core, 0], near_ref[own])]
    state += [jnp.where(is_even, state_ref[core, x], near_ref[x]) for x in range(own)]
    state += [jnp.where(is_even, near_ref[x], state_ref[core, x]) for x in range(own)]
    state += [jnp.where(is_even, near_ref[own], far_ref[core, 0])]
    for x in range(2 * own):
        here, f = planes_ref[x + 1], state[x + 1]
        term = (here - planes_ref[x + 2]) * (f - state[x + 2])
        term = term + (here - planes_ref[x]) * (f - state[x])
        for axis in (0, 1):
            for up in (True, False):
                term = term + drop(here, axis, up) * drop(f, axis, up)
        terms[x] = -0.5 * term

    groups = send_ref.shape[0] + 1
    chunk = keep_ref.shape[1]
    for x in range(own):
        mine, other = core * own + x, (1 - core) * own + x
        adjoint_ref[x] = planes_ref[1 + mine]
        partner_ref[x, :ny] = planes_ref[1 + other]
        for k in range(groups):
            at = lax.rem(lax.axis_index("pole") + k, groups) * chunk
            at = pl.multiple_of(at, chunk)
            for side, plane in enumerate((mine, other)):
                share = terms[plane, pl.ds(at, chunk), :]
                if k:
                    send_ref[k - 1, side, x] = share
                elif side:
                    partner_ref[x, ny:] = share
                else:
                    keep_ref[x] = share


def whole_grid(conductivity, misfit, forward_states, pole_shifts, pole_weights, pole_order):
    members, own, ny, nz = forward_states.shape
    groups = lax.axis_size("pole")
    peers = lax.axis_size("space")
    even = lax.axis_index("space") % 2 == 0
    mine, theirs, far, fetch_near = gather_blocks([conductivity, misfit], forward_states, "space")
    half, rows = peers * own // 4, ny // 2

    def field(count, extent):
        return (count, extent, rows, 2 * HALF)

    def held(*shape):
        return pltpu.VMEM(shape, jnp.float32)

    vmem = pl.BlockSpec(memory_space=pltpu.VMEM)
    shapes = [
        field(12, half),
        field(4, half + 1),
        field(4, half),
        field(8, half),
        field(8, half),
        field(8, half),
        field(8, half),
        field(5, half + 1),
        (half, rows, 2 * HALF),
        (TILE, 2 * HALF),
    ]
    coefficients = pl.pallas_call(
        setup_kernel,
        out_shape=[jax.ShapeDtypeStruct(shape, jnp.float32) for shape in shapes],
        in_specs=[vmem] * 5,
        out_specs=[vmem] * len(shapes),
        scratch_shapes=[held(*field(8, half + 2))],
        compiler_params=pltpu.CompilerParams(vmem_limit_bytes=6 * 1024 * 1024),
        name="setup",
    )(pole_order[None], pole_shifts[None], pole_weights[None], mine[0], theirs[0])
    coefficients, near = fetch_near(coefficients)
    planes = pl.pallas_call(
        functools.partial(solve_kernel, own=own),
        out_shape=jax.ShapeDtypeStruct((2 * own + 2, ny, nz), jnp.float32),
        in_specs=[vmem] * (2 + len(shapes)),
        out_specs=vmem,
        scratch_shapes=[
            held(*field(8, half)),
            held(*field(8, half + 2)),
            held(*field(8, half)),
            held(*field(8, half + 2)),
            held(*field(8, half + 2)),
            held(*field(8, half)),
            held(*field(1, half + 2)),
            held(*field(1, half + 2)),
        ],
        compiler_params=pltpu.CompilerParams(vmem_limit_bytes=12 * 1024 * 1024),
        name="solve",
    )(mine[1], theirs[1], *coefficients)
    chunk = ny // groups
    adjoint, gradient, partner, send = pl.pallas_call(
        finish_kernel,
        out_shape=[
            jax.ShapeDtypeStruct((own, ny, nz), jnp.float32),
            jax.ShapeDtypeStruct((own, chunk, nz), jnp.float32),
            jax.ShapeDtypeStruct((own, ny + chunk, nz), jnp.float32),
            jax.ShapeDtypeStruct((groups - 1, 2, own, chunk, nz), jnp.float32),
        ],
        in_specs=[vmem] * 4,
        out_specs=[vmem] * 4,
        scratch_shapes=[held(2 * own, ny, nz)],
        compiler_params=pltpu.CompilerParams(vmem_limit_bytes=4 * 1024 * 1024),
        name="finish",
    )(planes, forward_states, far, near)

    arrived = lax.ppermute(partner, "space", [(i, i ^ 1) for i in range(peers)])
    shares = []
    for k in range(1, groups):
        for side in (0, 1):
            pairs = [
                (i * peers + j, (i + k) % groups * peers + (j ^ side))
                for i in range(groups)
                for j in range(peers)
            ]
            shares.append(lax.ppermute(send[k - 1, side], ("pole", "space"), pairs))
    theirs = arrived[:, :ny]
    adjoint_states = jnp.stack(
        [jnp.where(even, adjoint, theirs), jnp.where(even, theirs, adjoint)]
    )
    adjoint_states, arrived = lax.optimization_barrier((adjoint_states, arrived))
    return adjoint_states, gradient + arrived[:, ny:] + sum(shares)


def plus_side(field, which_dim):
    extent = field.shape[which_dim]
    inner_part = lax.slice_in_dim(field, 1, extent, axis=which_dim)
    zero_plane = jnp.zeros_like(lax.slice_in_dim(field, 0, 1, axis=which_dim))
    return jnp.concatenate([inner_part, zero_plane], axis=which_dim)


def minus_side(field, which_dim):
    extent = field.shape[which_dim]
    inner_part = lax.slice_in_dim(field, 0, extent - 1, axis=which_dim)
    zero_plane = jnp.zeros_like(lax.slice_in_dim(field, 0, 1, axis=which_dim))
    return jnp.concatenate([zero_plane, inner_part], axis=which_dim)


def coarse_pick(faces, which_dim, offset):
    extent_x, extent_y, extent_z = faces.shape
    blocks = faces.reshape(extent_x // 2, 2, extent_y // 2, 2, extent_z // 2, 2)
    chosen = lax.index_in_dim(blocks, offset, axis=2 * which_dim + 1, keepdims=True)
    return jnp.sum(chosen, axis=(1, 3, 5))


def side_terms(field, plus_faces, minus_faces, widened):
    result = plus_faces[0] * (field - widened[:, 2:]) + minus_faces[0] * (field - widened[:, :-2])
    for which_dim in (1, 2):
        result = result + plus_faces[which_dim] * (field - plus_side(field, which_dim + 1))
        result = result + minus_faces[which_dim] * (field - minus_side(field, which_dim + 1))
    return result


def fine_image(field, plus_faces, minus_faces, shift_value):
    widened = extended(field, (("space", 1),), 1)
    return shift_value * field + side_terms(field, plus_faces, minus_faces, widened)


def coarse_image(field, plus_faces, minus_faces, shift_value):
    widened = extended(field, (("space", 1),), 1)
    return shift_value * field + side_terms(field, plus_faces, minus_faces, widened)


def restrict(field):
    members, extent_x, extent_y, extent_z = field.shape
    shaped = field.reshape(members, extent_x // 2, 2, extent_y // 2, 2, extent_z // 2, 2)
    return jnp.sum(shaped, axis=(2, 4, 6))


def prolong(field):
    return jnp.repeat(jnp.repeat(jnp.repeat(field, 2, axis=1), 2, axis=2), 2, axis=3)


def precondition(residual, fine, coarse):
    plus_faces, minus_faces, shift_value, diagonal = fine
    coarse_plus, coarse_minus, coarse_shift, coarse_diagonal = coarse
    smooth_one = DAMPING * residual / diagonal
    coarse_rhs = restrict(residual - fine_image(smooth_one, plus_faces, minus_faces, shift_value))
    coarse_one = DAMPING * coarse_rhs / coarse_diagonal
    coarse_two = (
        coarse_one
        + DAMPING
        * (coarse_rhs - coarse_image(coarse_one, coarse_plus, coarse_minus, coarse_shift))
        / coarse_diagonal
    )
    corrected = smooth_one + prolong(coarse_two)
    return (
        corrected
        + DAMPING
        * (residual - fine_image(corrected, plus_faces, minus_faces, shift_value))
        / diagonal
    )


def expand(values):
    return values.reshape(-1, 1, 1, 1)


def cell_sums(values):
    return jnp.sum(values, axis=(1, 2, 3))


def norm_sum(residual, precond):
    return lax.psum(cell_sums(residual * precond), "space")


def solve(rhs, fine, coarse):
    plus_faces, minus_faces, shift_value, diagonal = fine
    iterate = jnp.zeros_like(rhs)
    residual = rhs
    precond = precondition(residual, fine, coarse)
    gamma_now = norm_sum(residual, precond)
    search = precond
    for turn_index in range(ITERS):
        image_field = fine_image(search, plus_faces, minus_faces, shift_value)
        curve = lax.psum(cell_sums(search * image_field), "space")
        step_length = gamma_now / curve
        iterate = iterate + expand(step_length) * search
        if turn_index + 1 < ITERS:
            residual = residual - expand(step_length) * image_field
            precond = precondition(residual, fine, coarse)
            gamma_next = norm_sum(residual, precond)
            search = precond + expand(gamma_next / gamma_now) * search
            gamma_now = gamma_next
    return iterate


def divided(conductivity, misfit, forward_states, pole_shifts, pole_weights, pole_order):
    widened_kappa = extended(conductivity, (("space", 0),), 1)
    plus_faces = [
        0.5 * (conductivity + widened_kappa[2:]),
        0.5 * (conductivity + plus_side(conductivity, 1)),
        0.5 * (conductivity + plus_side(conductivity, 2)),
    ]
    minus_faces = [
        0.5 * (conductivity + widened_kappa[:-2]),
        0.5 * (conductivity + minus_side(conductivity, 1)),
        0.5 * (conductivity + minus_side(conductivity, 2)),
    ]
    base_diagonal = (
        plus_faces[0]
        + plus_faces[1]
        + plus_faces[2]
        + minus_faces[0]
        + minus_faces[1]
        + minus_faces[2]
    )
    coarse_plus = [coarse_pick(plus_faces[which_dim], which_dim, 1) for which_dim in range(3)]
    coarse_minus = [coarse_pick(minus_faces[which_dim], which_dim, 0) for which_dim in range(3)]
    coarse_base = (
        coarse_plus[0]
        + coarse_plus[1]
        + coarse_plus[2]
        + coarse_minus[0]
        + coarse_minus[1]
        + coarse_minus[2]
    )
    pole_index = jnp.arange(pole_shifts.shape[0], dtype=jnp.int32)
    matches = pole_order[:, None] == pole_index[None, :]
    shift_local = jnp.sum(jnp.where(matches, pole_shifts[None, :], 0.0), axis=1)
    weight_local = jnp.sum(jnp.where(matches, pole_weights[None, :], 0.0), axis=1)
    members = forward_states.shape[0]

    def solve_group(shift_part, weight_part):
        shift_value = expand(shift_part)
        fine = (plus_faces, minus_faces, shift_value, base_diagonal[None] + shift_value)
        coarse = (
            coarse_plus,
            coarse_minus,
            8.0 * shift_value,
            coarse_base[None] + 8.0 * shift_value,
        )
        return solve(expand(weight_part) * misfit[None], fine, coarse)

    adjoint_states = jnp.concatenate(
        [
            solve_group(shift_local[member : member + 1], weight_local[member : member + 1])
            for member in range(members)
        ],
        axis=0,
    )
    widened = extended(jnp.stack([adjoint_states, forward_states]), (("space", 2),), 1)
    term = (adjoint_states - widened[0, :, 2:]) * (forward_states - widened[1, :, 2:])
    term = term + (adjoint_states - widened[0, :, :-2]) * (forward_states - widened[1, :, :-2])
    for which_dim in (2, 3):
        term = term + (adjoint_states - plus_side(adjoint_states, which_dim)) * (
            forward_states - plus_side(forward_states, which_dim)
        )
        term = term + (adjoint_states - minus_side(adjoint_states, which_dim)) * (
            forward_states - minus_side(forward_states, which_dim)
        )
    local_term = -0.5 * jnp.sum(term, axis=0)
    gradient = lax.psum_scatter(local_term, "pole", scatter_dimension=1, tiled=True)
    return (adjoint_states, gradient)


def solution(mesh):
    in_specs = (
        P("space", None, None),
        P("space", None, None),
        P("pole", "space", None, None),
        P(),
        P(),
        P("pole"),
    )
    out_specs = (P("pole", "space", None, None), P("space", "pole", None))

    def body(conductivity, misfit, forward_states, *poles):
        nx = conductivity.shape[0] * lax.axis_size("space")
        _, ny, nz = conductivity.shape
        peers = lax.axis_size("space")
        small = nx * ny * nz <= REPLICATED_CELLS and forward_states.shape[:2] == (2, 2)
        if small and nz == 2 * HALF and peers > 2 and peers & (peers - 1) == 0:
            return whole_grid(conductivity, misfit, forward_states, *poles)
        return divided(conductivity, misfit, forward_states, *poles)

    return jax.shard_map(
        body, mesh=mesh, in_specs=in_specs, out_specs=out_specs, check_vma=False
    )
```

```python
import functools

import jax
import jax.numpy as jnp
from jax import lax
from jax.experimental import pallas as pl
from jax.experimental.pallas import tpu as pltpu
from jax.sharding import PartitionSpec as P

ITERS = 2
DAMPING = 0.8
KEPT = 2.0 - DAMPING
REPLICATED_CELLS = 32 * 64 * 128
HALF = 64
TILE = 8
UNROLL = 8


def extended(array, sides, width):
    for axis, dim in sides:
        peers, length = (lax.axis_size(axis), array.shape[dim])
        up = [(i, (i + 1) % peers) for i in range(peers - 1)]
        down = [(j, i) for i, j in up]
        last = lax.slice_in_dim(array, length - width, length, axis=dim)
        leading = lax.slice_in_dim(array, 0, width, axis=dim)
        before = lax.ppermute(last, axis, up)
        after = lax.ppermute(leading, axis, down)
        array = jnp.concatenate([before, array, after], axis=dim)
    return array


def lane_index(shape):
    return lax.broadcasted_iota(jnp.int32, shape, len(shape) - 1)


def row_index(shape):
    return lax.broadcasted_iota(jnp.int32, shape, len(shape) - 2)


def roll(block, shift, axis):
    return pltpu.roll(block, shift % block.shape[axis], axis)


def inverse(value):
    guess = pl.reciprocal(value, approx=True)
    return guess * (2.0 - value * guess)


def tree_sum(values):
    while len(values) > 1:
        values = [sum(values[at : at + 2]) for at in range(0, len(values), 2)]
    return values[0]


def grand_total(acc):
    line = jnp.sum(acc, axis=0, keepdims=True)
    return jnp.broadcast_to(jnp.sum(line, axis=1, keepdims=True), acc.shape)


def swap_masks(peers, flip):
    falling = []
    mask = peers // 2
    while mask > 1:
        falling.append(mask)
        mask //= 2
    rotated = falling[-1:] + falling[:-1]
    return (rotated, falling) if flip else (falling, rotated)


def block_pair(u, holder, peers, flip):
    even, odd = swap_masks(peers, flip)
    parity = holder % 2
    top = jnp.where(parity == 0, even.index(peers // 2), odd.index(peers // 2))
    below = u & ((1 << top) - 1)
    base = ((u >> top) << (top + 1)) | below
    upper = jnp.where(holder >= peers // 2, 1, 0)
    first = base | (upper << top)
    second = base | ((1 - upper) << top)
    home = holder
    for step, (mask_even, mask_odd) in enumerate(zip(even, odd)):
        mask = jnp.where(parity == 0, mask_even, mask_odd)
        home = home ^ (((first >> step) & 1) * mask)
    return first, second, home


def prepare_kernel(kappa_ref, misfit_ref, kappa_out, misfit_out, *, axis, peers):
    at_ = Layout(kappa_ref.shape[1] // 2)
    upper = jnp.where(lax.axis_index(axis) >= peers // 2, 1, 0)
    at_.deal(kappa_ref, kappa_out, upper)
    at_.deal(misfit_ref, misfit_out, upper)


def join_kernel(*refs, masks, axis, peers):
    place = lax.axis_index(axis)
    at_ = Layout(refs[0].shape[1] // 2)
    for at, (even, odd) in enumerate(masks):
        partner = place ^ jnp.where(place % 2 == 0, even, odd)
        refs[4 + at][0] = refs[at][...]
        at_.deal(refs[2 + at], refs[4 + at].at[1], jnp.where(partner >= peers // 2, 1, 0))


def gather_blocks(blocks, states, axis):
    peers = lax.axis_size(axis)
    even = lax.axis_index(axis) % 2 == 0
    swap = [(i, i ^ 1) for i in range(peers)]
    over = [(i, i + 1 if i % 2 else i - 1) for i in range(1, peers - 1)]
    vmem = pl.BlockSpec(memory_space=pltpu.VMEM)
    swaps = [list(zip(*swap_masks(peers, flip))) for flip in (False, True)]
    own = pl.pallas_call(
        functools.partial(prepare_kernel, axis=axis, peers=peers),
        out_shape=[jax.ShapeDtypeStruct(block.shape, jnp.float32) for block in blocks],
        in_specs=[vmem] * 2,
        out_specs=[vmem] * 2,
        compiler_params=pltpu.CompilerParams(vmem_limit_bytes=1024 * 1024),
        name="prepare",
    )(*blocks)
    held = list(blocks)
    for step in range(len(swaps[0])):
        arrived = []
        for at in (0, 1):
            masks = swaps[at][step]
            pairs = [(i, i ^ masks[i % 2]) for i in range(peers)]
            arrived.append(lax.ppermute(held[at], axis, pairs))
        if step:
            held = [jnp.concatenate(pair, axis=0) for pair in zip(held, arrived)]
            continue
        masks = [swaps[at][0] for at in (0, 1)]
        shape = jax.ShapeDtypeStruct((2, *blocks[0].shape), jnp.float32)
        held[:] = pl.pallas_call(
            functools.partial(join_kernel, masks=masks, axis=axis, peers=peers),
            out_shape=[shape] * 2,
            in_specs=[vmem] * 4,
            out_specs=[vmem] * 2,
            compiler_params=pltpu.CompilerParams(vmem_limit_bytes=1024 * 1024),
            name="join",
        )(*own, *arrived)
        held[1], states = lax.optimization_barrier((held[1], states))
        far = lax.ppermute(jnp.where(even, states[:, :1], states[:, -1:]), axis, over)
    other = [lax.ppermute(part, axis, swap) for part in held]

    def fetch_near(after):
        late, states_late, far_late = lax.optimization_barrier((after, states, far))
        given = jnp.concatenate([states_late, far_late], axis=1)
        return late, lax.ppermute(jnp.where(even, given[1], given[0]), axis, swap)

    return held, other, far, fetch_near


CLASSES = [(a, b, c) for a in (0, 1) for b in (0, 1) for c in (0, 1)]
PAIRS = [(p, q) for p in (0, 1) for q in (0, 1)]


def cls(a, b, c):
    return 4 * a + 2 * b + c


def inner_faces(p, q):
    return (
        (2 * p + q, cls(0, p, q), cls(1, p, q)),
        (4 + 2 * p + q, cls(p, 0, q), cls(p, 1, q)),
        (8 + 2 * p + q, cls(p, q, 0), cls(p, q, 1)),
    )


class Layout:
    def __init__(self, rows):
        self.tiles = rows // TILE
        self.lane = lane_index((TILE, 2 * HALF))
        self.row = row_index((TILE, 2 * HALF))
        self.left = self.lane < HALF
        self.zero = jnp.zeros((TILE, 2 * HALF), jnp.float32)

    def tile(self, j):
        return pl.ds(TILE * j, TILE)

    def every(self, b, j):
        return pl.ds(b + 2 * j, TILE, stride=2 * self.tiles)

    def row_before(self, load, j):
        return load(j - 1) if j else roll(load(self.tiles - 1), 1, 0)

    def row_after(self, load, j):
        return load(j + 1) if j + 1 < self.tiles else roll(load(0), -1, 0)

    def seam(self, ref, low, high):
        last = ref.shape[1] - 1
        for j in range(self.tiles):
            for k in low:
                moved = roll(ref[k, last - 1, self.tile(j)], HALF, 1)
                ref[k, 0, self.tile(j)] = jnp.where(self.left, 0.0, moved)
            for k in high:
                moved = roll(ref[k, 1, self.tile(j)], HALF, 1)
                ref[k, last, self.tile(j)] = jnp.where(self.left, moved, 0.0)

    def seam_fine(self, ref):
        count = ref.shape[0]
        self.seam(
            ref,
            [k for k in range(count) if k % 8 >= 4],
            [k for k in range(count) if k % 8 < 4],
        )

    def dealt(self, b, j):
        return pl.ds(TILE * (self.tiles * b + j), TILE)

    def deal(self, block_ref, out_ref, upper):
        odd = jnp.where(self.left, upper, 1 - upper)
        column = 2 * (self.lane % HALF) + odd
        for x in range(block_ref.shape[0]):
            for b in (0, 1):
                for j in range(self.tiles):
                    rows = block_ref[x, self.every(b, j), :]
                    out_ref[x, self.dealt(b, j), :] = jnp.take_along_axis(rows, column, axis=1)

    def arrange(self, mine_ref, theirs_ref, place, flip, store):
        blocks, own = mine_ref.shape[:2]

        def pair(u, carry):
            for ref, holder in ((mine_ref, place), (theirs_ref, place ^ 1)):
                first, second, home = block_pair(u, holder, 2 * blocks, flip)
                for x in range(own):
                    spot = home * (own // 2) + x // 2
                    for b in (0, 1):
                        for j in range(self.tiles):
                            one = ref[first, x, self.dealt(b, j), :]
                            two = ref[second, x, self.dealt(b, j), :]
                            store(cls(x % 2, b, 0), spot, j, jnp.where(self.left, one, two))
                            odd = roll(jnp.where(self.left, two, one), HALF, 1)
                            store(cls(x % 2, b, 1), spot, j, odd)
            return carry

        lax.fori_loop(0, blocks // 2, pair, 0)


def setup_kernel(
    order_ref,
    shifts_ref,
    weights_ref,
    mine_ref,
    theirs_ref,
    inner,
    outer_x,
    outer_y,
    outer_z,
    inner_sum,
    diagonal,
    damped,
    coarse_off,
    coarse_damped,
    chosen,
    half_kappa,
):
    half = inner.shape[1]
    at_ = Layout(inner.shape[2])
    tile, tiles = at_.tile, at_.tiles
    place = lax.axis_index("space")
    pole = jnp.where(place % 2 == 0, order_ref[:, 0:1], order_ref[:, 1:2])
    taken = lane_index(shifts_ref.shape) == pole
    shift = jnp.sum(jnp.where(taken, shifts_ref[...], 0.0), axis=1, keepdims=True)
    weight = jnp.sum(jnp.where(taken, weights_ref[...], 0.0), axis=1, keepdims=True)
    shift = jnp.broadcast_to(shift, at_.zero.shape)
    chosen[...] = jnp.broadcast_to(weight, at_.zero.shape)

    def keep(k, spot, j, value):
        half_kappa[k, spot + 1, tile(j)] = 0.5 * value

    at_.arrange(mine_ref, theirs_ref, place, False, keep)
    at_.seam_fine(half_kappa)

    z_low = jnp.where(at_.lane % HALF > 0, 1.0, 0.0)
    z_high = jnp.where(at_.lane % HALF < HALF - 1, 1.0, 0.0)
    y_low = [jnp.where(at_.row > 0, 1.0, 0.0)] + [None] * (tiles - 1)
    y_high = [None] * (tiles - 1) + [jnp.where(at_.row < TILE - 1, 1.0, 0.0)]

    def masked(mask, value):
        return value if mask is None else mask * value

    def plane(i, carry):
        for j in range(tiles):
            kap = [half_kappa[k, i + 1, tile(j)] for k in range(8)]
            inside = [[] for _ in range(8)]
            outside = [[] for _ in range(8)]
            off = [[] for _ in range(5)]
            for p, q in PAIRS:
                for face_at, low, high in inner_faces(p, q):
                    face = kap[low] + kap[high]
                    inner[face_at, i, tile(j)] = face
                    inside[low].append(face)
                    inside[high].append(face)
                at = 2 * p + q

                low, high = cls(0, p, q), cls(1, p, q)
                minus = kap[low] + half_kappa[high, i, tile(j)]
                plus = kap[high] + half_kappa[low, i + 2, tile(j)]
                outside[low].append(minus)
                outside[high].append(plus)
                outer_x[at, i, tile(j)] = minus
                off[0].append(minus)

                low, high = cls(p, 0, q), cls(p, 1, q)
                side = at_.row_before(lambda r: half_kappa[high, i + 1, tile(r)], j)
                minus = kap[low] + masked(y_low[j], side)
                side = at_.row_after(lambda r: half_kappa[low, i + 1, tile(r)], j)
                plus = kap[high] + masked(y_high[j], side)
                outside[low].append(minus)
                outside[high].append(plus)
                minus, plus = masked(y_low[j], minus), masked(y_high[j], plus)
                outer_y[at, i, tile(j)] = minus
                off[1].append(minus)
                off[2].append(plus)

                low, high = cls(p, q, 0), cls(p, q, 1)
                minus = kap[low] + z_low * roll(kap[high], 1, 1)
                plus = kap[high] + z_high * roll(kap[low], -1, 1)
                outside[low].append(minus)
                outside[high].append(plus)
                minus, plus = z_low * minus, z_high * plus
                outer_z[at, i, tile(j)] = minus
                outer_z[4 + at, i, tile(j)] = plus
                off[3].append(minus)
                off[4].append(plus)
            coarse_total = []
            for k in range(8):
                within, without = tree_sum(inside[k]), tree_sum(outside[k])
                inner_sum[k, i, tile(j)] = within
                base = within + without + shift
                diagonal[k, i, tile(j)] = base
                coarse_total.append(without)
                damped[k, i, tile(j)] = (DAMPING / KEPT) * inverse(base)
            for at, part in enumerate(off):
                coarse_off[at, i, tile(j)] = tree_sum(part)
            coarse_damped[i, tile(j)] = DAMPING * inverse(tree_sum(coarse_total) + 8.0 * shift)
        return carry

    lax.fori_loop(0, half, plane, 0, unroll=UNROLL)
    for j in range(tiles):
        part = []
        for p, q in PAIRS:
            face = half_kappa[cls(0, p, q), half + 1, tile(j)]
            face = face + half_kappa[cls(1, p, q), half, tile(j)]
            outer_x[2 * p + q, half, tile(j)] = face
            part.append(face)
        coarse_off[0, half, tile(j)] = tree_sum(part)


def solve_kernel(
    mine_ref,
    theirs_ref,
    inner,
    outer_x,
    outer_y,
    outer_z,
    inner_sum,
    diagonal,
    damped,
    coarse_off,
    coarse_damped,
    chosen,
    planes,
    residual,
    scaled,
    partial,
    first_dir,
    second_dir,
    image,
    coarse_one,
    coarse_two,
    *,
    own,
):
    half, rows = inner.shape[1:3]
    at_ = Layout(rows)
    tile, tiles, zero = at_.tile, at_.tiles, at_.zero
    place = lax.axis_index("space")
    core = place % 2
    weight = KEPT * chosen[...]

    def begin(k, spot, j, value):
        res = weight * value
        residual[k, spot, tile(j)] = res
        scaled[k, spot + 1, tile(j)] = damped[k, spot, tile(j)] * res

    at_.arrange(mine_ref, theirs_ref, place, True, begin)
    at_.seam_fine(scaled)

    def rows_of(ref, i):
        cache = {}

        def load(k, j, step):
            if abs(j - step) > 1:
                return ref[k, i, tile(j)]
            if (k, j) not in cache:
                cache[k, j] = ref[k, i, tile(j)]
            return cache[k, j]

        def get(k, j):
            return load(k, j, j)

        def before(k, j):
            return at_.row_before(lambda r: load(k, r, j), j)

        def after(k, j):
            return at_.row_after(lambda r: load(k, r, j), j)

        return get, before, after

    def stencil(field, i, both):
        get, before, after = rows_of(field, i + 1)
        face_get, _, face_after = rows_of(outer_y, i)
        for j in range(tiles):
            here = [get(k, j) for k in range(8)]
            terms = [[] for _ in range(8)]
            for p, q in PAIRS:
                at = 2 * p + q
                for face_at, low, high in inner_faces(p, q):
                    face = inner[face_at, i, tile(j)]
                    terms[low].append(face * here[high])
                    if both:
                        terms[high].append(face * here[low])
                low, high = cls(0, p, q), cls(1, p, q)
                terms[low].append(outer_x[at, i, tile(j)] * field[high, i, tile(j)])
                if both:
                    side = field[low, i + 2, tile(j)]
                    terms[high].append(outer_x[at, i + 1, tile(j)] * side)
                low, high = cls(p, 0, q), cls(p, 1, q)
                terms[low].append(face_get(at, j) * before(high, j))
                if both:
                    terms[high].append(face_after(at, j) * after(low, j))
                low, high = cls(p, q, 0), cls(p, q, 1)
                terms[low].append(outer_z[at, i, tile(j)] * roll(here[high], 1, 1))
                if both:
                    terms[high].append(outer_z[4 + at, i, tile(j)] * roll(here[low], -1, 1))
            yield j, here, [tree_sum(part) if part else None for part in terms]

    def coarse_sides(field, i, j):
        here = field[0, i + 1, tile(j)]
        return here, (
            (field[0, i, tile(j)], field[0, i + 2, tile(j)]),
            (
                at_.row_before(lambda r: field[0, i + 1, tile(r)], j),
                at_.row_after(lambda r: field[0, i + 1, tile(r)], j),
            ),
            (roll(here, 1, 1), roll(here, -1, 1)),
        )

    def precondition(result):
        def down(i, carry):
            for j, _, sums in stencil(scaled, i, True):
                res = [residual[k, i, tile(j)] for k in range(8)]
                parts = [res[k] + sums[k] for k in range(8)]
                for k in range(8):
                    partial[k, i, tile(j)] = parts[k]
                rhs = tree_sum(parts) - (1.0 / KEPT) * tree_sum(res)
                coarse_one[0, i + 1, tile(j)] = coarse_damped[i, tile(j)] * rhs
            return carry

        lax.fori_loop(0, half, down, 0, unroll=UNROLL)
        at_.seam(coarse_one, [0], [0])

        def smooth(i, carry):
            for j in range(tiles):
                here, sides = coarse_sides(coarse_one, i, j)
                total = coarse_off[0, i, tile(j)] * sides[0][0]
                total = total + coarse_off[0, i + 1, tile(j)] * sides[0][1]
                more = coarse_off[1, i, tile(j)] * sides[1][0]
                more = more + coarse_off[2, i, tile(j)] * sides[1][1]
                most = coarse_off[3, i, tile(j)] * sides[2][0]
                most = most + coarse_off[4, i, tile(j)] * sides[2][1]
                coarse_two[0, i + 1, tile(j)] = KEPT * here + coarse_damped[
                    i, tile(j)
                ] * (total + more + most)
            return carry

        lax.fori_loop(0, half, smooth, 0, unroll=UNROLL)
        at_.seam(coarse_two, [0], [0])

        def up(i, gamma):
            face_get, _, face_after = rows_of(outer_y, i)
            for j in range(tiles):
                here, sides = coarse_sides(coarse_two, i, j)
                kept = ((1.0 - DAMPING) / KEPT) * here
                dots = []
                for a, b, c in CLASSES:
                    k = cls(a, b, c)
                    value = tree_sum(
                        [
                            partial[k, i, tile(j)],
                            inner_sum[k, i, tile(j)] * here,
                            outer_x[2 * b + c, i + a, tile(j)] * sides[0][a],
                            (face_after if b else face_get)(2 * a + c, j) * sides[1][b],
                            outer_z[4 * c + 2 * a + b, i, tile(j)] * sides[2][c],
                        ]
                    )
                    new = kept + damped[k, i, tile(j)] * value
                    result[k, i + 1, tile(j)] = new
                    dots.append(residual[k, i, tile(j)] * new)
                gamma = gamma + tree_sum(dots)
            return gamma

        gamma = lax.fori_loop(0, half, up, zero, unroll=UNROLL)
        at_.seam_fine(result)
        return grand_total(gamma)

    gamma = precondition(first_dir)

    def apply(i, acc):
        for j, here, sums in stencil(first_dir, i, True):
            dots = []
            for k in range(8):
                value = diagonal[k, i, tile(j)] * here[k] - sums[k]
                image[k, i, tile(j)] = value
                dots.append(here[k] * value)
            acc = acc + tree_sum(dots)
        return acc

    curve = grand_total(lax.fori_loop(0, half, apply, zero, unroll=UNROLL))
    step_one = gamma / curve

    def update(i, carry):
        for j in range(tiles):
            for k in range(8):
                new = residual[k, i, tile(j)] - step_one * image[k, i, tile(j)]
                residual[k, i, tile(j)] = new
                scaled[k, i + 1, tile(j)] = damped[k, i, tile(j)] * new
        return carry

    lax.fori_loop(0, half, update, 0, unroll=UNROLL)
    at_.seam_fine(scaled)

    gamma_next = precondition(second_dir)

    def bend(i, carry):
        own_part, face_part = carry
        for j, here, sums in stencil(second_dir, i, False):
            own_part = own_part + tree_sum(
                [here[k] * (diagonal[k, i, tile(j)] * here[k]) for k in range(8)]
            )
            face_part = face_part + tree_sum([here[k] * sums[k] for k in range(7)])
        return own_part, face_part

    own_part, face_part = lax.fori_loop(0, half, bend, (zero, zero), unroll=UNROLL)
    ratio = gamma_next / gamma
    curve_next = grand_total(own_part - 2.0 * face_part)
    step_two = gamma_next / (curve_next - ratio * ratio * curve)
    step_first = (step_one + step_two * ratio) * (1.0 / KEPT)
    step_two = step_two * (1.0 / KEPT)

    start = (place - core) * (own // 2)
    upper = jnp.where(start >= half, 1, 0)
    start = start - half * upper
    even = at_.lane % 2 == 0
    source = at_.lane // 2 + HALF * upper
    for at in range(2 * own + 2):
        a = (at + 1) % 2
        spot = start + (at + 1) // 2
        for b in (0, 1):
            for j in range(tiles):
                both = [
                    step_first * first_dir[cls(a, b, c), spot, tile(j)]
                    + step_two * second_dir[cls(a, b, c), spot, tile(j)]
                    for c in (0, 1)
                ]
                planes[at, at_.every(b, j), :] = jnp.where(
                    even,
                    jnp.take_along_axis(both[0], source, axis=1),
                    jnp.take_along_axis(both[1], source, axis=1),
                )


def finish_kernel(planes_ref, state_ref, far_ref, near_ref, adjoint_ref, keep_ref, partner_ref, send_ref, terms):
    own, ny, nz = adjoint_ref.shape
    core = lax.axis_index("space") % 2
    full = (ny, nz)
    y_at = row_index(full)
    z_at = lane_index(full)

    def drop(value, axis, up):
        moved = roll(value, -1 if up else 1, axis)
        at = (y_at, z_at)[axis]
        edge = full[axis] - 1 if up else 0
        return value - jnp.where(at == edge, 0.0, moved)

    is_even = core == 0
    state = [jnp.where(is_even, far_ref[core, 0], near_ref[own])]
    state += [jnp.where(is_even, state_ref[core, x], near_ref[x]) for x in range(own)]
    state += [jnp.where(is_even, near_ref[x], state_ref[core, x]) for x in range(own)]
    state += [jnp.where(is_even, near_ref[own], far_ref[core, 0])]
    for x in range(2 * own):
        here, f = planes_ref[x + 1], state[x + 1]
        term = (here - planes_ref[x + 2]) * (f - state[x + 2])
        term = term + (here - planes_ref[x]) * (f - state[x])
        for axis in (0, 1):
            for up in (True, False):
                term = term + drop(here, axis, up) * drop(f, axis, up)
        terms[x] = -0.5 * term

    groups = send_ref.shape[0] + 1
    chunk = keep_ref.shape[1]
    for x in range(own):
        mine, other = core * own + x, (1 - core) * own + x
        adjoint_ref[x] = planes_ref[1 + mine]
        partner_ref[x, :ny] = planes_ref[1 + other]
        for k in range(groups):
            at = lax.rem(lax.axis_index("pole") + k, groups) * chunk
            at = pl.multiple_of(at, chunk)
            for side, plane in enumerate((mine, other)):
                share = terms[plane, pl.ds(at, chunk), :]
                if k:
                    send_ref[k - 1, side, x] = share
                elif side:
                    partner_ref[x, ny:] = share
                else:
                    keep_ref[x] = share


def whole_grid(conductivity, misfit, forward_states, pole_shifts, pole_weights, pole_order):
    members, own, ny, nz = forward_states.shape
    groups = lax.axis_size("pole")
    peers = lax.axis_size("space")
    even = lax.axis_index("space") % 2 == 0
    mine, theirs, far, fetch_near = gather_blocks([conductivity, misfit], forward_states, "space")
    half, rows = peers * own // 4, ny // 2

    def field(count, extent):
        return (count, extent, rows, 2 * HALF)

    def held(*shape):
        return pltpu.VMEM(shape, jnp.float32)

    vmem = pl.BlockSpec(memory_space=pltpu.VMEM)
    shapes = [
        field(12, half),
        field(4, half + 1),
        field(4, half),
        field(8, half),
        field(8, half),
        field(8, half),
        field(8, half),
        field(5, half + 1),
        (half, rows, 2 * HALF),
        (TILE, 2 * HALF),
    ]
    coefficients = pl.pallas_call(
        setup_kernel,
        out_shape=[jax.ShapeDtypeStruct(shape, jnp.float32) for shape in shapes],
        in_specs=[vmem] * 5,
        out_specs=[vmem] * len(shapes),
        scratch_shapes=[held(*field(8, half + 2))],
        compiler_params=pltpu.CompilerParams(vmem_limit_bytes=6 * 1024 * 1024),
        name="setup",
    )(pole_order[None], pole_shifts[None], pole_weights[None], mine[0], theirs[0])
    coefficients, near = fetch_near(coefficients)
    planes = pl.pallas_call(
        functools.partial(solve_kernel, own=own),
        out_shape=jax.ShapeDtypeStruct((2 * own + 2, ny, nz), jnp.float32),
        in_specs=[vmem] * (2 + len(shapes)),
        out_specs=vmem,
        scratch_shapes=[
            held(*field(8, half)),
            held(*field(8, half + 2)),
            held(*field(8, half)),
            held(*field(8, half + 2)),
            held(*field(8, half + 2)),
            held(*field(8, half)),
            held(*field(1, half + 2)),
            held(*field(1, half + 2)),
        ],
        compiler_params=pltpu.CompilerParams(vmem_limit_bytes=12 * 1024 * 1024),
        name="solve",
    )(mine[1], theirs[1], *coefficients)
    chunk = ny // groups
    adjoint, gradient, partner, send = pl.pallas_call(
        finish_kernel,
        out_shape=[
            jax.ShapeDtypeStruct((own, ny, nz), jnp.float32),
            jax.ShapeDtypeStruct((own, chunk, nz), jnp.float32),
            jax.ShapeDtypeStruct((own, ny + chunk, nz), jnp.float32),
            jax.ShapeDtypeStruct((groups - 1, 2, own, chunk, nz), jnp.float32),
        ],
        in_specs=[vmem] * 4,
        out_specs=[vmem] * 4,
        scratch_shapes=[held(2 * own, ny, nz)],
        compiler_params=pltpu.CompilerParams(vmem_limit_bytes=4 * 1024 * 1024),
        name="finish",
    )(planes, forward_states, far, near)

    arrived = lax.ppermute(partner, "space", [(i, i ^ 1) for i in range(peers)])
    shares = []
    for k in range(1, groups):
        for side in (0, 1):
            pairs = [
                (i * peers + j, (i + k) % groups * peers + (j ^ side))
                for i in range(groups)
                for j in range(peers)
            ]
            shares.append(lax.ppermute(send[k - 1, side], ("pole", "space"), pairs))
    theirs = arrived[:, :ny]
    adjoint_states = jnp.stack(
        [jnp.where(even, adjoint, theirs), jnp.where(even, theirs, adjoint)]
    )
    adjoint_states, arrived = lax.optimization_barrier((adjoint_states, arrived))
    return adjoint_states, gradient + arrived[:, ny:] + sum(shares)


def plus_side(field, which_dim):
    extent = field.shape[which_dim]
    inner_part = lax.slice_in_dim(field, 1, extent, axis=which_dim)
    zero_plane = jnp.zeros_like(lax.slice_in_dim(field, 0, 1, axis=which_dim))
    return jnp.concatenate([inner_part, zero_plane], axis=which_dim)


def minus_side(field, which_dim):
    extent = field.shape[which_dim]
    inner_part = lax.slice_in_dim(field, 0, extent - 1, axis=which_dim)
    zero_plane = jnp.zeros_like(lax.slice_in_dim(field, 0, 1, axis=which_dim))
    return jnp.concatenate([zero_plane, inner_part], axis=which_dim)


def coarse_pick(faces, which_dim, offset):
    extent_x, extent_y, extent_z = faces.shape
    blocks = faces.reshape(extent_x // 2, 2, extent_y // 2, 2, extent_z // 2, 2)
    chosen = lax.index_in_dim(blocks, offset, axis=2 * which_dim + 1, keepdims=True)
    return jnp.sum(chosen, axis=(1, 3, 5))


def side_terms(field, plus_faces, minus_faces, widened):
    result = plus_faces[0] * (field - widened[:, 2:]) + minus_faces[0] * (field - widened[:, :-2])
    for which_dim in (1, 2):
        result = result + plus_faces[which_dim] * (field - plus_side(field, which_dim + 1))
        result = result + minus_faces[which_dim] * (field - minus_side(field, which_dim + 1))
    return result


def fine_image(field, plus_faces, minus_faces, shift_value):
    widened = extended(field, (("space", 1),), 1)
    return shift_value * field + side_terms(field, plus_faces, minus_faces, widened)


def coarse_image(field, plus_faces, minus_faces, shift_value):
    widened = extended(field, (("space", 1),), 1)
    return shift_value * field + side_terms(field, plus_faces, minus_faces, widened)


def restrict(field):
    members, extent_x, extent_y, extent_z = field.shape
    shaped = field.reshape(members, extent_x // 2, 2, extent_y // 2, 2, extent_z // 2, 2)
    return jnp.sum(shaped, axis=(2, 4, 6))


def prolong(field):
    return jnp.repeat(jnp.repeat(jnp.repeat(field, 2, axis=1), 2, axis=2), 2, axis=3)


def precondition(residual, fine, coarse):
    plus_faces, minus_faces, shift_value, diagonal = fine
    coarse_plus, coarse_minus, coarse_shift, coarse_diagonal = coarse
    smooth_one = DAMPING * residual / diagonal
    coarse_rhs = restrict(residual - fine_image(smooth_one, plus_faces, minus_faces, shift_value))
    coarse_one = DAMPING * coarse_rhs / coarse_diagonal
    coarse_two = (
        coarse_one
        + DAMPING
        * (coarse_rhs - coarse_image(coarse_one, coarse_plus, coarse_minus, coarse_shift))
        / coarse_diagonal
    )
    corrected = smooth_one + prolong(coarse_two)
    return (
        corrected
        + DAMPING
        * (residual - fine_image(corrected, plus_faces, minus_faces, shift_value))
        / diagonal
    )


def expand(values):
    return values.reshape(-1, 1, 1, 1)


def cell_sums(values):
    return jnp.sum(values, axis=(1, 2, 3))


def norm_sum(residual, precond):
    return lax.psum(cell_sums(residual * precond), "space")


def solve(rhs, fine, coarse):
    plus_faces, minus_faces, shift_value, diagonal = fine
    iterate = jnp.zeros_like(rhs)
    residual = rhs
    precond = precondition(residual, fine, coarse)
    gamma_now = norm_sum(residual, precond)
    search = precond
    for turn_index in range(ITERS):
        image_field = fine_image(search, plus_faces, minus_faces, shift_value)
        curve = lax.psum(cell_sums(search * image_field), "space")
        step_length = gamma_now / curve
        iterate = iterate + expand(step_length) * search
        if turn_index + 1 < ITERS:
            residual = residual - expand(step_length) * image_field
            precond = precondition(residual, fine, coarse)
            gamma_next = norm_sum(residual, precond)
            search = precond + expand(gamma_next / gamma_now) * search
            gamma_now = gamma_next
    return iterate


def divided(conductivity, misfit, forward_states, pole_shifts, pole_weights, pole_order):
    widened_kappa = extended(conductivity, (("space", 0),), 1)
    plus_faces = [
        0.5 * (conductivity + widened_kappa[2:]),
        0.5 * (conductivity + plus_side(conductivity, 1)),
        0.5 * (conductivity + plus_side(conductivity, 2)),
    ]
    minus_faces = [
        0.5 * (conductivity + widened_kappa[:-2]),
        0.5 * (conductivity + minus_side(conductivity, 1)),
        0.5 * (conductivity + minus_side(conductivity, 2)),
    ]
    base_diagonal = (
        plus_faces[0]
        + plus_faces[1]
        + plus_faces[2]
        + minus_faces[0]
        + minus_faces[1]
        + minus_faces[2]
    )
    coarse_plus = [coarse_pick(plus_faces[which_dim], which_dim, 1) for which_dim in range(3)]
    coarse_minus = [coarse_pick(minus_faces[which_dim], which_dim, 0) for which_dim in range(3)]
    coarse_base = (
        coarse_plus[0]
        + coarse_plus[1]
        + coarse_plus[2]
        + coarse_minus[0]
        + coarse_minus[1]
        + coarse_minus[2]
    )
    pole_index = jnp.arange(pole_shifts.shape[0], dtype=jnp.int32)
    matches = pole_order[:, None] == pole_index[None, :]
    shift_local = jnp.sum(jnp.where(matches, pole_shifts[None, :], 0.0), axis=1)
    weight_local = jnp.sum(jnp.where(matches, pole_weights[None, :], 0.0), axis=1)
    members = forward_states.shape[0]

    def solve_group(shift_part, weight_part):
        shift_value = expand(shift_part)
        fine = (plus_faces, minus_faces, shift_value, base_diagonal[None] + shift_value)
        coarse = (
            coarse_plus,
            coarse_minus,
            8.0 * shift_value,
            coarse_base[None] + 8.0 * shift_value,
        )
        return solve(expand(weight_part) * misfit[None], fine, coarse)

    adjoint_states = jnp.concatenate(
        [
            solve_group(shift_local[member : member + 1], weight_local[member : member + 1])
            for member in range(members)
        ],
        axis=0,
    )
    widened = extended(jnp.stack([adjoint_states, forward_states]), (("space", 2),), 1)
    term = (adjoint_states - widened[0, :, 2:]) * (forward_states - widened[1, :, 2:])
    term = term + (adjoint_states - widened[0, :, :-2]) * (forward_states - widened[1, :, :-2])
    for which_dim in (2, 3):
        term = term + (adjoint_states - plus_side(adjoint_states, which_dim)) * (
            forward_states - plus_side(forward_states, which_dim)
        )
        term = term + (adjoint_states - minus_side(adjoint_states, which_dim)) * (
            forward_states - minus_side(forward_states, which_dim)
        )
    local_term = -0.5 * jnp.sum(term, axis=0)
    gradient = lax.psum_scatter(local_term, "pole", scatter_dimension=1, tiled=True)
    return (adjoint_states, gradient)


def solution(mesh):
    in_specs = (
        P("space", None, None),
        P("space", None, None),
        P("pole", "space", None, None),
        P(),
        P(),
        P("pole"),
    )
    out_specs = (P("pole", "space", None, None), P("space", "pole", None))

    def body(conductivity, misfit, forward_states, *poles):
        nx = conductivity.shape[0] * lax.axis_size("space")
        _, ny, nz = conductivity.shape
        peers = lax.axis_size("space")
        small = nx * ny * nz <= REPLICATED_CELLS and forward_states.shape[:2] == (2, 2)
        if small and nz == 2 * HALF and peers > 2 and peers & (peers - 1) == 0:
            return whole_grid(conductivity, misfit, forward_states, *poles)
        return divided(conductivity, misfit, forward_states, *poles)

    return jax.shard_map(
        body, mesh=mesh, in_specs=in_specs, out_specs=out_specs, check_vma=False
    )
```

```python
import functools

import jax
import jax.numpy as jnp
from jax import lax
from jax.experimental import pallas as pl
from jax.experimental.pallas import tpu as pltpu
from jax.sharding import PartitionSpec as P

ITERS = 2
DAMPING = 0.8
KEPT = 2.0 - DAMPING
REPLICATED_CELLS = 32 * 64 * 128
HALF = 64
TILE = 8
UNROLL = 8


def extended(array, sides, width):
    for axis, dim in sides:
        peers, length = (lax.axis_size(axis), array.shape[dim])
        up = [(i, (i + 1) % peers) for i in range(peers - 1)]
        down = [(j, i) for i, j in up]
        last = lax.slice_in_dim(array, length - width, length, axis=dim)
        leading = lax.slice_in_dim(array, 0, width, axis=dim)
        before = lax.ppermute(last, axis, up)
        after = lax.ppermute(leading, axis, down)
        array = jnp.concatenate([before, array, after], axis=dim)
    return array


def lane_index(shape):
    return lax.broadcasted_iota(jnp.int32, shape, len(shape) - 1)


def row_index(shape):
    return lax.broadcasted_iota(jnp.int32, shape, len(shape) - 2)


def roll(block, shift, axis):
    return pltpu.roll(block, shift % block.shape[axis], axis)


def inverse(value):
    guess = pl.reciprocal(value, approx=True)
    return guess * (2.0 - value * guess)


def tree_sum(values):
    while len(values) > 1:
        values = [sum(values[at : at + 2]) for at in range(0, len(values), 2)]
    return values[0]


def grand_total(acc):
    line = jnp.sum(acc, axis=0, keepdims=True)
    return jnp.broadcast_to(jnp.sum(line, axis=1, keepdims=True), acc.shape)


def swap_masks(peers, flip):
    falling = []
    mask = peers // 2
    while mask > 1:
        falling.append(mask)
        mask //= 2
    if flip:
        return falling, falling[-1:] + falling[:-1]
    return falling[::-1], falling[:1] + falling[:0:-1]


def block_pair(u, holder, peers, flip):
    even, odd = swap_masks(peers, flip)
    parity = holder % 2
    top = jnp.where(parity == 0, even.index(peers // 2), odd.index(peers // 2))
    below = u & ((1 << top) - 1)
    base = ((u >> top) << (top + 1)) | below
    upper = jnp.where(holder >= peers // 2, 1, 0)
    first = base | (upper << top)
    second = base | ((1 - upper) << top)
    home = holder
    for step, (mask_even, mask_odd) in enumerate(zip(even, odd)):
        mask = jnp.where(parity == 0, mask_even, mask_odd)
        home = home ^ (((first >> step) & 1) * mask)
    return first, second, home


def prepare_kernel(kappa_ref, misfit_ref, kappa_out, misfit_out, *, axis, peers):
    at_ = Layout(kappa_ref.shape[1] // 2)
    upper = jnp.where(lax.axis_index(axis) >= peers // 2, 1, 0)
    at_.deal(kappa_ref, kappa_out, upper)
    at_.deal(misfit_ref, misfit_out, upper)


def join_kernel(*refs, masks, axis, peers):
    place = lax.axis_index(axis)
    at_ = Layout(refs[0].shape[1] // 2)
    for at, (even, odd) in enumerate(masks):
        partner = place ^ jnp.where(place % 2 == 0, even, odd)
        refs[4 + at][0] = refs[at][...]
        at_.deal(refs[2 + at], refs[4 + at].at[1], jnp.where(partner >= peers // 2, 1, 0))


def gather_blocks(blocks, states, axis):
    peers = lax.axis_size(axis)
    even = lax.axis_index(axis) % 2 == 0
    swap = [(i, i ^ 1) for i in range(peers)]
    over = [(i, i + 1 if i % 2 else i - 1) for i in range(1, peers - 1)]
    vmem = pl.BlockSpec(memory_space=pltpu.VMEM)
    swaps = [list(zip(*swap_masks(peers, flip))) for flip in (False, True)]
    own = pl.pallas_call(
        functools.partial(prepare_kernel, axis=axis, peers=peers),
        out_shape=[jax.ShapeDtypeStruct(block.shape, jnp.float32) for block in blocks],
        in_specs=[vmem] * 2,
        out_specs=[vmem] * 2,
        compiler_params=pltpu.CompilerParams(vmem_limit_bytes=1024 * 1024),
        name="prepare",
    )(*blocks)
    held = list(blocks)
    for step in range(len(swaps[0])):
        arrived = []
        for at in (0, 1):
            masks = swaps[at][step]
            pairs = [(i, i ^ masks[i % 2]) for i in range(peers)]
            arrived.append(lax.ppermute(held[at], axis, pairs))
        if step:
            held = [jnp.concatenate(pair, axis=0) for pair in zip(held, arrived)]
            continue
        masks = [swaps[at][0] for at in (0, 1)]
        shape = jax.ShapeDtypeStruct((2, *blocks[0].shape), jnp.float32)
        held[:] = pl.pallas_call(
            functools.partial(join_kernel, masks=masks, axis=axis, peers=peers),
            out_shape=[shape] * 2,
            in_specs=[vmem] * 4,
            out_specs=[vmem] * 2,
            compiler_params=pltpu.CompilerParams(vmem_limit_bytes=1024 * 1024),
            name="join",
        )(*own, *arrived)
        held[1], states = lax.optimization_barrier((held[1], states))
        far = lax.ppermute(jnp.where(even, states[:, :1], states[:, -1:]), axis, over)
    other = [lax.ppermute(part, axis, swap) for part in held]

    def fetch_near(after):
        late, states_late, far_late = lax.optimization_barrier((after, states, far))
        given = jnp.concatenate([states_late, far_late], axis=1)
        return late, lax.ppermute(jnp.where(even, given[1], given[0]), axis, swap)

    return held, other, far, fetch_near


CLASSES = [(a, b, c) for a in (0, 1) for b in (0, 1) for c in (0, 1)]
PAIRS = [(p, q) for p in (0, 1) for q in (0, 1)]


def cls(a, b, c):
    return 4 * a + 2 * b + c


def inner_faces(p, q):
    return (
        (2 * p + q, cls(0, p, q), cls(1, p, q)),
        (4 + 2 * p + q, cls(p, 0, q), cls(p, 1, q)),
        (8 + 2 * p + q, cls(p, q, 0), cls(p, q, 1)),
    )


class Layout:
    def __init__(self, rows):
        self.tiles = rows // TILE
        self.lane = lane_index((TILE, 2 * HALF))
        self.row = row_index((TILE, 2 * HALF))
        self.left = self.lane < HALF
        self.zero = jnp.zeros((TILE, 2 * HALF), jnp.float32)

    def tile(self, j):
        return pl.ds(TILE * j, TILE)

    def every(self, b, j):
        return pl.ds(b + 2 * j, TILE, stride=2 * self.tiles)

    def row_before(self, load, j):
        return load(j - 1) if j else roll(load(self.tiles - 1), 1, 0)

    def row_after(self, load, j):
        return load(j + 1) if j + 1 < self.tiles else roll(load(0), -1, 0)

    def seam(self, ref, low, high):
        last = ref.shape[1] - 1
        for j in range(self.tiles):
            for k in low:
                moved = roll(ref[k, last - 1, self.tile(j)], HALF, 1)
                ref[k, 0, self.tile(j)] = jnp.where(self.left, 0.0, moved)
            for k in high:
                moved = roll(ref[k, 1, self.tile(j)], HALF, 1)
                ref[k, last, self.tile(j)] = jnp.where(self.left, moved, 0.0)

    def seam_fine(self, ref):
        count = ref.shape[0]
        self.seam(
            ref,
            [k for k in range(count) if k % 8 >= 4],
            [k for k in range(count) if k % 8 < 4],
        )

    def dealt(self, b, j):
        return pl.ds(TILE * (self.tiles * b + j), TILE)

    def deal(self, block_ref, out_ref, upper):
        odd = jnp.where(self.left, upper, 1 - upper)
        column = 2 * (self.lane % HALF) + odd
        for x in range(block_ref.shape[0]):
            for b in (0, 1):
                for j in range(self.tiles):
                    rows = block_ref[x, self.every(b, j), :]
                    out_ref[x, self.dealt(b, j), :] = jnp.take_along_axis(rows, column, axis=1)

    def arrange(self, mine_ref, theirs_ref, place, flip, store):
        blocks, own = mine_ref.shape[:2]

        def pair(u, carry):
            for ref, holder in ((mine_ref, place), (theirs_ref, place ^ 1)):
                first, second, home = block_pair(u, holder, 2 * blocks, flip)
                for x in range(own):
                    spot = home * (own // 2) + x // 2
                    for b in (0, 1):
                        for j in range(self.tiles):
                            one = ref[first, x, self.dealt(b, j), :]
                            two = ref[second, x, self.dealt(b, j), :]
                            store(cls(x % 2, b, 0), spot, j, jnp.where(self.left, one, two))
                            odd = roll(jnp.where(self.left, two, one), HALF, 1)
                            store(cls(x % 2, b, 1), spot, j, odd)
            return carry

        lax.fori_loop(0, blocks // 2, pair, 0)


def setup_kernel(
    order_ref,
    shifts_ref,
    weights_ref,
    mine_ref,
    theirs_ref,
    inner,
    outer_x,
    outer_y,
    outer_z,
    inner_sum,
    diagonal,
    damped,
    coarse_off,
    coarse_damped,
    chosen,
    half_kappa,
):
    half = inner.shape[1]
    at_ = Layout(inner.shape[2])
    tile, tiles = at_.tile, at_.tiles
    place = lax.axis_index("space")
    pole = jnp.where(place % 2 == 0, order_ref[:, 0:1], order_ref[:, 1:2])
    taken = lane_index(shifts_ref.shape) == pole
    shift = jnp.sum(jnp.where(taken, shifts_ref[...], 0.0), axis=1, keepdims=True)
    weight = jnp.sum(jnp.where(taken, weights_ref[...], 0.0), axis=1, keepdims=True)
    shift = jnp.broadcast_to(shift, at_.zero.shape)
    chosen[...] = jnp.broadcast_to(weight, at_.zero.shape)

    def keep(k, spot, j, value):
        half_kappa[k, spot + 1, tile(j)] = 0.5 * value

    at_.arrange(mine_ref, theirs_ref, place, False, keep)
    at_.seam_fine(half_kappa)

    z_low = jnp.where(at_.lane % HALF > 0, 1.0, 0.0)
    z_high = jnp.where(at_.lane % HALF < HALF - 1, 1.0, 0.0)
    y_low = [jnp.where(at_.row > 0, 1.0, 0.0)] + [None] * (tiles - 1)
    y_high = [None] * (tiles - 1) + [jnp.where(at_.row < TILE - 1, 1.0, 0.0)]

    def masked(mask, value):
        return value if mask is None else mask * value

    def plane(i, carry):
        for j in range(tiles):
            kap = [half_kappa[k, i + 1, tile(j)] for k in range(8)]
            inside = [[] for _ in range(8)]
            outside = [[] for _ in range(8)]
            off = [[] for _ in range(5)]
            for p, q in PAIRS:
                for face_at, low, high in inner_faces(p, q):
                    face = kap[low] + kap[high]
                    inner[face_at, i, tile(j)] = face
                    inside[low].append(face)
                    inside[high].append(face)
                at = 2 * p + q

                low, high = cls(0, p, q), cls(1, p, q)
                minus = kap[low] + half_kappa[high, i, tile(j)]
                plus = kap[high] + half_kappa[low, i + 2, tile(j)]
                outside[low].append(minus)
                outside[high].append(plus)
                outer_x[at, i, tile(j)] = minus
                off[0].append(minus)

                low, high = cls(p, 0, q), cls(p, 1, q)
                side = at_.row_before(lambda r: half_kappa[high, i + 1, tile(r)], j)
                minus = kap[low] + masked(y_low[j], side)
                side = at_.row_after(lambda r: half_kappa[low, i + 1, tile(r)], j)
                plus = kap[high] + masked(y_high[j], side)
                outside[low].append(minus)
                outside[high].append(plus)
                minus, plus = masked(y_low[j], minus), masked(y_high[j], plus)
                outer_y[at, i, tile(j)] = minus
                off[1].append(minus)
                off[2].append(plus)

                low, high = cls(p, q, 0), cls(p, q, 1)
                minus = kap[low] + z_low * roll(kap[high], 1, 1)
                plus = kap[high] + z_high * roll(kap[low], -1, 1)
                outside[low].append(minus)
                outside[high].append(plus)
                minus, plus = z_low * minus, z_high * plus
                outer_z[at, i, tile(j)] = minus
                outer_z[4 + at, i, tile(j)] = plus
                off[3].append(minus)
                off[4].append(plus)
            coarse_total = []
            for k in range(8):
                within, without = tree_sum(inside[k]), tree_sum(outside[k])
                inner_sum[k, i, tile(j)] = within
                base = within + without + shift
                diagonal[k, i, tile(j)] = base
                coarse_total.append(without)
                damped[k, i, tile(j)] = (DAMPING / KEPT) * inverse(base)
            for at, part in enumerate(off):
                coarse_off[at, i, tile(j)] = tree_sum(part)
            coarse_damped[i, tile(j)] = DAMPING * inverse(tree_sum(coarse_total) + 8.0 * shift)
        return carry

    lax.fori_loop(0, half, plane, 0, unroll=UNROLL)
    for j in range(tiles):
        part = []
        for p, q in PAIRS:
            face = half_kappa[cls(0, p, q), half + 1, tile(j)]
            face = face + half_kappa[cls(1, p, q), half, tile(j)]
            outer_x[2 * p + q, half, tile(j)] = face
            part.append(face)
        coarse_off[0, half, tile(j)] = tree_sum(part)


def solve_kernel(
    mine_ref,
    theirs_ref,
    inner,
    outer_x,
    outer_y,
    outer_z,
    inner_sum,
    diagonal,
    damped,
    coarse_off,
    coarse_damped,
    chosen,
    planes,
    residual,
    scaled,
    partial,
    first_dir,
    second_dir,
    image,
    coarse_one,
    coarse_two,
    *,
    own,
):
    half, rows = inner.shape[1:3]
    at_ = Layout(rows)
    tile, tiles, zero = at_.tile, at_.tiles, at_.zero
    place = lax.axis_index("space")
    core = place % 2
    weight = KEPT * chosen[...]

    def begin(k, spot, j, value):
        res = weight * value
        residual[k, spot, tile(j)] = res
        scaled[k, spot + 1, tile(j)] = damped[k, spot, tile(j)] * res

    at_.arrange(mine_ref, theirs_ref, place, True, begin)
    at_.seam_fine(scaled)

    def rows_of(ref, i):
        cache = {}

        def load(k, j, step):
            if abs(j - step) > 1:
                return ref[k, i, tile(j)]
            if (k, j) not in cache:
                cache[k, j] = ref[k, i, tile(j)]
            return cache[k, j]

        def get(k, j):
            return load(k, j, j)

        def before(k, j):
            return at_.row_before(lambda r: load(k, r, j), j)

        def after(k, j):
            return at_.row_after(lambda r: load(k, r, j), j)

        return get, before, after

    def stencil(field, i, both):
        get, before, after = rows_of(field, i + 1)
        face_get, _, face_after = rows_of(outer_y, i)
        for j in range(tiles):
            here = [get(k, j) for k in range(8)]
            terms = [[] for _ in range(8)]
            for p, q in PAIRS:
                at = 2 * p + q
                for face_at, low, high in inner_faces(p, q):
                    face = inner[face_at, i, tile(j)]
                    terms[low].append(face * here[high])
                    if both:
                        terms[high].append(face * here[low])
                low, high = cls(0, p, q), cls(1, p, q)
                terms[low].append(outer_x[at, i, tile(j)] * field[high, i, tile(j)])
                if both:
                    side = field[low, i + 2, tile(j)]
                    terms[high].append(outer_x[at, i + 1, tile(j)] * side)
                low, high = cls(p, 0, q), cls(p, 1, q)
                terms[low].append(face_get(at, j) * before(high, j))
                if both:
                    terms[high].append(face_after(at, j) * after(low, j))
                low, high = cls(p, q, 0), cls(p, q, 1)
                terms[low].append(outer_z[at, i, tile(j)] * roll(here[high], 1, 1))
                if both:
                    terms[high].append(outer_z[4 + at, i, tile(j)] * roll(here[low], -1, 1))
            yield j, here, [tree_sum(part) if part else None for part in terms]

    def coarse_sides(field, i, j):
        here = field[0, i + 1, tile(j)]
        return here, (
            (field[0, i, tile(j)], field[0, i + 2, tile(j)]),
            (
                at_.row_before(lambda r: field[0, i + 1, tile(r)], j),
                at_.row_after(lambda r: field[0, i + 1, tile(r)], j),
            ),
            (roll(here, 1, 1), roll(here, -1, 1)),
        )

    def precondition(result):
        def down(i, carry):
            for j, _, sums in stencil(scaled, i, True):
                res = [residual[k, i, tile(j)] for k in range(8)]
                parts = [res[k] + sums[k] for k in range(8)]
                for k in range(8):
                    partial[k, i, tile(j)] = parts[k]
                rhs = tree_sum(parts) - (1.0 / KEPT) * tree_sum(res)
                coarse_one[0, i + 1, tile(j)] = coarse_damped[i, tile(j)] * rhs
            return carry

        lax.fori_loop(0, half, down, 0, unroll=UNROLL)
        at_.seam(coarse_one, [0], [0])

        def smooth(i, carry):
            for j in range(tiles):
                here, sides = coarse_sides(coarse_one, i, j)
                total = coarse_off[0, i, tile(j)] * sides[0][0]
                total = total + coarse_off[0, i + 1, tile(j)] * sides[0][1]
                more = coarse_off[1, i, tile(j)] * sides[1][0]
                more = more + coarse_off[2, i, tile(j)] * sides[1][1]
                most = coarse_off[3, i, tile(j)] * sides[2][0]
                most = most + coarse_off[4, i, tile(j)] * sides[2][1]
                coarse_two[0, i + 1, tile(j)] = KEPT * here + coarse_damped[
                    i, tile(j)
                ] * (total + more + most)
            return carry

        lax.fori_loop(0, half, smooth, 0, unroll=UNROLL)
        at_.seam(coarse_two, [0], [0])

        def up(i, gamma):
            face_get, _, face_after = rows_of(outer_y, i)
            for j in range(tiles):
                here, sides = coarse_sides(coarse_two, i, j)
                kept = ((1.0 - DAMPING) / KEPT) * here
                dots = []
                for a, b, c in CLASSES:
                    k = cls(a, b, c)
                    value = tree_sum(
                        [
                            partial[k, i, tile(j)],
                            inner_sum[k, i, tile(j)] * here,
                            outer_x[2 * b + c, i + a, tile(j)] * sides[0][a],
                            (face_after if b else face_get)(2 * a + c, j) * sides[1][b],
                            outer_z[4 * c + 2 * a + b, i, tile(j)] * sides[2][c],
                        ]
                    )
                    new = kept + damped[k, i, tile(j)] * value
                    result[k, i + 1, tile(j)] = new
                    dots.append(residual[k, i, tile(j)] * new)
                gamma = gamma + tree_sum(dots)
            return gamma

        gamma = lax.fori_loop(0, half, up, zero, unroll=UNROLL)
        at_.seam_fine(result)
        return grand_total(gamma)

    gamma = precondition(first_dir)

    def apply(i, acc):
        for j, here, sums in stencil(first_dir, i, True):
            dots = []
            for k in range(8):
                value = diagonal[k, i, tile(j)] * here[k] - sums[k]
                image[k, i, tile(j)] = value
                dots.append(here[k] * value)
            acc = acc + tree_sum(dots)
        return acc

    curve = grand_total(lax.fori_loop(0, half, apply, zero, unroll=UNROLL))
    step_one = gamma / curve

    def update(i, carry):
        for j in range(tiles):
            for k in range(8):
                new = residual[k, i, tile(j)] - step_one * image[k, i, tile(j)]
                residual[k, i, tile(j)] = new
                scaled[k, i + 1, tile(j)] = damped[k, i, tile(j)] * new
        return carry

    lax.fori_loop(0, half, update, 0, unroll=UNROLL)
    at_.seam_fine(scaled)

    gamma_next = precondition(second_dir)

    def bend(i, carry):
        own_part, face_part = carry
        for j, here, sums in stencil(second_dir, i, False):
            own_part = own_part + tree_sum(
                [here[k] * (diagonal[k, i, tile(j)] * here[k]) for k in range(8)]
            )
            face_part = face_part + tree_sum([here[k] * sums[k] for k in range(7)])
        return own_part, face_part

    own_part, face_part = lax.fori_loop(0, half, bend, (zero, zero), unroll=UNROLL)
    ratio = gamma_next / gamma
    curve_next = grand_total(own_part - 2.0 * face_part)
    step_two = gamma_next / (curve_next - ratio * ratio * curve)
    step_first = (step_one + step_two * ratio) * (1.0 / KEPT)
    step_two = step_two * (1.0 / KEPT)

    start = (place - core) * (own // 2)
    upper = jnp.where(start >= half, 1, 0)
    start = start - half * upper
    even = at_.lane % 2 == 0
    source = at_.lane // 2 + HALF * upper
    for at in range(2 * own + 2):
        a = (at + 1) % 2
        spot = start + (at + 1) // 2
        for b in (0, 1):
            for j in range(tiles):
                both = [
                    step_first * first_dir[cls(a, b, c), spot, tile(j)]
                    + step_two * second_dir[cls(a, b, c), spot, tile(j)]
                    for c in (0, 1)
                ]
                planes[at, at_.every(b, j), :] = jnp.where(
                    even,
                    jnp.take_along_axis(both[0], source, axis=1),
                    jnp.take_along_axis(both[1], source, axis=1),
                )


def finish_kernel(planes_ref, state_ref, far_ref, near_ref, adjoint_ref, keep_ref, partner_ref, send_ref, terms):
    own, ny, nz = adjoint_ref.shape
    core = lax.axis_index("space") % 2
    full = (ny, nz)
    y_at = row_index(full)
    z_at = lane_index(full)

    def drop(value, axis, up):
        moved = roll(value, -1 if up else 1, axis)
        at = (y_at, z_at)[axis]
        edge = full[axis] - 1 if up else 0
        return value - jnp.where(at == edge, 0.0, moved)

    is_even = core == 0
    state = [jnp.where(is_even, far_ref[core, 0], near_ref[own])]
    state += [jnp.where(is_even, state_ref[core, x], near_ref[x]) for x in range(own)]
    state += [jnp.where(is_even, near_ref[x], state_ref[core, x]) for x in range(own)]
    state += [jnp.where(is_even, near_ref[own], far_ref[core, 0])]
    for x in range(2 * own):
        here, f = planes_ref[x + 1], state[x + 1]
        term = (here - planes_ref[x + 2]) * (f - state[x + 2])
        term = term + (here - planes_ref[x]) * (f - state[x])
        for axis in (0, 1):
            for up in (True, False):
                term = term + drop(here, axis, up) * drop(f, axis, up)
        terms[x] = -0.5 * term

    groups = send_ref.shape[0] + 1
    chunk = keep_ref.shape[1]
    for x in range(own):
        mine, other = core * own + x, (1 - core) * own + x
        adjoint_ref[x] = planes_ref[1 + mine]
        partner_ref[x, :ny] = planes_ref[1 + other]
        for k in range(groups):
            at = lax.rem(lax.axis_index("pole") + k, groups) * chunk
            at = pl.multiple_of(at, chunk)
            for side, plane in enumerate((mine, other)):
                share = terms[plane, pl.ds(at, chunk), :]
                if k:
                    send_ref[k - 1, side, x] = share
                elif side:
                    partner_ref[x, ny:] = share
                else:
                    keep_ref[x] = share


def whole_grid(conductivity, misfit, forward_states, pole_shifts, pole_weights, pole_order):
    members, own, ny, nz = forward_states.shape
    groups = lax.axis_size("pole")
    peers = lax.axis_size("space")
    even = lax.axis_index("space") % 2 == 0
    mine, theirs, far, fetch_near = gather_blocks([conductivity, misfit], forward_states, "space")
    half, rows = peers * own // 4, ny // 2

    def field(count, extent):
        return (count, extent, rows, 2 * HALF)

    def held(*shape):
        return pltpu.VMEM(shape, jnp.float32)

    vmem = pl.BlockSpec(memory_space=pltpu.VMEM)
    shapes = [
        field(12, half),
        field(4, half + 1),
        field(4, half),
        field(8, half),
        field(8, half),
        field(8, half),
        field(8, half),
        field(5, half + 1),
        (half, rows, 2 * HALF),
        (TILE, 2 * HALF),
    ]
    coefficients = pl.pallas_call(
        setup_kernel,
        out_shape=[jax.ShapeDtypeStruct(shape, jnp.float32) for shape in shapes],
        in_specs=[vmem] * 5,
        out_specs=[vmem] * len(shapes),
        scratch_shapes=[held(*field(8, half + 2))],
        compiler_params=pltpu.CompilerParams(vmem_limit_bytes=6 * 1024 * 1024),
        name="setup",
    )(pole_order[None], pole_shifts[None], pole_weights[None], mine[0], theirs[0])
    coefficients, near = fetch_near(coefficients)
    planes = pl.pallas_call(
        functools.partial(solve_kernel, own=own),
        out_shape=jax.ShapeDtypeStruct((2 * own + 2, ny, nz), jnp.float32),
        in_specs=[vmem] * (2 + len(shapes)),
        out_specs=vmem,
        scratch_shapes=[
            held(*field(8, half)),
            held(*field(8, half + 2)),
            held(*field(8, half)),
            held(*field(8, half + 2)),
            held(*field(8, half + 2)),
            held(*field(8, half)),
            held(*field(1, half + 2)),
            held(*field(1, half + 2)),
        ],
        compiler_params=pltpu.CompilerParams(vmem_limit_bytes=12 * 1024 * 1024),
        name="solve",
    )(mine[1], theirs[1], *coefficients)
    chunk = ny // groups
    adjoint, gradient, partner, send = pl.pallas_call(
        finish_kernel,
        out_shape=[
            jax.ShapeDtypeStruct((own, ny, nz), jnp.float32),
            jax.ShapeDtypeStruct((own, chunk, nz), jnp.float32),
            jax.ShapeDtypeStruct((own, ny + chunk, nz), jnp.float32),
            jax.ShapeDtypeStruct((groups - 1, 2, own, chunk, nz), jnp.float32),
        ],
        in_specs=[vmem] * 4,
        out_specs=[vmem] * 4,
        scratch_shapes=[held(2 * own, ny, nz)],
        compiler_params=pltpu.CompilerParams(vmem_limit_bytes=4 * 1024 * 1024),
        name="finish",
    )(planes, forward_states, far, near)

    arrived = lax.ppermute(partner, "space", [(i, i ^ 1) for i in range(peers)])
    shares = []
    for k in range(1, groups):
        for side in (0, 1):
            pairs = [
                (i * peers + j, (i + k) % groups * peers + (j ^ side))
                for i in range(groups)
                for j in range(peers)
            ]
            shares.append(lax.ppermute(send[k - 1, side], ("pole", "space"), pairs))
    theirs = arrived[:, :ny]
    adjoint_states = jnp.stack(
        [jnp.where(even, adjoint, theirs), jnp.where(even, theirs, adjoint)]
    )
    adjoint_states, arrived = lax.optimization_barrier((adjoint_states, arrived))
    return adjoint_states, gradient + arrived[:, ny:] + sum(shares)


def plus_side(field, which_dim):
    extent = field.shape[which_dim]
    inner_part = lax.slice_in_dim(field, 1, extent, axis=which_dim)
    zero_plane = jnp.zeros_like(lax.slice_in_dim(field, 0, 1, axis=which_dim))
    return jnp.concatenate([inner_part, zero_plane], axis=which_dim)


def minus_side(field, which_dim):
    extent = field.shape[which_dim]
    inner_part = lax.slice_in_dim(field, 0, extent - 1, axis=which_dim)
    zero_plane = jnp.zeros_like(lax.slice_in_dim(field, 0, 1, axis=which_dim))
    return jnp.concatenate([zero_plane, inner_part], axis=which_dim)


def coarse_pick(faces, which_dim, offset):
    extent_x, extent_y, extent_z = faces.shape
    blocks = faces.reshape(extent_x // 2, 2, extent_y // 2, 2, extent_z // 2, 2)
    chosen = lax.index_in_dim(blocks, offset, axis=2 * which_dim + 1, keepdims=True)
    return jnp.sum(chosen, axis=(1, 3, 5))


def side_terms(field, plus_faces, minus_faces, widened):
    result = plus_faces[0] * (field - widened[:, 2:]) + minus_faces[0] * (field - widened[:, :-2])
    for which_dim in (1, 2):
        result = result + plus_faces[which_dim] * (field - plus_side(field, which_dim + 1))
        result = result + minus_faces[which_dim] * (field - minus_side(field, which_dim + 1))
    return result


def fine_image(field, plus_faces, minus_faces, shift_value):
    widened = extended(field, (("space", 1),), 1)
    return shift_value * field + side_terms(field, plus_faces, minus_faces, widened)


def coarse_image(field, plus_faces, minus_faces, shift_value):
    widened = extended(field, (("space", 1),), 1)
    return shift_value * field + side_terms(field, plus_faces, minus_faces, widened)


def restrict(field):
    members, extent_x, extent_y, extent_z = field.shape
    shaped = field.reshape(members, extent_x // 2, 2, extent_y // 2, 2, extent_z // 2, 2)
    return jnp.sum(shaped, axis=(2, 4, 6))


def prolong(field):
    return jnp.repeat(jnp.repeat(jnp.repeat(field, 2, axis=1), 2, axis=2), 2, axis=3)


def precondition(residual, fine, coarse):
    plus_faces, minus_faces, shift_value, diagonal = fine
    coarse_plus, coarse_minus, coarse_shift, coarse_diagonal = coarse
    smooth_one = DAMPING * residual / diagonal
    coarse_rhs = restrict(residual - fine_image(smooth_one, plus_faces, minus_faces, shift_value))
    coarse_one = DAMPING * coarse_rhs / coarse_diagonal
    coarse_two = (
        coarse_one
        + DAMPING
        * (coarse_rhs - coarse_image(coarse_one, coarse_plus, coarse_minus, coarse_shift))
        / coarse_diagonal
    )
    corrected = smooth_one + prolong(coarse_two)
    return (
        corrected
        + DAMPING
        * (residual - fine_image(corrected, plus_faces, minus_faces, shift_value))
        / diagonal
    )


def expand(values):
    return values.reshape(-1, 1, 1, 1)


def cell_sums(values):
    return jnp.sum(values, axis=(1, 2, 3))


def norm_sum(residual, precond):
    return lax.psum(cell_sums(residual * precond), "space")


def solve(rhs, fine, coarse):
    plus_faces, minus_faces, shift_value, diagonal = fine
    iterate = jnp.zeros_like(rhs)
    residual = rhs
    precond = precondition(residual, fine, coarse)
    gamma_now = norm_sum(residual, precond)
    search = precond
    for turn_index in range(ITERS):
        image_field = fine_image(search, plus_faces, minus_faces, shift_value)
        curve = lax.psum(cell_sums(search * image_field), "space")
        step_length = gamma_now / curve
        iterate = iterate + expand(step_length) * search
        if turn_index + 1 < ITERS:
            residual = residual - expand(step_length) * image_field
            precond = precondition(residual, fine, coarse)
            gamma_next = norm_sum(residual, precond)
            search = precond + expand(gamma_next / gamma_now) * search
            gamma_now = gamma_next
    return iterate


def divided(conductivity, misfit, forward_states, pole_shifts, pole_weights, pole_order):
    widened_kappa = extended(conductivity, (("space", 0),), 1)
    plus_faces = [
        0.5 * (conductivity + widened_kappa[2:]),
        0.5 * (conductivity + plus_side(conductivity, 1)),
        0.5 * (conductivity + plus_side(conductivity, 2)),
    ]
    minus_faces = [
        0.5 * (conductivity + widened_kappa[:-2]),
        0.5 * (conductivity + minus_side(conductivity, 1)),
        0.5 * (conductivity + minus_side(conductivity, 2)),
    ]
    base_diagonal = (
        plus_faces[0]
        + plus_faces[1]
        + plus_faces[2]
        + minus_faces[0]
        + minus_faces[1]
        + minus_faces[2]
    )
    coarse_plus = [coarse_pick(plus_faces[which_dim], which_dim, 1) for which_dim in range(3)]
    coarse_minus = [coarse_pick(minus_faces[which_dim], which_dim, 0) for which_dim in range(3)]
    coarse_base = (
        coarse_plus[0]
        + coarse_plus[1]
        + coarse_plus[2]
        + coarse_minus[0]
        + coarse_minus[1]
        + coarse_minus[2]
    )
    pole_index = jnp.arange(pole_shifts.shape[0], dtype=jnp.int32)
    matches = pole_order[:, None] == pole_index[None, :]
    shift_local = jnp.sum(jnp.where(matches, pole_shifts[None, :], 0.0), axis=1)
    weight_local = jnp.sum(jnp.where(matches, pole_weights[None, :], 0.0), axis=1)
    members = forward_states.shape[0]

    def solve_group(shift_part, weight_part):
        shift_value = expand(shift_part)
        fine = (plus_faces, minus_faces, shift_value, base_diagonal[None] + shift_value)
        coarse = (
            coarse_plus,
            coarse_minus,
            8.0 * shift_value,
            coarse_base[None] + 8.0 * shift_value,
        )
        return solve(expand(weight_part) * misfit[None], fine, coarse)

    adjoint_states = jnp.concatenate(
        [
            solve_group(shift_local[member : member + 1], weight_local[member : member + 1])
            for member in range(members)
        ],
        axis=0,
    )
    widened = extended(jnp.stack([adjoint_states, forward_states]), (("space", 2),), 1)
    term = (adjoint_states - widened[0, :, 2:]) * (forward_states - widened[1, :, 2:])
    term = term + (adjoint_states - widened[0, :, :-2]) * (forward_states - widened[1, :, :-2])
    for which_dim in (2, 3):
        term = term + (adjoint_states - plus_side(adjoint_states, which_dim)) * (
            forward_states - plus_side(forward_states, which_dim)
        )
        term = term + (adjoint_states - minus_side(adjoint_states, which_dim)) * (
            forward_states - minus_side(forward_states, which_dim)
        )
    local_term = -0.5 * jnp.sum(term, axis=0)
    gradient = lax.psum_scatter(local_term, "pole", scatter_dimension=1, tiled=True)
    return (adjoint_states, gradient)


def solution(mesh):
    in_specs = (
        P("space", None, None),
        P("space", None, None),
        P("pole", "space", None, None),
        P(),
        P(),
        P("pole"),
    )
    out_specs = (P("pole", "space", None, None), P("space", "pole", None))

    def body(conductivity, misfit, forward_states, *poles):
        nx = conductivity.shape[0] * lax.axis_size("space")
        _, ny, nz = conductivity.shape
        peers = lax.axis_size("space")
        small = nx * ny * nz <= REPLICATED_CELLS and forward_states.shape[:2] == (2, 2)
        if small and nz == 2 * HALF and peers > 2 and peers & (peers - 1) == 0:
            return whole_grid(conductivity, misfit, forward_states, *poles)
        return divided(conductivity, misfit, forward_states, *poles)

    return jax.shard_map(
        body, mesh=mesh, in_specs=in_specs, out_specs=out_specs, check_vma=False
    )
```

```python
import functools

import jax
import jax.numpy as jnp
from jax import lax
from jax.experimental import pallas as pl
from jax.experimental.pallas import tpu as pltpu
from jax.sharding import PartitionSpec as P

ITERS = 2
DAMPING = 0.8
KEPT = 2.0 - DAMPING
REPLICATED_CELLS = 32 * 64 * 128
HALF = 64
TILE = 8
UNROLL = 8


def extended(array, sides, width):
    for axis, dim in sides:
        peers, length = (lax.axis_size(axis), array.shape[dim])
        up = [(i, (i + 1) % peers) for i in range(peers - 1)]
        down = [(j, i) for i, j in up]
        last = lax.slice_in_dim(array, length - width, length, axis=dim)
        leading = lax.slice_in_dim(array, 0, width, axis=dim)
        before = lax.ppermute(last, axis, up)
        after = lax.ppermute(leading, axis, down)
        array = jnp.concatenate([before, array, after], axis=dim)
    return array


def lane_index(shape):
    return lax.broadcasted_iota(jnp.int32, shape, len(shape) - 1)


def row_index(shape):
    return lax.broadcasted_iota(jnp.int32, shape, len(shape) - 2)


def roll(block, shift, axis):
    return pltpu.roll(block, shift % block.shape[axis], axis)


def inverse(value):
    guess = pl.reciprocal(value, approx=True)
    return guess * (2.0 - value * guess)


def tree_sum(values):
    while len(values) > 1:
        values = [sum(values[at : at + 2]) for at in range(0, len(values), 2)]
    return values[0]


def grand_total(acc):
    line = jnp.sum(acc, axis=0, keepdims=True)
    return jnp.broadcast_to(jnp.sum(line, axis=1, keepdims=True), acc.shape)


def swap_masks(peers, flip):
    falling = []
    mask = peers // 2
    while mask > 1:
        falling.append(mask)
        mask //= 2
    if flip:
        return falling[:1] + falling[:0:-1], falling
    return falling, falling[-1:] + falling[:-1]


def block_pair(u, holder, peers, flip):
    even, odd = swap_masks(peers, flip)
    parity = holder % 2
    top = jnp.where(parity == 0, even.index(peers // 2), odd.index(peers // 2))
    below = u & ((1 << top) - 1)
    base = ((u >> top) << (top + 1)) | below
    upper = jnp.where(holder >= peers // 2, 1, 0)
    first = base | (upper << top)
    second = base | ((1 - upper) << top)
    home = holder
    for step, (mask_even, mask_odd) in enumerate(zip(even, odd)):
        mask = jnp.where(parity == 0, mask_even, mask_odd)
        home = home ^ (((first >> step) & 1) * mask)
    return first, second, home


def prepare_kernel(kappa_ref, misfit_ref, kappa_out, misfit_out, *, axis, peers):
    at_ = Layout(kappa_ref.shape[1] // 2)
    upper = jnp.where(lax.axis_index(axis) >= peers // 2, 1, 0)
    at_.deal(kappa_ref, kappa_out, upper)
    at_.deal(misfit_ref, misfit_out, upper)


def join_kernel(*refs, masks, axis, peers):
    place = lax.axis_index(axis)
    at_ = Layout(refs[0].shape[1] // 2)
    for at, (even, odd) in enumerate(masks):
        partner = place ^ jnp.where(place % 2 == 0, even, odd)
        refs[4 + at][0] = refs[at][...]
        at_.deal(refs[2 + at], refs[4 + at].at[1], jnp.where(partner >= peers // 2, 1, 0))


def gather_blocks(blocks, states, axis):
    peers = lax.axis_size(axis)
    even = lax.axis_index(axis) % 2 == 0
    swap = [(i, i ^ 1) for i in range(peers)]
    over = [(i, i + 1 if i % 2 else i - 1) for i in range(1, peers - 1)]
    vmem = pl.BlockSpec(memory_space=pltpu.VMEM)
    swaps = [list(zip(*swap_masks(peers, flip))) for flip in (False, True)]
    own = pl.pallas_call(
        functools.partial(prepare_kernel, axis=axis, peers=peers),
        out_shape=[jax.ShapeDtypeStruct(block.shape, jnp.float32) for block in blocks],
        in_specs=[vmem] * 2,
        out_specs=[vmem] * 2,
        compiler_params=pltpu.CompilerParams(vmem_limit_bytes=1024 * 1024),
        name="prepare",
    )(*blocks)
    held = list(blocks)
    for step in range(len(swaps[0])):
        arrived = []
        for at in (0, 1):
            masks = swaps[at][step]
            pairs = [(i, i ^ masks[i % 2]) for i in range(peers)]
            arrived.append(lax.ppermute(held[at], axis, pairs))
        if step:
            held = [jnp.concatenate(pair, axis=0) for pair in zip(held, arrived)]
            continue
        masks = [swaps[at][0] for at in (0, 1)]
        shape = jax.ShapeDtypeStruct((2, *blocks[0].shape), jnp.float32)
        held[:] = pl.pallas_call(
            functools.partial(join_kernel, masks=masks, axis=axis, peers=peers),
            out_shape=[shape] * 2,
            in_specs=[vmem] * 4,
            out_specs=[vmem] * 2,
            compiler_params=pltpu.CompilerParams(vmem_limit_bytes=1024 * 1024),
            name="join",
        )(*own, *arrived)
        held[1], states = lax.optimization_barrier((held[1], states))
        far = lax.ppermute(jnp.where(even, states[:, :1], states[:, -1:]), axis, over)
    other = [lax.ppermute(part, axis, swap) for part in held]

    def fetch_near(after):
        late, states_late, far_late = lax.optimization_barrier((after, states, far))
        given = jnp.concatenate([states_late, far_late], axis=1)
        return late, lax.ppermute(jnp.where(even, given[1], given[0]), axis, swap)

    return held, other, far, fetch_near


CLASSES = [(a, b, c) for a in (0, 1) for b in (0, 1) for c in (0, 1)]
PAIRS = [(p, q) for p in (0, 1) for q in (0, 1)]


def cls(a, b, c):
    return 4 * a + 2 * b + c


def inner_faces(p, q):
    return (
        (2 * p + q, cls(0, p, q), cls(1, p, q)),
        (4 + 2 * p + q, cls(p, 0, q), cls(p, 1, q)),
        (8 + 2 * p + q, cls(p, q, 0), cls(p, q, 1)),
    )


class Layout:
    def __init__(self, rows):
        self.tiles = rows // TILE
        self.lane = lane_index((TILE, 2 * HALF))
        self.row = row_index((TILE, 2 * HALF))
        self.left = self.lane < HALF
        self.zero = jnp.zeros((TILE, 2 * HALF), jnp.float32)

    def tile(self, j):
        return pl.ds(TILE * j, TILE)

    def every(self, b, j):
        return pl.ds(b + 2 * j, TILE, stride=2 * self.tiles)

    def row_before(self, load, j):
        return load(j - 1) if j else roll(load(self.tiles - 1), 1, 0)

    def row_after(self, load, j):
        return load(j + 1) if j + 1 < self.tiles else roll(load(0), -1, 0)

    def seam(self, ref, low, high):
        last = ref.shape[1] - 1
        for j in range(self.tiles):
            for k in low:
                moved = roll(ref[k, last - 1, self.tile(j)], HALF, 1)
                ref[k, 0, self.tile(j)] = jnp.where(self.left, 0.0, moved)
            for k in high:
                moved = roll(ref[k, 1, self.tile(j)], HALF, 1)
                ref[k, last, self.tile(j)] = jnp.where(self.left, moved, 0.0)

    def seam_fine(self, ref):
        count = ref.shape[0]
        self.seam(
            ref,
            [k for k in range(count) if k % 8 >= 4],
            [k for k in range(count) if k % 8 < 4],
        )

    def dealt(self, b, j):
        return pl.ds(TILE * (self.tiles * b + j), TILE)

    def deal(self, block_ref, out_ref, upper):
        odd = jnp.where(self.left, upper, 1 - upper)
        column = 2 * (self.lane % HALF) + odd
        for x in range(block_ref.shape[0]):
            for b in (0, 1):
                for j in range(self.tiles):
                    rows = block_ref[x, self.every(b, j), :]
                    out_ref[x, self.dealt(b, j), :] = jnp.take_along_axis(rows, column, axis=1)

    def arrange(self, mine_ref, theirs_ref, place, flip, store):
        blocks, own = mine_ref.shape[:2]

        def pair(u, carry):
            for ref, holder in ((mine_ref, place), (theirs_ref, place ^ 1)):
                first, second, home = block_pair(u, holder, 2 * blocks, flip)
                for x in range(own):
                    spot = home * (own // 2) + x // 2
                    for b in (0, 1):
                        for j in range(self.tiles):
                            one = ref[first, x, self.dealt(b, j), :]
                            two = ref[second, x, self.dealt(b, j), :]
                            store(cls(x % 2, b, 0), spot, j, jnp.where(self.left, one, two))
                            odd = roll(jnp.where(self.left, two, one), HALF, 1)
                            store(cls(x % 2, b, 1), spot, j, odd)
            return carry

        lax.fori_loop(0, blocks // 2, pair, 0)


def setup_kernel(
    order_ref,
    shifts_ref,
    weights_ref,
    mine_ref,
    theirs_ref,
    inner,
    outer_x,
    outer_y,
    outer_z,
    inner_sum,
    diagonal,
    damped,
    coarse_off,
    coarse_damped,
    chosen,
    half_kappa,
):
    half = inner.shape[1]
    at_ = Layout(inner.shape[2])
    tile, tiles = at_.tile, at_.tiles
    place = lax.axis_index("space")
    pole = jnp.where(place % 2 == 0, order_ref[:, 0:1], order_ref[:, 1:2])
    taken = lane_index(shifts_ref.shape) == pole
    shift = jnp.sum(jnp.where(taken, shifts_ref[...], 0.0), axis=1, keepdims=True)
    weight = jnp.sum(jnp.where(taken, weights_ref[...], 0.0), axis=1, keepdims=True)
    shift = jnp.broadcast_to(shift, at_.zero.shape)
    chosen[...] = jnp.broadcast_to(weight, at_.zero.shape)

    def keep(k, spot, j, value):
        half_kappa[k, spot + 1, tile(j)] = 0.5 * value

    at_.arrange(mine_ref, theirs_ref, place, False, keep)
    at_.seam_fine(half_kappa)

    z_low = jnp.where(at_.lane % HALF > 0, 1.0, 0.0)
    z_high = jnp.where(at_.lane % HALF < HALF - 1, 1.0, 0.0)
    y_low = [jnp.where(at_.row > 0, 1.0, 0.0)] + [None] * (tiles - 1)
    y_high = [None] * (tiles - 1) + [jnp.where(at_.row < TILE - 1, 1.0, 0.0)]

    def masked(mask, value):
        return value if mask is None else mask * value

    def plane(i, carry):
        for j in range(tiles):
            kap = [half_kappa[k, i + 1, tile(j)] for k in range(8)]
            inside = [[] for _ in range(8)]
            outside = [[] for _ in range(8)]
            off = [[] for _ in range(5)]
            for p, q in PAIRS:
                for face_at, low, high in inner_faces(p, q):
                    face = kap[low] + kap[high]
                    inner[face_at, i, tile(j)] = face
                    inside[low].append(face)
                    inside[high].append(face)
                at = 2 * p + q

                low, high = cls(0, p, q), cls(1, p, q)
                minus = kap[low] + half_kappa[high, i, tile(j)]
                plus = kap[high] + half_kappa[low, i + 2, tile(j)]
                outside[low].append(minus)
                outside[high].append(plus)
                outer_x[at, i, tile(j)] = minus
                off[0].append(minus)

                low, high = cls(p, 0, q), cls(p, 1, q)
                side = at_.row_before(lambda r: half_kappa[high, i + 1, tile(r)], j)
                minus = kap[low] + masked(y_low[j], side)
                side = at_.row_after(lambda r: half_kappa[low, i + 1, tile(r)], j)
                plus = kap[high] + masked(y_high[j], side)
                outside[low].append(minus)
                outside[high].append(plus)
                minus, plus = masked(y_low[j], minus), masked(y_high[j], plus)
                outer_y[at, i, tile(j)] = minus
                off[1].append(minus)
                off[2].append(plus)

                low, high = cls(p, q, 0), cls(p, q, 1)
                minus = kap[low] + z_low * roll(kap[high], 1, 1)
                plus = kap[high] + z_high * roll(kap[low], -1, 1)
                outside[low].append(minus)
                outside[high].append(plus)
                minus, plus = z_low * minus, z_high * plus
                outer_z[at, i, tile(j)] = minus
                outer_z[4 + at, i, tile(j)] = plus
                off[3].append(minus)
                off[4].append(plus)
            coarse_total = []
            for k in range(8):
                within, without = tree_sum(inside[k]), tree_sum(outside[k])
                inner_sum[k, i, tile(j)] = within
                base = within + without + shift
                diagonal[k, i, tile(j)] = base
                coarse_total.append(without)
                damped[k, i, tile(j)] = (DAMPING / KEPT) * inverse(base)
            for at, part in enumerate(off):
                coarse_off[at, i, tile(j)] = tree_sum(part)
            coarse_damped[i, tile(j)] = DAMPING * inverse(tree_sum(coarse_total) + 8.0 * shift)
        return carry

    lax.fori_loop(0, half, plane, 0, unroll=UNROLL)
    for j in range(tiles):
        part = []
        for p, q in PAIRS:
            face = half_kappa[cls(0, p, q), half + 1, tile(j)]
            face = face + half_kappa[cls(1, p, q), half, tile(j)]
            outer_x[2 * p + q, half, tile(j)] = face
            part.append(face)
        coarse_off[0, half, tile(j)] = tree_sum(part)


def solve_kernel(
    mine_ref,
    theirs_ref,
    inner,
    outer_x,
    outer_y,
    outer_z,
    inner_sum,
    diagonal,
    damped,
    coarse_off,
    coarse_damped,
    chosen,
    planes,
    residual,
    scaled,
    partial,
    first_dir,
    second_dir,
    image,
    coarse_one,
    coarse_two,
    *,
    own,
):
    half, rows = inner.shape[1:3]
    at_ = Layout(rows)
    tile, tiles, zero = at_.tile, at_.tiles, at_.zero
    place = lax.axis_index("space")
    core = place % 2
    weight = KEPT * chosen[...]

    def begin(k, spot, j, value):
        res = weight * value
        residual[k, spot, tile(j)] = res
        scaled[k, spot + 1, tile(j)] = damped[k, spot, tile(j)] * res

    at_.arrange(mine_ref, theirs_ref, place, True, begin)
    at_.seam_fine(scaled)

    def rows_of(ref, i):
        cache = {}

        def load(k, j, step):
            if abs(j - step) > 1:
                return ref[k, i, tile(j)]
            if (k, j) not in cache:
                cache[k, j] = ref[k, i, tile(j)]
            return cache[k, j]

        def get(k, j):
            return load(k, j, j)

        def before(k, j):
            return at_.row_before(lambda r: load(k, r, j), j)

        def after(k, j):
            return at_.row_after(lambda r: load(k, r, j), j)

        return get, before, after

    def stencil(field, i, both):
        get, before, after = rows_of(field, i + 1)
        face_get, _, face_after = rows_of(outer_y, i)
        for j in range(tiles):
            here = [get(k, j) for k in range(8)]
            terms = [[] for _ in range(8)]
            for p, q in PAIRS:
                at = 2 * p + q
                for face_at, low, high in inner_faces(p, q):
                    face = inner[face_at, i, tile(j)]
                    terms[low].append(face * here[high])
                    if both:
                        terms[high].append(face * here[low])
                low, high = cls(0, p, q), cls(1, p, q)
                terms[low].append(outer_x[at, i, tile(j)] * field[high, i, tile(j)])
                if both:
                    side = field[low, i + 2, tile(j)]
                    terms[high].append(outer_x[at, i + 1, tile(j)] * side)
                low, high = cls(p, 0, q), cls(p, 1, q)
                terms[low].append(face_get(at, j) * before(high, j))
                if both:
                    terms[high].append(face_after(at, j) * after(low, j))
                low, high = cls(p, q, 0), cls(p, q, 1)
                terms[low].append(outer_z[at, i, tile(j)] * roll(here[high], 1, 1))
                if both:
                    terms[high].append(outer_z[4 + at, i, tile(j)] * roll(here[low], -1, 1))
            yield j, here, [tree_sum(part) if part else None for part in terms]

    def coarse_sides(field, i, j):
        here = field[0, i + 1, tile(j)]
        return here, (
            (field[0, i, tile(j)], field[0, i + 2, tile(j)]),
            (
                at_.row_before(lambda r: field[0, i + 1, tile(r)], j),
                at_.row_after(lambda r: field[0, i + 1, tile(r)], j),
            ),
            (roll(here, 1, 1), roll(here, -1, 1)),
        )

    def precondition(result):
        def down(i, carry):
            for j, _, sums in stencil(scaled, i, True):
                res = [residual[k, i, tile(j)] for k in range(8)]
                parts = [res[k] + sums[k] for k in range(8)]
                for k in range(8):
                    partial[k, i, tile(j)] = parts[k]
                rhs = tree_sum(parts) - (1.0 / KEPT) * tree_sum(res)
                coarse_one[0, i + 1, tile(j)] = coarse_damped[i, tile(j)] * rhs
            return carry

        lax.fori_loop(0, half, down, 0, unroll=UNROLL)
        at_.seam(coarse_one, [0], [0])

        def smooth(i, carry):
            for j in range(tiles):
                here, sides = coarse_sides(coarse_one, i, j)
                total = coarse_off[0, i, tile(j)] * sides[0][0]
                total = total + coarse_off[0, i + 1, tile(j)] * sides[0][1]
                more = coarse_off[1, i, tile(j)] * sides[1][0]
                more = more + coarse_off[2, i, tile(j)] * sides[1][1]
                most = coarse_off[3, i, tile(j)] * sides[2][0]
                most = most + coarse_off[4, i, tile(j)] * sides[2][1]
                coarse_two[0, i + 1, tile(j)] = KEPT * here + coarse_damped[
                    i, tile(j)
                ] * (total + more + most)
            return carry

        lax.fori_loop(0, half, smooth, 0, unroll=UNROLL)
        at_.seam(coarse_two, [0], [0])

        def up(i, gamma):
            face_get, _, face_after = rows_of(outer_y, i)
            for j in range(tiles):
                here, sides = coarse_sides(coarse_two, i, j)
                kept = ((1.0 - DAMPING) / KEPT) * here
                dots = []
                for a, b, c in CLASSES:
                    k = cls(a, b, c)
                    value = tree_sum(
                        [
                            partial[k, i, tile(j)],
                            inner_sum[k, i, tile(j)] * here,
                            outer_x[2 * b + c, i + a, tile(j)] * sides[0][a],
                            (face_after if b else face_get)(2 * a + c, j) * sides[1][b],
                            outer_z[4 * c + 2 * a + b, i, tile(j)] * sides[2][c],
                        ]
                    )
                    new = kept + damped[k, i, tile(j)] * value
                    result[k, i + 1, tile(j)] = new
                    dots.append(residual[k, i, tile(j)] * new)
                gamma = gamma + tree_sum(dots)
            return gamma

        gamma = lax.fori_loop(0, half, up, zero, unroll=UNROLL)
        at_.seam_fine(result)
        return grand_total(gamma)

    gamma = precondition(first_dir)

    def apply(i, acc):
        for j, here, sums in stencil(first_dir, i, True):
            dots = []
            for k in range(8):
                value = diagonal[k, i, tile(j)] * here[k] - sums[k]
                image[k, i, tile(j)] = value
                dots.append(here[k] * value)
            acc = acc + tree_sum(dots)
        return acc

    curve = grand_total(lax.fori_loop(0, half, apply, zero, unroll=UNROLL))
    step_one = gamma / curve

    def update(i, carry):
        for j in range(tiles):
            for k in range(8):
                new = residual[k, i, tile(j)] - step_one * image[k, i, tile(j)]
                residual[k, i, tile(j)] = new
                scaled[k, i + 1, tile(j)] = damped[k, i, tile(j)] * new
        return carry

    lax.fori_loop(0, half, update, 0, unroll=UNROLL)
    at_.seam_fine(scaled)

    gamma_next = precondition(second_dir)

    def bend(i, carry):
        own_part, face_part = carry
        for j, here, sums in stencil(second_dir, i, False):
            own_part = own_part + tree_sum(
                [here[k] * (diagonal[k, i, tile(j)] * here[k]) for k in range(8)]
            )
            face_part = face_part + tree_sum([here[k] * sums[k] for k in range(7)])
        return own_part, face_part

    own_part, face_part = lax.fori_loop(0, half, bend, (zero, zero), unroll=UNROLL)
    ratio = gamma_next / gamma
    curve_next = grand_total(own_part - 2.0 * face_part)
    step_two = gamma_next / (curve_next - ratio * ratio * curve)
    step_first = (step_one + step_two * ratio) * (1.0 / KEPT)
    step_two = step_two * (1.0 / KEPT)

    start = (place - core) * (own // 2)
    upper = jnp.where(start >= half, 1, 0)
    start = start - half * upper
    even = at_.lane % 2 == 0
    source = at_.lane // 2 + HALF * upper
    for at in range(2 * own + 2):
        a = (at + 1) % 2
        spot = start + (at + 1) // 2
        for b in (0, 1):
            for j in range(tiles):
                both = [
                    step_first * first_dir[cls(a, b, c), spot, tile(j)]
                    + step_two * second_dir[cls(a, b, c), spot, tile(j)]
                    for c in (0, 1)
                ]
                planes[at, at_.every(b, j), :] = jnp.where(
                    even,
                    jnp.take_along_axis(both[0], source, axis=1),
                    jnp.take_along_axis(both[1], source, axis=1),
                )


def finish_kernel(planes_ref, state_ref, far_ref, near_ref, adjoint_ref, keep_ref, partner_ref, send_ref, terms):
    own, ny, nz = adjoint_ref.shape
    core = lax.axis_index("space") % 2
    full = (ny, nz)
    y_at = row_index(full)
    z_at = lane_index(full)

    def drop(value, axis, up):
        moved = roll(value, -1 if up else 1, axis)
        at = (y_at, z_at)[axis]
        edge = full[axis] - 1 if up else 0
        return value - jnp.where(at == edge, 0.0, moved)

    is_even = core == 0
    state = [jnp.where(is_even, far_ref[core, 0], near_ref[own])]
    state += [jnp.where(is_even, state_ref[core, x], near_ref[x]) for x in range(own)]
    state += [jnp.where(is_even, near_ref[x], state_ref[core, x]) for x in range(own)]
    state += [jnp.where(is_even, near_ref[own], far_ref[core, 0])]
    for x in range(2 * own):
        here, f = planes_ref[x + 1], state[x + 1]
        term = (here - planes_ref[x + 2]) * (f - state[x + 2])
        term = term + (here - planes_ref[x]) * (f - state[x])
        for axis in (0, 1):
            for up in (True, False):
                term = term + drop(here, axis, up) * drop(f, axis, up)
        terms[x] = -0.5 * term

    groups = send_ref.shape[0] + 1
    chunk = keep_ref.shape[1]
    for x in range(own):
        mine, other = core * own + x, (1 - core) * own + x
        adjoint_ref[x] = planes_ref[1 + mine]
        partner_ref[x, :ny] = planes_ref[1 + other]
        for k in range(groups):
            at = lax.rem(lax.axis_index("pole") + k, groups) * chunk
            at = pl.multiple_of(at, chunk)
            for side, plane in enumerate((mine, other)):
                share = terms[plane, pl.ds(at, chunk), :]
                if k:
                    send_ref[k - 1, side, x] = share
                elif side:
                    partner_ref[x, ny:] = share
                else:
                    keep_ref[x] = share


def whole_grid(conductivity, misfit, forward_states, pole_shifts, pole_weights, pole_order):
    members, own, ny, nz = forward_states.shape
    groups = lax.axis_size("pole")
    peers = lax.axis_size("space")
    even = lax.axis_index("space") % 2 == 0
    mine, theirs, far, fetch_near = gather_blocks([conductivity, misfit], forward_states, "space")
    half, rows = peers * own // 4, ny // 2

    def field(count, extent):
        return (count, extent, rows, 2 * HALF)

    def held(*shape):
        return pltpu.VMEM(shape, jnp.float32)

    vmem = pl.BlockSpec(memory_space=pltpu.VMEM)
    shapes = [
        field(12, half),
        field(4, half + 1),
        field(4, half),
        field(8, half),
        field(8, half),
        field(8, half),
        field(8, half),
        field(5, half + 1),
        (half, rows, 2 * HALF),
        (TILE, 2 * HALF),
    ]
    coefficients = pl.pallas_call(
        setup_kernel,
        out_shape=[jax.ShapeDtypeStruct(shape, jnp.float32) for shape in shapes],
        in_specs=[vmem] * 5,
        out_specs=[vmem] * len(shapes),
        scratch_shapes=[held(*field(8, half + 2))],
        compiler_params=pltpu.CompilerParams(vmem_limit_bytes=6 * 1024 * 1024),
        name="setup",
    )(pole_order[None], pole_shifts[None], pole_weights[None], mine[0], theirs[0])
    coefficients, near = fetch_near(coefficients)
    planes = pl.pallas_call(
        functools.partial(solve_kernel, own=own),
        out_shape=jax.ShapeDtypeStruct((2 * own + 2, ny, nz), jnp.float32),
        in_specs=[vmem] * (2 + len(shapes)),
        out_specs=vmem,
        scratch_shapes=[
            held(*field(8, half)),
            held(*field(8, half + 2)),
            held(*field(8, half)),
            held(*field(8, half + 2)),
            held(*field(8, half + 2)),
            held(*field(8, half)),
            held(*field(1, half + 2)),
            held(*field(1, half + 2)),
        ],
        compiler_params=pltpu.CompilerParams(vmem_limit_bytes=12 * 1024 * 1024),
        name="solve",
    )(mine[1], theirs[1], *coefficients)
    chunk = ny // groups
    adjoint, gradient, partner, send = pl.pallas_call(
        finish_kernel,
        out_shape=[
            jax.ShapeDtypeStruct((own, ny, nz), jnp.float32),
            jax.ShapeDtypeStruct((own, chunk, nz), jnp.float32),
            jax.ShapeDtypeStruct((own, ny + chunk, nz), jnp.float32),
            jax.ShapeDtypeStruct((groups - 1, 2, own, chunk, nz), jnp.float32),
        ],
        in_specs=[vmem] * 4,
        out_specs=[vmem] * 4,
        scratch_shapes=[held(2 * own, ny, nz)],
        compiler_params=pltpu.CompilerParams(vmem_limit_bytes=4 * 1024 * 1024),
        name="finish",
    )(planes, forward_states, far, near)

    arrived = lax.ppermute(partner, "space", [(i, i ^ 1) for i in range(peers)])
    shares = []
    for k in range(1, groups):
        for side in (0, 1):
            pairs = [
                (i * peers + j, (i + k) % groups * peers + (j ^ side))
                for i in range(groups)
                for j in range(peers)
            ]
            shares.append(lax.ppermute(send[k - 1, side], ("pole", "space"), pairs))
    theirs = arrived[:, :ny]
    adjoint_states = jnp.stack(
        [jnp.where(even, adjoint, theirs), jnp.where(even, theirs, adjoint)]
    )
    adjoint_states, arrived = lax.optimization_barrier((adjoint_states, arrived))
    return adjoint_states, gradient + arrived[:, ny:] + sum(shares)


def plus_side(field, which_dim):
    extent = field.shape[which_dim]
    inner_part = lax.slice_in_dim(field, 1, extent, axis=which_dim)
    zero_plane = jnp.zeros_like(lax.slice_in_dim(field, 0, 1, axis=which_dim))
    return jnp.concatenate([inner_part, zero_plane], axis=which_dim)


def minus_side(field, which_dim):
    extent = field.shape[which_dim]
    inner_part = lax.slice_in_dim(field, 0, extent - 1, axis=which_dim)
    zero_plane = jnp.zeros_like(lax.slice_in_dim(field, 0, 1, axis=which_dim))
    return jnp.concatenate([zero_plane, inner_part], axis=which_dim)


def coarse_pick(faces, which_dim, offset):
    extent_x, extent_y, extent_z = faces.shape
    blocks = faces.reshape(extent_x // 2, 2, extent_y // 2, 2, extent_z // 2, 2)
    chosen = lax.index_in_dim(blocks, offset, axis=2 * which_dim + 1, keepdims=True)
    return jnp.sum(chosen, axis=(1, 3, 5))


def side_terms(field, plus_faces, minus_faces, widened):
    result = plus_faces[0] * (field - widened[:, 2:]) + minus_faces[0] * (field - widened[:, :-2])
    for which_dim in (1, 2):
        result = result + plus_faces[which_dim] * (field - plus_side(field, which_dim + 1))
        result = result + minus_faces[which_dim] * (field - minus_side(field, which_dim + 1))
    return result


def fine_image(field, plus_faces, minus_faces, shift_value):
    widened = extended(field, (("space", 1),), 1)
    return shift_value * field + side_terms(field, plus_faces, minus_faces, widened)


def coarse_image(field, plus_faces, minus_faces, shift_value):
    widened = extended(field, (("space", 1),), 1)
    return shift_value * field + side_terms(field, plus_faces, minus_faces, widened)


def restrict(field):
    members, extent_x, extent_y, extent_z = field.shape
    shaped = field.reshape(members, extent_x // 2, 2, extent_y // 2, 2, extent_z // 2, 2)
    return jnp.sum(shaped, axis=(2, 4, 6))


def prolong(field):
    return jnp.repeat(jnp.repeat(jnp.repeat(field, 2, axis=1), 2, axis=2), 2, axis=3)


def precondition(residual, fine, coarse):
    plus_faces, minus_faces, shift_value, diagonal = fine
    coarse_plus, coarse_minus, coarse_shift, coarse_diagonal = coarse
    smooth_one = DAMPING * residual / diagonal
    coarse_rhs = restrict(residual - fine_image(smooth_one, plus_faces, minus_faces, shift_value))
    coarse_one = DAMPING * coarse_rhs / coarse_diagonal
    coarse_two = (
        coarse_one
        + DAMPING
        * (coarse_rhs - coarse_image(coarse_one, coarse_plus, coarse_minus, coarse_shift))
        / coarse_diagonal
    )
    corrected = smooth_one + prolong(coarse_two)
    return (
        corrected
        + DAMPING
        * (residual - fine_image(corrected, plus_faces, minus_faces, shift_value))
        / diagonal
    )


def expand(values):
    return values.reshape(-1, 1, 1, 1)


def cell_sums(values):
    return jnp.sum(values, axis=(1, 2, 3))


def norm_sum(residual, precond):
    return lax.psum(cell_sums(residual * precond), "space")


def solve(rhs, fine, coarse):
    plus_faces, minus_faces, shift_value, diagonal = fine
    iterate = jnp.zeros_like(rhs)
    residual = rhs
    precond = precondition(residual, fine, coarse)
    gamma_now = norm_sum(residual, precond)
    search = precond
    for turn_index in range(ITERS):
        image_field = fine_image(search, plus_faces, minus_faces, shift_value)
        curve = lax.psum(cell_sums(search * image_field), "space")
        step_length = gamma_now / curve
        iterate = iterate + expand(step_length) * search
        if turn_index + 1 < ITERS:
            residual = residual - expand(step_length) * image_field
            precond = precondition(residual, fine, coarse)
            gamma_next = norm_sum(residual, precond)
            search = precond + expand(gamma_next / gamma_now) * search
            gamma_now = gamma_next
    return iterate


def divided(conductivity, misfit, forward_states, pole_shifts, pole_weights, pole_order):
    widened_kappa = extended(conductivity, (("space", 0),), 1)
    plus_faces = [
        0.5 * (conductivity + widened_kappa[2:]),
        0.5 * (conductivity + plus_side(conductivity, 1)),
        0.5 * (conductivity + plus_side(conductivity, 2)),
    ]
    minus_faces = [
        0.5 * (conductivity + widened_kappa[:-2]),
        0.5 * (conductivity + minus_side(conductivity, 1)),
        0.5 * (conductivity + minus_side(conductivity, 2)),
    ]
    base_diagonal = (
        plus_faces[0]
        + plus_faces[1]
        + plus_faces[2]
        + minus_faces[0]
        + minus_faces[1]
        + minus_faces[2]
    )
    coarse_plus = [coarse_pick(plus_faces[which_dim], which_dim, 1) for which_dim in range(3)]
    coarse_minus = [coarse_pick(minus_faces[which_dim], which_dim, 0) for which_dim in range(3)]
    coarse_base = (
        coarse_plus[0]
        + coarse_plus[1]
        + coarse_plus[2]
        + coarse_minus[0]
        + coarse_minus[1]
        + coarse_minus[2]
    )
    pole_index = jnp.arange(pole_shifts.shape[0], dtype=jnp.int32)
    matches = pole_order[:, None] == pole_index[None, :]
    shift_local = jnp.sum(jnp.where(matches, pole_shifts[None, :], 0.0), axis=1)
    weight_local = jnp.sum(jnp.where(matches, pole_weights[None, :], 0.0), axis=1)
    members = forward_states.shape[0]

    def solve_group(shift_part, weight_part):
        shift_value = expand(shift_part)
        fine = (plus_faces, minus_faces, shift_value, base_diagonal[None] + shift_value)
        coarse = (
            coarse_plus,
            coarse_minus,
            8.0 * shift_value,
            coarse_base[None] + 8.0 * shift_value,
        )
        return solve(expand(weight_part) * misfit[None], fine, coarse)

    adjoint_states = jnp.concatenate(
        [
            solve_group(shift_local[member : member + 1], weight_local[member : member + 1])
            for member in range(members)
        ],
        axis=0,
    )
    widened = extended(jnp.stack([adjoint_states, forward_states]), (("space", 2),), 1)
    term = (adjoint_states - widened[0, :, 2:]) * (forward_states - widened[1, :, 2:])
    term = term + (adjoint_states - widened[0, :, :-2]) * (forward_states - widened[1, :, :-2])
    for which_dim in (2, 3):
        term = term + (adjoint_states - plus_side(adjoint_states, which_dim)) * (
            forward_states - plus_side(forward_states, which_dim)
        )
        term = term + (adjoint_states - minus_side(adjoint_states, which_dim)) * (
            forward_states - minus_side(forward_states, which_dim)
        )
    local_term = -0.5 * jnp.sum(term, axis=0)
    gradient = lax.psum_scatter(local_term, "pole", scatter_dimension=1, tiled=True)
    return (adjoint_states, gradient)


def solution(mesh):
    in_specs = (
        P("space", None, None),
        P("space", None, None),
        P("pole", "space", None, None),
        P(),
        P(),
        P("pole"),
    )
    out_specs = (P("pole", "space", None, None), P("space", "pole", None))

    def body(conductivity, misfit, forward_states, *poles):
        nx = conductivity.shape[0] * lax.axis_size("space")
        _, ny, nz = conductivity.shape
        peers = lax.axis_size("space")
        small = nx * ny * nz <= REPLICATED_CELLS and forward_states.shape[:2] == (2, 2)
        if small and nz == 2 * HALF and peers > 2 and peers & (peers - 1) == 0:
            return whole_grid(conductivity, misfit, forward_states, *poles)
        return divided(conductivity, misfit, forward_states, *poles)

    return jax.shard_map(
        body, mesh=mesh, in_specs=in_specs, out_specs=out_specs, check_vma=False
    )
```

```python
import functools

import jax
import jax.numpy as jnp
from jax import lax
from jax.experimental import pallas as pl
from jax.experimental.pallas import tpu as pltpu
from jax.sharding import PartitionSpec as P

ITERS = 2
DAMPING = 0.8
KEPT = 2.0 - DAMPING
REPLICATED_CELLS = 32 * 64 * 128
HALF = 64
TILE = 8
UNROLL = 8


def extended(array, sides, width):
    for axis, dim in sides:
        peers, length = (lax.axis_size(axis), array.shape[dim])
        up = [(i, (i + 1) % peers) for i in range(peers - 1)]
        down = [(j, i) for i, j in up]
        last = lax.slice_in_dim(array, length - width, length, axis=dim)
        leading = lax.slice_in_dim(array, 0, width, axis=dim)
        before = lax.ppermute(last, axis, up)
        after = lax.ppermute(leading, axis, down)
        array = jnp.concatenate([before, array, after], axis=dim)
    return array


def lane_index(shape):
    return lax.broadcasted_iota(jnp.int32, shape, len(shape) - 1)


def row_index(shape):
    return lax.broadcasted_iota(jnp.int32, shape, len(shape) - 2)


def roll(block, shift, axis):
    return pltpu.roll(block, shift % block.shape[axis], axis)


def inverse(value):
    guess = pl.reciprocal(value, approx=True)
    return guess * (2.0 - value * guess)


def tree_sum(values):
    while len(values) > 1:
        values = [sum(values[at : at + 2]) for at in range(0, len(values), 2)]
    return values[0]


def grand_total(acc):
    line = jnp.sum(acc, axis=0, keepdims=True)
    return jnp.broadcast_to(jnp.sum(line, axis=1, keepdims=True), acc.shape)


def swap_masks(peers, flip):
    falling = []
    mask = peers // 2
    while mask > 1:
        falling.append(mask)
        mask //= 2
    if flip:
        return falling[::-1], falling[:1] + falling[:0:-1]
    return falling, falling[-1:] + falling[:-1]


def block_pair(u, holder, peers, flip):
    even, odd = swap_masks(peers, flip)
    parity = holder % 2
    top = jnp.where(parity == 0, even.index(peers // 2), odd.index(peers // 2))
    below = u & ((1 << top) - 1)
    base = ((u >> top) << (top + 1)) | below
    upper = jnp.where(holder >= peers // 2, 1, 0)
    first = base | (upper << top)
    second = base | ((1 - upper) << top)
    home = holder
    for step, (mask_even, mask_odd) in enumerate(zip(even, odd)):
        mask = jnp.where(parity == 0, mask_even, mask_odd)
        home = home ^ (((first >> step) & 1) * mask)
    return first, second, home


def prepare_kernel(kappa_ref, misfit_ref, kappa_out, misfit_out, *, axis, peers):
    at_ = Layout(kappa_ref.shape[1] // 2)
    upper = jnp.where(lax.axis_index(axis) >= peers // 2, 1, 0)
    at_.deal(kappa_ref, kappa_out, upper)
    at_.deal(misfit_ref, misfit_out, upper)


def join_kernel(*refs, masks, axis, peers):
    place = lax.axis_index(axis)
    at_ = Layout(refs[0].shape[1] // 2)
    for at, (even, odd) in enumerate(masks):
        partner = place ^ jnp.where(place % 2 == 0, even, odd)
        refs[4 + at][0] = refs[at][...]
        at_.deal(refs[2 + at], refs[4 + at].at[1], jnp.where(partner >= peers // 2, 1, 0))


def gather_blocks(blocks, states, axis):
    peers = lax.axis_size(axis)
    even = lax.axis_index(axis) % 2 == 0
    swap = [(i, i ^ 1) for i in range(peers)]
    over = [(i, i + 1 if i % 2 else i - 1) for i in range(1, peers - 1)]
    vmem = pl.BlockSpec(memory_space=pltpu.VMEM)
    swaps = [list(zip(*swap_masks(peers, flip))) for flip in (False, True)]
    own = pl.pallas_call(
        functools.partial(prepare_kernel, axis=axis, peers=peers),
        out_shape=[jax.ShapeDtypeStruct(block.shape, jnp.float32) for block in blocks],
        in_specs=[vmem] * 2,
        out_specs=[vmem] * 2,
        compiler_params=pltpu.CompilerParams(vmem_limit_bytes=1024 * 1024),
        name="prepare",
    )(*blocks)
    held = list(blocks)
    for step in range(len(swaps[0])):
        arrived = []
        for at in (0, 1):
            masks = swaps[at][step]
            pairs = [(i, i ^ masks[i % 2]) for i in range(peers)]
            arrived.append(lax.ppermute(held[at], axis, pairs))
        if step:
            held = [jnp.concatenate(pair, axis=0) for pair in zip(held, arrived)]
            continue
        masks = [swaps[at][0] for at in (0, 1)]
        shape = jax.ShapeDtypeStruct((2, *blocks[0].shape), jnp.float32)
        held[:] = pl.pallas_call(
            functools.partial(join_kernel, masks=masks, axis=axis, peers=peers),
            out_shape=[shape] * 2,
            in_specs=[vmem] * 4,
            out_specs=[vmem] * 2,
            compiler_params=pltpu.CompilerParams(vmem_limit_bytes=1024 * 1024),
            name="join",
        )(*own, *arrived)
        held[1], states = lax.optimization_barrier((held[1], states))
        far = lax.ppermute(jnp.where(even, states[:, :1], states[:, -1:]), axis, over)
    held[1], far = lax.optimization_barrier((held[1], far))
    given = jnp.concatenate([states, far], axis=1)
    near = lax.ppermute(jnp.where(even, given[1], given[0]), axis, swap)
    other = [lax.ppermute(part, axis, swap) for part in held]
    return held, other, far, near


CLASSES = [(a, b, c) for a in (0, 1) for b in (0, 1) for c in (0, 1)]
PAIRS = [(p, q) for p in (0, 1) for q in (0, 1)]


def cls(a, b, c):
    return 4 * a + 2 * b + c


def inner_faces(p, q):
    return (
        (2 * p + q, cls(0, p, q), cls(1, p, q)),
        (4 + 2 * p + q, cls(p, 0, q), cls(p, 1, q)),
        (8 + 2 * p + q, cls(p, q, 0), cls(p, q, 1)),
    )


class Layout:
    def __init__(self, rows):
        self.tiles = rows // TILE
        self.lane = lane_index((TILE, 2 * HALF))
        self.row = row_index((TILE, 2 * HALF))
        self.left = self.lane < HALF
        self.zero = jnp.zeros((TILE, 2 * HALF), jnp.float32)

    def tile(self, j):
        return pl.ds(TILE * j, TILE)

    def every(self, b, j):
        return pl.ds(b + 2 * j, TILE, stride=2 * self.tiles)

    def row_before(self, load, j):
        return load(j - 1) if j else roll(load(self.tiles - 1), 1, 0)

    def row_after(self, load, j):
        return load(j + 1) if j + 1 < self.tiles else roll(load(0), -1, 0)

    def seam(self, ref, low, high):
        last = ref.shape[1] - 1
        for j in range(self.tiles):
            for k in low:
                moved = roll(ref[k, last - 1, self.tile(j)], HALF, 1)
                ref[k, 0, self.tile(j)] = jnp.where(self.left, 0.0, moved)
            for k in high:
                moved = roll(ref[k, 1, self.tile(j)], HALF, 1)
                ref[k, last, self.tile(j)] = jnp.where(self.left, moved, 0.0)

    def seam_fine(self, ref):
        count = ref.shape[0]
        self.seam(
            ref,
            [k for k in range(count) if k % 8 >= 4],
            [k for k in range(count) if k % 8 < 4],
        )

    def dealt(self, b, j):
        return pl.ds(TILE * (self.tiles * b + j), TILE)

    def deal(self, block_ref, out_ref, upper):
        odd = jnp.where(self.left, upper, 1 - upper)
        column = 2 * (self.lane % HALF) + odd
        for x in range(block_ref.shape[0]):
            for b in (0, 1):
                for j in range(self.tiles):
                    rows = block_ref[x, self.every(b, j), :]
                    out_ref[x, self.dealt(b, j), :] = jnp.take_along_axis(rows, column, axis=1)

    def arrange(self, mine_ref, theirs_ref, place, flip, store):
        blocks, own = mine_ref.shape[:2]

        def pair(u, carry):
            for ref, holder in ((mine_ref, place), (theirs_ref, place ^ 1)):
                first, second, home = block_pair(u, holder, 2 * blocks, flip)
                for x in range(own):
                    spot = home * (own // 2) + x // 2
                    for b in (0, 1):
                        for j in range(self.tiles):
                            one = ref[first, x, self.dealt(b, j), :]
                            two = ref[second, x, self.dealt(b, j), :]
                            store(cls(x % 2, b, 0), spot, j, jnp.where(self.left, one, two))
                            odd = roll(jnp.where(self.left, two, one), HALF, 1)
                            store(cls(x % 2, b, 1), spot, j, odd)
            return carry

        lax.fori_loop(0, blocks // 2, pair, 0, unroll=True)


def setup_kernel(
    order_ref,
    shifts_ref,
    weights_ref,
    mine_ref,
    theirs_ref,
    inner,
    outer_x,
    outer_y,
    outer_z,
    inner_sum,
    diagonal,
    damped,
    coarse_off,
    coarse_damped,
    chosen,
    half_kappa,
):
    half = inner.shape[1]
    at_ = Layout(inner.shape[2])
    tile, tiles = at_.tile, at_.tiles
    place = lax.axis_index("space")
    pole = jnp.where(place % 2 == 0, order_ref[:, 0:1], order_ref[:, 1:2])
    taken = lane_index(shifts_ref.shape) == pole
    shift = jnp.sum(jnp.where(taken, shifts_ref[...], 0.0), axis=1, keepdims=True)
    weight = jnp.sum(jnp.where(taken, weights_ref[...], 0.0), axis=1, keepdims=True)
    shift = jnp.broadcast_to(shift, at_.zero.shape)
    chosen[...] = jnp.broadcast_to(weight, at_.zero.shape)

    def keep(k, spot, j, value):
        half_kappa[k, spot + 1, tile(j)] = 0.5 * value

    at_.arrange(mine_ref, theirs_ref, place, False, keep)
    at_.seam_fine(half_kappa)

    z_low = jnp.where(at_.lane % HALF > 0, 1.0, 0.0)
    z_high = jnp.where(at_.lane % HALF < HALF - 1, 1.0, 0.0)
    y_low = [jnp.where(at_.row > 0, 1.0, 0.0)] + [None] * (tiles - 1)
    y_high = [None] * (tiles - 1) + [jnp.where(at_.row < TILE - 1, 1.0, 0.0)]

    def masked(mask, value):
        return value if mask is None else mask * value

    def plane(i, carry):
        for j in range(tiles):
            kap = [half_kappa[k, i + 1, tile(j)] for k in range(8)]
            inside = [[] for _ in range(8)]
            outside = [[] for _ in range(8)]
            off = [[] for _ in range(5)]
            for p, q in PAIRS:
                for face_at, low, high in inner_faces(p, q):
                    face = kap[low] + kap[high]
                    inner[face_at, i, tile(j)] = face
                    inside[low].append(face)
                    inside[high].append(face)
                at = 2 * p + q

                low, high = cls(0, p, q), cls(1, p, q)
                minus = kap[low] + half_kappa[high, i, tile(j)]
                plus = kap[high] + half_kappa[low, i + 2, tile(j)]
                outside[low].append(minus)
                outside[high].append(plus)
                outer_x[at, i, tile(j)] = minus
                off[0].append(minus)

                low, high = cls(p, 0, q), cls(p, 1, q)
                side = at_.row_before(lambda r: half_kappa[high, i + 1, tile(r)], j)
                minus = kap[low] + masked(y_low[j], side)
                side = at_.row_after(lambda r: half_kappa[low, i + 1, tile(r)], j)
                plus = kap[high] + masked(y_high[j], side)
                outside[low].append(minus)
                outside[high].append(plus)
                minus, plus = masked(y_low[j], minus), masked(y_high[j], plus)
                outer_y[at, i, tile(j)] = minus
                off[1].append(minus)
                off[2].append(plus)

                low, high = cls(p, q, 0), cls(p, q, 1)
                minus = kap[low] + z_low * roll(kap[high], 1, 1)
                plus = kap[high] + z_high * roll(kap[low], -1, 1)
                outside[low].append(minus)
                outside[high].append(plus)
                minus, plus = z_low * minus, z_high * plus
                outer_z[at, i, tile(j)] = minus
                outer_z[4 + at, i, tile(j)] = plus
                off[3].append(minus)
                off[4].append(plus)
            coarse_total = []
            for k in range(8):
                within, without = tree_sum(inside[k]), tree_sum(outside[k])
                inner_sum[k, i, tile(j)] = within
                base = within + without + shift
                diagonal[k, i, tile(j)] = base
                coarse_total.append(without)
                damped[k, i, tile(j)] = (DAMPING / KEPT) * inverse(base)
            for at, part in enumerate(off):
                coarse_off[at, i, tile(j)] = tree_sum(part)
            coarse_damped[i, tile(j)] = DAMPING * inverse(tree_sum(coarse_total) + 8.0 * shift)
        return carry

    lax.fori_loop(0, half, plane, 0, unroll=UNROLL)
    for j in range(tiles):
        part = []
        for p, q in PAIRS:
            face = half_kappa[cls(0, p, q), half + 1, tile(j)]
            face = face + half_kappa[cls(1, p, q), half, tile(j)]
            outer_x[2 * p + q, half, tile(j)] = face
            part.append(face)
        coarse_off[0, half, tile(j)] = tree_sum(part)


def solve_kernel(
    mine_ref,
    theirs_ref,
    inner,
    outer_x,
    outer_y,
    outer_z,
    inner_sum,
    diagonal,
    damped,
    coarse_off,
    coarse_damped,
    chosen,
    planes,
    residual,
    scaled,
    partial,
    first_dir,
    second_dir,
    image,
    coarse_one,
    coarse_two,
    *,
    own,
):
    half, rows = inner.shape[1:3]
    at_ = Layout(rows)
    tile, tiles, zero = at_.tile, at_.tiles, at_.zero
    place = lax.axis_index("space")
    core = place % 2

    def begin(k, spot, j, value):
        residual[k, spot, tile(j)] = value
        scaled[k, spot + 1, tile(j)] = damped[k, spot, tile(j)] * value

    at_.arrange(mine_ref, theirs_ref, place, True, begin)
    at_.seam_fine(scaled)

    def rows_of(ref, i):
        cache = {}

        def load(k, j, step):
            if abs(j - step) > 1:
                return ref[k, i, tile(j)]
            if (k, j) not in cache:
                cache[k, j] = ref[k, i, tile(j)]
            return cache[k, j]

        def get(k, j):
            return load(k, j, j)

        def before(k, j):
            return at_.row_before(lambda r: load(k, r, j), j)

        def after(k, j):
            return at_.row_after(lambda r: load(k, r, j), j)

        return get, before, after

    def stencil(field, i, both):
        get, before, after = rows_of(field, i + 1)
        face_get, _, face_after = rows_of(outer_y, i)
        for j in range(tiles):
            here = [get(k, j) for k in range(8)]
            terms = [[] for _ in range(8)]
            for p, q in PAIRS:
                at = 2 * p + q
                for face_at, low, high in inner_faces(p, q):
                    face = inner[face_at, i, tile(j)]
                    terms[low].append(face * here[high])
                    if both:
                        terms[high].append(face * here[low])
                low, high = cls(0, p, q), cls(1, p, q)
                terms[low].append(outer_x[at, i, tile(j)] * field[high, i, tile(j)])
                if both:
                    side = field[low, i + 2, tile(j)]
                    terms[high].append(outer_x[at, i + 1, tile(j)] * side)
                low, high = cls(p, 0, q), cls(p, 1, q)
                terms[low].append(face_get(at, j) * before(high, j))
                if both:
                    terms[high].append(face_after(at, j) * after(low, j))
                low, high = cls(p, q, 0), cls(p, q, 1)
                terms[low].append(outer_z[at, i, tile(j)] * roll(here[high], 1, 1))
                if both:
                    terms[high].append(outer_z[4 + at, i, tile(j)] * roll(here[low], -1, 1))
            yield j, here, [tree_sum(part) if part else None for part in terms]

    def coarse_sides(field, i, j):
        here = field[0, i + 1, tile(j)]
        return here, (
            (field[0, i, tile(j)], field[0, i + 2, tile(j)]),
            (
                at_.row_before(lambda r: field[0, i + 1, tile(r)], j),
                at_.row_after(lambda r: field[0, i + 1, tile(r)], j),
            ),
            (roll(here, 1, 1), roll(here, -1, 1)),
        )

    def precondition(result):
        def down(i, carry):
            for j, _, sums in stencil(scaled, i, True):
                res = [residual[k, i, tile(j)] for k in range(8)]
                parts = [res[k] + sums[k] for k in range(8)]
                for k in range(8):
                    partial[k, i, tile(j)] = parts[k]
                rhs = tree_sum(parts) - (1.0 / KEPT) * tree_sum(res)
                coarse_one[0, i + 1, tile(j)] = coarse_damped[i, tile(j)] * rhs
            return carry

        lax.fori_loop(0, half, down, 0, unroll=UNROLL)
        at_.seam(coarse_one, [0], [0])

        def smooth(i, carry):
            for j in range(tiles):
                here, sides = coarse_sides(coarse_one, i, j)
                total = coarse_off[0, i, tile(j)] * sides[0][0]
                total = total + coarse_off[0, i + 1, tile(j)] * sides[0][1]
                more = coarse_off[1, i, tile(j)] * sides[1][0]
                more = more + coarse_off[2, i, tile(j)] * sides[1][1]
                most = coarse_off[3, i, tile(j)] * sides[2][0]
                most = most + coarse_off[4, i, tile(j)] * sides[2][1]
                coarse_two[0, i + 1, tile(j)] = KEPT * here + coarse_damped[
                    i, tile(j)
                ] * (total + more + most)
            return carry

        lax.fori_loop(0, half, smooth, 0, unroll=UNROLL)
        at_.seam(coarse_two, [0], [0])

        def up(i, gamma):
            face_get, _, face_after = rows_of(outer_y, i)
            for j in range(tiles):
                here, sides = coarse_sides(coarse_two, i, j)
                kept = ((1.0 - DAMPING) / KEPT) * here
                dots = []
                for a, b, c in CLASSES:
                    k = cls(a, b, c)
                    value = tree_sum(
                        [
                            partial[k, i, tile(j)],
                            inner_sum[k, i, tile(j)] * here,
                            outer_x[2 * b + c, i + a, tile(j)] * sides[0][a],
                            (face_after if b else face_get)(2 * a + c, j) * sides[1][b],
                            outer_z[4 * c + 2 * a + b, i, tile(j)] * sides[2][c],
                        ]
                    )
                    new = kept + damped[k, i, tile(j)] * value
                    result[k, i + 1, tile(j)] = new
                    dots.append(residual[k, i, tile(j)] * new)
                gamma = gamma + tree_sum(dots)
            return gamma

        gamma = lax.fori_loop(0, half, up, zero, unroll=UNROLL)
        at_.seam_fine(result)
        return grand_total(gamma)

    gamma = precondition(first_dir)

    def apply(i, acc):
        for j, here, sums in stencil(first_dir, i, True):
            dots = []
            for k in range(8):
                value = diagonal[k, i, tile(j)] * here[k] - sums[k]
                image[k, i, tile(j)] = value
                dots.append(here[k] * value)
            acc = acc + tree_sum(dots)
        return acc

    curve = grand_total(lax.fori_loop(0, half, apply, zero, unroll=UNROLL))
    step_one = gamma / curve

    def update(i, carry):
        for j in range(tiles):
            for k in range(8):
                new = residual[k, i, tile(j)] - step_one * image[k, i, tile(j)]
                residual[k, i, tile(j)] = new
                scaled[k, i + 1, tile(j)] = damped[k, i, tile(j)] * new
        return carry

    lax.fori_loop(0, half, update, 0, unroll=UNROLL)
    at_.seam_fine(scaled)

    gamma_next = precondition(second_dir)

    def bend(i, carry):
        own_part, face_part = carry
        for j, here, sums in stencil(second_dir, i, False):
            own_part = own_part + tree_sum(
                [here[k] * (diagonal[k, i, tile(j)] * here[k]) for k in range(8)]
            )
            face_part = face_part + tree_sum([here[k] * sums[k] for k in range(7)])
        return own_part, face_part

    own_part, face_part = lax.fori_loop(0, half, bend, (zero, zero), unroll=UNROLL)
    ratio = gamma_next / gamma
    curve_next = grand_total(own_part - 2.0 * face_part)
    step_two = gamma_next / (curve_next - ratio * ratio * curve)
    weight = chosen[...]
    step_first = (step_one + step_two * ratio) * weight
    step_two = step_two * weight

    start = (place - core) * (own // 2)
    upper = jnp.where(start >= half, 1, 0)
    start = start - half * upper
    even = at_.lane % 2 == 0
    source = at_.lane // 2 + HALF * upper
    for at in range(2 * own + 2):
        a = (at + 1) % 2
        spot = start + (at + 1) // 2
        for b in (0, 1):
            for j in range(tiles):
                both = [
                    step_first * first_dir[cls(a, b, c), spot, tile(j)]
                    + step_two * second_dir[cls(a, b, c), spot, tile(j)]
                    for c in (0, 1)
                ]
                planes[at, at_.every(b, j), :] = jnp.where(
                    even,
                    jnp.take_along_axis(both[0], source, axis=1),
                    jnp.take_along_axis(both[1], source, axis=1),
                )


def finish_kernel(planes_ref, state_ref, far_ref, near_ref, adjoint_ref, keep_ref, partner_ref, send_ref, terms):
    own, ny, nz = adjoint_ref.shape
    core = lax.axis_index("space") % 2
    full = (ny, nz)
    y_at = row_index(full)
    z_at = lane_index(full)

    def drop(value, axis, up):
        moved = roll(value, -1 if up else 1, axis)
        at = (y_at, z_at)[axis]
        edge = full[axis] - 1 if up else 0
        return value - jnp.where(at == edge, 0.0, moved)

    is_even = core == 0
    state = [jnp.where(is_even, far_ref[core, 0], near_ref[own])]
    state += [jnp.where(is_even, state_ref[core, x], near_ref[x]) for x in range(own)]
    state += [jnp.where(is_even, near_ref[x], state_ref[core, x]) for x in range(own)]
    state += [jnp.where(is_even, near_ref[own], far_ref[core, 0])]
    for x in range(2 * own):
        here, f = planes_ref[x + 1], state[x + 1]
        term = (here - planes_ref[x + 2]) * (f - state[x + 2])
        term = term + (here - planes_ref[x]) * (f - state[x])
        for axis in (0, 1):
            for up in (True, False):
                term = term + drop(here, axis, up) * drop(f, axis, up)
        terms[x] = -0.5 * term

    groups = send_ref.shape[0] + 1
    chunk = keep_ref.shape[1]
    for x in range(own):
        mine, other = core * own + x, (1 - core) * own + x
        adjoint_ref[x] = planes_ref[1 + mine]
        partner_ref[x, :ny] = planes_ref[1 + other]
        for k in range(groups):
            at = lax.rem(lax.axis_index("pole") + k, groups) * chunk
            at = pl.multiple_of(at, chunk)
            for side, plane in enumerate((mine, other)):
                share = terms[plane, pl.ds(at, chunk), :]
                if k:
                    send_ref[k - 1, side, x] = share
                elif side:
                    partner_ref[x, ny:] = share
                else:
                    keep_ref[x] = share


def whole_grid(conductivity, misfit, forward_states, pole_shifts, pole_weights, pole_order):
    members, own, ny, nz = forward_states.shape
    groups = lax.axis_size("pole")
    peers = lax.axis_size("space")
    even = lax.axis_index("space") % 2 == 0
    mine, theirs, far, near = gather_blocks([conductivity, misfit], forward_states, "space")
    half, rows = peers * own // 4, ny // 2

    def field(count, extent):
        return (count, extent, rows, 2 * HALF)

    def held(*shape):
        return pltpu.VMEM(shape, jnp.float32)

    vmem = pl.BlockSpec(memory_space=pltpu.VMEM)
    shapes = [
        field(12, half),
        field(4, half + 1),
        field(4, half),
        field(8, half),
        field(8, half),
        field(8, half),
        field(8, half),
        field(5, half + 1),
        (half, rows, 2 * HALF),
        (TILE, 2 * HALF),
    ]
    coefficients = pl.pallas_call(
        setup_kernel,
        out_shape=[jax.ShapeDtypeStruct(shape, jnp.float32) for shape in shapes],
        in_specs=[vmem] * 5,
        out_specs=[vmem] * len(shapes),
        scratch_shapes=[held(*field(8, half + 2))],
        compiler_params=pltpu.CompilerParams(vmem_limit_bytes=6 * 1024 * 1024),
        name="setup",
    )(pole_order[None], pole_shifts[None], pole_weights[None], mine[0], theirs[0])
    planes = pl.pallas_call(
        functools.partial(solve_kernel, own=own),
        out_shape=jax.ShapeDtypeStruct((2 * own + 2, ny, nz), jnp.float32),
        in_specs=[vmem] * (2 + len(shapes)),
        out_specs=vmem,
        scratch_shapes=[
            held(*field(8, half)),
            held(*field(8, half + 2)),
            held(*field(8, half)),
            held(*field(8, half + 2)),
            held(*field(8, half + 2)),
            held(*field(8, half)),
            held(*field(1, half + 2)),
            held(*field(1, half + 2)),
        ],
        compiler_params=pltpu.CompilerParams(vmem_limit_bytes=12 * 1024 * 1024),
        name="solve",
    )(mine[1], theirs[1], *coefficients)
    chunk = ny // groups
    adjoint, gradient, partner, send = pl.pallas_call(
        finish_kernel,
        out_shape=[
            jax.ShapeDtypeStruct((own, ny, nz), jnp.float32),
            jax.ShapeDtypeStruct((own, chunk, nz), jnp.float32),
            jax.ShapeDtypeStruct((own, ny + chunk, nz), jnp.float32),
            jax.ShapeDtypeStruct((groups - 1, 2, own, chunk, nz), jnp.float32),
        ],
        in_specs=[vmem] * 4,
        out_specs=[vmem] * 4,
        scratch_shapes=[held(2 * own, ny, nz)],
        compiler_params=pltpu.CompilerParams(vmem_limit_bytes=4 * 1024 * 1024),
        name="finish",
    )(planes, forward_states, far, near)

    arrived = lax.ppermute(partner, "space", [(i, i ^ 1) for i in range(peers)])
    shares = []
    for k in range(1, groups):
        for side in (0, 1):
            pairs = [
                (i * peers + j, (i + k) % groups * peers + (j ^ side))
                for i in range(groups)
                for j in range(peers)
            ]
            shares.append(lax.ppermute(send[k - 1, side], ("pole", "space"), pairs))
    theirs = arrived[:, :ny]
    adjoint_states = jnp.stack(
        [jnp.where(even, adjoint, theirs), jnp.where(even, theirs, adjoint)]
    )
    adjoint_states, arrived = lax.optimization_barrier((adjoint_states, arrived))
    return adjoint_states, gradient + arrived[:, ny:] + sum(shares)


def plus_side(field, which_dim):
    extent = field.shape[which_dim]
    inner_part = lax.slice_in_dim(field, 1, extent, axis=which_dim)
    zero_plane = jnp.zeros_like(lax.slice_in_dim(field, 0, 1, axis=which_dim))
    return jnp.concatenate([inner_part, zero_plane], axis=which_dim)


def minus_side(field, which_dim):
    extent = field.shape[which_dim]
    inner_part = lax.slice_in_dim(field, 0, extent - 1, axis=which_dim)
    zero_plane = jnp.zeros_like(lax.slice_in_dim(field, 0, 1, axis=which_dim))
    return jnp.concatenate([zero_plane, inner_part], axis=which_dim)


def coarse_pick(faces, which_dim, offset):
    extent_x, extent_y, extent_z = faces.shape
    blocks = faces.reshape(extent_x // 2, 2, extent_y // 2, 2, extent_z // 2, 2)
    chosen = lax.index_in_dim(blocks, offset, axis=2 * which_dim + 1, keepdims=True)
    return jnp.sum(chosen, axis=(1, 3, 5))


def side_terms(field, plus_faces, minus_faces, widened):
    result = plus_faces[0] * (field - widened[:, 2:]) + minus_faces[0] * (field - widened[:, :-2])
    for which_dim in (1, 2):
        result = result + plus_faces[which_dim] * (field - plus_side(field, which_dim + 1))
        result = result + minus_faces[which_dim] * (field - minus_side(field, which_dim + 1))
    return result


def fine_image(field, plus_faces, minus_faces, shift_value):
    widened = extended(field, (("space", 1),), 1)
    return shift_value * field + side_terms(field, plus_faces, minus_faces, widened)


def coarse_image(field, plus_faces, minus_faces, shift_value):
    widened = extended(field, (("space", 1),), 1)
    return shift_value * field + side_terms(field, plus_faces, minus_faces, widened)


def restrict(field):
    members, extent_x, extent_y, extent_z = field.shape
    shaped = field.reshape(members, extent_x // 2, 2, extent_y // 2, 2, extent_z // 2, 2)
    return jnp.sum(shaped, axis=(2, 4, 6))


def prolong(field):
    return jnp.repeat(jnp.repeat(jnp.repeat(field, 2, axis=1), 2, axis=2), 2, axis=3)


def precondition(residual, fine, coarse):
    plus_faces, minus_faces, shift_value, diagonal = fine
    coarse_plus, coarse_minus, coarse_shift, coarse_diagonal = coarse
    smooth_one = DAMPING * residual / diagonal
    coarse_rhs = restrict(residual - fine_image(smooth_one, plus_faces, minus_faces, shift_value))
    coarse_one = DAMPING * coarse_rhs / coarse_diagonal
    coarse_two = (
        coarse_one
        + DAMPING
        * (coarse_rhs - coarse_image(coarse_one, coarse_plus, coarse_minus, coarse_shift))
        / coarse_diagonal
    )
    corrected = smooth_one + prolong(coarse_two)
    return (
        corrected
        + DAMPING
        * (residual - fine_image(corrected, plus_faces, minus_faces, shift_value))
        / diagonal
    )


def expand(values):
    return values.reshape(-1, 1, 1, 1)


def cell_sums(values):
    return jnp.sum(values, axis=(1, 2, 3))


def norm_sum(residual, precond):
    return lax.psum(cell_sums(residual * precond), "space")


def solve(rhs, fine, coarse):
    plus_faces, minus_faces, shift_value, diagonal = fine
    iterate = jnp.zeros_like(rhs)
    residual = rhs
    precond = precondition(residual, fine, coarse)
    gamma_now = norm_sum(residual, precond)
    search = precond
    for turn_index in range(ITERS):
        image_field = fine_image(search, plus_faces, minus_faces, shift_value)
        curve = lax.psum(cell_sums(search * image_field), "space")
        step_length = gamma_now / curve
        iterate = iterate + expand(step_length) * search
        if turn_index + 1 < ITERS:
            residual = residual - expand(step_length) * image_field
            precond = precondition(residual, fine, coarse)
            gamma_next = norm_sum(residual, precond)
            search = precond + expand(gamma_next / gamma_now) * search
            gamma_now = gamma_next
    return iterate


def divided(conductivity, misfit, forward_states, pole_shifts, pole_weights, pole_order):
    widened_kappa = extended(conductivity, (("space", 0),), 1)
    plus_faces = [
        0.5 * (conductivity + widened_kappa[2:]),
        0.5 * (conductivity + plus_side(conductivity, 1)),
        0.5 * (conductivity + plus_side(conductivity, 2)),
    ]
    minus_faces = [
        0.5 * (conductivity + widened_kappa[:-2]),
        0.5 * (conductivity + minus_side(conductivity, 1)),
        0.5 * (conductivity + minus_side(conductivity, 2)),
    ]
    base_diagonal = (
        plus_faces[0]
        + plus_faces[1]
        + plus_faces[2]
        + minus_faces[0]
        + minus_faces[1]
        + minus_faces[2]
    )
    coarse_plus = [coarse_pick(plus_faces[which_dim], which_dim, 1) for which_dim in range(3)]
    coarse_minus = [coarse_pick(minus_faces[which_dim], which_dim, 0) for which_dim in range(3)]
    coarse_base = (
        coarse_plus[0]
        + coarse_plus[1]
        + coarse_plus[2]
        + coarse_minus[0]
        + coarse_minus[1]
        + coarse_minus[2]
    )
    pole_index = jnp.arange(pole_shifts.shape[0], dtype=jnp.int32)
    matches = pole_order[:, None] == pole_index[None, :]
    shift_local = jnp.sum(jnp.where(matches, pole_shifts[None, :], 0.0), axis=1)
    weight_local = jnp.sum(jnp.where(matches, pole_weights[None, :], 0.0), axis=1)
    members = forward_states.shape[0]

    def solve_group(shift_part, weight_part):
        shift_value = expand(shift_part)
        fine = (plus_faces, minus_faces, shift_value, base_diagonal[None] + shift_value)
        coarse = (
            coarse_plus,
            coarse_minus,
            8.0 * shift_value,
            coarse_base[None] + 8.0 * shift_value,
        )
        return solve(expand(weight_part) * misfit[None], fine, coarse)

    adjoint_states = jnp.concatenate(
        [
            solve_group(shift_local[member : member + 1], weight_local[member : member + 1])
            for member in range(members)
        ],
        axis=0,
    )
    widened = extended(jnp.stack([adjoint_states, forward_states]), (("space", 2),), 1)
    term = (adjoint_states - widened[0, :, 2:]) * (forward_states - widened[1, :, 2:])
    term = term + (adjoint_states - widened[0, :, :-2]) * (forward_states - widened[1, :, :-2])
    for which_dim in (2, 3):
        term = term + (adjoint_states - plus_side(adjoint_states, which_dim)) * (
            forward_states - plus_side(forward_states, which_dim)
        )
        term = term + (adjoint_states - minus_side(adjoint_states, which_dim)) * (
            forward_states - minus_side(forward_states, which_dim)
        )
    local_term = -0.5 * jnp.sum(term, axis=0)
    gradient = lax.psum_scatter(local_term, "pole", scatter_dimension=1, tiled=True)
    return (adjoint_states, gradient)


def solution(mesh):
    in_specs = (
        P("space", None, None),
        P("space", None, None),
        P("pole", "space", None, None),
        P(),
        P(),
        P("pole"),
    )
    out_specs = (P("pole", "space", None, None), P("space", "pole", None))

    def body(conductivity, misfit, forward_states, *poles):
        nx = conductivity.shape[0] * lax.axis_size("space")
        _, ny, nz = conductivity.shape
        peers = lax.axis_size("space")
        small = nx * ny * nz <= REPLICATED_CELLS and forward_states.shape[:2] == (2, 2)
        if small and nz == 2 * HALF and peers > 2 and peers & (peers - 1) == 0:
            return whole_grid(conductivity, misfit, forward_states, *poles)
        return divided(conductivity, misfit, forward_states, *poles)

    return jax.shard_map(
        body, mesh=mesh, in_specs=in_specs, out_specs=out_specs, check_vma=False
    )
```

```python
import functools

import jax
import jax.numpy as jnp
from jax import lax
from jax.experimental import pallas as pl
from jax.experimental.pallas import tpu as pltpu
from jax.sharding import PartitionSpec as P

ITERS = 2
DAMPING = 0.8
KEPT = 2.0 - DAMPING
REPLICATED_CELLS = 32 * 64 * 128
HALF = 64
TILE = 8
UNROLL = 8


def extended(array, sides, width):
    for axis, dim in sides:
        peers, length = (lax.axis_size(axis), array.shape[dim])
        up = [(i, (i + 1) % peers) for i in range(peers - 1)]
        down = [(j, i) for i, j in up]
        last = lax.slice_in_dim(array, length - width, length, axis=dim)
        leading = lax.slice_in_dim(array, 0, width, axis=dim)
        before = lax.ppermute(last, axis, up)
        after = lax.ppermute(leading, axis, down)
        array = jnp.concatenate([before, array, after], axis=dim)
    return array


def lane_index(shape):
    return lax.broadcasted_iota(jnp.int32, shape, len(shape) - 1)


def row_index(shape):
    return lax.broadcasted_iota(jnp.int32, shape, len(shape) - 2)


def roll(block, shift, axis):
    return pltpu.roll(block, shift % block.shape[axis], axis)


def inverse(value):
    guess = pl.reciprocal(value, approx=True)
    return guess * (2.0 - value * guess)


def tree_sum(values):
    while len(values) > 1:
        values = [sum(values[at : at + 2]) for at in range(0, len(values), 2)]
    return values[0]


def grand_total(acc):
    line = jnp.sum(acc, axis=0, keepdims=True)
    return jnp.broadcast_to(jnp.sum(line, axis=1, keepdims=True), acc.shape)


def swap_masks(peers, flip):
    falling = []
    mask = peers // 2
    while mask > 1:
        falling.append(mask)
        mask //= 2
    if flip:
        return falling[::-1], falling[:1] + falling[:0:-1]
    return falling, falling[-1:] + falling[:-1]


def block_pair(u, holder, peers, flip):
    even, odd = swap_masks(peers, flip)
    parity = holder % 2
    top = jnp.where(parity == 0, even.index(peers // 2), odd.index(peers // 2))
    below = u & ((1 << top) - 1)
    base = ((u >> top) << (top + 1)) | below
    upper = jnp.where(holder >= peers // 2, 1, 0)
    first = base | (upper << top)
    second = base | ((1 - upper) << top)
    home = holder
    for step, (mask_even, mask_odd) in enumerate(zip(even, odd)):
        mask = jnp.where(parity == 0, mask_even, mask_odd)
        home = home ^ (((first >> step) & 1) * mask)
    return first, second, home


def prepare_kernel(kappa_ref, misfit_ref, kappa_out, misfit_out, *, axis, peers):
    at_ = Layout(kappa_ref.shape[1] // 2)
    upper = jnp.where(lax.axis_index(axis) >= peers // 2, 1, 0)
    at_.deal(kappa_ref, kappa_out, upper)
    at_.deal(misfit_ref, misfit_out, upper)


def join_kernel(*refs, masks, axis, peers):
    place = lax.axis_index(axis)
    at_ = Layout(refs[0].shape[1] // 2)
    for at, (even, odd) in enumerate(masks):
        partner = place ^ jnp.where(place % 2 == 0, even, odd)
        refs[4 + at][0] = refs[at][...]
        at_.deal(refs[2 + at], refs[4 + at].at[1], jnp.where(partner >= peers // 2, 1, 0))


def gather_blocks(blocks, states, axis):
    peers = lax.axis_size(axis)
    even = lax.axis_index(axis) % 2 == 0
    swap = [(i, i ^ 1) for i in range(peers)]
    over = [(i, i + 1 if i % 2 else i - 1) for i in range(1, peers - 1)]
    vmem = pl.BlockSpec(memory_space=pltpu.VMEM)
    swaps = [list(zip(*swap_masks(peers, flip))) for flip in (False, True)]
    own = pl.pallas_call(
        functools.partial(prepare_kernel, axis=axis, peers=peers),
        out_shape=[jax.ShapeDtypeStruct(block.shape, jnp.float32) for block in blocks],
        in_specs=[vmem] * 2,
        out_specs=[vmem] * 2,
        compiler_params=pltpu.CompilerParams(vmem_limit_bytes=1024 * 1024),
        name="prepare",
    )(*blocks)
    held = list(blocks)
    for step in range(len(swaps[0])):
        arrived = []
        for at in (0, 1):
            masks = swaps[at][step]
            pairs = [(i, i ^ masks[i % 2]) for i in range(peers)]
            arrived.append(lax.ppermute(held[at], axis, pairs))
        if step:
            held = [jnp.concatenate(pair, axis=0) for pair in zip(held, arrived)]
            continue
        masks = [swaps[at][0] for at in (0, 1)]
        shape = jax.ShapeDtypeStruct((2, *blocks[0].shape), jnp.float32)
        held[:] = pl.pallas_call(
            functools.partial(join_kernel, masks=masks, axis=axis, peers=peers),
            out_shape=[shape] * 2,
            in_specs=[vmem] * 4,
            out_specs=[vmem] * 2,
            compiler_params=pltpu.CompilerParams(vmem_limit_bytes=1024 * 1024),
            name="join",
        )(*own, *arrived)
        held[1], states = lax.optimization_barrier((held[1], states))
        far = lax.ppermute(jnp.where(even, states[:, :1], states[:, -1:]), axis, over)
    other = [lax.ppermute(part, axis, swap) for part in held]

    def fetch_near(after):
        late, states_late, far_late = lax.optimization_barrier((after, states, far))
        given = jnp.concatenate([states_late, far_late], axis=1)
        return late, lax.ppermute(jnp.where(even, given[1], given[0]), axis, swap)

    return held, other, far, fetch_near


CLASSES = [(a, b, c) for a in (0, 1) for b in (0, 1) for c in (0, 1)]
PAIRS = [(p, q) for p in (0, 1) for q in (0, 1)]


def cls(a, b, c):
    return 4 * a + 2 * b + c


def inner_faces(p, q):
    return (
        (2 * p + q, cls(0, p, q), cls(1, p, q)),
        (4 + 2 * p + q, cls(p, 0, q), cls(p, 1, q)),
        (8 + 2 * p + q, cls(p, q, 0), cls(p, q, 1)),
    )


class Layout:
    def __init__(self, rows):
        self.tiles = rows // TILE
        self.lane = lane_index((TILE, 2 * HALF))
        self.row = row_index((TILE, 2 * HALF))
        self.left = self.lane < HALF
        self.zero = jnp.zeros((TILE, 2 * HALF), jnp.float32)

    def tile(self, j):
        return pl.ds(TILE * j, TILE)

    def every(self, b, j):
        return pl.ds(b + 2 * j, TILE, stride=2 * self.tiles)

    def row_before(self, load, j):
        return load(j - 1) if j else roll(load(self.tiles - 1), 1, 0)

    def row_after(self, load, j):
        return load(j + 1) if j + 1 < self.tiles else roll(load(0), -1, 0)

    def seam(self, ref, low, high):
        last = ref.shape[1] - 1
        for j in range(self.tiles):
            for k in low:
                moved = roll(ref[k, last - 1, self.tile(j)], HALF, 1)
                ref[k, 0, self.tile(j)] = jnp.where(self.left, 0.0, moved)
            for k in high:
                moved = roll(ref[k, 1, self.tile(j)], HALF, 1)
                ref[k, last, self.tile(j)] = jnp.where(self.left, moved, 0.0)

    def seam_fine(self, ref):
        count = ref.shape[0]
        self.seam(
            ref,
            [k for k in range(count) if k % 8 >= 4],
            [k for k in range(count) if k % 8 < 4],
        )

    def dealt(self, b, j):
        return pl.ds(TILE * (self.tiles * b + j), TILE)

    def deal(self, block_ref, out_ref, upper):
        odd = jnp.where(self.left, upper, 1 - upper)
        column = 2 * (self.lane % HALF) + odd
        for x in range(block_ref.shape[0]):
            for b in (0, 1):
                for j in range(self.tiles):
                    rows = block_ref[x, self.every(b, j), :]
                    out_ref[x, self.dealt(b, j), :] = jnp.take_along_axis(rows, column, axis=1)

    def arrange(self, mine_ref, theirs_ref, place, flip, store):
        blocks, own = mine_ref.shape[:2]

        def pair(u, carry):
            for ref, holder in ((mine_ref, place), (theirs_ref, place ^ 1)):
                first, second, home = block_pair(u, holder, 2 * blocks, flip)
                for x in range(own):
                    spot = home * (own // 2) + x // 2
                    for b in (0, 1):
                        for j in range(self.tiles):
                            one = ref[first, x, self.dealt(b, j), :]
                            two = ref[second, x, self.dealt(b, j), :]
                            store(cls(x % 2, b, 0), spot, j, jnp.where(self.left, one, two))
                            odd = roll(jnp.where(self.left, two, one), HALF, 1)
                            store(cls(x % 2, b, 1), spot, j, odd)
            return carry

        lax.fori_loop(0, blocks // 2, pair, 0, unroll=True)


def setup_kernel(
    order_ref,
    shifts_ref,
    weights_ref,
    mine_ref,
    theirs_ref,
    inner,
    outer_x,
    outer_y,
    outer_z,
    inner_sum,
    diagonal,
    damped,
    coarse_off,
    coarse_damped,
    chosen,
    half_kappa,
):
    half = inner.shape[1]
    at_ = Layout(inner.shape[2])
    tile, tiles = at_.tile, at_.tiles
    place = lax.axis_index("space")
    pole = jnp.where(place % 2 == 0, order_ref[:, 0:1], order_ref[:, 1:2])
    taken = lane_index(shifts_ref.shape) == pole
    shift = jnp.sum(jnp.where(taken, shifts_ref[...], 0.0), axis=1, keepdims=True)
    weight = jnp.sum(jnp.where(taken, weights_ref[...], 0.0), axis=1, keepdims=True)
    shift = jnp.broadcast_to(shift, at_.zero.shape)
    chosen[...] = jnp.broadcast_to(weight, at_.zero.shape)

    def keep(k, spot, j, value):
        half_kappa[k, spot + 1, tile(j)] = 0.5 * value

    at_.arrange(mine_ref, theirs_ref, place, False, keep)
    at_.seam_fine(half_kappa)

    z_low = jnp.where(at_.lane % HALF > 0, 1.0, 0.0)
    z_high = jnp.where(at_.lane % HALF < HALF - 1, 1.0, 0.0)
    y_low = [jnp.where(at_.row > 0, 1.0, 0.0)] + [None] * (tiles - 1)
    y_high = [None] * (tiles - 1) + [jnp.where(at_.row < TILE - 1, 1.0, 0.0)]

    def masked(mask, value):
        return value if mask is None else mask * value

    def plane(i, carry):
        for j in range(tiles):
            kap = [half_kappa[k, i + 1, tile(j)] for k in range(8)]
            inside = [[] for _ in range(8)]
            outside = [[] for _ in range(8)]
            off = [[] for _ in range(5)]
            for p, q in PAIRS:
                for face_at, low, high in inner_faces(p, q):
                    face = kap[low] + kap[high]
                    inner[face_at, i, tile(j)] = face
                    inside[low].append(face)
                    inside[high].append(face)
                at = 2 * p + q

                low, high = cls(0, p, q), cls(1, p, q)
                minus = kap[low] + half_kappa[high, i, tile(j)]
                plus = kap[high] + half_kappa[low, i + 2, tile(j)]
                outside[low].append(minus)
                outside[high].append(plus)
                outer_x[at, i, tile(j)] = minus
                off[0].append(minus)

                low, high = cls(p, 0, q), cls(p, 1, q)
                side = at_.row_before(lambda r: half_kappa[high, i + 1, tile(r)], j)
                minus = kap[low] + masked(y_low[j], side)
                side = at_.row_after(lambda r: half_kappa[low, i + 1, tile(r)], j)
                plus = kap[high] + masked(y_high[j], side)
                outside[low].append(minus)
                outside[high].append(plus)
                minus, plus = masked(y_low[j], minus), masked(y_high[j], plus)
                outer_y[at, i, tile(j)] = minus
                off[1].append(minus)
                off[2].append(plus)

                low, high = cls(p, q, 0), cls(p, q, 1)
                minus = kap[low] + z_low * roll(kap[high], 1, 1)
                plus = kap[high] + z_high * roll(kap[low], -1, 1)
                outside[low].append(minus)
                outside[high].append(plus)
                minus, plus = z_low * minus, z_high * plus
                outer_z[at, i, tile(j)] = minus
                outer_z[4 + at, i, tile(j)] = plus
                off[3].append(minus)
                off[4].append(plus)
            coarse_total = []
            for k in range(8):
                within, without = tree_sum(inside[k]), tree_sum(outside[k])
                inner_sum[k, i, tile(j)] = within
                base = within + without + shift
                diagonal[k, i, tile(j)] = base
                coarse_total.append(without)
                damped[k, i, tile(j)] = (DAMPING / KEPT) * inverse(base)
            for at, part in enumerate(off):
                coarse_off[at, i, tile(j)] = tree_sum(part)
            coarse_damped[i, tile(j)] = DAMPING * inverse(tree_sum(coarse_total) + 8.0 * shift)
        return carry

    lax.fori_loop(0, half, plane, 0, unroll=UNROLL)
    for j in range(tiles):
        part = []
        for p, q in PAIRS:
            face = half_kappa[cls(0, p, q), half + 1, tile(j)]
            face = face + half_kappa[cls(1, p, q), half, tile(j)]
            outer_x[2 * p + q, half, tile(j)] = face
            part.append(face)
        coarse_off[0, half, tile(j)] = tree_sum(part)


def solve_kernel(
    mine_ref,
    theirs_ref,
    inner,
    outer_x,
    outer_y,
    outer_z,
    inner_sum,
    diagonal,
    damped,
    coarse_off,
    coarse_damped,
    chosen,
    planes,
    residual,
    scaled,
    partial,
    first_dir,
    second_dir,
    image,
    coarse_one,
    coarse_two,
    *,
    own,
):
    half, rows = inner.shape[1:3]
    at_ = Layout(rows)
    tile, tiles, zero = at_.tile, at_.tiles, at_.zero
    place = lax.axis_index("space")
    core = place % 2

    def begin(k, spot, j, value):
        residual[k, spot, tile(j)] = value
        scaled[k, spot + 1, tile(j)] = damped[k, spot, tile(j)] * value

    at_.arrange(mine_ref, theirs_ref, place, True, begin)
    at_.seam_fine(scaled)

    def rows_of(ref, i):
        cache = {}

        def load(k, j, step):
            if abs(j - step) > 1:
                return ref[k, i, tile(j)]
            if (k, j) not in cache:
                cache[k, j] = ref[k, i, tile(j)]
            return cache[k, j]

        def get(k, j):
            return load(k, j, j)

        def before(k, j):
            return at_.row_before(lambda r: load(k, r, j), j)

        def after(k, j):
            return at_.row_after(lambda r: load(k, r, j), j)

        return get, before, after

    def stencil(field, i, both):
        get, before, after = rows_of(field, i + 1)
        face_get, _, face_after = rows_of(outer_y, i)
        for j in range(tiles):
            here = [get(k, j) for k in range(8)]
            terms = [[] for _ in range(8)]
            for p, q in PAIRS:
                at = 2 * p + q
                for face_at, low, high in inner_faces(p, q):
                    face = inner[face_at, i, tile(j)]
                    terms[low].append(face * here[high])
                    if both:
                        terms[high].append(face * here[low])
                low, high = cls(0, p, q), cls(1, p, q)
                terms[low].append(outer_x[at, i, tile(j)] * field[high, i, tile(j)])
                if both:
                    side = field[low, i + 2, tile(j)]
                    terms[high].append(outer_x[at, i + 1, tile(j)] * side)
                low, high = cls(p, 0, q), cls(p, 1, q)
                terms[low].append(face_get(at, j) * before(high, j))
                if both:
                    terms[high].append(face_after(at, j) * after(low, j))
                low, high = cls(p, q, 0), cls(p, q, 1)
                terms[low].append(outer_z[at, i, tile(j)] * roll(here[high], 1, 1))
                if both:
                    terms[high].append(outer_z[4 + at, i, tile(j)] * roll(here[low], -1, 1))
            yield j, here, [tree_sum(part) if part else None for part in terms]

    def coarse_sides(field, i, j):
        here = field[0, i + 1, tile(j)]
        return here, (
            (field[0, i, tile(j)], field[0, i + 2, tile(j)]),
            (
                at_.row_before(lambda r: field[0, i + 1, tile(r)], j),
                at_.row_after(lambda r: field[0, i + 1, tile(r)], j),
            ),
            (roll(here, 1, 1), roll(here, -1, 1)),
        )

    def precondition(result):
        def down(i, carry):
            for j, _, sums in stencil(scaled, i, True):
                res = [residual[k, i, tile(j)] for k in range(8)]
                parts = [res[k] + sums[k] for k in range(8)]
                for k in range(8):
                    partial[k, i, tile(j)] = parts[k]
                rhs = tree_sum(parts) - (1.0 / KEPT) * tree_sum(res)
                coarse_one[0, i + 1, tile(j)] = coarse_damped[i, tile(j)] * rhs
            return carry

        lax.fori_loop(0, half, down, 0, unroll=UNROLL)
        at_.seam(coarse_one, [0], [0])

        def smooth(i, carry):
            for j in range(tiles):
                here, sides = coarse_sides(coarse_one, i, j)
                total = coarse_off[0, i, tile(j)] * sides[0][0]
                total = total + coarse_off[0, i + 1, tile(j)] * sides[0][1]
                more = coarse_off[1, i, tile(j)] * sides[1][0]
                more = more + coarse_off[2, i, tile(j)] * sides[1][1]
                most = coarse_off[3, i, tile(j)] * sides[2][0]
                most = most + coarse_off[4, i, tile(j)] * sides[2][1]
                coarse_two[0, i + 1, tile(j)] = KEPT * here + coarse_damped[
                    i, tile(j)
                ] * (total + more + most)
            return carry

        lax.fori_loop(0, half, smooth, 0, unroll=UNROLL)
        at_.seam(coarse_two, [0], [0])

        def up(i, gamma):
            face_get, _, face_after = rows_of(outer_y, i)
            for j in range(tiles):
                here, sides = coarse_sides(coarse_two, i, j)
                kept = ((1.0 - DAMPING) / KEPT) * here
                dots = []
                for a, b, c in CLASSES:
                    k = cls(a, b, c)
                    value = tree_sum(
                        [
                            partial[k, i, tile(j)],
                            inner_sum[k, i, tile(j)] * here,
                            outer_x[2 * b + c, i + a, tile(j)] * sides[0][a],
                            (face_after if b else face_get)(2 * a + c, j) * sides[1][b],
                            outer_z[4 * c + 2 * a + b, i, tile(j)] * sides[2][c],
                        ]
                    )
                    new = kept + damped[k, i, tile(j)] * value
                    result[k, i + 1, tile(j)] = new
                    dots.append(residual[k, i, tile(j)] * new)
                gamma = gamma + tree_sum(dots)
            return gamma

        gamma = lax.fori_loop(0, half, up, zero, unroll=UNROLL)
        at_.seam_fine(result)
        return grand_total(gamma)

    gamma = precondition(first_dir)

    def apply(i, acc):
        for j, here, sums in stencil(first_dir, i, True):
            dots = []
            for k in range(8):
                value = diagonal[k, i, tile(j)] * here[k] - sums[k]
                image[k, i, tile(j)] = value
                dots.append(here[k] * value)
            acc = acc + tree_sum(dots)
        return acc

    curve = grand_total(lax.fori_loop(0, half, apply, zero, unroll=UNROLL))
    step_one = gamma / curve

    def update(i, carry):
        for j in range(tiles):
            for k in range(8):
                new = residual[k, i, tile(j)] - step_one * image[k, i, tile(j)]
                residual[k, i, tile(j)] = new
                scaled[k, i + 1, tile(j)] = damped[k, i, tile(j)] * new
        return carry

    lax.fori_loop(0, half, update, 0, unroll=UNROLL)
    at_.seam_fine(scaled)

    gamma_next = precondition(second_dir)

    def bend(i, carry):
        own_part, face_part = carry
        for j, here, sums in stencil(second_dir, i, False):
            own_part = own_part + tree_sum(
                [here[k] * (diagonal[k, i, tile(j)] * here[k]) for k in range(8)]
            )
            face_part = face_part + tree_sum([here[k] * sums[k] for k in range(7)])
        return own_part, face_part

    own_part, face_part = lax.fori_loop(0, half, bend, (zero, zero), unroll=UNROLL)
    ratio = gamma_next / gamma
    curve_next = grand_total(own_part - 2.0 * face_part)
    step_two = gamma_next / (curve_next - ratio * ratio * curve)
    weight = chosen[...]
    step_first = (step_one + step_two * ratio) * weight
    step_two = step_two * weight

    start = (place - core) * (own // 2)
    upper = jnp.where(start >= half, 1, 0)
    start = start - half * upper
    even = at_.lane % 2 == 0
    source = at_.lane // 2 + HALF * upper
    for at in range(2 * own + 2):
        a = (at + 1) % 2
        spot = start + (at + 1) // 2
        for b in (0, 1):
            for j in range(tiles):
                both = [
                    step_first * first_dir[cls(a, b, c), spot, tile(j)]
                    + step_two * second_dir[cls(a, b, c), spot, tile(j)]
                    for c in (0, 1)
                ]
                planes[at, at_.every(b, j), :] = jnp.where(
                    even,
                    jnp.take_along_axis(both[0], source, axis=1),
                    jnp.take_along_axis(both[1], source, axis=1),
                )


def finish_kernel(planes_ref, state_ref, far_ref, near_ref, adjoint_ref, keep_ref, partner_ref, send_ref, terms):
    own, ny, nz = adjoint_ref.shape
    core = lax.axis_index("space") % 2
    full = (ny, nz)
    y_at = row_index(full)
    z_at = lane_index(full)

    def drop(value, axis, up):
        moved = roll(value, -1 if up else 1, axis)
        at = (y_at, z_at)[axis]
        edge = full[axis] - 1 if up else 0
        return value - jnp.where(at == edge, 0.0, moved)

    is_even = core == 0
    state = [jnp.where(is_even, far_ref[core, 0], near_ref[own])]
    state += [jnp.where(is_even, state_ref[core, x], near_ref[x]) for x in range(own)]
    state += [jnp.where(is_even, near_ref[x], state_ref[core, x]) for x in range(own)]
    state += [jnp.where(is_even, near_ref[own], far_ref[core, 0])]
    for x in range(2 * own):
        here, f = planes_ref[x + 1], state[x + 1]
        term = (here - planes_ref[x + 2]) * (f - state[x + 2])
        term = term + (here - planes_ref[x]) * (f - state[x])
        for axis in (0, 1):
            for up in (True, False):
                term = term + drop(here, axis, up) * drop(f, axis, up)
        terms[x] = -0.5 * term

    groups = send_ref.shape[0] + 1
    chunk = keep_ref.shape[1]
    for x in range(own):
        mine, other = core * own + x, (1 - core) * own + x
        adjoint_ref[x] = planes_ref[1 + mine]
        partner_ref[x, :ny] = planes_ref[1 + other]
        for k in range(groups):
            at = lax.rem(lax.axis_index("pole") + k, groups) * chunk
            at = pl.multiple_of(at, chunk)
            for side, plane in enumerate((mine, other)):
                share = terms[plane, pl.ds(at, chunk), :]
                if k:
                    send_ref[k - 1, side, x] = share
                elif side:
                    partner_ref[x, ny:] = share
                else:
                    keep_ref[x] = share


def whole_grid(conductivity, misfit, forward_states, pole_shifts, pole_weights, pole_order):
    members, own, ny, nz = forward_states.shape
    groups = lax.axis_size("pole")
    peers = lax.axis_size("space")
    even = lax.axis_index("space") % 2 == 0
    mine, theirs, far, fetch_near = gather_blocks([conductivity, misfit], forward_states, "space")
    half, rows = peers * own // 4, ny // 2

    def field(count, extent):
        return (count, extent, rows, 2 * HALF)

    def held(*shape):
        return pltpu.VMEM(shape, jnp.float32)

    vmem = pl.BlockSpec(memory_space=pltpu.VMEM)
    shapes = [
        field(12, half),
        field(4, half + 1),
        field(4, half),
        field(8, half),
        field(8, half),
        field(8, half),
        field(8, half),
        field(5, half + 1),
        (half, rows, 2 * HALF),
        (TILE, 2 * HALF),
    ]
    coefficients = pl.pallas_call(
        setup_kernel,
        out_shape=[jax.ShapeDtypeStruct(shape, jnp.float32) for shape in shapes],
        in_specs=[vmem] * 5,
        out_specs=[vmem] * len(shapes),
        scratch_shapes=[held(*field(8, half + 2))],
        compiler_params=pltpu.CompilerParams(vmem_limit_bytes=6 * 1024 * 1024),
        name="setup",
    )(pole_order[None], pole_shifts[None], pole_weights[None], mine[0], theirs[0])
    coefficients, near = fetch_near(coefficients)
    planes = pl.pallas_call(
        functools.partial(solve_kernel, own=own),
        out_shape=jax.ShapeDtypeStruct((2 * own + 2, ny, nz), jnp.float32),
        in_specs=[vmem] * (2 + len(shapes)),
        out_specs=vmem,
        scratch_shapes=[
            held(*field(8, half)),
            held(*field(8, half + 2)),
            held(*field(8, half)),
            held(*field(8, half + 2)),
            held(*field(8, half + 2)),
            held(*field(8, half)),
            held(*field(1, half + 2)),
            held(*field(1, half + 2)),
        ],
        compiler_params=pltpu.CompilerParams(vmem_limit_bytes=12 * 1024 * 1024),
        name="solve",
    )(mine[1], theirs[1], *coefficients)
    chunk = ny // groups
    adjoint, gradient, partner, send = pl.pallas_call(
        finish_kernel,
        out_shape=[
            jax.ShapeDtypeStruct((own, ny, nz), jnp.float32),
            jax.ShapeDtypeStruct((own, chunk, nz), jnp.float32),
            jax.ShapeDtypeStruct((own, ny + chunk, nz), jnp.float32),
            jax.ShapeDtypeStruct((groups - 1, 2, own, chunk, nz), jnp.float32),
        ],
        in_specs=[vmem] * 4,
        out_specs=[vmem] * 4,
        scratch_shapes=[held(2 * own, ny, nz)],
        compiler_params=pltpu.CompilerParams(vmem_limit_bytes=4 * 1024 * 1024),
        name="finish",
    )(planes, forward_states, far, near)

    arrived = lax.ppermute(partner, "space", [(i, i ^ 1) for i in range(peers)])
    shares = []
    for k in range(1, groups):
        for side in (0, 1):
            pairs = [
                (i * peers + j, (i + k) % groups * peers + (j ^ side))
                for i in range(groups)
                for j in range(peers)
            ]
            shares.append(lax.ppermute(send[k - 1, side], ("pole", "space"), pairs))
    theirs = arrived[:, :ny]
    adjoint_states = jnp.stack(
        [jnp.where(even, adjoint, theirs), jnp.where(even, theirs, adjoint)]
    )
    adjoint_states, arrived = lax.optimization_barrier((adjoint_states, arrived))
    return adjoint_states, gradient + arrived[:, ny:] + sum(shares)


def plus_side(field, which_dim):
    extent = field.shape[which_dim]
    inner_part = lax.slice_in_dim(field, 1, extent, axis=which_dim)
    zero_plane = jnp.zeros_like(lax.slice_in_dim(field, 0, 1, axis=which_dim))
    return jnp.concatenate([inner_part, zero_plane], axis=which_dim)


def minus_side(field, which_dim):
    extent = field.shape[which_dim]
    inner_part = lax.slice_in_dim(field, 0, extent - 1, axis=which_dim)
    zero_plane = jnp.zeros_like(lax.slice_in_dim(field, 0, 1, axis=which_dim))
    return jnp.concatenate([zero_plane, inner_part], axis=which_dim)


def coarse_pick(faces, which_dim, offset):
    extent_x, extent_y, extent_z = faces.shape
    blocks = faces.reshape(extent_x // 2, 2, extent_y // 2, 2, extent_z // 2, 2)
    chosen = lax.index_in_dim(blocks, offset, axis=2 * which_dim + 1, keepdims=True)
    return jnp.sum(chosen, axis=(1, 3, 5))


def side_terms(field, plus_faces, minus_faces, widened):
    result = plus_faces[0] * (field - widened[:, 2:]) + minus_faces[0] * (field - widened[:, :-2])
    for which_dim in (1, 2):
        result = result + plus_faces[which_dim] * (field - plus_side(field, which_dim + 1))
        result = result + minus_faces[which_dim] * (field - minus_side(field, which_dim + 1))
    return result


def fine_image(field, plus_faces, minus_faces, shift_value):
    widened = extended(field, (("space", 1),), 1)
    return shift_value * field + side_terms(field, plus_faces, minus_faces, widened)


def coarse_image(field, plus_faces, minus_faces, shift_value):
    widened = extended(field, (("space", 1),), 1)
    return shift_value * field + side_terms(field, plus_faces, minus_faces, widened)


def restrict(field):
    members, extent_x, extent_y, extent_z = field.shape
    shaped = field.reshape(members, extent_x // 2, 2, extent_y // 2, 2, extent_z // 2, 2)
    return jnp.sum(shaped, axis=(2, 4, 6))


def prolong(field):
    return jnp.repeat(jnp.repeat(jnp.repeat(field, 2, axis=1), 2, axis=2), 2, axis=3)


def precondition(residual, fine, coarse):
    plus_faces, minus_faces, shift_value, diagonal = fine
    coarse_plus, coarse_minus, coarse_shift, coarse_diagonal = coarse
    smooth_one = DAMPING * residual / diagonal
    coarse_rhs = restrict(residual - fine_image(smooth_one, plus_faces, minus_faces, shift_value))
    coarse_one = DAMPING * coarse_rhs / coarse_diagonal
    coarse_two = (
        coarse_one
        + DAMPING
        * (coarse_rhs - coarse_image(coarse_one, coarse_plus, coarse_minus, coarse_shift))
        / coarse_diagonal
    )
    corrected = smooth_one + prolong(coarse_two)
    return (
        corrected
        + DAMPING
        * (residual - fine_image(corrected, plus_faces, minus_faces, shift_value))
        / diagonal
    )


def expand(values):
    return values.reshape(-1, 1, 1, 1)


def cell_sums(values):
    return jnp.sum(values, axis=(1, 2, 3))


def norm_sum(residual, precond):
    return lax.psum(cell_sums(residual * precond), "space")


def solve(rhs, fine, coarse):
    plus_faces, minus_faces, shift_value, diagonal = fine
    iterate = jnp.zeros_like(rhs)
    residual = rhs
    precond = precondition(residual, fine, coarse)
    gamma_now = norm_sum(residual, precond)
    search = precond
    for turn_index in range(ITERS):
        image_field = fine_image(search, plus_faces, minus_faces, shift_value)
        curve = lax.psum(cell_sums(search * image_field), "space")
        step_length = gamma_now / curve
        iterate = iterate + expand(step_length) * search
        if turn_index + 1 < ITERS:
            residual = residual - expand(step_length) * image_field
            precond = precondition(residual, fine, coarse)
            gamma_next = norm_sum(residual, precond)
            search = precond + expand(gamma_next / gamma_now) * search
            gamma_now = gamma_next
    return iterate


def divided(conductivity, misfit, forward_states, pole_shifts, pole_weights, pole_order):
    widened_kappa = extended(conductivity, (("space", 0),), 1)
    plus_faces = [
        0.5 * (conductivity + widened_kappa[2:]),
        0.5 * (conductivity + plus_side(conductivity, 1)),
        0.5 * (conductivity + plus_side(conductivity, 2)),
    ]
    minus_faces = [
        0.5 * (conductivity + widened_kappa[:-2]),
        0.5 * (conductivity + minus_side(conductivity, 1)),
        0.5 * (conductivity + minus_side(conductivity, 2)),
    ]
    base_diagonal = (
        plus_faces[0]
        + plus_faces[1]
        + plus_faces[2]
        + minus_faces[0]
        + minus_faces[1]
        + minus_faces[2]
    )
    coarse_plus = [coarse_pick(plus_faces[which_dim], which_dim, 1) for which_dim in range(3)]
    coarse_minus = [coarse_pick(minus_faces[which_dim], which_dim, 0) for which_dim in range(3)]
    coarse_base = (
        coarse_plus[0]
        + coarse_plus[1]
        + coarse_plus[2]
        + coarse_minus[0]
        + coarse_minus[1]
        + coarse_minus[2]
    )
    pole_index = jnp.arange(pole_shifts.shape[0], dtype=jnp.int32)
    matches = pole_order[:, None] == pole_index[None, :]
    shift_local = jnp.sum(jnp.where(matches, pole_shifts[None, :], 0.0), axis=1)
    weight_local = jnp.sum(jnp.where(matches, pole_weights[None, :], 0.0), axis=1)
    members = forward_states.shape[0]

    def solve_group(shift_part, weight_part):
        shift_value = expand(shift_part)
        fine = (plus_faces, minus_faces, shift_value, base_diagonal[None] + shift_value)
        coarse = (
            coarse_plus,
            coarse_minus,
            8.0 * shift_value,
            coarse_base[None] + 8.0 * shift_value,
        )
        return solve(expand(weight_part) * misfit[None], fine, coarse)

    adjoint_states = jnp.concatenate(
        [
            solve_group(shift_local[member : member + 1], weight_local[member : member + 1])
            for member in range(members)
        ],
        axis=0,
    )
    widened = extended(jnp.stack([adjoint_states, forward_states]), (("space", 2),), 1)
    term = (adjoint_states - widened[0, :, 2:]) * (forward_states - widened[1, :, 2:])
    term = term + (adjoint_states - widened[0, :, :-2]) * (forward_states - widened[1, :, :-2])
    for which_dim in (2, 3):
        term = term + (adjoint_states - plus_side(adjoint_states, which_dim)) * (
            forward_states - plus_side(forward_states, which_dim)
        )
        term = term + (adjoint_states - minus_side(adjoint_states, which_dim)) * (
            forward_states - minus_side(forward_states, which_dim)
        )
    local_term = -0.5 * jnp.sum(term, axis=0)
    gradient = lax.psum_scatter(local_term, "pole", scatter_dimension=1, tiled=True)
    return (adjoint_states, gradient)


def solution(mesh):
    in_specs = (
        P("space", None, None),
        P("space", None, None),
        P("pole", "space", None, None),
        P(),
        P(),
        P("pole"),
    )
    out_specs = (P("pole", "space", None, None), P("space", "pole", None))

    def body(conductivity, misfit, forward_states, *poles):
        nx = conductivity.shape[0] * lax.axis_size("space")
        _, ny, nz = conductivity.shape
        peers = lax.axis_size("space")
        small = nx * ny * nz <= REPLICATED_CELLS and forward_states.shape[:2] == (2, 2)
        if small and nz == 2 * HALF and peers > 2 and peers & (peers - 1) == 0:
            return whole_grid(conductivity, misfit, forward_states, *poles)
        return divided(conductivity, misfit, forward_states, *poles)

    return jax.shard_map(
        body, mesh=mesh, in_specs=in_specs, out_specs=out_specs, check_vma=False
    )
```

```python
import functools

import jax
import jax.numpy as jnp
from jax import lax
from jax.experimental import pallas as pl
from jax.experimental.pallas import tpu as pltpu
from jax.sharding import PartitionSpec as P

ITERS = 2
DAMPING = 0.8
KEPT = 2.0 - DAMPING
REPLICATED_CELLS = 32 * 64 * 128
HALF = 64
TILE = 8
UNROLL = 8


def extended(array, sides, width):
    for axis, dim in sides:
        peers, length = (lax.axis_size(axis), array.shape[dim])
        up = [(i, (i + 1) % peers) for i in range(peers - 1)]
        down = [(j, i) for i, j in up]
        last = lax.slice_in_dim(array, length - width, length, axis=dim)
        leading = lax.slice_in_dim(array, 0, width, axis=dim)
        before = lax.ppermute(last, axis, up)
        after = lax.ppermute(leading, axis, down)
        array = jnp.concatenate([before, array, after], axis=dim)
    return array


def lane_index(shape):
    return lax.broadcasted_iota(jnp.int32, shape, len(shape) - 1)


def row_index(shape):
    return lax.broadcasted_iota(jnp.int32, shape, len(shape) - 2)


def roll(block, shift, axis):
    return pltpu.roll(block, shift % block.shape[axis], axis)


def inverse(value):
    guess = pl.reciprocal(value, approx=True)
    return guess * (2.0 - value * guess)


def tree_sum(values):
    while len(values) > 1:
        values = [sum(values[at : at + 2]) for at in range(0, len(values), 2)]
    return values[0]


def grand_total(acc):
    line = jnp.sum(acc, axis=0, keepdims=True)
    return jnp.broadcast_to(jnp.sum(line, axis=1, keepdims=True), acc.shape)


def swap_masks(peers, flip):
    falling = []
    mask = peers // 2
    while mask > 1:
        falling.append(mask)
        mask //= 2
    if flip:
        return falling[:1] + falling[:0:-1], falling[::-1]
    return falling, falling[-1:] + falling[:-1]


def block_pair(u, holder, peers, flip):
    even, odd = swap_masks(peers, flip)
    parity = holder % 2
    top = jnp.where(parity == 0, even.index(peers // 2), odd.index(peers // 2))
    below = u & ((1 << top) - 1)
    base = ((u >> top) << (top + 1)) | below
    upper = jnp.where(holder >= peers // 2, 1, 0)
    first = base | (upper << top)
    second = base | ((1 - upper) << top)
    home = holder
    for step, (mask_even, mask_odd) in enumerate(zip(even, odd)):
        mask = jnp.where(parity == 0, mask_even, mask_odd)
        home = home ^ (((first >> step) & 1) * mask)
    return first, second, home


def prepare_kernel(kappa_ref, misfit_ref, kappa_out, misfit_out, *, axis, peers):
    at_ = Layout(kappa_ref.shape[1] // 2)
    upper = jnp.where(lax.axis_index(axis) >= peers // 2, 1, 0)
    at_.deal(kappa_ref, kappa_out, upper)
    at_.deal(misfit_ref, misfit_out, upper)


def join_kernel(*refs, masks, axis, peers):
    place = lax.axis_index(axis)
    at_ = Layout(refs[0].shape[1] // 2)
    for at, (even, odd) in enumerate(masks):
        partner = place ^ jnp.where(place % 2 == 0, even, odd)
        refs[4 + at][0] = refs[at][...]
        at_.deal(refs[2 + at], refs[4 + at].at[1], jnp.where(partner >= peers // 2, 1, 0))


def gather_blocks(blocks, states, axis):
    peers = lax.axis_size(axis)
    even = lax.axis_index(axis) % 2 == 0
    swap = [(i, i ^ 1) for i in range(peers)]
    over = [(i, i + 1 if i % 2 else i - 1) for i in range(1, peers - 1)]
    vmem = pl.BlockSpec(memory_space=pltpu.VMEM)
    swaps = [list(zip(*swap_masks(peers, flip))) for flip in (False, True)]
    own = pl.pallas_call(
        functools.partial(prepare_kernel, axis=axis, peers=peers),
        out_shape=[jax.ShapeDtypeStruct(block.shape, jnp.float32) for block in blocks],
        in_specs=[vmem] * 2,
        out_specs=[vmem] * 2,
        compiler_params=pltpu.CompilerParams(vmem_limit_bytes=1024 * 1024),
        name="prepare",
    )(*blocks)
    held = list(blocks)
    for step in range(len(swaps[0])):
        arrived = []
        for at in (0, 1):
            masks = swaps[at][step]
            pairs = [(i, i ^ masks[i % 2]) for i in range(peers)]
            arrived.append(lax.ppermute(held[at], axis, pairs))
        if step:
            held = [jnp.concatenate(pair, axis=0) for pair in zip(held, arrived)]
            continue
        masks = [swaps[at][0] for at in (0, 1)]
        shape = jax.ShapeDtypeStruct((2, *blocks[0].shape), jnp.float32)
        held[:] = pl.pallas_call(
            functools.partial(join_kernel, masks=masks, axis=axis, peers=peers),
            out_shape=[shape] * 2,
            in_specs=[vmem] * 4,
            out_specs=[vmem] * 2,
            compiler_params=pltpu.CompilerParams(vmem_limit_bytes=1024 * 1024),
            name="join",
        )(*own, *arrived)
        held[1], states = lax.optimization_barrier((held[1], states))
        far = lax.ppermute(jnp.where(even, states[:, :1], states[:, -1:]), axis, over)
    other = [lax.ppermute(part, axis, swap) for part in held]

    def fetch_near(after):
        late, states_late, far_late = lax.optimization_barrier((after, states, far))
        given = jnp.concatenate([states_late, far_late], axis=1)
        return late, lax.ppermute(jnp.where(even, given[1], given[0]), axis, swap)

    return held, other, far, fetch_near


CLASSES = [(a, b, c) for a in (0, 1) for b in (0, 1) for c in (0, 1)]
PAIRS = [(p, q) for p in (0, 1) for q in (0, 1)]


def cls(a, b, c):
    return 4 * a + 2 * b + c


def inner_faces(p, q):
    return (
        (2 * p + q, cls(0, p, q), cls(1, p, q)),
        (4 + 2 * p + q, cls(p, 0, q), cls(p, 1, q)),
        (8 + 2 * p + q, cls(p, q, 0), cls(p, q, 1)),
    )


class Layout:
    def __init__(self, rows):
        self.tiles = rows // TILE
        self.lane = lane_index((TILE, 2 * HALF))
        self.row = row_index((TILE, 2 * HALF))
        self.left = self.lane < HALF
        self.zero = jnp.zeros((TILE, 2 * HALF), jnp.float32)

    def tile(self, j):
        return pl.ds(TILE * j, TILE)

    def every(self, b, j):
        return pl.ds(b + 2 * j, TILE, stride=2 * self.tiles)

    def row_before(self, load, j):
        return load(j - 1) if j else roll(load(self.tiles - 1), 1, 0)

    def row_after(self, load, j):
        return load(j + 1) if j + 1 < self.tiles else roll(load(0), -1, 0)

    def seam(self, ref, low, high):
        last = ref.shape[1] - 1
        for j in range(self.tiles):
            for k in low:
                moved = roll(ref[k, last - 1, self.tile(j)], HALF, 1)
                ref[k, 0, self.tile(j)] = jnp.where(self.left, 0.0, moved)
            for k in high:
                moved = roll(ref[k, 1, self.tile(j)], HALF, 1)
                ref[k, last, self.tile(j)] = jnp.where(self.left, moved, 0.0)

    def seam_fine(self, ref):
        count = ref.shape[0]
        self.seam(
            ref,
            [k for k in range(count) if k % 8 >= 4],
            [k for k in range(count) if k % 8 < 4],
        )

    def dealt(self, b, j):
        return pl.ds(TILE * (self.tiles * b + j), TILE)

    def deal(self, block_ref, out_ref, upper):
        odd = jnp.where(self.left, upper, 1 - upper)
        column = 2 * (self.lane % HALF) + odd
        for x in range(block_ref.shape[0]):
            for b in (0, 1):
                for j in range(self.tiles):
                    rows = block_ref[x, self.every(b, j), :]
                    out_ref[x, self.dealt(b, j), :] = jnp.take_along_axis(rows, column, axis=1)

    def arrange(self, mine_ref, theirs_ref, place, flip, store):
        blocks, own = mine_ref.shape[:2]

        def pair(u, carry):
            for ref, holder in ((mine_ref, place), (theirs_ref, place ^ 1)):
                first, second, home = block_pair(u, holder, 2 * blocks, flip)
                for x in range(own):
                    spot = home * (own // 2) + x // 2
                    for b in (0, 1):
                        for j in range(self.tiles):
                            one = ref[first, x, self.dealt(b, j), :]
                            two = ref[second, x, self.dealt(b, j), :]
                            store(cls(x % 2, b, 0), spot, j, jnp.where(self.left, one, two))
                            odd = roll(jnp.where(self.left, two, one), HALF, 1)
                            store(cls(x % 2, b, 1), spot, j, odd)
            return carry

        lax.fori_loop(0, blocks // 2, pair, 0, unroll=True)


def setup_kernel(
    order_ref,
    shifts_ref,
    weights_ref,
    mine_ref,
    theirs_ref,
    inner,
    outer_x,
    outer_y,
    outer_z,
    inner_sum,
    diagonal,
    damped,
    coarse_off,
    coarse_damped,
    chosen,
    half_kappa,
):
    half = inner.shape[1]
    at_ = Layout(inner.shape[2])
    tile, tiles = at_.tile, at_.tiles
    place = lax.axis_index("space")
    pole = jnp.where(place % 2 == 0, order_ref[:, 0:1], order_ref[:, 1:2])
    taken = lane_index(shifts_ref.shape) == pole
    shift = jnp.sum(jnp.where(taken, shifts_ref[...], 0.0), axis=1, keepdims=True)
    weight = jnp.sum(jnp.where(taken, weights_ref[...], 0.0), axis=1, keepdims=True)
    shift = jnp.broadcast_to(shift, at_.zero.shape)
    chosen[...] = jnp.broadcast_to(weight, at_.zero.shape)

    def keep(k, spot, j, value):
        half_kappa[k, spot + 1, tile(j)] = 0.5 * value

    at_.arrange(mine_ref, theirs_ref, place, False, keep)
    at_.seam_fine(half_kappa)

    z_low = jnp.where(at_.lane % HALF > 0, 1.0, 0.0)
    z_high = jnp.where(at_.lane % HALF < HALF - 1, 1.0, 0.0)
    y_low = [jnp.where(at_.row > 0, 1.0, 0.0)] + [None] * (tiles - 1)
    y_high = [None] * (tiles - 1) + [jnp.where(at_.row < TILE - 1, 1.0, 0.0)]

    def masked(mask, value):
        return value if mask is None else mask * value

    def plane(i, carry):
        for j in range(tiles):
            kap = [half_kappa[k, i + 1, tile(j)] for k in range(8)]
            inside = [[] for _ in range(8)]
            outside = [[] for _ in range(8)]
            off = [[] for _ in range(5)]
            for p, q in PAIRS:
                for face_at, low, high in inner_faces(p, q):
                    face = kap[low] + kap[high]
                    inner[face_at, i, tile(j)] = face
                    inside[low].append(face)
                    inside[high].append(face)
                at = 2 * p + q

                low, high = cls(0, p, q), cls(1, p, q)
                minus = kap[low] + half_kappa[high, i, tile(j)]
                plus = kap[high] + half_kappa[low, i + 2, tile(j)]
                outside[low].append(minus)
                outside[high].append(plus)
                outer_x[at, i, tile(j)] = minus
                off[0].append(minus)

                low, high = cls(p, 0, q), cls(p, 1, q)
                side = at_.row_before(lambda r: half_kappa[high, i + 1, tile(r)], j)
                minus = kap[low] + masked(y_low[j], side)
                side = at_.row_after(lambda r: half_kappa[low, i + 1, tile(r)], j)
                plus = kap[high] + masked(y_high[j], side)
                outside[low].append(minus)
                outside[high].append(plus)
                minus, plus = masked(y_low[j], minus), masked(y_high[j], plus)
                outer_y[at, i, tile(j)] = minus
                off[1].append(minus)
                off[2].append(plus)

                low, high = cls(p, q, 0), cls(p, q, 1)
                minus = kap[low] + z_low * roll(kap[high], 1, 1)
                plus = kap[high] + z_high * roll(kap[low], -1, 1)
                outside[low].append(minus)
                outside[high].append(plus)
                minus, plus = z_low * minus, z_high * plus
                outer_z[at, i, tile(j)] = minus
                outer_z[4 + at, i, tile(j)] = plus
                off[3].append(minus)
                off[4].append(plus)
            coarse_total = []
            for k in range(8):
                within, without = tree_sum(inside[k]), tree_sum(outside[k])
                base = within + without + shift
                inner_sum[k, i, tile(j)] = within + ((1.0 - DAMPING) / DAMPING) * base
                diagonal[k, i, tile(j)] = base
                coarse_total.append(without)
                damped[k, i, tile(j)] = (DAMPING / KEPT) * inverse(base)
            for at, part in enumerate(off):
                coarse_off[at, i, tile(j)] = tree_sum(part)
            coarse_damped[i, tile(j)] = DAMPING * inverse(tree_sum(coarse_total) + 8.0 * shift)
        return carry

    lax.fori_loop(0, half, plane, 0, unroll=UNROLL)
    for j in range(tiles):
        part = []
        for p, q in PAIRS:
            face = half_kappa[cls(0, p, q), half + 1, tile(j)]
            face = face + half_kappa[cls(1, p, q), half, tile(j)]
            outer_x[2 * p + q, half, tile(j)] = face
            part.append(face)
        coarse_off[0, half, tile(j)] = tree_sum(part)


def solve_kernel(
    mine_ref,
    theirs_ref,
    inner,
    outer_x,
    outer_y,
    outer_z,
    inner_sum,
    diagonal,
    damped,
    coarse_off,
    coarse_damped,
    chosen,
    planes,
    residual,
    scaled,
    partial,
    first_dir,
    second_dir,
    image,
    coarse_one,
    coarse_two,
    *,
    own,
):
    half, rows = inner.shape[1:3]
    at_ = Layout(rows)
    tile, tiles, zero = at_.tile, at_.tiles, at_.zero
    place = lax.axis_index("space")
    core = place % 2

    def begin(k, spot, j, value):
        residual[k, spot, tile(j)] = value
        scaled[k, spot + 1, tile(j)] = damped[k, spot, tile(j)] * value

    at_.arrange(mine_ref, theirs_ref, place, True, begin)
    at_.seam_fine(scaled)

    def rows_of(ref, i):
        cache = {}

        def load(k, j, step):
            if abs(j - step) > 1:
                return ref[k, i, tile(j)]
            if (k, j) not in cache:
                cache[k, j] = ref[k, i, tile(j)]
            return cache[k, j]

        def get(k, j):
            return load(k, j, j)

        def before(k, j):
            return at_.row_before(lambda r: load(k, r, j), j)

        def after(k, j):
            return at_.row_after(lambda r: load(k, r, j), j)

        return get, before, after

    def stencil(field, i, both):
        get, before, after = rows_of(field, i + 1)
        face_get, _, face_after = rows_of(outer_y, i)
        for j in range(tiles):
            here = [get(k, j) for k in range(8)]
            terms = [[] for _ in range(8)]
            for p, q in PAIRS:
                at = 2 * p + q
                for face_at, low, high in inner_faces(p, q):
                    face = inner[face_at, i, tile(j)]
                    terms[low].append(face * here[high])
                    if both:
                        terms[high].append(face * here[low])
                low, high = cls(0, p, q), cls(1, p, q)
                terms[low].append(outer_x[at, i, tile(j)] * field[high, i, tile(j)])
                if both:
                    side = field[low, i + 2, tile(j)]
                    terms[high].append(outer_x[at, i + 1, tile(j)] * side)
                low, high = cls(p, 0, q), cls(p, 1, q)
                terms[low].append(face_get(at, j) * before(high, j))
                if both:
                    terms[high].append(face_after(at, j) * after(low, j))
                low, high = cls(p, q, 0), cls(p, q, 1)
                terms[low].append(outer_z[at, i, tile(j)] * roll(here[high], 1, 1))
                if both:
                    terms[high].append(outer_z[4 + at, i, tile(j)] * roll(here[low], -1, 1))
            yield j, here, [tree_sum(part) if part else None for part in terms]

    def coarse_sides(field, i, j):
        here = field[0, i + 1, tile(j)]
        return here, (
            (field[0, i, tile(j)], field[0, i + 2, tile(j)]),
            (
                at_.row_before(lambda r: field[0, i + 1, tile(r)], j),
                at_.row_after(lambda r: field[0, i + 1, tile(r)], j),
            ),
            (roll(here, 1, 1), roll(here, -1, 1)),
        )

    def precondition(result):
        def down(i, carry):
            for j, _, sums in stencil(scaled, i, True):
                res = [residual[k, i, tile(j)] for k in range(8)]
                parts = [res[k] + sums[k] for k in range(8)]
                for k in range(8):
                    partial[k, i, tile(j)] = parts[k]
                rhs = tree_sum(parts) - (1.0 / KEPT) * tree_sum(res)
                coarse_one[0, i + 1, tile(j)] = coarse_damped[i, tile(j)] * rhs
            return carry

        lax.fori_loop(0, half, down, 0, unroll=UNROLL)
        at_.seam(coarse_one, [0], [0])

        def smooth(i, carry):
            for j in range(tiles):
                here, sides = coarse_sides(coarse_one, i, j)
                total = coarse_off[0, i, tile(j)] * sides[0][0]
                total = total + coarse_off[0, i + 1, tile(j)] * sides[0][1]
                more = coarse_off[1, i, tile(j)] * sides[1][0]
                more = more + coarse_off[2, i, tile(j)] * sides[1][1]
                most = coarse_off[3, i, tile(j)] * sides[2][0]
                most = most + coarse_off[4, i, tile(j)] * sides[2][1]
                coarse_two[0, i + 1, tile(j)] = KEPT * here + coarse_damped[
                    i, tile(j)
                ] * (total + more + most)
            return carry

        lax.fori_loop(0, half, smooth, 0, unroll=UNROLL)
        at_.seam(coarse_two, [0], [0])

        def up(i, gamma):
            face_get, _, face_after = rows_of(outer_y, i)
            for j in range(tiles):
                here, sides = coarse_sides(coarse_two, i, j)
                dots = []
                for a, b, c in CLASSES:
                    k = cls(a, b, c)
                    value = tree_sum(
                        [
                            partial[k, i, tile(j)],
                            inner_sum[k, i, tile(j)] * here,
                            outer_x[2 * b + c, i + a, tile(j)] * sides[0][a],
                            (face_after if b else face_get)(2 * a + c, j) * sides[1][b],
                            outer_z[4 * c + 2 * a + b, i, tile(j)] * sides[2][c],
                        ]
                    )
                    new = damped[k, i, tile(j)] * value
                    result[k, i + 1, tile(j)] = new
                    dots.append(residual[k, i, tile(j)] * new)
                gamma = gamma + tree_sum(dots)
            return gamma

        gamma = lax.fori_loop(0, half, up, zero, unroll=UNROLL)
        at_.seam_fine(result)
        return grand_total(gamma)

    gamma = precondition(first_dir)

    def apply(i, acc):
        for j, here, sums in stencil(first_dir, i, True):
            dots = []
            for k in range(8):
                value = diagonal[k, i, tile(j)] * here[k] - sums[k]
                image[k, i, tile(j)] = value
                dots.append(here[k] * value)
            acc = acc + tree_sum(dots)
        return acc

    curve = grand_total(lax.fori_loop(0, half, apply, zero, unroll=UNROLL))
    step_one = gamma / curve

    def update(i, carry):
        for j in range(tiles):
            for k in range(8):
                new = residual[k, i, tile(j)] - step_one * image[k, i, tile(j)]
                residual[k, i, tile(j)] = new
                scaled[k, i + 1, tile(j)] = damped[k, i, tile(j)] * new
        return carry

    lax.fori_loop(0, half, update, 0, unroll=UNROLL)
    at_.seam_fine(scaled)

    gamma_next = precondition(second_dir)

    def bend(i, carry):
        own_part, face_part = carry
        for j, here, sums in stencil(second_dir, i, False):
            own_part = own_part + tree_sum(
                [here[k] * (diagonal[k, i, tile(j)] * here[k]) for k in range(8)]
            )
            face_part = face_part + tree_sum([here[k] * sums[k] for k in range(7)])
        return own_part, face_part

    own_part, face_part = lax.fori_loop(0, half, bend, (zero, zero), unroll=UNROLL)
    ratio = gamma_next / gamma
    curve_next = grand_total(own_part - 2.0 * face_part)
    step_two = gamma_next / (curve_next - ratio * ratio * curve)
    weight = chosen[...]
    step_first = (step_one + step_two * ratio) * weight
    step_two = step_two * weight

    start = (place - core) * (own // 2)
    upper = jnp.where(start >= half, 1, 0)
    start = start - half * upper
    even = at_.lane % 2 == 0
    source = at_.lane // 2 + HALF * upper
    for at in range(2 * own + 2):
        a = (at + 1) % 2
        spot = start + (at + 1) // 2
        for b in (0, 1):
            for j in range(tiles):
                both = [
                    step_first * first_dir[cls(a, b, c), spot, tile(j)]
                    + step_two * second_dir[cls(a, b, c), spot, tile(j)]
                    for c in (0, 1)
                ]
                planes[at, at_.every(b, j), :] = jnp.where(
                    even,
                    jnp.take_along_axis(both[0], source, axis=1),
                    jnp.take_along_axis(both[1], source, axis=1),
                )


def finish_kernel(planes_ref, state_ref, far_ref, near_ref, adjoint_ref, keep_ref, partner_ref, send_ref, terms):
    own, ny, nz = adjoint_ref.shape
    core = lax.axis_index("space") % 2
    full = (ny, nz)
    y_at = row_index(full)
    z_at = lane_index(full)

    def drop(value, axis, up):
        moved = roll(value, -1 if up else 1, axis)
        at = (y_at, z_at)[axis]
        edge = full[axis] - 1 if up else 0
        return value - jnp.where(at == edge, 0.0, moved)

    is_even = core == 0
    state = [jnp.where(is_even, far_ref[core, 0], near_ref[own])]
    state += [jnp.where(is_even, state_ref[core, x], near_ref[x]) for x in range(own)]
    state += [jnp.where(is_even, near_ref[x], state_ref[core, x]) for x in range(own)]
    state += [jnp.where(is_even, near_ref[own], far_ref[core, 0])]
    for x in range(2 * own):
        here, f = planes_ref[x + 1], state[x + 1]
        term = (here - planes_ref[x + 2]) * (f - state[x + 2])
        term = term + (here - planes_ref[x]) * (f - state[x])
        for axis in (0, 1):
            for up in (True, False):
                term = term + drop(here, axis, up) * drop(f, axis, up)
        terms[x] = -0.5 * term

    groups = send_ref.shape[0] + 1
    chunk = keep_ref.shape[1]
    for x in range(own):
        mine, other = core * own + x, (1 - core) * own + x
        adjoint_ref[x] = planes_ref[1 + mine]
        partner_ref[x, :ny] = planes_ref[1 + other]
        for k in range(groups):
            at = lax.rem(lax.axis_index("pole") + k, groups) * chunk
            at = pl.multiple_of(at, chunk)
            for side, plane in enumerate((mine, other)):
                share = terms[plane, pl.ds(at, chunk), :]
                if k:
                    send_ref[k - 1, side, x] = share
                elif side:
                    partner_ref[x, ny:] = share
                else:
                    keep_ref[x] = share


def whole_grid(conductivity, misfit, forward_states, pole_shifts, pole_weights, pole_order):
    members, own, ny, nz = forward_states.shape
    groups = lax.axis_size("pole")
    peers = lax.axis_size("space")
    even = lax.axis_index("space") % 2 == 0
    mine, theirs, far, fetch_near = gather_blocks([conductivity, misfit], forward_states, "space")
    half, rows = peers * own // 4, ny // 2

    def field(count, extent):
        return (count, extent, rows, 2 * HALF)

    def held(*shape):
        return pltpu.VMEM(shape, jnp.float32)

    vmem = pl.BlockSpec(memory_space=pltpu.VMEM)
    shapes = [
        field(12, half),
        field(4, half + 1),
        field(4, half),
        field(8, half),
        field(8, half),
        field(8, half),
        field(8, half),
        field(5, half + 1),
        (half, rows, 2 * HALF),
        (TILE, 2 * HALF),
    ]
    coefficients = pl.pallas_call(
        setup_kernel,
        out_shape=[jax.ShapeDtypeStruct(shape, jnp.float32) for shape in shapes],
        in_specs=[vmem] * 5,
        out_specs=[vmem] * len(shapes),
        scratch_shapes=[held(*field(8, half + 2))],
        compiler_params=pltpu.CompilerParams(vmem_limit_bytes=6 * 1024 * 1024),
        name="setup",
    )(pole_order[None], pole_shifts[None], pole_weights[None], mine[0], theirs[0])
    coefficients, near = fetch_near(coefficients)
    planes = pl.pallas_call(
        functools.partial(solve_kernel, own=own),
        out_shape=jax.ShapeDtypeStruct((2 * own + 2, ny, nz), jnp.float32),
        in_specs=[vmem] * (2 + len(shapes)),
        out_specs=vmem,
        scratch_shapes=[
            held(*field(8, half)),
            held(*field(8, half + 2)),
            held(*field(8, half)),
            held(*field(8, half + 2)),
            held(*field(8, half + 2)),
            held(*field(8, half)),
            held(*field(1, half + 2)),
            held(*field(1, half + 2)),
        ],
        compiler_params=pltpu.CompilerParams(vmem_limit_bytes=12 * 1024 * 1024),
        name="solve",
    )(mine[1], theirs[1], *coefficients)
    chunk = ny // groups
    adjoint, gradient, partner, send = pl.pallas_call(
        finish_kernel,
        out_shape=[
            jax.ShapeDtypeStruct((own, ny, nz), jnp.float32),
            jax.ShapeDtypeStruct((own, chunk, nz), jnp.float32),
            jax.ShapeDtypeStruct((own, ny + chunk, nz), jnp.float32),
            jax.ShapeDtypeStruct((groups - 1, 2, own, chunk, nz), jnp.float32),
        ],
        in_specs=[vmem] * 4,
        out_specs=[vmem] * 4,
        scratch_shapes=[held(2 * own, ny, nz)],
        compiler_params=pltpu.CompilerParams(vmem_limit_bytes=4 * 1024 * 1024),
        name="finish",
    )(planes, forward_states, far, near)

    arrived = lax.ppermute(partner, "space", [(i, i ^ 1) for i in range(peers)])
    shares = []
    for k in range(1, groups):
        for side in (0, 1):
            pairs = [
                (i * peers + j, (i + k) % groups * peers + (j ^ side))
                for i in range(groups)
                for j in range(peers)
            ]
            shares.append(lax.ppermute(send[k - 1, side], ("pole", "space"), pairs))
    theirs = arrived[:, :ny]
    adjoint_states = jnp.stack(
        [jnp.where(even, adjoint, theirs), jnp.where(even, theirs, adjoint)]
    )
    adjoint_states, arrived = lax.optimization_barrier((adjoint_states, arrived))
    return adjoint_states, gradient + arrived[:, ny:] + sum(shares)


def plus_side(field, which_dim):
    extent = field.shape[which_dim]
    inner_part = lax.slice_in_dim(field, 1, extent, axis=which_dim)
    zero_plane = jnp.zeros_like(lax.slice_in_dim(field, 0, 1, axis=which_dim))
    return jnp.concatenate([inner_part, zero_plane], axis=which_dim)


def minus_side(field, which_dim):
    extent = field.shape[which_dim]
    inner_part = lax.slice_in_dim(field, 0, extent - 1, axis=which_dim)
    zero_plane = jnp.zeros_like(lax.slice_in_dim(field, 0, 1, axis=which_dim))
    return jnp.concatenate([zero_plane, inner_part], axis=which_dim)


def coarse_pick(faces, which_dim, offset):
    extent_x, extent_y, extent_z = faces.shape
    blocks = faces.reshape(extent_x // 2, 2, extent_y // 2, 2, extent_z // 2, 2)
    chosen = lax.index_in_dim(blocks, offset, axis=2 * which_dim + 1, keepdims=True)
    return jnp.sum(chosen, axis=(1, 3, 5))


def side_terms(field, plus_faces, minus_faces, widened):
    result = plus_faces[0] * (field - widened[:, 2:]) + minus_faces[0] * (field - widened[:, :-2])
    for which_dim in (1, 2):
        result = result + plus_faces[which_dim] * (field - plus_side(field, which_dim + 1))
        result = result + minus_faces[which_dim] * (field - minus_side(field, which_dim + 1))
    return result


def fine_image(field, plus_faces, minus_faces, shift_value):
    widened = extended(field, (("space", 1),), 1)
    return shift_value * field + side_terms(field, plus_faces, minus_faces, widened)


def coarse_image(field, plus_faces, minus_faces, shift_value):
    widened = extended(field, (("space", 1),), 1)
    return shift_value * field + side_terms(field, plus_faces, minus_faces, widened)


def restrict(field):
    members, extent_x, extent_y, extent_z = field.shape
    shaped = field.reshape(members, extent_x // 2, 2, extent_y // 2, 2, extent_z // 2, 2)
    return jnp.sum(shaped, axis=(2, 4, 6))


def prolong(field):
    return jnp.repeat(jnp.repeat(jnp.repeat(field, 2, axis=1), 2, axis=2), 2, axis=3)


def precondition(residual, fine, coarse):
    plus_faces, minus_faces, shift_value, diagonal = fine
    coarse_plus, coarse_minus, coarse_shift, coarse_diagonal = coarse
    smooth_one = DAMPING * residual / diagonal
    coarse_rhs = restrict(residual - fine_image(smooth_one, plus_faces, minus_faces, shift_value))
    coarse_one = DAMPING * coarse_rhs / coarse_diagonal
    coarse_two = (
        coarse_one
        + DAMPING
        * (coarse_rhs - coarse_image(coarse_one, coarse_plus, coarse_minus, coarse_shift))
        / coarse_diagonal
    )
    corrected = smooth_one + prolong(coarse_two)
    return (
        corrected
        + DAMPING
        * (residual - fine_image(corrected, plus_faces, minus_faces, shift_value))
        / diagonal
    )


def expand(values):
    return values.reshape(-1, 1, 1, 1)


def cell_sums(values):
    return jnp.sum(values, axis=(1, 2, 3))


def norm_sum(residual, precond):
    return lax.psum(cell_sums(residual * precond), "space")


def solve(rhs, fine, coarse):
    plus_faces, minus_faces, shift_value, diagonal = fine
    iterate = jnp.zeros_like(rhs)
    residual = rhs
    precond = precondition(residual, fine, coarse)
    gamma_now = norm_sum(residual, precond)
    search = precond
    for turn_index in range(ITERS):
        image_field = fine_image(search, plus_faces, minus_faces, shift_value)
        curve = lax.psum(cell_sums(search * image_field), "space")
        step_length = gamma_now / curve
        iterate = iterate + expand(step_length) * search
        if turn_index + 1 < ITERS:
            residual = residual - expand(step_length) * image_field
            precond = precondition(residual, fine, coarse)
            gamma_next = norm_sum(residual, precond)
            search = precond + expand(gamma_next / gamma_now) * search
            gamma_now = gamma_next
    return iterate


def divided(conductivity, misfit, forward_states, pole_shifts, pole_weights, pole_order):
    widened_kappa = extended(conductivity, (("space", 0),), 1)
    plus_faces = [
        0.5 * (conductivity + widened_kappa[2:]),
        0.5 * (conductivity + plus_side(conductivity, 1)),
        0.5 * (conductivity + plus_side(conductivity, 2)),
    ]
    minus_faces = [
        0.5 * (conductivity + widened_kappa[:-2]),
        0.5 * (conductivity + minus_side(conductivity, 1)),
        0.5 * (conductivity + minus_side(conductivity, 2)),
    ]
    base_diagonal = (
        plus_faces[0]
        + plus_faces[1]
        + plus_faces[2]
        + minus_faces[0]
        + minus_faces[1]
        + minus_faces[2]
    )
    coarse_plus = [coarse_pick(plus_faces[which_dim], which_dim, 1) for which_dim in range(3)]
    coarse_minus = [coarse_pick(minus_faces[which_dim], which_dim, 0) for which_dim in range(3)]
    coarse_base = (
        coarse_plus[0]
        + coarse_plus[1]
        + coarse_plus[2]
        + coarse_minus[0]
        + coarse_minus[1]
        + coarse_minus[2]
    )
    pole_index = jnp.arange(pole_shifts.shape[0], dtype=jnp.int32)
    matches = pole_order[:, None] == pole_index[None, :]
    shift_local = jnp.sum(jnp.where(matches, pole_shifts[None, :], 0.0), axis=1)
    weight_local = jnp.sum(jnp.where(matches, pole_weights[None, :], 0.0), axis=1)
    members = forward_states.shape[0]

    def solve_group(shift_part, weight_part):
        shift_value = expand(shift_part)
        fine = (plus_faces, minus_faces, shift_value, base_diagonal[None] + shift_value)
        coarse = (
            coarse_plus,
            coarse_minus,
            8.0 * shift_value,
            coarse_base[None] + 8.0 * shift_value,
        )
        return solve(expand(weight_part) * misfit[None], fine, coarse)

    adjoint_states = jnp.concatenate(
        [
            solve_group(shift_local[member : member + 1], weight_local[member : member + 1])
            for member in range(members)
        ],
        axis=0,
    )
    widened = extended(jnp.stack([adjoint_states, forward_states]), (("space", 2),), 1)
    term = (adjoint_states - widened[0, :, 2:]) * (forward_states - widened[1, :, 2:])
    term = term + (adjoint_states - widened[0, :, :-2]) * (forward_states - widened[1, :, :-2])
    for which_dim in (2, 3):
        term = term + (adjoint_states - plus_side(adjoint_states, which_dim)) * (
            forward_states - plus_side(forward_states, which_dim)
        )
        term = term + (adjoint_states - minus_side(adjoint_states, which_dim)) * (
            forward_states - minus_side(forward_states, which_dim)
        )
    local_term = -0.5 * jnp.sum(term, axis=0)
    gradient = lax.psum_scatter(local_term, "pole", scatter_dimension=1, tiled=True)
    return (adjoint_states, gradient)


def solution(mesh):
    in_specs = (
        P("space", None, None),
        P("space", None, None),
        P("pole", "space", None, None),
        P(),
        P(),
        P("pole"),
    )
    out_specs = (P("pole", "space", None, None), P("space", "pole", None))

    def body(conductivity, misfit, forward_states, *poles):
        nx = conductivity.shape[0] * lax.axis_size("space")
        _, ny, nz = conductivity.shape
        peers = lax.axis_size("space")
        small = nx * ny * nz <= REPLICATED_CELLS and forward_states.shape[:2] == (2, 2)
        if small and nz == 2 * HALF and peers > 2 and peers & (peers - 1) == 0:
            return whole_grid(conductivity, misfit, forward_states, *poles)
        return divided(conductivity, misfit, forward_states, *poles)

    return jax.shard_map(
        body, mesh=mesh, in_specs=in_specs, out_specs=out_specs, check_vma=False
    )
```

```python
import functools

import jax
import jax.numpy as jnp
from jax import lax
from jax.experimental import pallas as pl
from jax.experimental.pallas import tpu as pltpu
from jax.sharding import PartitionSpec as P

ITERS = 2
DAMPING = 0.8
KEPT = 2.0 - DAMPING
REPLICATED_CELLS = 32 * 64 * 128
HALF = 64
TILE = 8
UNROLL = 8


def extended(array, sides, width):
    for axis, dim in sides:
        peers, length = (lax.axis_size(axis), array.shape[dim])
        up = [(i, (i + 1) % peers) for i in range(peers - 1)]
        down = [(j, i) for i, j in up]
        last = lax.slice_in_dim(array, length - width, length, axis=dim)
        leading = lax.slice_in_dim(array, 0, width, axis=dim)
        before = lax.ppermute(last, axis, up)
        after = lax.ppermute(leading, axis, down)
        array = jnp.concatenate([before, array, after], axis=dim)
    return array


def lane_index(shape):
    return lax.broadcasted_iota(jnp.int32, shape, len(shape) - 1)


def row_index(shape):
    return lax.broadcasted_iota(jnp.int32, shape, len(shape) - 2)


def roll(block, shift, axis):
    return pltpu.roll(block, shift % block.shape[axis], axis)


def inverse(value):
    guess = pl.reciprocal(value, approx=True)
    return guess * (2.0 - value * guess)


def tree_sum(values):
    while len(values) > 1:
        values = [sum(values[at : at + 2]) for at in range(0, len(values), 2)]
    return values[0]


def grand_total(acc):
    line = jnp.sum(acc, axis=0, keepdims=True)
    return jnp.broadcast_to(jnp.sum(line, axis=1, keepdims=True), acc.shape)


def swap_masks(peers, flip):
    falling = []
    mask = peers // 2
    while mask > 1:
        falling.append(mask)
        mask //= 2
    if flip:
        return falling[::-1], falling[:1] + falling[:0:-1]
    return falling, falling[-1:] + falling[:-1]


def block_pair(u, holder, peers, flip):
    even, odd = swap_masks(peers, flip)
    parity = holder % 2
    top = jnp.where(parity == 0, even.index(peers // 2), odd.index(peers // 2))
    below = u & ((1 << top) - 1)
    base = ((u >> top) << (top + 1)) | below
    upper = jnp.where(holder >= peers // 2, 1, 0)
    first = base | (upper << top)
    second = base | ((1 - upper) << top)
    home = holder
    for step, (mask_even, mask_odd) in enumerate(zip(even, odd)):
        mask = jnp.where(parity == 0, mask_even, mask_odd)
        home = home ^ (((first >> step) & 1) * mask)
    return first, second, home


def prepare_kernel(kappa_ref, misfit_ref, kappa_out, misfit_out, *, axis, peers):
    at_ = Layout(kappa_ref.shape[1] // 2)
    upper = jnp.where(lax.axis_index(axis) >= peers // 2, 1, 0)
    at_.deal(kappa_ref, kappa_out, upper)
    at_.deal(misfit_ref, misfit_out, upper)


def join_kernel(*refs, masks, axis, peers):
    place = lax.axis_index(axis)
    at_ = Layout(refs[0].shape[1] // 2)
    for at, (even, odd) in enumerate(masks):
        partner = place ^ jnp.where(place % 2 == 0, even, odd)
        refs[4 + at][0] = refs[at][...]
        at_.deal(refs[2 + at], refs[4 + at].at[1], jnp.where(partner >= peers // 2, 1, 0))


def gather_blocks(blocks, states, axis):
    peers = lax.axis_size(axis)
    even = lax.axis_index(axis) % 2 == 0
    swap = [(i, i ^ 1) for i in range(peers)]
    over = [(i, i + 1 if i % 2 else i - 1) for i in range(1, peers - 1)]
    vmem = pl.BlockSpec(memory_space=pltpu.VMEM)
    swaps = [list(zip(*swap_masks(peers, flip))) for flip in (False, True)]
    own = pl.pallas_call(
        functools.partial(prepare_kernel, axis=axis, peers=peers),
        out_shape=[jax.ShapeDtypeStruct(block.shape, jnp.float32) for block in blocks],
        in_specs=[vmem] * 2,
        out_specs=[vmem] * 2,
        compiler_params=pltpu.CompilerParams(vmem_limit_bytes=1024 * 1024),
        name="prepare",
    )(*blocks)
    held = list(blocks)
    for step in range(len(swaps[0])):
        arrived = []
        for at in (0, 1):
            masks = swaps[at][step]
            pairs = [(i, i ^ masks[i % 2]) for i in range(peers)]
            arrived.append(lax.ppermute(held[at], axis, pairs))
        if step:
            held = [jnp.concatenate(pair, axis=0) for pair in zip(held, arrived)]
            continue
        masks = [swaps[at][0] for at in (0, 1)]
        shape = jax.ShapeDtypeStruct((2, *blocks[0].shape), jnp.float32)
        held[:] = pl.pallas_call(
            functools.partial(join_kernel, masks=masks, axis=axis, peers=peers),
            out_shape=[shape] * 2,
            in_specs=[vmem] * 4,
            out_specs=[vmem] * 2,
            compiler_params=pltpu.CompilerParams(vmem_limit_bytes=1024 * 1024),
            name="join",
        )(*own, *arrived)
        held[1], states = lax.optimization_barrier((held[1], states))
        far = lax.ppermute(jnp.where(even, states[:, :1], states[:, -1:]), axis, over)
    other = [lax.ppermute(part, axis, swap) for part in held]

    def fetch_near(after):
        late, states_late, far_late = lax.optimization_barrier((after, states, far))
        given = jnp.concatenate([states_late, far_late], axis=1)
        return late, lax.ppermute(jnp.where(even, given[1], given[0]), axis, swap)

    return held, other, far, fetch_near


CLASSES = [(a, b, c) for a in (0, 1) for b in (0, 1) for c in (0, 1)]
PAIRS = [(p, q) for p in (0, 1) for q in (0, 1)]


def cls(a, b, c):
    return 4 * a + 2 * b + c


def inner_faces(p, q):
    return (
        (2 * p + q, cls(0, p, q), cls(1, p, q)),
        (4 + 2 * p + q, cls(p, 0, q), cls(p, 1, q)),
        (8 + 2 * p + q, cls(p, q, 0), cls(p, q, 1)),
    )


class Layout:
    def __init__(self, rows):
        self.tiles = rows // TILE
        self.lane = lane_index((TILE, 2 * HALF))
        self.row = row_index((TILE, 2 * HALF))
        self.left = self.lane < HALF
        self.zero = jnp.zeros((TILE, 2 * HALF), jnp.float32)

    def tile(self, j):
        return pl.ds(TILE * j, TILE)

    def every(self, b, j):
        return pl.ds(b + 2 * j, TILE, stride=2 * self.tiles)

    def row_before(self, load, j):
        return load(j - 1) if j else roll(load(self.tiles - 1), 1, 0)

    def row_after(self, load, j):
        return load(j + 1) if j + 1 < self.tiles else roll(load(0), -1, 0)

    def seam(self, ref, low, high):
        last = ref.shape[1] - 1
        for j in range(self.tiles):
            for k in low:
                moved = roll(ref[k, last - 1, self.tile(j)], HALF, 1)
                ref[k, 0, self.tile(j)] = jnp.where(self.left, 0.0, moved)
            for k in high:
                moved = roll(ref[k, 1, self.tile(j)], HALF, 1)
                ref[k, last, self.tile(j)] = jnp.where(self.left, moved, 0.0)

    def seam_fine(self, ref):
        count = ref.shape[0]
        self.seam(
            ref,
            [k for k in range(count) if k % 8 >= 4],
            [k for k in range(count) if k % 8 < 4],
        )

    def dealt(self, b, j):
        return pl.ds(TILE * (self.tiles * b + j), TILE)

    def deal(self, block_ref, out_ref, upper):
        odd = jnp.where(self.left, upper, 1 - upper)
        column = 2 * (self.lane % HALF) + odd
        for x in range(block_ref.shape[0]):
            for b in (0, 1):
                for j in range(self.tiles):
                    rows = block_ref[x, self.every(b, j), :]
                    out_ref[x, self.dealt(b, j), :] = jnp.take_along_axis(rows, column, axis=1)

    def arrange(self, mine_ref, theirs_ref, place, flip, store):
        blocks, own = mine_ref.shape[:2]

        def pair(u, carry):
            for ref, holder in ((mine_ref, place), (theirs_ref, place ^ 1)):
                first, second, home = block_pair(u, holder, 2 * blocks, flip)
                for x in range(own):
                    spot = home * (own // 2) + x // 2
                    for b in (0, 1):
                        for j in range(self.tiles):
                            one = ref[first, x, self.dealt(b, j), :]
                            two = ref[second, x, self.dealt(b, j), :]
                            store(cls(x % 2, b, 0), spot, j, jnp.where(self.left, one, two))
                            odd = roll(jnp.where(self.left, two, one), HALF, 1)
                            store(cls(x % 2, b, 1), spot, j, odd)
            return carry

        lax.fori_loop(0, blocks // 2, pair, 0, unroll=True)


def setup_kernel(
    order_ref,
    shifts_ref,
    weights_ref,
    mine_ref,
    theirs_ref,
    inner,
    outer_x,
    outer_y,
    outer_z,
    inner_sum,
    diagonal,
    damped,
    coarse_off,
    coarse_damped,
    chosen,
    half_kappa,
):
    half = inner.shape[1]
    at_ = Layout(inner.shape[2])
    tile, tiles = at_.tile, at_.tiles
    place = lax.axis_index("space")
    pole = jnp.where(place % 2 == 0, order_ref[:, 0:1], order_ref[:, 1:2])
    taken = lane_index(shifts_ref.shape) == pole
    shift = jnp.sum(jnp.where(taken, shifts_ref[...], 0.0), axis=1, keepdims=True)
    weight = jnp.sum(jnp.where(taken, weights_ref[...], 0.0), axis=1, keepdims=True)
    shift = jnp.broadcast_to(shift, at_.zero.shape)
    chosen[...] = jnp.broadcast_to(weight, at_.zero.shape)

    def keep(k, spot, j, value):
        half_kappa[k, spot + 1, tile(j)] = 0.5 * value

    at_.arrange(mine_ref, theirs_ref, place, False, keep)
    at_.seam_fine(half_kappa)

    z_low = jnp.where(at_.lane % HALF > 0, 1.0, 0.0)
    z_high = jnp.where(at_.lane % HALF < HALF - 1, 1.0, 0.0)
    y_low = [jnp.where(at_.row > 0, 1.0, 0.0)] + [None] * (tiles - 1)
    y_high = [None] * (tiles - 1) + [jnp.where(at_.row < TILE - 1, 1.0, 0.0)]

    def masked(mask, value):
        return value if mask is None else mask * value

    def plane(i, carry):
        for j in range(tiles):
            kap = [half_kappa[k, i + 1, tile(j)] for k in range(8)]
            inside = [[] for _ in range(8)]
            outside = [[] for _ in range(8)]
            off = [[] for _ in range(5)]
            for p, q in PAIRS:
                for face_at, low, high in inner_faces(p, q):
                    face = kap[low] + kap[high]
                    inner[face_at, i, tile(j)] = face
                    inside[low].append(face)
                    inside[high].append(face)
                at = 2 * p + q

                low, high = cls(0, p, q), cls(1, p, q)
                minus = kap[low] + half_kappa[high, i, tile(j)]
                plus = kap[high] + half_kappa[low, i + 2, tile(j)]
                outside[low].append(minus)
                outside[high].append(plus)
                outer_x[at, i, tile(j)] = minus
                off[0].append(minus)

                low, high = cls(p, 0, q), cls(p, 1, q)
                side = at_.row_before(lambda r: half_kappa[high, i + 1, tile(r)], j)
                minus = kap[low] + masked(y_low[j], side)
                side = at_.row_after(lambda r: half_kappa[low, i + 1, tile(r)], j)
                plus = kap[high] + masked(y_high[j], side)
                outside[low].append(minus)
                outside[high].append(plus)
                minus, plus = masked(y_low[j], minus), masked(y_high[j], plus)
                outer_y[at, i, tile(j)] = minus
                off[1].append(minus)
                off[2].append(plus)

                low, high = cls(p, q, 0), cls(p, q, 1)
                minus = kap[low] + z_low * roll(kap[high], 1, 1)
                plus = kap[high] + z_high * roll(kap[low], -1, 1)
                outside[low].append(minus)
                outside[high].append(plus)
                minus, plus = z_low * minus, z_high * plus
                outer_z[at, i, tile(j)] = minus
                outer_z[4 + at, i, tile(j)] = plus
                off[3].append(minus)
                off[4].append(plus)
            coarse_total = []
            for k in range(8):
                within, without = tree_sum(inside[k]), tree_sum(outside[k])
                base = within + without + shift
                inner_sum[k, i, tile(j)] = within + ((1.0 - DAMPING) / DAMPING) * base
                diagonal[k, i, tile(j)] = base
                coarse_total.append(without)
                damped[k, i, tile(j)] = (DAMPING / KEPT) * inverse(base)
            for at, part in enumerate(off):
                coarse_off[at, i, tile(j)] = tree_sum(part)
            coarse_damped[i, tile(j)] = DAMPING * inverse(tree_sum(coarse_total) + 8.0 * shift)
        return carry

    lax.fori_loop(0, half, plane, 0, unroll=UNROLL)
    for j in range(tiles):
        part = []
        for p, q in PAIRS:
            face = half_kappa[cls(0, p, q), half + 1, tile(j)]
            face = face + half_kappa[cls(1, p, q), half, tile(j)]
            outer_x[2 * p + q, half, tile(j)] = face
            part.append(face)
        coarse_off[0, half, tile(j)] = tree_sum(part)


def solve_kernel(
    mine_ref,
    theirs_ref,
    inner,
    outer_x,
    outer_y,
    outer_z,
    inner_sum,
    diagonal,
    damped,
    coarse_off,
    coarse_damped,
    chosen,
    planes,
    residual,
    scaled,
    partial,
    first_dir,
    second_dir,
    image,
    coarse_one,
    coarse_two,
    *,
    own,
):
    half, rows = inner.shape[1:3]
    at_ = Layout(rows)
    tile, tiles, zero = at_.tile, at_.tiles, at_.zero
    place = lax.axis_index("space")
    core = place % 2

    def begin(k, spot, j, value):
        residual[k, spot, tile(j)] = value
        scaled[k, spot + 1, tile(j)] = damped[k, spot, tile(j)] * value

    at_.arrange(mine_ref, theirs_ref, place, True, begin)
    at_.seam_fine(scaled)

    def rows_of(ref, i):
        cache = {}

        def load(k, j, step):
            if abs(j - step) > 1:
                return ref[k, i, tile(j)]
            if (k, j) not in cache:
                cache[k, j] = ref[k, i, tile(j)]
            return cache[k, j]

        def get(k, j):
            return load(k, j, j)

        def before(k, j):
            return at_.row_before(lambda r: load(k, r, j), j)

        def after(k, j):
            return at_.row_after(lambda r: load(k, r, j), j)

        return get, before, after

    def stencil(field, i, both):
        get, before, after = rows_of(field, i + 1)
        face_get, _, face_after = rows_of(outer_y, i)
        for j in range(tiles):
            here = [get(k, j) for k in range(8)]
            terms = [[] for _ in range(8)]
            for p, q in PAIRS:
                at = 2 * p + q
                for face_at, low, high in inner_faces(p, q):
                    face = inner[face_at, i, tile(j)]
                    terms[low].append(face * here[high])
                    if both:
                        terms[high].append(face * here[low])
                low, high = cls(0, p, q), cls(1, p, q)
                terms[low].append(outer_x[at, i, tile(j)] * field[high, i, tile(j)])
                if both:
                    side = field[low, i + 2, tile(j)]
                    terms[high].append(outer_x[at, i + 1, tile(j)] * side)
                low, high = cls(p, 0, q), cls(p, 1, q)
                terms[low].append(face_get(at, j) * before(high, j))
                if both:
                    terms[high].append(face_after(at, j) * after(low, j))
                low, high = cls(p, q, 0), cls(p, q, 1)
                terms[low].append(outer_z[at, i, tile(j)] * roll(here[high], 1, 1))
                if both:
                    terms[high].append(outer_z[4 + at, i, tile(j)] * roll(here[low], -1, 1))
            yield j, here, [tree_sum(part) if part else None for part in terms]

    def coarse_sides(field, i, j):
        here = field[0, i + 1, tile(j)]
        return here, (
            (field[0, i, tile(j)], field[0, i + 2, tile(j)]),
            (
                at_.row_before(lambda r: field[0, i + 1, tile(r)], j),
                at_.row_after(lambda r: field[0, i + 1, tile(r)], j),
            ),
            (roll(here, 1, 1), roll(here, -1, 1)),
        )

    def precondition(result):
        def down(i, carry):
            for j, _, sums in stencil(scaled, i, True):
                res = [residual[k, i, tile(j)] for k in range(8)]
                parts = [res[k] + sums[k] for k in range(8)]
                for k in range(8):
                    partial[k, i, tile(j)] = parts[k]
                rhs = tree_sum(parts) - (1.0 / KEPT) * tree_sum(res)
                coarse_one[0, i + 1, tile(j)] = coarse_damped[i, tile(j)] * rhs
            return carry

        lax.fori_loop(0, half, down, 0, unroll=UNROLL)
        at_.seam(coarse_one, [0], [0])

        def smooth(i, carry):
            for j in range(tiles):
                here, sides = coarse_sides(coarse_one, i, j)
                total = coarse_off[0, i, tile(j)] * sides[0][0]
                total = total + coarse_off[0, i + 1, tile(j)] * sides[0][1]
                more = coarse_off[1, i, tile(j)] * sides[1][0]
                more = more + coarse_off[2, i, tile(j)] * sides[1][1]
                most = coarse_off[3, i, tile(j)] * sides[2][0]
                most = most + coarse_off[4, i, tile(j)] * sides[2][1]
                coarse_two[0, i + 1, tile(j)] = KEPT * here + coarse_damped[
                    i, tile(j)
                ] * (total + more + most)
            return carry

        lax.fori_loop(0, half, smooth, 0, unroll=UNROLL)
        at_.seam(coarse_two, [0], [0])

        def up(i, gamma):
            face_get, _, face_after = rows_of(outer_y, i)
            for j in range(tiles):
                here, sides = coarse_sides(coarse_two, i, j)
                dots = []
                for a, b, c in CLASSES:
                    k = cls(a, b, c)
                    value = tree_sum(
                        [
                            partial[k, i, tile(j)],
                            inner_sum[k, i, tile(j)] * here,
                            outer_x[2 * b + c, i + a, tile(j)] * sides[0][a],
                            (face_after if b else face_get)(2 * a + c, j) * sides[1][b],
                            outer_z[4 * c + 2 * a + b, i, tile(j)] * sides[2][c],
                        ]
                    )
                    new = damped[k, i, tile(j)] * value
                    result[k, i + 1, tile(j)] = new
                    dots.append(residual[k, i, tile(j)] * new)
                gamma = gamma + tree_sum(dots)
            return gamma

        gamma = lax.fori_loop(0, half, up, zero, unroll=UNROLL)
        at_.seam_fine(result)
        return grand_total(gamma)

    gamma = precondition(first_dir)

    def apply(i, acc):
        for j, here, sums in stencil(first_dir, i, True):
            dots = []
            for k in range(8):
                value = diagonal[k, i, tile(j)] * here[k] - sums[k]
                image[k, i, tile(j)] = value
                dots.append(here[k] * value)
            acc = acc + tree_sum(dots)
        return acc

    curve = grand_total(lax.fori_loop(0, half, apply, zero, unroll=UNROLL))
    step_one = gamma / curve

    def update(i, carry):
        for j in range(tiles):
            for k in range(8):
                new = residual[k, i, tile(j)] - step_one * image[k, i, tile(j)]
                residual[k, i, tile(j)] = new
                scaled[k, i + 1, tile(j)] = damped[k, i, tile(j)] * new
        return carry

    lax.fori_loop(0, half, update, 0, unroll=UNROLL)
    at_.seam_fine(scaled)

    gamma_next = precondition(second_dir)

    def bend(i, carry):
        own_part, face_part = carry
        for j, here, sums in stencil(second_dir, i, False):
            own_part = own_part + tree_sum(
                [here[k] * (diagonal[k, i, tile(j)] * here[k]) for k in range(8)]
            )
            face_part = face_part + tree_sum([here[k] * sums[k] for k in range(7)])
        return own_part, face_part

    own_part, face_part = lax.fori_loop(0, half, bend, (zero, zero), unroll=UNROLL)
    ratio = gamma_next / gamma
    curve_next = grand_total(own_part - 2.0 * face_part)
    step_two = gamma_next / (curve_next - ratio * ratio * curve)
    weight = chosen[...]
    step_first = (step_one + step_two * ratio) * weight
    step_two = step_two * weight

    start = (place - core) * (own // 2)
    upper = jnp.where(start >= half, 1, 0)
    start = start - half * upper
    even = at_.lane % 2 == 0
    source = at_.lane // 2 + HALF * upper
    for at in range(2 * own + 2):
        a = (at + 1) % 2
        spot = start + (at + 1) // 2
        for b in (0, 1):
            for j in range(tiles):
                both = [
                    step_first * first_dir[cls(a, b, c), spot, tile(j)]
                    + step_two * second_dir[cls(a, b, c), spot, tile(j)]
                    for c in (0, 1)
                ]
                planes[at, at_.every(b, j), :] = jnp.where(
                    even,
                    jnp.take_along_axis(both[0], source, axis=1),
                    jnp.take_along_axis(both[1], source, axis=1),
                )


def finish_kernel(planes_ref, state_ref, far_ref, near_ref, adjoint_ref, keep_ref, partner_ref, send_ref, terms):
    own, ny, nz = adjoint_ref.shape
    core = lax.axis_index("space") % 2
    full = (ny, nz)
    y_at = row_index(full)
    z_at = lane_index(full)

    def drop(value, axis, up):
        moved = roll(value, -1 if up else 1, axis)
        at = (y_at, z_at)[axis]
        edge = full[axis] - 1 if up else 0
        return value - jnp.where(at == edge, 0.0, moved)

    is_even = core == 0
    state = [jnp.where(is_even, far_ref[core, 0], near_ref[own])]
    state += [jnp.where(is_even, state_ref[core, x], near_ref[x]) for x in range(own)]
    state += [jnp.where(is_even, near_ref[x], state_ref[core, x]) for x in range(own)]
    state += [jnp.where(is_even, near_ref[own], far_ref[core, 0])]
    for x in range(2 * own):
        here, f = planes_ref[x + 1], state[x + 1]
        term = (here - planes_ref[x + 2]) * (f - state[x + 2])
        term = term + (here - planes_ref[x]) * (f - state[x])
        for axis in (0, 1):
            for up in (True, False):
                term = term + drop(here, axis, up) * drop(f, axis, up)
        terms[x] = -0.5 * term

    groups = send_ref.shape[0] + 1
    chunk = keep_ref.shape[1]
    for x in range(own):
        mine, other = core * own + x, (1 - core) * own + x
        adjoint_ref[x] = planes_ref[1 + mine]
        partner_ref[x, :ny] = planes_ref[1 + other]
        for k in range(groups):
            at = lax.rem(lax.axis_index("pole") + k, groups) * chunk
            at = pl.multiple_of(at, chunk)
            for side, plane in enumerate((mine, other)):
                share = terms[plane, pl.ds(at, chunk), :]
                if k:
                    send_ref[k - 1, side, x] = share
                elif side:
                    partner_ref[x, ny:] = share
                else:
                    keep_ref[x] = share


def whole_grid(conductivity, misfit, forward_states, pole_shifts, pole_weights, pole_order):
    members, own, ny, nz = forward_states.shape
    groups = lax.axis_size("pole")
    peers = lax.axis_size("space")
    even = lax.axis_index("space") % 2 == 0
    mine, theirs, far, fetch_near = gather_blocks([conductivity, misfit], forward_states, "space")
    half, rows = peers * own // 4, ny // 2

    def field(count, extent):
        return (count, extent, rows, 2 * HALF)

    def held(*shape):
        return pltpu.VMEM(shape, jnp.float32)

    vmem = pl.BlockSpec(memory_space=pltpu.VMEM)
    shapes = [
        field(12, half),
        field(4, half + 1),
        field(4, half),
        field(8, half),
        field(8, half),
        field(8, half),
        field(8, half),
        field(5, half + 1),
        (half, rows, 2 * HALF),
        (TILE, 2 * HALF),
    ]
    coefficients = pl.pallas_call(
        setup_kernel,
        out_shape=[jax.ShapeDtypeStruct(shape, jnp.float32) for shape in shapes],
        in_specs=[vmem] * 5,
        out_specs=[vmem] * len(shapes),
        scratch_shapes=[held(*field(8, half + 2))],
        compiler_params=pltpu.CompilerParams(vmem_limit_bytes=6 * 1024 * 1024),
        name="setup",
    )(pole_order[None], pole_shifts[None], pole_weights[None], mine[0], theirs[0])
    coefficients, near = fetch_near(coefficients)
    planes = pl.pallas_call(
        functools.partial(solve_kernel, own=own),
        out_shape=jax.ShapeDtypeStruct((2 * own + 2, ny, nz), jnp.float32),
        in_specs=[vmem] * (2 + len(shapes)),
        out_specs=vmem,
        scratch_shapes=[
            held(*field(8, half)),
            held(*field(8, half + 2)),
            held(*field(8, half)),
            held(*field(8, half + 2)),
            held(*field(8, half + 2)),
            held(*field(8, half)),
            held(*field(1, half + 2)),
            held(*field(1, half + 2)),
        ],
        compiler_params=pltpu.CompilerParams(vmem_limit_bytes=12 * 1024 * 1024),
        name="solve",
    )(mine[1], theirs[1], *coefficients)
    chunk = ny // groups
    adjoint, gradient, partner, send = pl.pallas_call(
        finish_kernel,
        out_shape=[
            jax.ShapeDtypeStruct((own, ny, nz), jnp.float32),
            jax.ShapeDtypeStruct((own, chunk, nz), jnp.float32),
            jax.ShapeDtypeStruct((own, ny + chunk, nz), jnp.float32),
            jax.ShapeDtypeStruct((groups - 1, 2, own, chunk, nz), jnp.float32),
        ],
        in_specs=[vmem] * 4,
        out_specs=[vmem] * 4,
        scratch_shapes=[held(2 * own, ny, nz)],
        compiler_params=pltpu.CompilerParams(vmem_limit_bytes=4 * 1024 * 1024),
        name="finish",
    )(planes, forward_states, far, near)

    arrived = lax.ppermute(partner, "space", [(i, i ^ 1) for i in range(peers)])
    shares = []
    for k in range(1, groups):
        for side in (0, 1):
            pairs = [
                (i * peers + j, (i + k) % groups * peers + (j ^ side))
                for i in range(groups)
                for j in range(peers)
            ]
            shares.append(lax.ppermute(send[k - 1, side], ("pole", "space"), pairs))
    theirs = arrived[:, :ny]
    adjoint_states = jnp.stack(
        [jnp.where(even, adjoint, theirs), jnp.where(even, theirs, adjoint)]
    )
    adjoint_states, arrived = lax.optimization_barrier((adjoint_states, arrived))
    return adjoint_states, gradient + arrived[:, ny:] + sum(shares)


def plus_side(field, which_dim):
    extent = field.shape[which_dim]
    inner_part = lax.slice_in_dim(field, 1, extent, axis=which_dim)
    zero_plane = jnp.zeros_like(lax.slice_in_dim(field, 0, 1, axis=which_dim))
    return jnp.concatenate([inner_part, zero_plane], axis=which_dim)


def minus_side(field, which_dim):
    extent = field.shape[which_dim]
    inner_part = lax.slice_in_dim(field, 0, extent - 1, axis=which_dim)
    zero_plane = jnp.zeros_like(lax.slice_in_dim(field, 0, 1, axis=which_dim))
    return jnp.concatenate([zero_plane, inner_part], axis=which_dim)


def coarse_pick(faces, which_dim, offset):
    extent_x, extent_y, extent_z = faces.shape
    blocks = faces.reshape(extent_x // 2, 2, extent_y // 2, 2, extent_z // 2, 2)
    chosen = lax.index_in_dim(blocks, offset, axis=2 * which_dim + 1, keepdims=True)
    return jnp.sum(chosen, axis=(1, 3, 5))


def side_terms(field, plus_faces, minus_faces, widened):
    result = plus_faces[0] * (field - widened[:, 2:]) + minus_faces[0] * (field - widened[:, :-2])
    for which_dim in (1, 2):
        result = result + plus_faces[which_dim] * (field - plus_side(field, which_dim + 1))
        result = result + minus_faces[which_dim] * (field - minus_side(field, which_dim + 1))
    return result


def fine_image(field, plus_faces, minus_faces, shift_value):
    widened = extended(field, (("space", 1),), 1)
    return shift_value * field + side_terms(field, plus_faces, minus_faces, widened)


def coarse_image(field, plus_faces, minus_faces, shift_value):
    widened = extended(field, (("space", 1),), 1)
    return shift_value * field + side_terms(field, plus_faces, minus_faces, widened)


def restrict(field):
    members, extent_x, extent_y, extent_z = field.shape
    shaped = field.reshape(members, extent_x // 2, 2, extent_y // 2, 2, extent_z // 2, 2)
    return jnp.sum(shaped, axis=(2, 4, 6))


def prolong(field):
    return jnp.repeat(jnp.repeat(jnp.repeat(field, 2, axis=1), 2, axis=2), 2, axis=3)


def precondition(residual, fine, coarse):
    plus_faces, minus_faces, shift_value, diagonal = fine
    coarse_plus, coarse_minus, coarse_shift, coarse_diagonal = coarse
    smooth_one = DAMPING * residual / diagonal
    coarse_rhs = restrict(residual - fine_image(smooth_one, plus_faces, minus_faces, shift_value))
    coarse_one = DAMPING * coarse_rhs / coarse_diagonal
    coarse_two = (
        coarse_one
        + DAMPING
        * (coarse_rhs - coarse_image(coarse_one, coarse_plus, coarse_minus, coarse_shift))
        / coarse_diagonal
    )
    corrected = smooth_one + prolong(coarse_two)
    return (
        corrected
        + DAMPING
        * (residual - fine_image(corrected, plus_faces, minus_faces, shift_value))
        / diagonal
    )


def expand(values):
    return values.reshape(-1, 1, 1, 1)


def cell_sums(values):
    return jnp.sum(values, axis=(1, 2, 3))


def norm_sum(residual, precond):
    return lax.psum(cell_sums(residual * precond), "space")


def solve(rhs, fine, coarse):
    plus_faces, minus_faces, shift_value, diagonal = fine
    iterate = jnp.zeros_like(rhs)
    residual = rhs
    precond = precondition(residual, fine, coarse)
    gamma_now = norm_sum(residual, precond)
    search = precond
    for turn_index in range(ITERS):
        image_field = fine_image(search, plus_faces, minus_faces, shift_value)
        curve = lax.psum(cell_sums(search * image_field), "space")
        step_length = gamma_now / curve
        iterate = iterate + expand(step_length) * search
        if turn_index + 1 < ITERS:
            residual = residual - expand(step_length) * image_field
            precond = precondition(residual, fine, coarse)
            gamma_next = norm_sum(residual, precond)
            search = precond + expand(gamma_next / gamma_now) * search
            gamma_now = gamma_next
    return iterate


def divided(conductivity, misfit, forward_states, pole_shifts, pole_weights, pole_order):
    widened_kappa = extended(conductivity, (("space", 0),), 1)
    plus_faces = [
        0.5 * (conductivity + widened_kappa[2:]),
        0.5 * (conductivity + plus_side(conductivity, 1)),
        0.5 * (conductivity + plus_side(conductivity, 2)),
    ]
    minus_faces = [
        0.5 * (conductivity + widened_kappa[:-2]),
        0.5 * (conductivity + minus_side(conductivity, 1)),
        0.5 * (conductivity + minus_side(conductivity, 2)),
    ]
    base_diagonal = (
        plus_faces[0]
        + plus_faces[1]
        + plus_faces[2]
        + minus_faces[0]
        + minus_faces[1]
        + minus_faces[2]
    )
    coarse_plus = [coarse_pick(plus_faces[which_dim], which_dim, 1) for which_dim in range(3)]
    coarse_minus = [coarse_pick(minus_faces[which_dim], which_dim, 0) for which_dim in range(3)]
    coarse_base = (
        coarse_plus[0]
        + coarse_plus[1]
        + coarse_plus[2]
        + coarse_minus[0]
        + coarse_minus[1]
        + coarse_minus[2]
    )
    pole_index = jnp.arange(pole_shifts.shape[0], dtype=jnp.int32)
    matches = pole_order[:, None] == pole_index[None, :]
    shift_local = jnp.sum(jnp.where(matches, pole_shifts[None, :], 0.0), axis=1)
    weight_local = jnp.sum(jnp.where(matches, pole_weights[None, :], 0.0), axis=1)
    members = forward_states.shape[0]

    def solve_group(shift_part, weight_part):
        shift_value = expand(shift_part)
        fine = (plus_faces, minus_faces, shift_value, base_diagonal[None] + shift_value)
        coarse = (
            coarse_plus,
            coarse_minus,
            8.0 * shift_value,
            coarse_base[None] + 8.0 * shift_value,
        )
        return solve(expand(weight_part) * misfit[None], fine, coarse)

    adjoint_states = jnp.concatenate(
        [
            solve_group(shift_local[member : member + 1], weight_local[member : member + 1])
            for member in range(members)
        ],
        axis=0,
    )
    widened = extended(jnp.stack([adjoint_states, forward_states]), (("space", 2),), 1)
    term = (adjoint_states - widened[0, :, 2:]) * (forward_states - widened[1, :, 2:])
    term = term + (adjoint_states - widened[0, :, :-2]) * (forward_states - widened[1, :, :-2])
    for which_dim in (2, 3):
        term = term + (adjoint_states - plus_side(adjoint_states, which_dim)) * (
            forward_states - plus_side(forward_states, which_dim)
        )
        term = term + (adjoint_states - minus_side(adjoint_states, which_dim)) * (
            forward_states - minus_side(forward_states, which_dim)
        )
    local_term = -0.5 * jnp.sum(term, axis=0)
    gradient = lax.psum_scatter(local_term, "pole", scatter_dimension=1, tiled=True)
    return (adjoint_states, gradient)


def solution(mesh):
    in_specs = (
        P("space", None, None),
        P("space", None, None),
        P("pole", "space", None, None),
        P(),
        P(),
        P("pole"),
    )
    out_specs = (P("pole", "space", None, None), P("space", "pole", None))

    def body(conductivity, misfit, forward_states, *poles):
        nx = conductivity.shape[0] * lax.axis_size("space")
        _, ny, nz = conductivity.shape
        peers = lax.axis_size("space")
        small = nx * ny * nz <= REPLICATED_CELLS and forward_states.shape[:2] == (2, 2)
        if small and nz == 2 * HALF and peers > 2 and peers & (peers - 1) == 0:
            return whole_grid(conductivity, misfit, forward_states, *poles)
        return divided(conductivity, misfit, forward_states, *poles)

    return jax.shard_map(
        body, mesh=mesh, in_specs=in_specs, out_specs=out_specs, check_vma=False
    )
```

```python
import functools

import jax
import jax.numpy as jnp
from jax import lax
from jax.experimental import pallas as pl
from jax.experimental.pallas import tpu as pltpu
from jax.sharding import PartitionSpec as P

ITERS = 2
DAMPING = 0.8
KEPT = 2.0 - DAMPING
REPLICATED_CELLS = 32 * 64 * 128
HALF = 64
TILE = 8
UNROLL = 8


def extended(array, sides, width):
    for axis, dim in sides:
        peers, length = (lax.axis_size(axis), array.shape[dim])
        up = [(i, (i + 1) % peers) for i in range(peers - 1)]
        down = [(j, i) for i, j in up]
        last = lax.slice_in_dim(array, length - width, length, axis=dim)
        leading = lax.slice_in_dim(array, 0, width, axis=dim)
        before = lax.ppermute(last, axis, up)
        after = lax.ppermute(leading, axis, down)
        array = jnp.concatenate([before, array, after], axis=dim)
    return array


def lane_index(shape):
    return lax.broadcasted_iota(jnp.int32, shape, len(shape) - 1)


def row_index(shape):
    return lax.broadcasted_iota(jnp.int32, shape, len(shape) - 2)


def roll(block, shift, axis):
    return pltpu.roll(block, shift % block.shape[axis], axis)


def inverse(value):
    guess = pl.reciprocal(value, approx=True)
    return guess * (2.0 - value * guess)


def tree_sum(values):
    while len(values) > 1:
        values = [sum(values[at : at + 2]) for at in range(0, len(values), 2)]
    return values[0]


def grand_total(acc):
    line = jnp.sum(acc, axis=0, keepdims=True)
    return jnp.broadcast_to(jnp.sum(line, axis=1, keepdims=True), acc.shape)


def swap_masks(peers, flip):
    falling = []
    mask = peers // 2
    while mask > 1:
        falling.append(mask)
        mask //= 2
    if flip:
        return falling[::-1], falling[:1] + falling[:0:-1]
    return falling, falling[-1:] + falling[:-1]


def block_pair(u, holder, peers, flip):
    even, odd = swap_masks(peers, flip)
    parity = holder % 2
    top = jnp.where(parity == 0, even.index(peers // 2), odd.index(peers // 2))
    below = u & ((1 << top) - 1)
    base = ((u >> top) << (top + 1)) | below
    upper = jnp.where(holder >= peers // 2, 1, 0)
    first = base | (upper << top)
    second = base | ((1 - upper) << top)
    home = holder
    for step, (mask_even, mask_odd) in enumerate(zip(even, odd)):
        mask = jnp.where(parity == 0, mask_even, mask_odd)
        home = home ^ (((first >> step) & 1) * mask)
    return first, second, home


def prepare_kernel(kappa_ref, misfit_ref, kappa_out, misfit_out, *, axis, peers):
    at_ = Layout(kappa_ref.shape[1] // 2)
    upper = jnp.where(lax.axis_index(axis) >= peers // 2, 1, 0)
    at_.deal(kappa_ref, kappa_out, upper)
    at_.deal(misfit_ref, misfit_out, upper)


def join_kernel(*refs, masks, axis, peers):
    place = lax.axis_index(axis)
    at_ = Layout(refs[0].shape[1] // 2)
    for at, (even, odd) in enumerate(masks):
        partner = place ^ jnp.where(place % 2 == 0, even, odd)
        refs[4 + at][0] = refs[at][...]
        at_.deal(refs[2 + at], refs[4 + at].at[1], jnp.where(partner >= peers // 2, 1, 0))


def gather_blocks(blocks, states, axis):
    peers = lax.axis_size(axis)
    even = lax.axis_index(axis) % 2 == 0
    swap = [(i, i ^ 1) for i in range(peers)]
    over = [(i, i + 1 if i % 2 else i - 1) for i in range(1, peers - 1)]
    vmem = pl.BlockSpec(memory_space=pltpu.VMEM)
    swaps = [list(zip(*swap_masks(peers, flip))) for flip in (False, True)]
    own = pl.pallas_call(
        functools.partial(prepare_kernel, axis=axis, peers=peers),
        out_shape=[jax.ShapeDtypeStruct(block.shape, jnp.float32) for block in blocks],
        in_specs=[vmem] * 2,
        out_specs=[vmem] * 2,
        compiler_params=pltpu.CompilerParams(vmem_limit_bytes=1024 * 1024),
        name="prepare",
    )(*blocks)
    held = list(blocks)
    for step in range(len(swaps[0])):
        arrived = []
        for at in (0, 1):
            masks = swaps[at][step]
            pairs = [(i, i ^ masks[i % 2]) for i in range(peers)]
            arrived.append(lax.ppermute(held[at], axis, pairs))
        if step:
            held = [jnp.concatenate(pair, axis=0) for pair in zip(held, arrived)]
            continue
        masks = [swaps[at][0] for at in (0, 1)]
        shape = jax.ShapeDtypeStruct((2, *blocks[0].shape), jnp.float32)
        held[:] = pl.pallas_call(
            functools.partial(join_kernel, masks=masks, axis=axis, peers=peers),
            out_shape=[shape] * 2,
            in_specs=[vmem] * 4,
            out_specs=[vmem] * 2,
            compiler_params=pltpu.CompilerParams(vmem_limit_bytes=1024 * 1024),
            name="join",
        )(*own, *arrived)
        held[1], states = lax.optimization_barrier((held[1], states))
        far = lax.ppermute(jnp.where(even, states[:, :1], states[:, -1:]), axis, over)
    other = [lax.ppermute(part, axis, swap) for part in held]

    def fetch_near(after):
        late, states_late, far_late = lax.optimization_barrier((after, states, far))
        given = jnp.concatenate([states_late, far_late], axis=1)
        return late, lax.ppermute(jnp.where(even, given[1], given[0]), axis, swap)

    return held, other, far, fetch_near


CLASSES = [(a, b, c) for a in (0, 1) for b in (0, 1) for c in (0, 1)]
PAIRS = [(p, q) for p in (0, 1) for q in (0, 1)]


def cls(a, b, c):
    return 4 * a + 2 * b + c


def inner_faces(p, q):
    return (
        (2 * p + q, cls(0, p, q), cls(1, p, q)),
        (4 + 2 * p + q, cls(p, 0, q), cls(p, 1, q)),
        (8 + 2 * p + q, cls(p, q, 0), cls(p, q, 1)),
    )


class Layout:
    def __init__(self, rows):
        self.tiles = rows // TILE
        self.lane = lane_index((TILE, 2 * HALF))
        self.row = row_index((TILE, 2 * HALF))
        self.left = self.lane < HALF
        self.zero = jnp.zeros((TILE, 2 * HALF), jnp.float32)

    def tile(self, j):
        return pl.ds(TILE * j, TILE)

    def every(self, b, j):
        return pl.ds(b + 2 * j, TILE, stride=2 * self.tiles)

    def row_before(self, load, j):
        return load(j - 1) if j else roll(load(self.tiles - 1), 1, 0)

    def row_after(self, load, j):
        return load(j + 1) if j + 1 < self.tiles else roll(load(0), -1, 0)

    def seam(self, ref, low, high):
        last = ref.shape[1] - 1
        for j in range(self.tiles):
            for k in low:
                moved = roll(ref[k, last - 1, self.tile(j)], HALF, 1)
                ref[k, 0, self.tile(j)] = jnp.where(self.left, 0.0, moved)
            for k in high:
                moved = roll(ref[k, 1, self.tile(j)], HALF, 1)
                ref[k, last, self.tile(j)] = jnp.where(self.left, moved, 0.0)

    def seam_fine(self, ref):
        count = ref.shape[0]
        self.seam(
            ref,
            [k for k in range(count) if k % 8 >= 4],
            [k for k in range(count) if k % 8 < 4],
        )

    def dealt(self, b, j):
        return pl.ds(TILE * (self.tiles * b + j), TILE)

    def deal(self, block_ref, out_ref, upper):
        odd = jnp.where(self.left, upper, 1 - upper)
        column = 2 * (self.lane % HALF) + odd
        for x in range(block_ref.shape[0]):
            for b in (0, 1):
                for j in range(self.tiles):
                    rows = block_ref[x, self.every(b, j), :]
                    out_ref[x, self.dealt(b, j), :] = jnp.take_along_axis(rows, column, axis=1)

    def arrange(self, mine_ref, theirs_ref, place, flip, store):
        blocks, own = mine_ref.shape[:2]

        def pair(u, carry):
            for ref, holder in ((mine_ref, place), (theirs_ref, place ^ 1)):
                first, second, home = block_pair(u, holder, 2 * blocks, flip)
                for x in range(own):
                    spot = home * (own // 2) + x // 2
                    for b in (0, 1):
                        for j in range(self.tiles):
                            one = ref[first, x, self.dealt(b, j), :]
                            two = ref[second, x, self.dealt(b, j), :]
                            store(cls(x % 2, b, 0), spot, j, jnp.where(self.left, one, two))
                            odd = roll(jnp.where(self.left, two, one), HALF, 1)
                            store(cls(x % 2, b, 1), spot, j, odd)
            return carry

        lax.fori_loop(0, blocks // 2, pair, 0, unroll=True)


def setup_kernel(
    order_ref,
    shifts_ref,
    weights_ref,
    mine_ref,
    theirs_ref,
    inner,
    outer_x,
    outer_y,
    outer_z,
    inner_sum,
    diagonal,
    damped,
    coarse_off,
    coarse_damped,
    chosen,
    kappa,
):
    half = inner.shape[1]
    at_ = Layout(inner.shape[2])
    tile, tiles = at_.tile, at_.tiles
    place = lax.axis_index("space")
    pole = jnp.where(place % 2 == 0, order_ref[:, 0:1], order_ref[:, 1:2])
    taken = lane_index(shifts_ref.shape) == pole
    shift = jnp.sum(jnp.where(taken, shifts_ref[...], 0.0), axis=1, keepdims=True)
    weight = jnp.sum(jnp.where(taken, weights_ref[...], 0.0), axis=1, keepdims=True)
    shift = jnp.broadcast_to(2.0 * shift, at_.zero.shape)
    chosen[...] = jnp.broadcast_to(2.0 * weight, at_.zero.shape)

    def keep(k, spot, j, value):
        kappa[k, spot + 1, tile(j)] = value

    at_.arrange(mine_ref, theirs_ref, place, False, keep)
    at_.seam_fine(kappa)

    z_low = jnp.where(at_.lane % HALF > 0, 1.0, 0.0)
    z_high = jnp.where(at_.lane % HALF < HALF - 1, 1.0, 0.0)
    y_low = [jnp.where(at_.row > 0, 1.0, 0.0)] + [None] * (tiles - 1)
    y_high = [None] * (tiles - 1) + [jnp.where(at_.row < TILE - 1, 1.0, 0.0)]

    def masked(mask, value):
        return value if mask is None else mask * value

    def plane(i, carry):
        for j in range(tiles):
            kap = [kappa[k, i + 1, tile(j)] for k in range(8)]
            inside = [[] for _ in range(8)]
            outside = [[] for _ in range(8)]
            off = [[] for _ in range(5)]
            for p, q in PAIRS:
                for face_at, low, high in inner_faces(p, q):
                    face = kap[low] + kap[high]
                    inner[face_at, i, tile(j)] = face
                    inside[low].append(face)
                    inside[high].append(face)
                at = 2 * p + q

                low, high = cls(0, p, q), cls(1, p, q)
                minus = kap[low] + kappa[high, i, tile(j)]
                plus = kap[high] + kappa[low, i + 2, tile(j)]
                outside[low].append(minus)
                outside[high].append(plus)
                outer_x[at, i, tile(j)] = minus
                off[0].append(minus)

                low, high = cls(p, 0, q), cls(p, 1, q)
                side = at_.row_before(lambda r: kappa[high, i + 1, tile(r)], j)
                minus = kap[low] + masked(y_low[j], side)
                side = at_.row_after(lambda r: kappa[low, i + 1, tile(r)], j)
                plus = kap[high] + masked(y_high[j], side)
                outside[low].append(minus)
                outside[high].append(plus)
                minus, plus = masked(y_low[j], minus), masked(y_high[j], plus)
                outer_y[at, i, tile(j)] = minus
                off[1].append(minus)
                off[2].append(plus)

                low, high = cls(p, q, 0), cls(p, q, 1)
                minus = kap[low] + z_low * roll(kap[high], 1, 1)
                plus = kap[high] + z_high * roll(kap[low], -1, 1)
                outside[low].append(minus)
                outside[high].append(plus)
                minus, plus = z_low * minus, z_high * plus
                outer_z[at, i, tile(j)] = minus
                outer_z[4 + at, i, tile(j)] = plus
                off[3].append(minus)
                off[4].append(plus)
            coarse_total = []
            for k in range(8):
                within, without = tree_sum(inside[k]), tree_sum(outside[k])
                base = within + without + shift
                inner_sum[k, i, tile(j)] = within + ((1.0 - DAMPING) / DAMPING) * base
                diagonal[k, i, tile(j)] = base
                coarse_total.append(without)
                damped[k, i, tile(j)] = (DAMPING / KEPT) * inverse(base)
            for at, part in enumerate(off):
                coarse_off[at, i, tile(j)] = tree_sum(part)
            coarse_damped[i, tile(j)] = DAMPING * inverse(tree_sum(coarse_total) + 8.0 * shift)
        return carry

    lax.fori_loop(0, half, plane, 0, unroll=UNROLL)
    for j in range(tiles):
        part = []
        for p, q in PAIRS:
            face = kappa[cls(0, p, q), half + 1, tile(j)]
            face = face + kappa[cls(1, p, q), half, tile(j)]
            outer_x[2 * p + q, half, tile(j)] = face
            part.append(face)
        coarse_off[0, half, tile(j)] = tree_sum(part)


def solve_kernel(
    mine_ref,
    theirs_ref,
    inner,
    outer_x,
    outer_y,
    outer_z,
    inner_sum,
    diagonal,
    damped,
    coarse_off,
    coarse_damped,
    chosen,
    planes,
    residual,
    scaled,
    partial,
    first_dir,
    second_dir,
    image,
    coarse_one,
    coarse_two,
    *,
    own,
):
    half, rows = inner.shape[1:3]
    at_ = Layout(rows)
    tile, tiles, zero = at_.tile, at_.tiles, at_.zero
    place = lax.axis_index("space")
    core = place % 2

    def begin(k, spot, j, value):
        residual[k, spot, tile(j)] = value
        scaled[k, spot + 1, tile(j)] = damped[k, spot, tile(j)] * value

    at_.arrange(mine_ref, theirs_ref, place, True, begin)
    at_.seam_fine(scaled)

    def rows_of(ref, i):
        cache = {}

        def load(k, j, step):
            if abs(j - step) > 1:
                return ref[k, i, tile(j)]
            if (k, j) not in cache:
                cache[k, j] = ref[k, i, tile(j)]
            return cache[k, j]

        def get(k, j):
            return load(k, j, j)

        def before(k, j):
            return at_.row_before(lambda r: load(k, r, j), j)

        def after(k, j):
            return at_.row_after(lambda r: load(k, r, j), j)

        return get, before, after

    def stencil(field, i, both):
        get, before, after = rows_of(field, i + 1)
        face_get, _, face_after = rows_of(outer_y, i)
        for j in range(tiles):
            here = [get(k, j) for k in range(8)]
            terms = [[] for _ in range(8)]
            for p, q in PAIRS:
                at = 2 * p + q
                for face_at, low, high in inner_faces(p, q):
                    face = inner[face_at, i, tile(j)]
                    terms[low].append(face * here[high])
                    if both:
                        terms[high].append(face * here[low])
                low, high = cls(0, p, q), cls(1, p, q)
                terms[low].append(outer_x[at, i, tile(j)] * field[high, i, tile(j)])
                if both:
                    side = field[low, i + 2, tile(j)]
                    terms[high].append(outer_x[at, i + 1, tile(j)] * side)
                low, high = cls(p, 0, q), cls(p, 1, q)
                terms[low].append(face_get(at, j) * before(high, j))
                if both:
                    terms[high].append(face_after(at, j) * after(low, j))
                low, high = cls(p, q, 0), cls(p, q, 1)
                terms[low].append(outer_z[at, i, tile(j)] * roll(here[high], 1, 1))
                if both:
                    terms[high].append(outer_z[4 + at, i, tile(j)] * roll(here[low], -1, 1))
            yield j, here, [tree_sum(part) if part else None for part in terms]

    def coarse_sides(field, i, j):
        here = field[0, i + 1, tile(j)]
        return here, (
            (field[0, i, tile(j)], field[0, i + 2, tile(j)]),
            (
                at_.row_before(lambda r: field[0, i + 1, tile(r)], j),
                at_.row_after(lambda r: field[0, i + 1, tile(r)], j),
            ),
            (roll(here, 1, 1), roll(here, -1, 1)),
        )

    def precondition(result):
        def down(i, carry):
            for j, _, sums in stencil(scaled, i, True):
                res = [residual[k, i, tile(j)] for k in range(8)]
                parts = [res[k] + sums[k] for k in range(8)]
                for k in range(8):
                    partial[k, i, tile(j)] = parts[k]
                rhs = tree_sum(parts) - (1.0 / KEPT) * tree_sum(res)
                coarse_one[0, i + 1, tile(j)] = coarse_damped[i, tile(j)] * rhs
            return carry

        lax.fori_loop(0, half, down, 0, unroll=UNROLL)
        at_.seam(coarse_one, [0], [0])

        def smooth(i, carry):
            for j in range(tiles):
                here, sides = coarse_sides(coarse_one, i, j)
                total = coarse_off[0, i, tile(j)] * sides[0][0]
                total = total + coarse_off[0, i + 1, tile(j)] * sides[0][1]
                more = coarse_off[1, i, tile(j)] * sides[1][0]
                more = more + coarse_off[2, i, tile(j)] * sides[1][1]
                most = coarse_off[3, i, tile(j)] * sides[2][0]
                most = most + coarse_off[4, i, tile(j)] * sides[2][1]
                coarse_two[0, i + 1, tile(j)] = KEPT * here + coarse_damped[
                    i, tile(j)
                ] * (total + more + most)
            return carry

        lax.fori_loop(0, half, smooth, 0, unroll=UNROLL)
        at_.seam(coarse_two, [0], [0])

        def up(i, gamma):
            face_get, _, face_after = rows_of(outer_y, i)
            for j in range(tiles):
                here, sides = coarse_sides(coarse_two, i, j)
                dots = []
                for a, b, c in CLASSES:
                    k = cls(a, b, c)
                    value = tree_sum(
                        [
                            partial[k, i, tile(j)],
                            inner_sum[k, i, tile(j)] * here,
                            outer_x[2 * b + c, i + a, tile(j)] * sides[0][a],
                            (face_after if b else face_get)(2 * a + c, j) * sides[1][b],
                            outer_z[4 * c + 2 * a + b, i, tile(j)] * sides[2][c],
                        ]
                    )
                    new = damped[k, i, tile(j)] * value
                    result[k, i + 1, tile(j)] = new
                    dots.append(residual[k, i, tile(j)] * new)
                gamma = gamma + tree_sum(dots)
            return gamma

        gamma = lax.fori_loop(0, half, up, zero, unroll=UNROLL)
        at_.seam_fine(result)
        return grand_total(gamma)

    gamma = precondition(first_dir)

    def apply(i, acc):
        for j, here, sums in stencil(first_dir, i, True):
            dots = []
            for k in range(8):
                value = diagonal[k, i, tile(j)] * here[k] - sums[k]
                image[k, i, tile(j)] = value
                dots.append(here[k] * value)
            acc = acc + tree_sum(dots)
        return acc

    curve = grand_total(lax.fori_loop(0, half, apply, zero, unroll=UNROLL))
    step_one = gamma / curve

    def update(i, carry):
        for j in range(tiles):
            for k in range(8):
                new = residual[k, i, tile(j)] - step_one * image[k, i, tile(j)]
                residual[k, i, tile(j)] = new
                scaled[k, i + 1, tile(j)] = damped[k, i, tile(j)] * new
        return carry

    lax.fori_loop(0, half, update, 0, unroll=UNROLL)
    at_.seam_fine(scaled)

    gamma_next = precondition(second_dir)

    def bend(i, carry):
        own_part, face_part = carry
        for j, here, sums in stencil(second_dir, i, False):
            own_part = own_part + tree_sum(
                [here[k] * (diagonal[k, i, tile(j)] * here[k]) for k in range(8)]
            )
            face_part = face_part + tree_sum([here[k] * sums[k] for k in range(7)])
        return own_part, face_part

    own_part, face_part = lax.fori_loop(0, half, bend, (zero, zero), unroll=UNROLL)
    ratio = gamma_next / gamma
    curve_next = grand_total(own_part - 2.0 * face_part)
    step_two = gamma_next / (curve_next - ratio * ratio * curve)
    weight = chosen[...]
    step_first = (step_one + step_two * ratio) * weight
    step_two = step_two * weight

    start = (place - core) * (own // 2)
    upper = jnp.where(start >= half, 1, 0)
    start = start - half * upper
    even = at_.lane % 2 == 0
    source = at_.lane // 2 + HALF * upper
    for at in range(2 * own + 2):
        a = (at + 1) % 2
        spot = start + (at + 1) // 2
        for b in (0, 1):
            for j in range(tiles):
                both = [
                    step_first * first_dir[cls(a, b, c), spot, tile(j)]
                    + step_two * second_dir[cls(a, b, c), spot, tile(j)]
                    for c in (0, 1)
                ]
                planes[at, at_.every(b, j), :] = jnp.where(
                    even,
                    jnp.take_along_axis(both[0], source, axis=1),
                    jnp.take_along_axis(both[1], source, axis=1),
                )


def finish_kernel(planes_ref, state_ref, far_ref, near_ref, adjoint_ref, keep_ref, partner_ref, send_ref, terms):
    own, ny, nz = adjoint_ref.shape
    core = lax.axis_index("space") % 2
    full = (ny, nz)
    y_at = row_index(full)
    z_at = lane_index(full)

    def drop(value, axis, up):
        moved = roll(value, -1 if up else 1, axis)
        at = (y_at, z_at)[axis]
        edge = full[axis] - 1 if up else 0
        return value - jnp.where(at == edge, 0.0, moved)

    is_even = core == 0
    state = [jnp.where(is_even, far_ref[core, 0], near_ref[own])]
    state += [jnp.where(is_even, state_ref[core, x], near_ref[x]) for x in range(own)]
    state += [jnp.where(is_even, near_ref[x], state_ref[core, x]) for x in range(own)]
    state += [jnp.where(is_even, near_ref[own], far_ref[core, 0])]
    for x in range(2 * own):
        here, f = planes_ref[x + 1], state[x + 1]
        term = (here - planes_ref[x + 2]) * (f - state[x + 2])
        term = term + (here - planes_ref[x]) * (f - state[x])
        for axis in (0, 1):
            for up in (True, False):
                term = term + drop(here, axis, up) * drop(f, axis, up)
        terms[x] = -0.5 * term

    groups = send_ref.shape[0] + 1
    chunk = keep_ref.shape[1]
    for x in range(own):
        mine, other = core * own + x, (1 - core) * own + x
        adjoint_ref[x] = planes_ref[1 + mine]
        partner_ref[x, :ny] = planes_ref[1 + other]
        for k in range(groups):
            at = lax.rem(lax.axis_index("pole") + k, groups) * chunk
            at = pl.multiple_of(at, chunk)
            for side, plane in enumerate((mine, other)):
                share = terms[plane, pl.ds(at, chunk), :]
                if k:
                    send_ref[k - 1, side, x] = share
                elif side:
                    partner_ref[x, ny:] = share
                else:
                    keep_ref[x] = share


def whole_grid(conductivity, misfit, forward_states, pole_shifts, pole_weights, pole_order):
    members, own, ny, nz = forward_states.shape
    groups = lax.axis_size("pole")
    peers = lax.axis_size("space")
    even = lax.axis_index("space") % 2 == 0
    mine, theirs, far, fetch_near = gather_blocks([conductivity, misfit], forward_states, "space")
    half, rows = peers * own // 4, ny // 2

    def field(count, extent):
        return (count, extent, rows, 2 * HALF)

    def held(*shape):
        return pltpu.VMEM(shape, jnp.float32)

    vmem = pl.BlockSpec(memory_space=pltpu.VMEM)
    shapes = [
        field(12, half),
        field(4, half + 1),
        field(4, half),
        field(8, half),
        field(8, half),
        field(8, half),
        field(8, half),
        field(5, half + 1),
        (half, rows, 2 * HALF),
        (TILE, 2 * HALF),
    ]
    coefficients = pl.pallas_call(
        setup_kernel,
        out_shape=[jax.ShapeDtypeStruct(shape, jnp.float32) for shape in shapes],
        in_specs=[vmem] * 5,
        out_specs=[vmem] * len(shapes),
        scratch_shapes=[held(*field(8, half + 2))],
        compiler_params=pltpu.CompilerParams(vmem_limit_bytes=6 * 1024 * 1024),
        name="setup",
    )(pole_order[None], pole_shifts[None], pole_weights[None], mine[0], theirs[0])
    coefficients, near = fetch_near(coefficients)
    planes = pl.pallas_call(
        functools.partial(solve_kernel, own=own),
        out_shape=jax.ShapeDtypeStruct((2 * own + 2, ny, nz), jnp.float32),
        in_specs=[vmem] * (2 + len(shapes)),
        out_specs=vmem,
        scratch_shapes=[
            held(*field(8, half)),
            held(*field(8, half + 2)),
            held(*field(8, half)),
            held(*field(8, half + 2)),
            held(*field(8, half + 2)),
            held(*field(8, half)),
            held(*field(1, half + 2)),
            held(*field(1, half + 2)),
        ],
        compiler_params=pltpu.CompilerParams(vmem_limit_bytes=12 * 1024 * 1024),
        name="solve",
    )(mine[1], theirs[1], *coefficients)
    chunk = ny // groups
    adjoint, gradient, partner, send = pl.pallas_call(
        finish_kernel,
        out_shape=[
            jax.ShapeDtypeStruct((own, ny, nz), jnp.float32),
            jax.ShapeDtypeStruct((own, chunk, nz), jnp.float32),
            jax.ShapeDtypeStruct((own, ny + chunk, nz), jnp.float32),
            jax.ShapeDtypeStruct((groups - 1, 2, own, chunk, nz), jnp.float32),
        ],
        in_specs=[vmem] * 4,
        out_specs=[vmem] * 4,
        scratch_shapes=[held(2 * own, ny, nz)],
        compiler_params=pltpu.CompilerParams(vmem_limit_bytes=4 * 1024 * 1024),
        name="finish",
    )(planes, forward_states, far, near)

    arrived = lax.ppermute(partner, "space", [(i, i ^ 1) for i in range(peers)])
    shares = []
    for k in range(1, groups):
        for side in (0, 1):
            pairs = [
                (i * peers + j, (i + k) % groups * peers + (j ^ side))
                for i in range(groups)
                for j in range(peers)
            ]
            shares.append(lax.ppermute(send[k - 1, side], ("pole", "space"), pairs))
    theirs = arrived[:, :ny]
    adjoint_states = jnp.stack(
        [jnp.where(even, adjoint, theirs), jnp.where(even, theirs, adjoint)]
    )
    adjoint_states, arrived = lax.optimization_barrier((adjoint_states, arrived))
    return adjoint_states, gradient + arrived[:, ny:] + sum(shares)


def plus_side(field, which_dim):
    extent = field.shape[which_dim]
    inner_part = lax.slice_in_dim(field, 1, extent, axis=which_dim)
    zero_plane = jnp.zeros_like(lax.slice_in_dim(field, 0, 1, axis=which_dim))
    return jnp.concatenate([inner_part, zero_plane], axis=which_dim)


def minus_side(field, which_dim):
    extent = field.shape[which_dim]
    inner_part = lax.slice_in_dim(field, 0, extent - 1, axis=which_dim)
    zero_plane = jnp.zeros_like(lax.slice_in_dim(field, 0, 1, axis=which_dim))
    return jnp.concatenate([zero_plane, inner_part], axis=which_dim)


def coarse_pick(faces, which_dim, offset):
    extent_x, extent_y, extent_z = faces.shape
    blocks = faces.reshape(extent_x // 2, 2, extent_y // 2, 2, extent_z // 2, 2)
    chosen = lax.index_in_dim(blocks, offset, axis=2 * which_dim + 1, keepdims=True)
    return jnp.sum(chosen, axis=(1, 3, 5))


def side_terms(field, plus_faces, minus_faces, widened):
    result = plus_faces[0] * (field - widened[:, 2:]) + minus_faces[0] * (field - widened[:, :-2])
    for which_dim in (1, 2):
        result = result + plus_faces[which_dim] * (field - plus_side(field, which_dim + 1))
        result = result + minus_faces[which_dim] * (field - minus_side(field, which_dim + 1))
    return result


def fine_image(field, plus_faces, minus_faces, shift_value):
    widened = extended(field, (("space", 1),), 1)
    return shift_value * field + side_terms(field, plus_faces, minus_faces, widened)


def coarse_image(field, plus_faces, minus_faces, shift_value):
    widened = extended(field, (("space", 1),), 1)
    return shift_value * field + side_terms(field, plus_faces, minus_faces, widened)


def restrict(field):
    members, extent_x, extent_y, extent_z = field.shape
    shaped = field.reshape(members, extent_x // 2, 2, extent_y // 2, 2, extent_z // 2, 2)
    return jnp.sum(shaped, axis=(2, 4, 6))


def prolong(field):
    return jnp.repeat(jnp.repeat(jnp.repeat(field, 2, axis=1), 2, axis=2), 2, axis=3)


def precondition(residual, fine, coarse):
    plus_faces, minus_faces, shift_value, diagonal = fine
    coarse_plus, coarse_minus, coarse_shift, coarse_diagonal = coarse
    smooth_one = DAMPING * residual / diagonal
    coarse_rhs = restrict(residual - fine_image(smooth_one, plus_faces, minus_faces, shift_value))
    coarse_one = DAMPING * coarse_rhs / coarse_diagonal
    coarse_two = (
        coarse_one
        + DAMPING
        * (coarse_rhs - coarse_image(coarse_one, coarse_plus, coarse_minus, coarse_shift))
        / coarse_diagonal
    )
    corrected = smooth_one + prolong(coarse_two)
    return (
        corrected
        + DAMPING
        * (residual - fine_image(corrected, plus_faces, minus_faces, shift_value))
        / diagonal
    )


def expand(values):
    return values.reshape(-1, 1, 1, 1)


def cell_sums(values):
    return jnp.sum(values, axis=(1, 2, 3))


def norm_sum(residual, precond):
    return lax.psum(cell_sums(residual * precond), "space")


def solve(rhs, fine, coarse):
    plus_faces, minus_faces, shift_value, diagonal = fine
    iterate = jnp.zeros_like(rhs)
    residual = rhs
    precond = precondition(residual, fine, coarse)
    gamma_now = norm_sum(residual, precond)
    search = precond
    for turn_index in range(ITERS):
        image_field = fine_image(search, plus_faces, minus_faces, shift_value)
        curve = lax.psum(cell_sums(search * image_field), "space")
        step_length = gamma_now / curve
        iterate = iterate + expand(step_length) * search
        if turn_index + 1 < ITERS:
            residual = residual - expand(step_length) * image_field
            precond = precondition(residual, fine, coarse)
            gamma_next = norm_sum(residual, precond)
            search = precond + expand(gamma_next / gamma_now) * search
            gamma_now = gamma_next
    return iterate


def divided(conductivity, misfit, forward_states, pole_shifts, pole_weights, pole_order):
    widened_kappa = extended(conductivity, (("space", 0),), 1)
    plus_faces = [
        0.5 * (conductivity + widened_kappa[2:]),
        0.5 * (conductivity + plus_side(conductivity, 1)),
        0.5 * (conductivity + plus_side(conductivity, 2)),
    ]
    minus_faces = [
        0.5 * (conductivity + widened_kappa[:-2]),
        0.5 * (conductivity + minus_side(conductivity, 1)),
        0.5 * (conductivity + minus_side(conductivity, 2)),
    ]
    base_diagonal = (
        plus_faces[0]
        + plus_faces[1]
        + plus_faces[2]
        + minus_faces[0]
        + minus_faces[1]
        + minus_faces[2]
    )
    coarse_plus = [coarse_pick(plus_faces[which_dim], which_dim, 1) for which_dim in range(3)]
    coarse_minus = [coarse_pick(minus_faces[which_dim], which_dim, 0) for which_dim in range(3)]
    coarse_base = (
        coarse_plus[0]
        + coarse_plus[1]
        + coarse_plus[2]
        + coarse_minus[0]
        + coarse_minus[1]
        + coarse_minus[2]
    )
    pole_index = jnp.arange(pole_shifts.shape[0], dtype=jnp.int32)
    matches = pole_order[:, None] == pole_index[None, :]
    shift_local = jnp.sum(jnp.where(matches, pole_shifts[None, :], 0.0), axis=1)
    weight_local = jnp.sum(jnp.where(matches, pole_weights[None, :], 0.0), axis=1)
    members = forward_states.shape[0]

    def solve_group(shift_part, weight_part):
        shift_value = expand(shift_part)
        fine = (plus_faces, minus_faces, shift_value, base_diagonal[None] + shift_value)
        coarse = (
            coarse_plus,
            coarse_minus,
            8.0 * shift_value,
            coarse_base[None] + 8.0 * shift_value,
        )
        return solve(expand(weight_part) * misfit[None], fine, coarse)

    adjoint_states = jnp.concatenate(
        [
            solve_group(shift_local[member : member + 1], weight_local[member : member + 1])
            for member in range(members)
        ],
        axis=0,
    )
    widened = extended(jnp.stack([adjoint_states, forward_states]), (("space", 2),), 1)
    term = (adjoint_states - widened[0, :, 2:]) * (forward_states - widened[1, :, 2:])
    term = term + (adjoint_states - widened[0, :, :-2]) * (forward_states - widened[1, :, :-2])
    for which_dim in (2, 3):
        term = term + (adjoint_states - plus_side(adjoint_states, which_dim)) * (
            forward_states - plus_side(forward_states, which_dim)
        )
        term = term + (adjoint_states - minus_side(adjoint_states, which_dim)) * (
            forward_states - minus_side(forward_states, which_dim)
        )
    local_term = -0.5 * jnp.sum(term, axis=0)
    gradient = lax.psum_scatter(local_term, "pole", scatter_dimension=1, tiled=True)
    return (adjoint_states, gradient)


def solution(mesh):
    in_specs = (
        P("space", None, None),
        P("space", None, None),
        P("pole", "space", None, None),
        P(),
        P(),
        P("pole"),
    )
    out_specs = (P("pole", "space", None, None), P("space", "pole", None))

    def body(conductivity, misfit, forward_states, *poles):
        nx = conductivity.shape[0] * lax.axis_size("space")
        _, ny, nz = conductivity.shape
        peers = lax.axis_size("space")
        small = nx * ny * nz <= REPLICATED_CELLS and forward_states.shape[:2] == (2, 2)
        if small and nz == 2 * HALF and peers > 2 and peers & (peers - 1) == 0:
            return whole_grid(conductivity, misfit, forward_states, *poles)
        return divided(conductivity, misfit, forward_states, *poles)

    return jax.shard_map(
        body, mesh=mesh, in_specs=in_specs, out_specs=out_specs, check_vma=False
    )
```
